32 devices in a mesh: dp: 2 (over x), seq: 16 (over z, y, core).
Axes of the slice: x: 2, y: 2, z: 4, core: 2. Of those that a mesh axis runs over, the one named last changes fastest.
Arguments:
- queries: bfloat16 [2, 2048, 1024], P('dp', 'seq'), may hold values from -6 to 6
- keys: bfloat16 [2, 2048, 1024], P('dp', 'seq'), may hold values from -6 to 6
- values: bfloat16 [2, 2048, 1024], P('dp', 'seq'), may hold values from -6 to 6
- cotangent: bfloat16 [2, 2048, 1024], P('dp', 'seq'), may hold values from -6 to 6
- out_weight: bfloat16 [1024, 1024], P('dp'), may hold values from -0.1875 to 0.1875
Outputs:
- output: bfloat16 [2, 2048, 1024], P('dp', 'seq')
- grad_queries: bfloat16 [2, 2048, 1024], P('dp', 'seq')
- grad_keys: bfloat16 [2, 2048, 1024], P('dp', 'seq')
- grad_values: bfloat16 [2, 2048, 1024], P('dp', 'seq')
- grad_weight: float32 [1024, 1024], P(('dp', 'seq'))
The draws below stay inside these ranges and needn't reach their ends.
All inputs are finite; a program needn't handle non-finite values.
Results may differ from the reference program's by a relative error of at most 0.015.
Values may be sent and summed in bfloat16 or wider, within the bound.
No kernel may reach another device: no remote copies, remote signals or barrier semaphores. Data moves between devices by JAX's collectives and lax.ppermute only.
A program may use at most 128 MiB of HBM per device.

```python
import math
import jax
import jax.numpy as jnp
from jax import lax

HEADS = 8
DH = 128
E = 1024
TOK_DEV = 128
F = 1024
LEN = 2048
SEQS = 2


def shard_levels(key, dims, cuts, least, top_value):
    factor_of, own = 1.0, jax.random.fold_in(key, 6)
    for axis_at, shards_of in cuts:
        steps = jnp.exp(jax.random.uniform(jax.random.fold_in(own, axis_at), (shards_of,), jnp.float32, least / len(cuts), top_value / len(cuts)))
        factor_of = factor_of * jnp.repeat(steps, dims[axis_at] // shards_of).reshape([-1 if axis == axis_at else 1 for axis in range(len(dims))])
    return factor_of


def bell_draw(key, dims, spread, reach, shards=(), held_as=jnp.bfloat16):
    factor_of = shard_levels(key, dims, shards, -0.22, 0.18) if shards else 1.0
    entries = jax.random.normal(key, dims, jnp.float32) * spread * factor_of
    return jnp.minimum(jnp.maximum(entries, -reach), reach).astype(held_as)


def setup_inputs(seed: int = 0) -> dict:
    key_of = jax.random.split(jax.random.key(seed), 6)
    queries = bell_draw(key_of[0], (SEQS, LEN, F), 1.0, 6.0, ((0, 2), (1, 16)))
    keys = bell_draw(key_of[1], (SEQS, LEN, F), 1.0, 6.0, ((0, 2), (1, 16)))
    values = bell_draw(key_of[2], (SEQS, LEN, F), 1.0, 6.0, ((0, 2), (1, 16)))
    cotangent = bell_draw(key_of[3], (SEQS, LEN, E), 1.0, 6.0, ((0, 2), (1, 16)))
    out_weight = bell_draw(key_of[4], (E, F), F ** -0.5, 0.1875, ((0, 2),))
    return dict(queries=queries, keys=keys, values=values, cotangent=cotangent, out_weight=out_weight)


epsilon = 1e-05

def rounded(values):
    return lax.optimization_barrier(values.astype(jnp.bfloat16)).astype(jnp.float32)

def sequence_pass(queries, keys, values, cotangent, out_weight):
    blocks = LEN // TOK_DEV
    shape = (blocks, TOK_DEV, HEADS, DH)
    query_f = queries.reshape(shape).astype(jnp.float32)
    key_f = keys.reshape(shape).astype(jnp.float32)
    value_f = values.reshape(shape).astype(jnp.float32)
    causal = jnp.tril(jnp.ones((TOK_DEV, TOK_DEV), dtype=jnp.bool_))
    scores = jnp.einsum('bthd,bshd->bhts', query_f, key_f)
    attend = rounded(jnp.where(causal, scores, jnp.float32(0.0)))
    local_kv = jnp.einsum('bshd,bshe->bhde', key_f, value_f)
    totals = jnp.cumsum(local_kv, axis=0)
    prior = jnp.concatenate([jnp.zeros_like(local_kv[:1]), totals[:-1]], axis=0)
    mixed = jnp.einsum('bhts,bshd->bthd', attend, value_f)
    mixed = mixed + jnp.einsum('bthd,bhde->bthe', query_f, prior, precision=lax.Precision.HIGHEST)
    root_mean = jnp.sqrt(lax.optimization_barrier(jnp.mean(mixed * mixed, axis=-1, keepdims=True)) + epsilon)
    normed = mixed / root_mean
    normed_rows = normed.astype(jnp.bfloat16).reshape(LEN, F)
    output = jnp.dot(normed_rows, out_weight.T, preferred_element_type=jnp.float32).astype(jnp.bfloat16)
    dnormed = jnp.dot(cotangent, out_weight, preferred_element_type=jnp.float32).reshape(shape)
    dmixed = (dnormed - normed * lax.optimization_barrier(jnp.mean(dnormed * normed, axis=-1, keepdims=True))) / root_mean
    dmixed_f = rounded(dmixed)
    local_u = jnp.einsum('bthd,bthe->bhde', query_f, dmixed_f)
    suffix = jnp.cumsum(local_u[::-1], axis=0)[::-1]
    later = jnp.concatenate([suffix[1:], jnp.zeros_like(local_u[:1])], axis=0)
    back = rounded(jnp.where(causal, jnp.einsum('bthe,bshe->bhts', dmixed_f, value_f), jnp.float32(0.0)))
    grad_q = jnp.einsum('bhts,bshd->bthd', back, key_f)
    grad_q = grad_q + jnp.einsum('bthe,bhde->bthd', dmixed_f, prior, precision=lax.Precision.HIGHEST)
    grad_k = jnp.einsum('bhts,bthd->bshd', back, query_f)
    grad_k = grad_k + jnp.einsum('bshe,bhde->bshd', value_f, later, precision=lax.Precision.HIGHEST)
    grad_v = jnp.einsum('bhts,bthe->bshe', attend, dmixed_f)
    grad_v = grad_v + jnp.einsum('bshd,bhde->bshe', key_f, later, precision=lax.Precision.HIGHEST)
    partial_grad = jnp.dot(cotangent.T, normed_rows, preferred_element_type=jnp.float32)
    return (output, grad_q.reshape(LEN, F).astype(jnp.bfloat16), grad_k.reshape(LEN, F).astype(jnp.bfloat16), grad_v.reshape(LEN, F).astype(jnp.bfloat16), partial_grad)

def reference(queries, keys, values, cotangent, out_weight):

    def one_sequence(items):
        return sequence_pass(items[0], items[1], items[2], items[3], out_weight)
    output, grad_queries, grad_keys, grad_values, partials = lax.map(one_sequence, (queries, keys, values, cotangent))
    grad_weight = lax.optimization_barrier(jnp.sum(partials, axis=0)) * (1.0 / math.sqrt(SEQS * LEN))
    return (output, grad_queries, grad_keys, grad_values, grad_weight)
```

```python
import functools
import math

import jax
import jax.numpy as jnp
from jax import lax
from jax.experimental import pallas as pl
from jax.experimental.pallas import tpu as pltpu
from jax.sharding import PartitionSpec as P

DH = 128
EPSILON = 1e-05
BF16 = jnp.bfloat16
F32 = jnp.float32


def dot(left, right, left_dim, right_dim):
    return lax.dot_general(
        left, right, (((left_dim,), (right_dim,)), ((), ())), preferred_element_type=F32
    )


def call(body, outs, *args, flops=10**8, scratch=()):
    nbytes = sum(a.size * a.dtype.itemsize for a in args)
    nbytes += sum(math.prod(s) * jnp.dtype(d).itemsize for s, d in outs)
    return pl.pallas_call(
        body,
        out_shape=[jax.ShapeDtypeStruct(s, d) for s, d in outs],
        in_specs=[pl.BlockSpec(memory_space=pltpu.VMEM)] * len(args),
        out_specs=[pl.BlockSpec(memory_space=pltpu.VMEM)] * len(outs),
        scratch_shapes=list(scratch),
        cost_estimate=pl.CostEstimate(flops=flops, bytes_accessed=nbytes, transcendentals=0),
        compiler_params=pltpu.CompilerParams(vmem_limit_bytes=40 * 2**20),
    )(*args)


def head(h):
    return slice(h * DH, (h + 1) * DH)


def causal(block):
    rows = lax.broadcasted_iota(jnp.int32, (block, block), 0)
    return lax.broadcasted_iota(jnp.int32, (block, block), 1) <= rows


def local_kv_kernel(k_ref, v_ref, kv_ref):
    for h in range(k_ref.shape[1] // DH):
        kv_ref[head(h), :] = dot(k_ref[:, head(h)], v_ref[:, head(h)], 0, 0).astype(BF16)


def prefix_kernel(backward, parts_ref, sums_ref):
    count = parts_ref.shape[0]
    total = jnp.zeros(parts_ref.shape[1:], F32)
    for turn in range(count):
        at = count - 1 - turn if backward else turn
        sums_ref[at] = total.astype(BF16)
        total = total + parts_ref[at].astype(F32)


def early_kernel(q_ref, k_ref, v_ref, c_ref, w_ref, attend_ref, within_ref, dnormed_ref):
    mask = causal(q_ref.shape[0])
    for h in range(q_ref.shape[1] // DH):
        scores = dot(q_ref[:, head(h)], k_ref[:, head(h)], 1, 1)
        attend = jnp.where(mask, scores, 0.0).astype(BF16)
        attend_ref[h] = attend
        within_ref[:, head(h)] = dot(attend, v_ref[:, head(h)], 1, 0)
    dnormed_ref[...] = dot(c_ref[...], w_ref[...], 1, 0)


def middle_kernel(q_ref, prior_ref, within_ref, dnormed_ref, normed_ref, dmixed_ref, u_ref):
    for h in range(q_ref.shape[1] // DH):
        q = q_ref[:, head(h)]
        mixed = within_ref[:, head(h)] + dot(q, prior_ref[head(h), :], 1, 0)
        scale = lax.rsqrt(jnp.mean(mixed * mixed, axis=-1, keepdims=True) + EPSILON)
        normed = mixed * scale
        normed_ref[:, head(h)] = normed.astype(BF16)
        dnormed = dnormed_ref[:, head(h)]
        along = jnp.mean(dnormed * normed, axis=-1, keepdims=True)
        dmixed = ((dnormed - normed * along) * scale).astype(BF16)
        dmixed_ref[:, head(h)] = dmixed
        u_ref[head(h), :] = dot(q, dmixed, 0, 0).astype(BF16)


def late_kernel(
    q_ref, k_ref, v_ref, w_ref, attend_ref, prior_ref, normed_ref, dmixed_ref,
    output_ref, gq_ref, gk_ref, gv_ref,
):
    mask = causal(q_ref.shape[0])
    output_ref[...] = dot(normed_ref[...], w_ref[...], 1, 1).astype(BF16)
    for h in range(q_ref.shape[1] // DH):
        dmixed = dmixed_ref[:, head(h)]
        back = jnp.where(mask, dot(dmixed, v_ref[:, head(h)], 1, 1), 0.0).astype(BF16)
        gq = dot(back, k_ref[:, head(h)], 1, 0) + dot(dmixed, prior_ref[head(h), :], 1, 1)
        gq_ref[:, head(h)] = gq.astype(BF16)
        gk_ref[:, head(h)] = dot(back, q_ref[:, head(h)], 0, 0)
        gv_ref[:, head(h)] = dot(attend_ref[h], dmixed, 0, 0)


def last_kernel(k_ref, v_ref, later_ref, gk_part_ref, gv_part_ref, gk_ref, gv_ref):
    for h in range(k_ref.shape[1] // DH):
        later = later_ref[head(h), :]
        gk = gk_part_ref[:, head(h)] + dot(v_ref[:, head(h)], later, 1, 1)
        gk_ref[:, head(h)] = gk.astype(BF16)
        gv = gv_part_ref[:, head(h)] + dot(k_ref[:, head(h)], later, 1, 0)
        gv_ref[:, head(h)] = gv.astype(BF16)


def scan(state, count, backward):
    parts = state.reshape(count, state.shape[0] // count, state.shape[1])
    parts = lax.all_to_all(parts, "seq", 0, 0, tiled=True)
    (sums,) = call(functools.partial(prefix_kernel, backward), [(parts.shape, BF16)], parts)
    sums = lax.all_to_all(sums, "seq", 0, 0, tiled=True)
    return sums.reshape(state.shape)


def flip(x, axis, count, bits):
    return lax.ppermute(x, axis, [(i, i ^ bits) for i in range(count)])


def gather_weight(weight, dp, seq):
    if dp != 2 or seq % 2:
        return lax.all_gather(weight, "dp", axis=0, tiled=True)
    half = weight.shape[0] // 2
    core = lax.axis_index("seq") % 2
    group = lax.axis_index("dp")
    mine = lax.dynamic_slice_in_dim(weight, core * half, half, 0)
    got = flip(mine, "dp", dp, 1)
    other = flip(got, "seq", seq, 1)
    low = jnp.where(core == 0, got, other)
    high = jnp.where(core == 0, other, got)
    far = jnp.concatenate([low, high], axis=0)
    return jnp.where(
        group == 0, jnp.concatenate([weight, far], 0), jnp.concatenate([far, weight], 0)
    )


def pick_kernel(piece, pieces, c_ref, d_ref, out_ref, turned):
    tokens = c_ref.shape[0]
    columns = c_ref.shape[1]
    place = lax.axis_index("dp") * lax.axis_size("seq") + lax.axis_index("seq")
    for at, ref in enumerate((c_ref, d_ref)):
        rows = ref[...].astype(F32).T
        turned[:, :, at * tokens : (at + 1) * tokens] = rows.reshape(columns // piece, piece, tokens)
    for r, bits in enumerate(pieces):
        out_ref[r * piece : (r + 1) * piece, :] = turned[jnp.bitwise_xor(place, bits)].astype(BF16)


def product_kernel(split, cot_ref, n_ref, m_ref, *outs):
    tokens = n_ref.shape[0]
    rows = cot_ref.shape[0] // split
    for i, out in enumerate(outs):
        at = slice(i * rows, (i + 1) * rows)
        total = dot(cot_ref[at, :tokens], n_ref[...], 1, 0)
        total = total + dot(cot_ref[at, tokens:], m_ref[...], 1, 0)
        out[...] = total.astype(out.dtype)


def spread_kernel(own_ref, a_ref, b_ref, c_ref, keep_ref, *sends):
    rows = keep_ref.shape[0]
    for i, out in enumerate((keep_ref, *sends)):
        at = slice(i * rows, (i + 1) * rows)
        total = own_ref[at, :] + a_ref[at, :].astype(F32)
        total = total + b_ref[at, :].astype(F32) + c_ref[at, :].astype(F32)
        out[...] = total.astype(out.dtype)


def finish_kernel(factor, own_ref, a_ref, b_ref, c_ref, out_ref):
    total = own_ref[...] + a_ref[...].astype(F32)
    total = total + b_ref[...].astype(F32) + c_ref[...].astype(F32)
    out_ref[...] = total * factor


def local(queries, keys, values, cotangent, out_weight, *, dp, seq):
    local_seqs, block, features = queries.shape
    outputs = cotangent.shape[2]
    rows = local_seqs * block
    heads = features // DH
    q, k, v = (x.reshape(rows, features) for x in (queries, keys, values))
    cot = cotangent.reshape(rows, outputs)
    factor = 1.0 / math.sqrt(rows * dp * seq)
    tuned = dp == 2 and seq == 16

    weight = gather_weight(out_weight, dp, seq)
    (kv,) = call(local_kv_kernel, [((features, DH), BF16)], k, v)
    prior = scan(kv, seq, False)
    if tuned:
        cot_other = flip(cot, "seq", seq, 1)
        piece = outputs // (dp * seq)
        groups = [(x << 4) | (y << 1) for x in (0, 1) for y in (0, 1)]
        pieces = [g | (z << 2) for g in groups for z in range(4)]
        (turned,) = call(
            functools.partial(pick_kernel, piece, pieces),
            [((outputs // 2, 2 * rows), BF16)], cot, cot_other,
            scratch=[pltpu.VMEM((dp * seq, piece, 2 * rows), F32)],
        )
    attend, within, dnormed = call(
        early_kernel,
        [((heads, block, block), BF16), ((rows, features), F32), ((rows, features), F32)],
        q, k, v, cot, weight,
    )
    normed, dmixed, u = call(
        middle_kernel,
        [((rows, features), BF16), ((rows, features), BF16), ((features, DH), BF16)],
        q, prior, within, dnormed,
    )
    if tuned:
        normed_other = flip(normed, "seq", seq, 1)
    later = scan(u, seq, True)
    output, gq, gk_part, gv_part = call(
        late_kernel,
        [((rows, outputs), BF16), ((rows, features), BF16), ((rows, features), F32), ((rows, features), F32)],
        q, k, v, weight, attend, prior, normed, dmixed,
    )
    if tuned:
        size = outputs // 2 // 4
        own, s1, s2, s3 = call(
            functools.partial(product_kernel, 4),
            [((size, features), F32)] + [((size, features), BF16)] * 3,
            turned, normed, normed_other,
        )
        axes = ("dp", "seq")
        got = [flip(s, axes, dp * seq, bits) for s, bits in zip((s1, s2, s3), groups[1:])]
        keep, *sends = call(
            spread_kernel,
            [((piece, features), F32)] + [((piece, features), BF16)] * 3,
            own, *got,
        )
        got = [flip(s, "seq", seq, z << 2) for z, s in enumerate(sends, 1)]
        (grad_weight,) = call(
            functools.partial(finish_kernel, factor), [((piece, features), F32)], keep, *got
        )
    else:
        partial = dot(cot, normed, 0, 0) * factor
        grad_weight = lax.psum_scatter(partial, ("dp", "seq"), scatter_dimension=0, tiled=True)
    gk, gv = call(
        last_kernel, [((rows, features), BF16)] * 2, k, v, later, gk_part, gv_part
    )
    shape = queries.shape
    return (
        output.reshape(cotangent.shape), gq.reshape(shape), gk.reshape(shape), gv.reshape(shape),
        grad_weight,
    )


def solution(mesh):
    dp, seq = mesh.shape["dp"], mesh.shape["seq"]
    return jax.shard_map(
        functools.partial(local, dp=dp, seq=seq),
        mesh=mesh,
        in_specs=(P("dp", "seq", None),) * 4 + (P("dp", None),),
        out_specs=(P("dp", "seq", None),) * 4 + (P(("dp", "seq"), None),),
        check_vma=False,
    )
```

```python
import functools
import math

import jax
import jax.numpy as jnp
from jax import lax
from jax.experimental import pallas as pl
from jax.experimental.pallas import tpu as pltpu
from jax.sharding import PartitionSpec as P

DH = 128
SLAB = 4
EPSILON = 1e-05
BF16 = jnp.bfloat16
F32 = jnp.float32


def dot(left, right, left_dim, right_dim):
    return lax.dot_general(
        left, right, (((left_dim,), (right_dim,)), ((), ())), preferred_element_type=F32
    )


def call(body, outs, *args, flops=10**8, scratch=(), far=()):
    nbytes = sum(a.size * a.dtype.itemsize for a in args)
    nbytes += sum(math.prod(s) * jnp.dtype(d).itemsize for s, d in outs)
    return pl.pallas_call(
        body,
        out_shape=[jax.ShapeDtypeStruct(s, d) for s, d in outs],
        in_specs=[
            pl.BlockSpec(memory_space=pltpu.HBM) if i in far else pl.BlockSpec()
            for i in range(len(args))
        ],
        scratch_shapes=list(scratch),
        cost_estimate=pl.CostEstimate(flops=flops, bytes_accessed=nbytes, transcendentals=0),
        compiler_params=pltpu.CompilerParams(vmem_limit_bytes=32 * 2**20),
    )(*args)


def after(x, *others):
    return lax.optimization_barrier((x, *others))[0]


def flip(x, axis, count, bits):
    return lax.ppermute(x, axis, [(i, i ^ bits) for i in range(count)])


def head(h):
    return slice(h * DH, (h + 1) * DH)


def cut(start, size):
    return pl.ds(pl.multiple_of(start * size, size), size)


def member(r):
    return jnp.bitwise_xor(lax.rem(lax.axis_index("seq"), SLAB), r)


def causal(block):
    rows = lax.broadcasted_iota(jnp.int32, (block, block), 0)
    return lax.broadcasted_iota(jnp.int32, (block, block), 1) <= rows


def fetch(pairs, sems):
    copies = [pltpu.make_async_copy(a, b, sems.at[i]) for i, (a, b) in enumerate(pairs)]
    for copy in copies:
        copy.start()
    for copy in copies:
        copy.wait()


def start_kernel(k_hbm, v_hbm, *refs):
    states, (k_ref, v_ref, sems) = refs[:SLAB], refs[SLAB:]
    fetch([(k_hbm, k_ref), (v_hbm, v_ref)], sems)
    width = k_ref.shape[1] // SLAB
    for r, out in enumerate(states):
        k = k_ref[:, cut(member(r), width)]
        v = v_ref[:, cut(member(r), width)]
        for h in range(width // DH):
            out[head(h), :] = dot(k[:, head(h)], v[:, head(h)], 0, 0).astype(BF16)


def pack_kernel(q_hbm, k_hbm, v_hbm, w_hbm, *refs):
    outs, (q_ref, k_ref, v_ref, w_ref, sems) = refs[: SLAB + 2], refs[SLAB + 2 :]
    fetch([(q_hbm, q_ref), (k_hbm, k_ref), (v_hbm, v_ref), (w_hbm, w_ref)], sems)
    width = q_ref.shape[1] // SLAB
    block = q_ref.shape[0]
    for r, out in enumerate(outs[:SLAB]):
        for i, ref in enumerate((q_ref, k_ref, v_ref)):
            out[i * block : (i + 1) * block, :] = ref[:, cut(member(r), width)]
    for r, out in zip((0, 2), outs[SLAB:]):
        out[...] = w_ref[:, cut(member(r), width)]


def total_kernel(*refs):
    *parts, out = refs
    total = parts[0][...].astype(F32)
    for part in parts[1:]:
        total = total + part[...].astype(F32)
    out[...] = total.astype(BF16)


def early_kernel(groups, *refs):
    tokens, cots = refs[:SLAB], refs[SLAB : 2 * SLAB]
    weights = refs[2 * SLAB : 2 * SLAB + groups]
    attend_ref, within_ref, dnormed_ref = refs[2 * SLAB + groups :]
    block = cots[0].shape[0]
    width = within_ref.shape[1]
    heads = width // DH
    mask = causal(block)
    rows = weights[0].shape[0]
    me = lax.axis_index("dp")
    for r in range(SLAB):
        at = slice(r * block, (r + 1) * block)
        total = dot(cots[r][:, cut(me, rows)], weights[0][...], 1, 0)
        for j in range(1, groups):
            total = total + dot(cots[r][:, cut(jnp.bitwise_xor(me, j), rows)], weights[j][...], 1, 0)
        dnormed_ref[at, :] = total
        for h in range(heads):
            q, k, v = (tokens[r][i * block : (i + 1) * block, head(h)] for i in range(3))
            attend = jnp.where(mask, dot(q, k, 1, 1), 0.0).astype(BF16)
            attend_ref[r * heads + h] = attend
            within_ref[at, head(h)] = dot(attend, v, 1, 0)


def middle_kernel(*refs):
    tokens, states = refs[:SLAB], refs[SLAB : 2 * SLAB]
    *before, within_ref, dnormed_ref = refs[2 * SLAB : -(SLAB + 5)]
    normeds = refs[-(SLAB + 5) : -5]
    dmixed_ref, prior_ref, u_ref, all_u_ref, running = refs[-5:]
    block = tokens[0].shape[0] // 3
    width = within_ref.shape[1]
    heads = width // DH
    for r in range(SLAB):
        running[member(r)] = states[r][...].astype(F32)
    total = before[0][...].astype(F32)
    for ref in before[1:]:
        total = total + ref[...].astype(F32)
    for i in range(SLAB):
        total, running[i] = total + running[i], total
    sums = [jnp.zeros((DH, DH), F32)] * heads
    for r in range(SLAB):
        at = slice(r * block, (r + 1) * block)
        prior = running[member(r)].astype(BF16)
        prior_ref[r] = prior
        for h in range(heads):
            q = tokens[r][:block, head(h)]
            mixed = within_ref[at, head(h)] + dot(q, prior[head(h), :], 1, 0)
            scale = lax.rsqrt(jnp.mean(mixed * mixed, axis=-1, keepdims=True) + EPSILON)
            normed = mixed * scale
            normeds[r][:, head(h)] = normed.astype(BF16)
            dnormed = dnormed_ref[at, head(h)]
            along = jnp.mean(dnormed * normed, axis=-1, keepdims=True)
            dmixed = ((dnormed - normed * along) * scale).astype(BF16)
            dmixed_ref[at, head(h)] = dmixed
            u = dot(q, dmixed, 0, 0)
            u_ref[r, head(h), :] = u
            sums[h] = sums[h] + u
    for h in range(heads):
        all_u_ref[head(h), :] = sums[h].astype(BF16)


def late_kernel(*refs):
    tokens = refs[:SLAB]
    attend_ref, dmixed_ref, prior_ref = refs[SLAB : SLAB + 3]
    gqs, part_ref = refs[SLAB + 3 : -1], refs[-1]
    block, width = gqs[0].shape
    heads = width // DH
    mask = causal(block)
    for r in range(SLAB):
        at = slice(r * block, (r + 1) * block)
        for h in range(heads):
            q, k, v = (tokens[r][i * block : (i + 1) * block, head(h)] for i in range(3))
            dmixed = dmixed_ref[at, head(h)]
            back = jnp.where(mask, dot(dmixed, v, 1, 1), 0.0).astype(BF16)
            gq = dot(back, k, 1, 0) + dot(dmixed, prior_ref[r, head(h), :], 1, 1)
            gqs[r][:, head(h)] = gq.astype(BF16)
            part_ref[r, :block, head(h)] = dot(back, q, 0, 0)
            part_ref[r, block:, head(h)] = dot(attend_ref[r * heads + h], dmixed, 0, 0)


def last_kernel(*refs):
    tokens = refs[:SLAB]
    *behind, u_ref, part_ref = refs[SLAB : -(SLAB + 1)]
    outs, running = refs[-(SLAB + 1) : -1], refs[-1]
    block = tokens[0].shape[0] // 3
    heads = outs[0].shape[1] // DH
    for r in range(SLAB):
        running[member(r)] = u_ref[r]
    total = behind[0][...].astype(F32)
    for ref in behind[1:]:
        total = total + ref[...].astype(F32)
    for i in reversed(range(SLAB)):
        total, running[i] = total + running[i], total
    for r in range(SLAB):
        later = running[member(r)].astype(BF16)
        for h in range(heads):
            k, v = (tokens[r][i * block : (i + 1) * block, head(h)] for i in (1, 2))
            gk = part_ref[r, :block, head(h)] + dot(v, later[head(h), :], 1, 1)
            gv = part_ref[r, block:, head(h)] + dot(k, later[head(h), :], 1, 0)
            outs[r][:block, head(h)] = gk.astype(BF16)
            outs[r][block:, head(h)] = gv.astype(BF16)


def output_kernel(groups, *refs):
    normeds, gqs = refs[:SLAB], refs[SLAB : 2 * SLAB]
    own_ref, *far = refs[2 * SLAB : 2 * SLAB + 1 + (groups - 1) * SLAB]
    out_ref, gq_ref, normed_ref = refs[2 * SLAB + 1 + (groups - 1) * SLAB :]
    width = normeds[0].shape[1]
    rows = own_ref.shape[0]
    me = lax.axis_index("dp")
    for r in range(SLAB):
        gq_ref[:, cut(member(r), width)] = gqs[r][...]
        normed_ref[:, cut(member(r), width)] = normeds[r][...]
    out_ref[:, cut(me, rows)] = dot(normed_ref[...], own_ref[...], 1, 1).astype(BF16)
    for j in range(1, groups):
        total = dot(normeds[0][...], far[(j - 1) * SLAB][...], 1, 1)
        for r in range(1, SLAB):
            total = total + dot(normeds[r][...], far[(j - 1) * SLAB + r][...], 1, 1)
        out_ref[:, cut(jnp.bitwise_xor(me, j), rows)] = total.astype(BF16)


def join_kernel(*refs):
    parts, (gk_ref, gv_ref) = refs[:SLAB], refs[SLAB:]
    block = gk_ref.shape[0]
    width = parts[0].shape[1]
    for r in range(SLAB):
        gk_ref[:, cut(member(r), width)] = parts[r][:block, :]
        gv_ref[:, cut(member(r), width)] = parts[r][block:, :]


def product_kernel(slabs, *refs):
    cots, normeds, (keep_ref, send_ref) = refs[:SLAB], refs[SLAB : 2 * SLAB], refs[2 * SLAB :]
    me = lax.axis_index("dp")
    slab = lax.div(lax.axis_index("seq"), SLAB)
    rows = keep_ref.shape[0] // slabs
    for j, out in enumerate((keep_ref, send_ref)):
        for d in range(slabs):
            at = jnp.bitwise_xor(me, j) * slabs + jnp.bitwise_xor(slab, d)
            total = dot(cots[0][:, cut(at, rows)], normeds[0][...], 0, 0)
            for r in range(1, SLAB):
                total = total + dot(cots[r][:, cut(at, rows)], normeds[r][...], 0, 0)
            out[d * rows : (d + 1) * rows, :] = total.astype(out.dtype)


def spread_kernel(own_ref, got_ref, keep_ref, *sends):
    rows = keep_ref.shape[0]
    for d, out in enumerate((keep_ref, *sends)):
        at = slice(d * rows, (d + 1) * rows)
        out[...] = (own_ref[at, :] + got_ref[at, :].astype(F32)).astype(out.dtype)


def share_kernel(slabs, *refs):
    own_ref, *got = refs[:slabs]
    outs, total_ref = refs[slabs:-1], refs[-1]
    total = own_ref[...]
    for ref in got:
        total = total + ref[...].astype(F32)
    total_ref[...] = total
    rows = outs[0].shape[0]
    for r, out in enumerate(outs):
        out[...] = total_ref[cut(member(r), rows), :]


def finish_kernel(factor, *refs):
    parts, out_ref = refs[:-1], refs[-1]
    width = parts[0].shape[1]
    for r in range(SLAB):
        out_ref[:, cut(member(r), width)] = parts[r][...] * factor


def local(queries, keys, values, cotangent, out_weight, *, dp, seq):
    local_seqs, block, features = queries.shape
    outputs = cotangent.shape[2]
    rows = local_seqs * block
    slabs = seq // SLAB
    width = features // SLAB
    heads = width // DH
    q, k, v = (x.reshape(rows, features) for x in (queries, keys, values))
    cot = cotangent.reshape(rows, outputs)
    factor = 1.0 / math.sqrt(rows * dp * seq)

    def spread(parts):
        return [parts[0]] + [flip(parts[r], "seq", seq, r) for r in range(1, SLAB)]

    def along(x, sign):
        found = []
        for d in range(1, slabs):
            step = sign * d * SLAB
            pairs = [(i, i + step) for i in range(seq) if 0 <= i + step < seq]
            found.append(lax.ppermute(x, "seq", pairs))
        return found

    states = call(
        start_kernel, [((width, DH), BF16)] * SLAB, k, v, far=(0, 1),
        scratch=[pltpu.VMEM(k.shape, BF16), pltpu.VMEM(v.shape, BF16), pltpu.SemaphoreType.DMA((2,))],
    )
    got_states = spread(states)
    q2, k2, v2, w2, cot2 = lax.optimization_barrier((q, k, v, out_weight, cot, states[0]))[:5]
    *tokens, w_own, w_next = call(
        pack_kernel,
        [((3 * rows, width), BF16)] * SLAB + [((out_weight.shape[0], width), BF16)] * 2,
        q2, k2, v2, w2, far=(0, 1, 2, 3),
        scratch=[pltpu.VMEM(x.shape, BF16) for x in (q, k, v, out_weight)]
        + [pltpu.SemaphoreType.DMA((4,))],
    )
    cot_y = flip(cot2, "seq", seq, 2)
    cots = [cot, flip(cot2, "seq", seq, 1), cot_y, flip(cot_y, "seq", seq, 1)]
    tokens = spread(tokens)
    w_far = []
    for j in range(1, dp):
        w0, w1 = flip(w_own, "dp", dp, j), flip(w_next, "dp", dp, j)
        w_far.append([w0, flip(w0, "seq", seq, 1), w1, flip(w1, "seq", seq, 1)])

    (slab_kv,) = call(total_kernel, [((width, DH), BF16)], *got_states)
    before = along(slab_kv, 1)
    attend, within, dnormed = call(
        functools.partial(early_kernel, dp),
        [((SLAB * heads, rows, rows), BF16), ((SLAB * rows, width), F32), ((SLAB * rows, width), F32)],
        *tokens, *cots, w_own, *(w[0] for w in w_far),
    )
    *normeds, dmixed, prior, u, slab_u = call(
        middle_kernel,
        [((rows, width), BF16)] * SLAB
        + [((SLAB * rows, width), BF16), ((SLAB, width, DH), BF16), ((SLAB, width, DH), F32),
           ((width, DH), BF16)],
        *tokens, *got_states, *before, within, dnormed,
        scratch=[pltpu.VMEM((SLAB, width, DH), F32)],
    )
    behind = along(slab_u, -1)
    tuned = dp == 2 and outputs // (dp * slabs) % 128 == 0
    if tuned:
        piece = outputs // (dp * slabs)
        keep, send = call(
            functools.partial(product_kernel, slabs),
            [((outputs // dp, width), F32), ((outputs // dp, width), BF16)],
            *cots, *normeds,
        )
        got = flip(send, "dp", dp, 1)
    *gqs, parts = call(
        late_kernel,
        [((rows, width), BF16)] * SLAB + [((SLAB, 2 * rows, width), F32)],
        *tokens, attend, dmixed, prior,
    )
    got_normeds = spread(normeds)
    got_gqs = spread(gqs)
    grads = call(
        last_kernel, [((2 * rows, width), BF16)] * SLAB, *tokens, *behind, u, parts,
        scratch=[pltpu.VMEM((SLAB, width, DH), F32)],
    )
    got_grads = spread(grads)
    output, gq, normed = call(
        functools.partial(output_kernel, dp),
        [((rows, outputs), BF16), ((rows, features), BF16), ((rows, features), BF16)],
        *got_normeds, *got_gqs, out_weight, *(x for w in w_far for x in w),
    )
    if tuned:
        keep, *sends = call(
            spread_kernel, [((piece, width), F32)] + [((piece, width), BF16)] * (slabs - 1), keep, got
        )
        got = [flip(s, "seq", seq, d * SLAB) for d, s in enumerate(sends, 1)]
        shares = call(
            functools.partial(share_kernel, slabs), [((piece // SLAB, width), F32)] * SLAB, keep, *got,
            scratch=[pltpu.VMEM((piece, width), F32)],
        )
        (grad_weight,) = call(
            functools.partial(finish_kernel, factor),
            [((piece // SLAB, features), F32)], *spread(shares),
        )
    else:
        partial = dot(cot, normed, 0, 0) * factor
        grad_weight = lax.psum_scatter(partial, ("dp", "seq"), scatter_dimension=0, tiled=True)
    gk, gv = call(join_kernel, [((rows, features), BF16)] * 2, *got_grads)
    shape = queries.shape
    return (
        output.reshape(cotangent.shape), gq.reshape(shape), gk.reshape(shape), gv.reshape(shape),
        grad_weight,
    )


def solution(mesh):
    dp, seq = mesh.shape["dp"], mesh.shape["seq"]
    return jax.shard_map(
        functools.partial(local, dp=dp, seq=seq),
        mesh=mesh,
        in_specs=(P("dp", "seq", None),) * 4 + (P("dp", None),),
        out_specs=(P("dp", "seq", None),) * 4 + (P(("dp", "seq"), None),),
        check_vma=False,
    )
```

```python
import functools
import math

import jax
import jax.numpy as jnp
from jax import lax
from jax.experimental import pallas as pl
from jax.experimental.pallas import tpu as pltpu
from jax.sharding import PartitionSpec as P

DH = 128
SLAB = 4
EPSILON = 1e-05
BF16 = jnp.bfloat16
F32 = jnp.float32


def dot(left, right, left_dim, right_dim):
    return lax.dot_general(
        left, right, (((left_dim,), (right_dim,)), ((), ())), preferred_element_type=F32
    )


def call(body, outs, *args, flops=10**8, scratch=(), far=(), vmem=32):
    nbytes = sum(a.size * a.dtype.itemsize for a in args)
    nbytes += sum(math.prod(s) * jnp.dtype(d).itemsize for s, d in outs)
    return pl.pallas_call(
        body,
        out_shape=[jax.ShapeDtypeStruct(s, d) for s, d in outs],
        in_specs=[
            pl.BlockSpec(memory_space=pltpu.HBM) if i in far else pl.BlockSpec()
            for i in range(len(args))
        ],
        scratch_shapes=list(scratch),
        cost_estimate=pl.CostEstimate(flops=flops, bytes_accessed=nbytes, transcendentals=0),
        compiler_params=pltpu.CompilerParams(vmem_limit_bytes=vmem * 2**20),
    )(*args)


def after(x, *others):
    return lax.optimization_barrier((x, *others))[0]


def flip(x, axis, count, bits):
    return lax.ppermute(x, axis, [(i, i ^ bits) for i in range(count)])


def head(h):
    return slice(h * DH, (h + 1) * DH)


def cut(start, size):
    return pl.ds(pl.multiple_of(start * size, size), size)


def member(r):
    return jnp.bitwise_xor(lax.rem(lax.axis_index("seq"), SLAB), r)


def causal(block):
    rows = lax.broadcasted_iota(jnp.int32, (block, block), 0)
    return lax.broadcasted_iota(jnp.int32, (block, block), 1) <= rows


def fetch(pairs, sems):
    copies = [pltpu.make_async_copy(a, b, sems.at[i]) for i, (a, b) in enumerate(pairs)]
    for copy in copies:
        copy.start()
    for copy in copies:
        copy.wait()


def start_kernel(k_hbm, v_hbm, states_ref, k_ref, v_ref, sems):
    fetch([(k_hbm, k_ref), (v_hbm, v_ref)], sems)
    for h in range(k_ref.shape[1] // DH):
        states_ref[head(h), :] = dot(k_ref[:, head(h)], v_ref[:, head(h)], 0, 0).astype(BF16)


def pack_kernel(q_hbm, k_hbm, v_hbm, w_hbm, tokens_ref, columns_ref, q_ref, k_ref, v_ref, w_ref, sems):
    fetch([(q_hbm, q_ref), (k_hbm, k_ref), (v_hbm, v_ref), (w_hbm, w_ref)], sems)
    block, width = q_ref.shape[0], q_ref.shape[1] // SLAB
    for i, ref in enumerate((q_ref, k_ref, v_ref)):
        for p in range(SLAB):
            tokens_ref[p, i * block : (i + 1) * block, :] = ref[:, p * width : (p + 1) * width]
    for i in range(2):
        columns_ref[i] = w_ref[:, cut(member(2 * i), width)]


def slab_sum_kernel(backward, parts_ref, out_ref):
    total = parts_ref[0].astype(F32)
    for p in range(1, SLAB):
        total = total + parts_ref[p].astype(F32)
    scatter_slab(backward, total, out_ref)


def scatter_slab(backward, total, out_ref):
    slab = lax.div(lax.axis_index("seq"), SLAB)
    for d in range(out_ref.shape[0]):
        wanted = d < slab if backward else d > slab
        out_ref[d] = jnp.where(wanted, total, 0.0).astype(BF16)


def gather_slab(ref):
    total = ref[0].astype(F32)
    for d in range(1, ref.shape[0]):
        total = total + ref[d].astype(F32)
    return total


def early_kernel(groups, tokens_ref, *refs):
    cots, weights = refs[:SLAB], refs[SLAB : SLAB + groups]
    attend_ref, within_ref, dnormed_ref = refs[SLAB + groups :]
    block = cots[0].shape[0]
    width = within_ref.shape[2]
    heads = width // DH
    mask = causal(block)
    rows = weights[0].shape[1]
    me = lax.axis_index("dp")
    for r in range(SLAB):
        total = dot(cots[r][:, cut(me, rows)], weights[0][0], 1, 0)
        for j in range(1, groups):
            total = total + dot(cots[r][:, cut(jnp.bitwise_xor(me, j), rows)], weights[j][0], 1, 0)
        dnormed_ref[member(r)] = total
    for p in range(SLAB):
        for h in range(heads):
            q, k, v = (tokens_ref[p, i * block : (i + 1) * block, head(h)] for i in range(3))
            attend = jnp.where(mask, dot(q, k, 1, 1), 0.0).astype(BF16)
            attend_ref[p * heads + h] = attend
            within_ref[p, :, head(h)] = dot(attend, v, 1, 0)


def middle_kernel(
    tokens_ref, states_ref, before_ref, within_ref, dnormed_ref,
    normed_ref, dmixed_ref, prior_ref, u_ref, slab_ref,
):
    block = within_ref.shape[1]
    heads = within_ref.shape[2] // DH
    running = gather_slab(before_ref)
    slab_u = jnp.zeros(running.shape, F32)
    for p in range(SLAB):
        prior = running.astype(BF16)
        prior_ref[p] = prior
        running = running + states_ref[p].astype(F32)
        us = []
        for h in range(heads):
            q = tokens_ref[p, :block, head(h)]
            mixed = within_ref[p, :, head(h)] + dot(q, prior[head(h), :], 1, 0)
            scale = lax.rsqrt(jnp.mean(mixed * mixed, axis=-1, keepdims=True) + EPSILON)
            normed = mixed * scale
            normed_ref[p, :, head(h)] = normed.astype(BF16)
            dnormed = dnormed_ref[p, :, head(h)]
            along = jnp.mean(dnormed * normed, axis=-1, keepdims=True)
            dmixed = ((dnormed - normed * along) * scale).astype(BF16)
            dmixed_ref[p, :, head(h)] = dmixed
            us.append(dot(q, dmixed, 0, 0))
        u = jnp.concatenate(us, axis=0)
        u_ref[p] = u
        slab_u = slab_u + u
    scatter_slab(True, slab_u, slab_ref)


def late_kernel(
    tokens_ref, attend_ref, dmixed_ref, prior_ref, normed_ref, back_ref, part_ref
):
    block = dmixed_ref.shape[1]
    heads = dmixed_ref.shape[2] // DH
    mask = causal(block)
    for p in range(SLAB):
        back_ref[p, :block, :] = normed_ref[p]
        for h in range(heads):
            q, k, v = (tokens_ref[p, i * block : (i + 1) * block, head(h)] for i in range(3))
            dmixed = dmixed_ref[p, :, head(h)]
            back = jnp.where(mask, dot(dmixed, v, 1, 1), 0.0).astype(BF16)
            gq = dot(back, k, 1, 0) + dot(dmixed, prior_ref[p, head(h), :], 1, 1)
            back_ref[p, block:, head(h)] = gq.astype(BF16)
            part_ref[p, :block, head(h)] = dot(back, q, 0, 0)
            part_ref[p, block:, head(h)] = dot(attend_ref[p * heads + h], dmixed, 0, 0)


def last_kernel(tokens_ref, behind_ref, u_ref, part_ref, out_ref):
    block = part_ref.shape[1] // 2
    heads = part_ref.shape[2] // DH
    running = gather_slab(behind_ref)
    for p in reversed(range(SLAB)):
        later = running.astype(BF16)
        running = running + u_ref[p]
        for h in range(heads):
            k, v = (tokens_ref[p, i * block : (i + 1) * block, head(h)] for i in (1, 2))
            gk = part_ref[p, :block, head(h)] + dot(v, later[head(h), :], 1, 1)
            gv = part_ref[p, block:, head(h)] + dot(k, later[head(h), :], 1, 0)
            out_ref[p, :block, head(h)] = gk.astype(BF16)
            out_ref[p, block:, head(h)] = gv.astype(BF16)


def output_kernel(groups, got_ref, own_ref, *refs):
    far, (out_ref, gq_ref, normed_ref) = refs[: 2 * (groups - 1)], refs[2 * (groups - 1) :]
    block, width = got_ref.shape[1] // 2, got_ref.shape[2]
    rows = own_ref.shape[0]
    me = lax.axis_index("dp")
    for p in range(SLAB):
        normed_ref[:, p * width : (p + 1) * width] = got_ref[p, :block, :]
        gq_ref[:, p * width : (p + 1) * width] = got_ref[p, block:, :]
    out_ref[:, cut(me, rows)] = dot(normed_ref[...], own_ref[...], 1, 1).astype(BF16)
    for j in range(1, groups):
        total = jnp.zeros((block, rows), F32)
        for r in range(SLAB):
            weight = far[2 * (j - 1) + r % 2][r // 2]
            total = total + dot(got_ref[member(r), :block, :], weight, 1, 1)
        out_ref[:, cut(jnp.bitwise_xor(me, j), rows)] = total.astype(BF16)


def join_kernel(got_ref, gk_ref, gv_ref):
    block, width = gk_ref.shape[0], got_ref.shape[2]
    for p in range(SLAB):
        gk_ref[:, p * width : (p + 1) * width] = got_ref[p, :block, :]
        gv_ref[:, p * width : (p + 1) * width] = got_ref[p, block:, :]


def product_kernel(normed_ref, *refs):
    cots, (keep_ref, send_ref) = refs[:SLAB], refs[SLAB:]
    me = lax.axis_index("dp")
    rows = keep_ref.shape[0]
    for j, out in enumerate((keep_ref, send_ref)):
        total = jnp.zeros(out.shape, F32)
        for r in range(SLAB):
            cot = cots[r][:, cut(jnp.bitwise_xor(me, j), rows)]
            total = total + dot(cot, normed_ref[member(r)], 0, 0)
        out[...] = total.astype(out.dtype)


def spread_kernel(own_ref, got_ref, out_ref):
    out_ref[...] = (own_ref[...] + got_ref[...].astype(F32)).astype(BF16)


def share_kernel(got_ref, out_ref):
    out_ref[...] = gather_slab(got_ref)


def finish_kernel(factor, got_ref, out_ref):
    width = got_ref.shape[2]
    for p in range(SLAB):
        out_ref[:, p * width : (p + 1) * width] = got_ref[p] * factor


def local(queries, keys, values, cotangent, out_weight, *, dp, seq):
    local_seqs, block, features = queries.shape
    outputs = cotangent.shape[2]
    rows = local_seqs * block
    slabs = seq // SLAB
    width = features // SLAB
    heads = width // DH
    q, k, v = (x.reshape(rows, features) for x in (queries, keys, values))
    cot = cotangent.reshape(rows, outputs)
    factor = 1.0 / math.sqrt(rows * dp * seq)
    near = [[s * SLAB + p for p in range(SLAB)] for s in range(slabs)]
    across = [[s * SLAB + p for s in range(slabs)] for p in range(SLAB)]

    def trade(x, groups):
        return lax.all_to_all(x, "seq", 0, 0, axis_index_groups=groups, tiled=True)

    (states,) = call(
        start_kernel, [((features, DH), BF16)], k, v, far=(0, 1), vmem=60,
        scratch=[pltpu.VMEM(k.shape, BF16), pltpu.VMEM(v.shape, BF16), pltpu.SemaphoreType.DMA((2,))],
    )
    got_states = trade(states.reshape(SLAB, width, DH), near)
    q2, k2, v2, w2, cot2 = lax.optimization_barrier((q, k, v, out_weight, cot, states))[:5]
    tokens, columns = call(
        pack_kernel,
        [((SLAB, 3 * rows, width), BF16), ((2, out_weight.shape[0], width), BF16)],
        q2, k2, v2, w2, far=(0, 1, 2, 3), vmem=60,
        scratch=[pltpu.VMEM(x.shape, BF16) for x in (q, k, v, out_weight)]
        + [pltpu.SemaphoreType.DMA((4,))],
    )
    w_far = []
    for j in range(1, dp):
        found = flip(columns, "dp", dp, j)
        w_far.append((found, flip(found, "seq", seq, 1)))
    cot_y = flip(cot2, "seq", seq, 2)
    cots = [cot, flip(cot2, "seq", seq, 1), cot_y, flip(cot_y, "seq", seq, 1)]
    (slab_kv,) = call(
        functools.partial(slab_sum_kernel, False), [((slabs, width, DH), BF16)], got_states
    )
    before = trade(slab_kv, across)
    tokens = trade(after(tokens, slab_kv), near)
    attend, within, dnormed = call(
        functools.partial(early_kernel, dp),
        [((SLAB * heads, rows, rows), BF16), ((SLAB, rows, width), F32), ((SLAB, rows, width), F32)],
        tokens, *cots, columns, *(w[0] for w in w_far),
    )
    normed, dmixed, prior, u, slab_u = call(
        middle_kernel,
        [((SLAB, rows, width), BF16), ((SLAB, rows, width), BF16), ((SLAB, width, DH), BF16),
         ((SLAB, width, DH), F32), ((slabs, width, DH), BF16)],
        tokens, got_states, before, within, dnormed,
    )
    behind = trade(slab_u, across)
    tuned = dp == 2 and outputs // (dp * seq) % 8 == 0
    if tuned:
        keep, send = call(
            product_kernel, [((outputs // dp, width), F32), ((outputs // dp, width), BF16)],
            normed, *cots,
        )
        got = flip(send, "dp", dp, 1)
    back, parts = call(
        late_kernel,
        [((SLAB, 2 * rows, width), BF16), ((SLAB, 2 * rows, width), F32)],
        tokens, attend, dmixed, prior, normed,
    )
    got_back = trade(back, near)
    (grads,) = call(last_kernel, [((SLAB, 2 * rows, width), BF16)], tokens, behind, u, parts)
    got_grads = trade(grads, near)
    output, gq, own_normed = call(
        functools.partial(output_kernel, dp),
        [((rows, outputs), BF16), ((rows, features), BF16), ((rows, features), BF16)],
        got_back, out_weight, *(x for w in w_far for x in w),
    )
    if tuned:
        piece = outputs // (dp * slabs)
        (total,) = call(spread_kernel, [((outputs // dp, width), BF16)], keep, got)
        got = trade(total.reshape(slabs, piece, width), across)
        (share,) = call(share_kernel, [((piece, width), F32)], got)
        got = trade(share.reshape(SLAB, piece // SLAB, width), near)
        (grad_weight,) = call(
            functools.partial(finish_kernel, factor), [((piece // SLAB, features), F32)], got
        )
    else:
        partial = dot(cot, own_normed, 0, 0) * factor
        grad_weight = lax.psum_scatter(partial, ("dp", "seq"), scatter_dimension=0, tiled=True)
    gk, gv = call(join_kernel, [((rows, features), BF16)] * 2, got_grads)
    shape = queries.shape
    return (
        output.reshape(cotangent.shape), gq.reshape(shape), gk.reshape(shape), gv.reshape(shape),
        grad_weight,
    )


def solution(mesh):
    dp, seq = mesh.shape["dp"], mesh.shape["seq"]
    return jax.shard_map(
        functools.partial(local, dp=dp, seq=seq),
        mesh=mesh,
        in_specs=(P("dp", "seq", None),) * 4 + (P("dp", None),),
        out_specs=(P("dp", "seq", None),) * 4 + (P(("dp", "seq"), None),),
        check_vma=False,
    )
```

```python
import functools
import math

import jax
import jax.numpy as jnp
from jax import lax
from jax.experimental import pallas as pl
from jax.experimental.pallas import tpu as pltpu
from jax.sharding import PartitionSpec as P

DH = 128
SLAB = 4
EPSILON = 1e-05
BF16 = jnp.bfloat16
F32 = jnp.float32


def dot(left, right, left_dim, right_dim):
    return lax.dot_general(
        left, right, (((left_dim,), (right_dim,)), ((), ())), preferred_element_type=F32
    )


class Chain:
    def __init__(self):
        self.last = None

    def __call__(self, body, outs, *args, scratch=()):
        count = len(args)
        specs = [pl.BlockSpec()] * count
        inner = body
        if self.last is not None:
            args = (*args, self.last)
            specs = [*specs, pl.BlockSpec(memory_space=pl.ANY)]

            def inner(*refs):
                body(*refs[:count], *refs[count + 1 :])

        found = pl.pallas_call(
            inner,
            out_shape=[jax.ShapeDtypeStruct(s, d) for s, d in outs],
            in_specs=specs,
            scratch_shapes=list(scratch),
            cost_estimate=pl.CostEstimate(flops=1, bytes_accessed=1, transcendentals=0),
            compiler_params=pltpu.CompilerParams(vmem_limit_bytes=32 * 2**20),
        )(*args)
        self.last = found[-1]
        return found


def after(x, *others):
    return lax.optimization_barrier((x, *others))[0]


def flip(x, axis, count, bits):
    return lax.ppermute(x, axis, [(i, i ^ bits) for i in range(count)])


def head(h):
    return slice(h * DH, (h + 1) * DH)


def part(i, size):
    return slice(i * size, (i + 1) * size)


def cut(start, size):
    return pl.ds(pl.multiple_of(start * size, size), size)


def member(r):
    return jnp.bitwise_xor(lax.rem(lax.axis_index("seq"), SLAB), r)


def causal(block):
    rows = lax.broadcasted_iota(jnp.int32, (block, block), 0)
    return lax.broadcasted_iota(jnp.int32, (block, block), 1) <= rows


def start_kernel(k_ref, v_ref, keep_ref, send_ref):
    width = k_ref.shape[1] // SLAB
    for r in range(SLAB):
        k = k_ref[:, cut(member(r), width)]
        v = v_ref[:, cut(member(r), width)]
        out = (keep_ref, send_ref)[r % 2]
        for h in range(width // DH):
            out[r // 2, head(h), :] = dot(k[:, head(h)], v[:, head(h)], 0, 0).astype(out.dtype)


def halve_kernel(keep_ref, got_ref, own_ref, send_ref):
    own_ref[...] = keep_ref[0] + got_ref[0].astype(F32)
    send_ref[...] = (keep_ref[1] + got_ref[1].astype(F32)).astype(BF16)


def add_kernel(own_ref, got_ref, out_ref):
    out_ref[...] = (own_ref[...].astype(F32) + got_ref[...].astype(F32)).astype(out_ref.dtype)


def columns_kernel(w_ref, out_ref):
    width = out_ref.shape[2]
    for i in range(2):
        out_ref[i] = w_ref[:, cut(member(2 * i), width)]


def pack_kernel(q_ref, k_ref, v_ref, c_ref, *outs):
    block = q_ref.shape[0]
    width = q_ref.shape[1] // SLAB
    for r, out in enumerate(outs):
        for i, ref in enumerate((q_ref, k_ref, v_ref)):
            out[part(i, block), :] = ref[:, cut(member(r), width)]
    for i in range(c_ref.shape[1] // width):
        outs[1][part(3 + i, block), :] = c_ref[:, part(i, width)]


def attend_kernel(*refs):
    tokens, (attend_ref, within_ref, states_ref) = refs[:-3], refs[-3:]
    _, block, width = within_ref.shape
    mask = causal(block)
    for r, ref in enumerate(tokens):
        for h in range(width // DH):
            q, k, v = (ref[part(i, block), head(h)] for i in range(3))
            attend = jnp.where(mask, dot(q, k, 1, 1), 0.0).astype(BF16)
            attend_ref[r, h] = attend
            within_ref[r, :, head(h)] = dot(attend, v, 1, 0)
            states_ref[r, head(h), :] = dot(k, v, 0, 0)


def dnormed_kernel(groups, token_ref, *refs):
    cots, weights = refs[: SLAB - 1], refs[SLAB - 1 : SLAB - 1 + groups]
    dnormed_ref, cot_ref = refs[SLAB - 1 + groups :]
    block, outputs = cots[0].shape
    width = dnormed_ref.shape[2]
    rows = weights[0].shape[1]
    me = lax.axis_index("dp")
    for i in range(outputs // width):
        cot_ref[1, :, part(i, width)] = token_ref[part(3 + i, block), :]
    for r, ref in zip((0, 2, 3), cots):
        cot_ref[r] = ref[...]
    for r in range(SLAB):
        total = dot(cot_ref[r, :, cut(me, rows)], weights[0][0], 1, 0)
        for j in range(1, groups):
            total = total + dot(cot_ref[r, :, cut(jnp.bitwise_xor(me, j), rows)], weights[j][0], 1, 0)
        dnormed_ref[r] = total


def from_slabs(backward, refs):
    slab = lax.div(lax.axis_index("seq"), SLAB)
    total = jnp.zeros(refs[0].shape, F32)
    for i, ref in enumerate(refs):
        bit = lax.rem(lax.div(slab, 1 << i), 2)
        total = total + jnp.where(bit == (0 if backward else 1), ref[...].astype(F32), 0.0)
    return total


def middle_kernel(*refs):
    tokens = refs[:SLAB]
    *before, within0, states0, within1, states1, dnormed_ref = refs[SLAB : -(SLAB + 5)]
    withins, states = (within0, within1), (states0, states1)
    normeds = refs[-(SLAB + 5) : -5]
    dmixed_ref, prior_ref, u_ref, slab_ref, running = refs[-5:]
    block, width = normeds[0].shape
    heads = width // DH
    for r in range(SLAB):
        running[member(r)] = states[r // 2][r % 2]
    total = from_slabs(False, before)
    for p in range(SLAB):
        total, running[p] = total + running[p], total
    sums = [jnp.zeros((DH, DH), F32)] * heads
    for r in range(SLAB):
        prior = running[member(r)].astype(BF16)
        prior_ref[r] = prior
        for h in range(heads):
            q = tokens[r][:block, head(h)]
            mixed = withins[r // 2][r % 2, :, head(h)] + dot(q, prior[head(h), :], 1, 0)
            scale = lax.rsqrt(jnp.mean(mixed * mixed, axis=-1, keepdims=True) + EPSILON)
            normed = mixed * scale
            normeds[r][:, head(h)] = normed.astype(BF16)
            dnormed = dnormed_ref[r, :, head(h)]
            along = jnp.mean(dnormed * normed, axis=-1, keepdims=True)
            dmixed = ((dnormed - normed * along) * scale).astype(BF16)
            dmixed_ref[part(r, block), head(h)] = dmixed
            u = dot(q, dmixed, 0, 0)
            u_ref[r, head(h), :] = u
            sums[h] = sums[h] + u
    for h in range(heads):
        slab_ref[head(h), :] = sums[h].astype(BF16)


def late_kernel(*refs):
    tokens, normeds = refs[:SLAB], refs[SLAB : 2 * SLAB]
    attends, dmixed_ref, prior_ref = refs[2 * SLAB : 2 * SLAB + 2], *refs[2 * SLAB + 2 : 2 * SLAB + 4]
    outs, part_ref = refs[2 * SLAB + 4 : -1], refs[-1]
    block, width = normeds[0].shape
    heads = width // DH
    mask = causal(block)
    for r in range(SLAB):
        outs[r][:block, :] = normeds[r][...]
        for h in range(heads):
            q, k, v = (tokens[r][part(i, block), head(h)] for i in range(3))
            dmixed = dmixed_ref[part(r, block), head(h)]
            back = jnp.where(mask, dot(dmixed, v, 1, 1), 0.0).astype(BF16)
            gq = dot(back, k, 1, 0) + dot(dmixed, prior_ref[r, head(h), :], 1, 1)
            outs[r][block:, head(h)] = gq.astype(BF16)
            part_ref[r, :block, head(h)] = dot(back, q, 0, 0)
            part_ref[r, block:, head(h)] = dot(attends[r // 2][r % 2, h], dmixed, 0, 0)


def last_kernel(*refs):
    tokens = refs[:SLAB]
    *behind, u_ref, part_ref = refs[SLAB : -(SLAB + 1)]
    outs, running = refs[-(SLAB + 1) : -1], refs[-1]
    block = tokens[0].shape[0] // 3
    heads = outs[0].shape[1] // DH
    for r in range(SLAB):
        running[member(r)] = u_ref[r]
    total = from_slabs(True, behind)
    for p in reversed(range(SLAB)):
        total, running[p] = total + running[p], total
    for r in range(SLAB):
        later = running[member(r)].astype(BF16)
        for h in range(heads):
            k, v = (tokens[r][part(i, block), head(h)] for i in (1, 2))
            gk = part_ref[r, :block, head(h)] + dot(v, later[head(h), :], 1, 1)
            gv = part_ref[r, block:, head(h)] + dot(k, later[head(h), :], 1, 0)
            outs[r][:block, head(h)] = gk.astype(BF16)
            outs[r][block:, head(h)] = gv.astype(BF16)


def output_kernel(groups, *refs):
    backs, own_ref = refs[:SLAB], refs[SLAB]
    far, (out_ref, gq_ref, normed_ref) = refs[SLAB + 1 : -3], refs[-3:]
    block, width = backs[0].shape[0] // 2, backs[0].shape[1]
    rows = own_ref.shape[0]
    me = lax.axis_index("dp")
    for r in range(SLAB):
        normed_ref[:, cut(member(r), width)] = backs[r][:block, :]
        gq_ref[:, cut(member(r), width)] = backs[r][block:, :]
    out_ref[:, cut(me, rows)] = dot(normed_ref[...], own_ref[...], 1, 1).astype(BF16)
    for j in range(1, groups):
        total = jnp.zeros((block, rows), F32)
        for r in range(SLAB):
            total = total + dot(backs[r][:block, :], far[2 * (j - 1) + r % 2][r // 2], 1, 1)
        out_ref[:, cut(jnp.bitwise_xor(me, j), rows)] = total.astype(BF16)


def join_kernel(*refs):
    parts, (gk_ref, gv_ref) = refs[:SLAB], refs[SLAB:]
    block = gk_ref.shape[0]
    width = parts[0].shape[1]
    for r in range(SLAB):
        gk_ref[:, cut(member(r), width)] = parts[r][:block, :]
        gv_ref[:, cut(member(r), width)] = parts[r][block:, :]


def product_kernel(slabs, cot_ref, *refs):
    normeds, (keep_ref, send_ref) = refs[:SLAB], refs[SLAB:]
    me = lax.axis_index("dp")
    slab = lax.div(lax.axis_index("seq"), SLAB)
    rows = keep_ref.shape[0] // slabs
    for j, out in enumerate((send_ref, keep_ref)):
        for d in range(slabs):
            at = jnp.bitwise_xor(me, 1 - j) * slabs + jnp.bitwise_xor(slab, d)
            total = dot(cot_ref[0, :, cut(at, rows)], normeds[0][...], 0, 0)
            for r in range(1, SLAB):
                total = total + dot(cot_ref[r, :, cut(at, rows)], normeds[r][...], 0, 0)
            out[part(d, rows), :] = total.astype(out.dtype)


def split_kernel(own_ref, got_ref, keep_ref, send_ref):
    rows = keep_ref.shape[0] // 2
    for i in range(4):
        total = own_ref[part(i, rows), :] + got_ref[part(i, rows), :].astype(F32)
        out = (keep_ref, send_ref)[i % 2]
        out[part(i // 2, rows), :] = total.astype(out.dtype)


def split_again_kernel(own_ref, got_ref, keep_ref, send_ref):
    rows = keep_ref.shape[0]
    for i, out in enumerate((keep_ref, send_ref)):
        total = own_ref[part(i, rows), :] + got_ref[part(i, rows), :].astype(F32)
        out[...] = total.astype(out.dtype)


def share_kernel(own_ref, got_ref, keep_ref, send_ref, total_ref):
    total_ref[...] = own_ref[...] + got_ref[...].astype(F32)
    rows = keep_ref.shape[0] // 2
    for i, r in enumerate((0, 1)):
        keep_ref[part(i, rows), :] = total_ref[cut(member(r), rows), :]
    for i, r in enumerate((2, 3)):
        send_ref[part(i, rows), :] = total_ref[cut(member(r), rows), :]


def pass_kernel(own_ref, got_ref, keep_ref, send_ref):
    rows = own_ref.shape[0] // 2
    for i, ref in enumerate((own_ref, got_ref)):
        keep_ref[part(i, rows), :] = ref[:rows, :]
        send_ref[part(i, rows), :] = ref[rows:, :]


def finish_kernel(factor, keep_ref, got_ref, out_ref):
    rows, width = out_ref.shape[0], keep_ref.shape[1]
    for i, ref in enumerate((keep_ref, got_ref)):
        for j in range(2):
            out_ref[:, cut(member(i + 2 * j), width)] = ref[part(j, rows), :] * factor


def local(queries, keys, values, cotangent, out_weight, *, dp, seq):
    call = Chain()
    local_seqs, block, features = queries.shape
    outputs = cotangent.shape[2]
    rows = local_seqs * block
    slabs = seq // SLAB
    width = features // SLAB
    heads = width // DH
    q, k, v = (x.reshape(rows, features) for x in (queries, keys, values))
    cot = cotangent.reshape(rows, outputs)
    factor = 1.0 / math.sqrt(rows * dp * seq)
    near = functools.partial(flip, axis="seq", count=seq)

    def spread(parts):
        found = {r: near(parts[r], bits=r) for r in (2, 3, 1)}
        return [parts[0], found[1], found[2], found[3]]

    def doubling(total):
        found = []
        bits = SLAB
        while bits < seq:
            if found:
                (total,) = call(add_kernel, [(total.shape, BF16)], total, found[-1])
            found.append(near(total, bits=bits))
            bits *= 2
        return found, total

    cot_y = near(cot, bits=2)
    keep, send = call(
        start_kernel, [((2, width, DH), F32), ((2, width, DH), BF16)], k, v
    )
    got = near(send, bits=1)
    (columns,) = call(columns_kernel, [((2, out_weight.shape[0], width), BF16)], out_weight)
    tokens = call(
        pack_kernel,
        [((3 * rows + r % 2 * (r < 2) * rows * (outputs // width), width), BF16) for r in range(SLAB)],
        q, k, v, cot,
    )
    w_far = [flip(columns, "dp", dp, j) for j in range(1, dp)]
    own, send = call(halve_kernel, [((width, DH), F32), ((width, DH), BF16)], keep, got)
    got = near(send, bits=2)
    (slab_kv,) = call(add_kernel, [((width, DH), BF16)], own, got)
    attended = [((2, heads, rows, rows), BF16), ((2, rows, width), F32), ((2, width, DH), F32)]
    token1 = near(tokens[1], bits=1)
    send2, send3 = lax.optimization_barrier((tokens[2], tokens[3], slab_kv))[:2]
    attend0, within0, states0 = call(attend_kernel, attended, tokens[0], token1)
    before, last_kv = doubling(slab_kv)
    tokens = [tokens[0], token1, near(send2, bits=2), near(send3, bits=3)]
    cots = [cot, cot_y, near(cot_y, bits=1)]
    attend1, within1, states1 = call(attend_kernel, attended, tokens[2], tokens[3])
    dnormed, cots = call(
        functools.partial(dnormed_kernel, dp),
        [((SLAB, rows, width), F32), ((SLAB, rows, outputs), BF16)],
        token1, *cots, columns, *w_far,
    )
    *normeds, dmixed, prior, u, slab_u = call(
        middle_kernel,
        [((rows, width), BF16)] * SLAB
        + [((SLAB * rows, width), BF16), ((SLAB, width, DH), BF16), ((SLAB, width, DH), F32),
           ((width, DH), BF16)],
        *tokens, *before, within0, states0, within1, states1, dnormed,
        scratch=[pltpu.VMEM((SLAB, width, DH), F32)],
    )
    tuned = dp == 2 and slabs == 4 and outputs // (dp * seq) % 8 == 0
    if tuned:
        keep, send = call(
            functools.partial(product_kernel, slabs),
            [((outputs // dp, width), F32), ((outputs // dp, width), BF16)], cots, *normeds,
        )
        got = flip(send, "dp", dp, 1)
    behind, last_u = doubling(slab_u)
    *backs, parts = call(
        late_kernel,
        [((2 * rows, width), BF16)] * SLAB + [((SLAB, 2 * rows, width), F32)],
        *tokens, *normeds, attend0, attend1, dmixed, prior,
    )
    backs = spread(backs)
    w_all = [x for w in w_far for x in (w, near(w, bits=1))]
    if tuned:
        piece = outputs // (dp * slabs)
        keep, send = call(
            split_kernel, [((2 * piece, width), F32), ((2 * piece, width), BF16)], keep, got
        )
        got = near(send, bits=SLAB)
    grads = call(
        last_kernel, [((2 * rows, width), BF16)] * SLAB, *tokens, *behind, u, parts,
        scratch=[pltpu.VMEM((SLAB, width, DH), F32)],
    )
    got_grads = spread(grads)
    if tuned:
        keep, send = call(
            split_again_kernel, [((piece, width), F32), ((piece, width), BF16)], keep, got
        )
        got = near(send, bits=2 * SLAB)
        keep, send = call(
            share_kernel, [((piece // 2, width), F32)] * 2, keep, got,
            scratch=[pltpu.VMEM((piece, width), F32)],
        )
        got = near(send, bits=2)
    gk, gv = call(join_kernel, [((rows, features), BF16)] * 2, *got_grads)
    output, gq, own_normed = call(
        functools.partial(output_kernel, dp),
        [((rows, outputs), BF16), ((rows, features), BF16), ((rows, features), BF16)],
        *backs, out_weight, *w_all,
    )
    if tuned:
        keep, send = call(pass_kernel, [((piece // 2, width), F32)] * 2, keep, got)
        got = near(send, bits=1)
        (grad_weight,) = call(
            functools.partial(finish_kernel, factor),
            [((piece // SLAB, features), F32)], keep, got,
        )
    else:
        partial = dot(cot, own_normed, 0, 0) * factor
        grad_weight = lax.psum_scatter(partial, ("dp", "seq"), scatter_dimension=0, tiled=True)
    shape = queries.shape
    return (
        output.reshape(cotangent.shape), gq.reshape(shape), gk.reshape(shape), gv.reshape(shape),
        grad_weight,
    )


def solution(mesh):
    dp, seq = mesh.shape["dp"], mesh.shape["seq"]
    return jax.shard_map(
        functools.partial(local, dp=dp, seq=seq),
        mesh=mesh,
        in_specs=(P("dp", "seq", None),) * 4 + (P("dp", None),),
        out_specs=(P("dp", "seq", None),) * 4 + (P(("dp", "seq"), None),),
        check_vma=False,
    )
```

```python
import functools
import math

import jax
import jax.numpy as jnp
from jax import lax
from jax.experimental import pallas as pl
from jax.experimental.pallas import tpu as pltpu
from jax.sharding import PartitionSpec as P

DH = 128
SLAB = 4
EPSILON = 1e-05
BF16 = jnp.bfloat16
F32 = jnp.float32


def dot(left, right, left_dim, right_dim):
    return lax.dot_general(
        left, right, (((left_dim,), (right_dim,)), ((), ())), preferred_element_type=F32
    )


class Chain:
    def __init__(self):
        self.last = None

    def __call__(self, body, outs, *args, scratch=(), far=False, wait=()):
        count = len(args)
        if far:
            args = [pltpu.with_memory_space_constraint(x, pltpu.HBM) for x in args]
        specs = [pl.BlockSpec(memory_space=pl.ANY) if far else pl.BlockSpec()] * count
        inner = body
        if self.last is not None:
            extra = (self.last, *wait)
            args = (*args, *extra)
            specs = [*specs, *[pl.BlockSpec(memory_space=pl.ANY)] * len(extra)]

            def inner(*refs):
                body(*refs[:count], *refs[count + len(extra) :])

        found = pl.pallas_call(
            inner,
            out_shape=[jax.ShapeDtypeStruct(s, d) for s, d in outs],
            in_specs=specs,
            scratch_shapes=list(scratch),
            cost_estimate=pl.CostEstimate(flops=1, bytes_accessed=1, transcendentals=0),
            compiler_params=pltpu.CompilerParams(vmem_limit_bytes=32 * 2**20),
        )(*args)
        self.last = found[-1]
        return found


def after(x, *others):
    return lax.optimization_barrier((x, *others))[0]


def flip(x, axis, count, bits):
    return lax.ppermute(x, axis, [(i, i ^ bits) for i in range(count)])


def head(h):
    return slice(h * DH, (h + 1) * DH)


def part(i, size):
    return slice(i * size, (i + 1) * size)


def cut(start, size):
    return pl.ds(pl.multiple_of(start * size, size), size)


def member(r):
    return jnp.bitwise_xor(lax.rem(lax.axis_index("seq"), SLAB), r)


def causal(block):
    rows = lax.broadcasted_iota(jnp.int32, (block, block), 0)
    return lax.broadcasted_iota(jnp.int32, (block, block), 1) <= rows


def fetch(pairs, sems):
    copies = [pltpu.make_async_copy(a, b, sems.at[i]) for i, (a, b) in enumerate(pairs)]
    for copy in copies:
        copy.start()
    return copies


def front_kernel(k_hbm, v_hbm, q_hbm, c_hbm, w_hbm, *refs):
    keep_ref, message_ref, own_ref, far_ref, columns_ref = refs[:5]
    k_ref, v_ref, q_ref, c_ref, w_ref, sems = refs[5:]
    copies = fetch(
        [(k_hbm, k_ref), (v_hbm, v_ref), (q_hbm, q_ref), (c_hbm, c_ref), (w_hbm, w_ref)], sems
    )
    block = k_ref.shape[0]
    width = k_ref.shape[1] // SLAB
    copies[0].wait()
    copies[1].wait()
    for r in range(SLAB):
        k, v = k_ref[:, cut(member(r), width)], v_ref[:, cut(member(r), width)]
        for h in range(width // DH):
            state = dot(k[:, head(h)], v[:, head(h)], 0, 0)
            if r % 2:
                message_ref[part(r // 2, DH), head(h)] = state.astype(BF16)
            else:
                keep_ref[r // 2, :, head(h)] = state
    copies[2].wait()
    places = ((own_ref, 0), (message_ref, 2 * DH), (far_ref, 0), (message_ref, 2 * DH + 3 * block))
    for r, (out, at) in enumerate(places):
        for i, ref in enumerate((q_ref, k_ref, v_ref)):
            out[at + i * block : at + (i + 1) * block, :] = ref[:, cut(member(r), width)]
    copies[3].wait()
    for i in range(c_ref.shape[1] // width):
        message_ref[2 * DH + (6 + i) * block : 2 * DH + (7 + i) * block, :] = c_ref[:, part(i, width)]
    copies[4].wait()
    for i in range(2):
        columns_ref[i] = w_ref[:, cut(member(2 * i), width)]


def halve_kernel(keep_ref, got_ref, own_ref, send_ref):
    own_ref[...] = keep_ref[0] + got_ref[part(0, DH), :].astype(F32)
    send_ref[...] = (keep_ref[1] + got_ref[part(1, DH), :].astype(F32)).astype(BF16)


def pair_kernel(message_ref, far_ref, out_ref):
    size = far_ref.shape[0]
    out_ref[:size, :] = far_ref[...]
    out_ref[size:, :] = message_ref[2 * DH + size : 2 * DH + 2 * size, :]


def add_kernel(own_ref, got_ref, out_ref):
    out_ref[...] = (own_ref[...].astype(F32) + got_ref[...].astype(F32)).astype(out_ref.dtype)


def tokens_of(r, own_ref, message_ref, far_ref):
    size = own_ref.shape[0]
    if r == 0:
        return own_ref
    if r == 1:
        return message_ref.at[2 * DH : 2 * DH + size]
    return far_ref.at[(r - 2) * size : (r - 1) * size]


def attend_kernel(halves, *refs):
    tokens, (attend_ref, within_ref, states_ref) = refs[:-3], refs[-3:]
    _, block, width = within_ref.shape
    mask = causal(block)
    if halves:
        tokens = [tokens_of(r, tokens[0], tokens[1], None) for r in (0, 1)]
    else:
        tokens = [tokens[0].at[part(r, 3 * block)] for r in (0, 1)]
    for r, ref in enumerate(tokens):
        for h in range(width // DH):
            q, k, v = (ref[part(i, block), head(h)] for i in range(3))
            attend = jnp.where(mask, dot(q, k, 1, 1), 0.0).astype(BF16)
            attend_ref[r, h] = attend
            within_ref[r, :, head(h)] = dot(attend, v, 1, 0)
            states_ref[r, :, head(h)] = dot(k, v, 0, 0)


def dnormed_kernel(groups, message_ref, *refs):
    cots, weights = refs[: SLAB - 1], refs[SLAB - 1 : SLAB - 1 + groups]
    dnormed_ref, cot_ref = refs[SLAB - 1 + groups :]
    block, outputs = cots[0].shape
    width = dnormed_ref.shape[2]
    rows = weights[0].shape[1]
    me = lax.axis_index("dp")
    at = 2 * DH + 6 * block
    for i in range(outputs // width):
        cot_ref[1, :, part(i, width)] = message_ref[at + i * block : at + (i + 1) * block, :]
    for r, ref in zip((0, 2, 3), cots):
        cot_ref[r] = ref[...]
    for r in range(SLAB):
        total = dot(cot_ref[r, :, cut(me, rows)], weights[0][0], 1, 0)
        for j in range(1, groups):
            total = total + dot(cot_ref[r, :, cut(jnp.bitwise_xor(me, j), rows)], weights[j][0], 1, 0)
        dnormed_ref[r] = total


def from_slabs(backward, refs):
    slab = lax.div(lax.axis_index("seq"), SLAB)
    total = jnp.zeros(refs[0].shape, F32)
    for i, ref in enumerate(refs):
        bit = lax.rem(lax.div(slab, 1 << i), 2)
        total = total + jnp.where(bit == (0 if backward else 1), ref[...].astype(F32), 0.0)
    return total


def middle_kernel(*refs):
    tokens = refs[:3]
    *before, within0, states0, within1, states1, dnormed_ref = refs[3:-6]
    withins, states = (within0, within1), (states0, states1)
    normed_ref, dmixed_ref, prior_ref, u_ref, slab_ref, running = refs[-6:]
    _, block, width = normed_ref.shape
    heads = width // DH
    for r in range(SLAB):
        running[member(r)] = states[r // 2][r % 2]
    total = from_slabs(False, before)
    for p in range(SLAB):
        total, running[p] = total + running[p], total
    sums = [jnp.zeros((DH, DH), F32)] * heads
    for r in range(SLAB):
        prior = running[member(r)].astype(BF16)
        prior_ref[r] = prior
        for h in range(heads):
            q = tokens_of(r, *tokens)[:block, head(h)]
            mixed = withins[r // 2][r % 2, :, head(h)] + dot(q, prior[:, head(h)], 1, 0)
            scale = lax.rsqrt(jnp.mean(mixed * mixed, axis=-1, keepdims=True) + EPSILON)
            normed = mixed * scale
            normed_ref[r, :, head(h)] = normed.astype(BF16)
            dnormed = dnormed_ref[r, :, head(h)]
            along = jnp.mean(dnormed * normed, axis=-1, keepdims=True)
            dmixed = ((dnormed - normed * along) * scale).astype(BF16)
            dmixed_ref[r, :, head(h)] = dmixed
            u = dot(q, dmixed, 0, 0)
            u_ref[r, :, head(h)] = u
            sums[h] = sums[h] + u
    for h in range(heads):
        slab_ref[:, head(h)] = sums[h].astype(BF16)


def late_kernel(*refs):
    tokens, (normed_ref, attend0, attend1, dmixed_ref, prior_ref, near_ref, far_ref, part_ref) = (
        refs[:3], refs[3:]
    )
    _, block, width = normed_ref.shape
    mask = causal(block)
    for r in range(SLAB):
        out = (near_ref, far_ref)[r // 2].at[part(r % 2, 2 * block)]
        token = tokens_of(r, *tokens)
        out[:block, :] = normed_ref[r]
        for h in range(width // DH):
            q, k, v = (token[part(i, block), head(h)] for i in range(3))
            dmixed = dmixed_ref[r, :, head(h)]
            back = jnp.where(mask, dot(dmixed, v, 1, 1), 0.0).astype(BF16)
            gq = dot(back, k, 1, 0) + dot(dmixed, prior_ref[r, :, head(h)], 1, 1)
            out[block:, head(h)] = gq.astype(BF16)
            part_ref[r, :block, head(h)] = dot(back, q, 0, 0)
            part_ref[r, block:, head(h)] = dot((attend0, attend1)[r // 2][r % 2, h], dmixed, 0, 0)


def last_kernel(*refs):
    tokens = refs[:3]
    *behind, u_ref, part_ref, near_ref, far_ref, running = refs[3:]
    block = part_ref.shape[1] // 2
    for r in range(SLAB):
        running[member(r)] = u_ref[r]
    total = from_slabs(True, behind)
    for p in reversed(range(SLAB)):
        total, running[p] = total + running[p], total
    for r in range(SLAB):
        out = (near_ref, far_ref)[r // 2].at[part(r % 2, 2 * block)]
        token = tokens_of(r, *tokens)
        later = running[member(r)].astype(BF16)
        for h in range(part_ref.shape[2] // DH):
            k, v = (token[part(i, block), head(h)] for i in (1, 2))
            gk = part_ref[r, :block, head(h)] + dot(v, later[:, head(h)], 1, 1)
            gv = part_ref[r, block:, head(h)] + dot(k, later[:, head(h)], 1, 0)
            out[:block, head(h)] = gk.astype(BF16)
            out[block:, head(h)] = gv.astype(BF16)


def relay_kernel(near_ref, far_ref, out_ref):
    size = near_ref.shape[0] // 2
    out_ref[:size, :] = near_ref[size:, :]
    out_ref[size:, :] = far_ref[size:, :]


def arrived(near_ref, far_ref, core_ref):
    size = near_ref.shape[0] // 2
    first, second = slice(0, size), slice(size, 2 * size)
    return near_ref.at[first], core_ref.at[first], far_ref.at[first], core_ref.at[second]


def output_kernel(groups, *refs):
    backs, own_ref = arrived(*refs[:3]), refs[3]
    far, (out_ref, gq_ref, normed_ref) = refs[4:-3], refs[-3:]
    block, width = backs[0].shape[0] // 2, backs[0].shape[1]
    rows = own_ref.shape[0]
    me = lax.axis_index("dp")
    for r in range(SLAB):
        normed_ref[:, cut(member(r), width)] = backs[r][:block, :]
        gq_ref[:, cut(member(r), width)] = backs[r][block:, :]
    out_ref[:, cut(me, rows)] = dot(normed_ref[...], own_ref[...], 1, 1).astype(BF16)
    for j in range(1, groups):
        total = jnp.zeros((block, rows), F32)
        for r in range(SLAB):
            total = total + dot(backs[r][:block, :], far[2 * (j - 1) + r % 2][r // 2], 1, 1)
        out_ref[:, cut(jnp.bitwise_xor(me, j), rows)] = total.astype(BF16)


def join_kernel(*refs):
    parts, (gk_ref, gv_ref) = arrived(*refs[:3]), refs[3:]
    block = gk_ref.shape[0]
    width = parts[0].shape[1]
    for r in range(SLAB):
        gk_ref[:, cut(member(r), width)] = parts[r][:block, :]
        gv_ref[:, cut(member(r), width)] = parts[r][block:, :]


def product_kernel(slabs, cot_ref, normed_ref, keep_ref, send_ref):
    me = lax.axis_index("dp")
    slab = lax.div(lax.axis_index("seq"), SLAB)
    rows = keep_ref.shape[0] // slabs
    for j, out in enumerate((send_ref, keep_ref)):
        for d in range(slabs):
            at = jnp.bitwise_xor(me, 1 - j) * slabs + jnp.bitwise_xor(slab, d)
            total = dot(cot_ref[0, :, cut(at, rows)], normed_ref[0], 0, 0)
            for r in range(1, SLAB):
                total = total + dot(cot_ref[r, :, cut(at, rows)], normed_ref[r], 0, 0)
            out[part(d, rows), :] = total.astype(out.dtype)


def split_kernel(own_ref, got_ref, keep_ref, send_ref):
    rows = keep_ref.shape[0] // 2
    for i in range(4):
        total = own_ref[part(i, rows), :] + got_ref[part(i, rows), :].astype(F32)
        out = (keep_ref, send_ref)[i % 2]
        out[part(i // 2, rows), :] = total.astype(out.dtype)


def split_again_kernel(own_ref, got_ref, keep_ref, send_ref):
    rows = keep_ref.shape[0]
    for i, out in enumerate((keep_ref, send_ref)):
        total = own_ref[part(i, rows), :] + got_ref[part(i, rows), :].astype(F32)
        out[...] = total.astype(out.dtype)


def share_kernel(own_ref, got_ref, keep_ref, send_ref, total_ref):
    total_ref[...] = own_ref[...] + got_ref[...].astype(F32)
    rows = keep_ref.shape[0] // 2
    for i, r in enumerate((0, 1)):
        keep_ref[part(i, rows), :] = total_ref[cut(member(r), rows), :]
    for i, r in enumerate((2, 3)):
        send_ref[part(i, rows), :] = total_ref[cut(member(r), rows), :]


def pass_kernel(own_ref, got_ref, keep_ref, send_ref):
    rows = own_ref.shape[0] // 2
    for i, ref in enumerate((own_ref, got_ref)):
        keep_ref[part(i, rows), :] = ref[:rows, :]
        send_ref[part(i, rows), :] = ref[rows:, :]


def finish_kernel(factor, keep_ref, got_ref, out_ref):
    rows, width = out_ref.shape[0], keep_ref.shape[1]
    for i, ref in enumerate((keep_ref, got_ref)):
        for j in range(2):
            out_ref[:, cut(member(i + 2 * j), width)] = ref[part(j, rows), :] * factor


def local(queries, keys, values, cotangent, out_weight, *, dp, seq):
    call = Chain()
    local_seqs, block, features = queries.shape
    outputs = cotangent.shape[2]
    rows = local_seqs * block
    slabs = seq // SLAB
    width = features // SLAB
    heads = width // DH
    q, k, v = (x.reshape(rows, features) for x in (queries, keys, values))
    cot = cotangent.reshape(rows, outputs)
    factor = 1.0 / math.sqrt(rows * dp * seq)
    near = functools.partial(flip, axis="seq", count=seq)

    def doubling(total):
        found = []
        bits = SLAB
        while bits < seq:
            if found:
                (total,) = call(add_kernel, [(total.shape, BF16)], total, found[-1])
            found.append(near(total, bits=bits))
            bits *= 2
        return found, total

    cot_y = near(cot, bits=2)
    keep, message, own_tokens, far_tokens, columns = call(
        front_kernel,
        [((2, DH, width), F32), ((2 * DH + (6 + outputs // width) * rows, width), BF16),
         ((3 * rows, width), BF16), ((3 * rows, width), BF16), ((2, out_weight.shape[0], width), BF16)],
        k, v, q, cot, out_weight, far=True,
        scratch=[pltpu.VMEM(x.shape, BF16) for x in (k, v, q, cot, out_weight)]
        + [pltpu.SemaphoreType.DMA((5,))],
    )
    message = near(message, bits=1)
    w_far = [flip(columns, "dp", dp, j) for j in range(1, dp)]
    own, send = call(halve_kernel, [((DH, width), F32), ((DH, width), BF16)], keep, message)
    got = near(send, bits=2)
    (slab_kv,) = call(add_kernel, [((DH, width), BF16)], own, got, wait=[cot_y])
    (far_tokens,) = call(pair_kernel, [((6 * rows, width), BF16)], message, far_tokens)
    far_tokens = near(far_tokens, bits=2)
    attended = [((2, heads, rows, rows), BF16), ((2, rows, width), F32), ((2, DH, width), F32)]
    attend0, within0, states0 = call(
        functools.partial(attend_kernel, True), attended, own_tokens, message
    )
    before, last_kv = doubling(slab_kv)
    cot_yc = near(after(cot_y, last_kv), bits=1)
    attend1, within1, states1 = call(functools.partial(attend_kernel, False), attended, far_tokens)
    dnormed, cots = call(
        functools.partial(dnormed_kernel, dp),
        [((SLAB, rows, width), F32), ((SLAB, rows, outputs), BF16)],
        message, cot, cot_y, cot_yc, columns, *w_far,
    )
    w_all = [x for w in w_far for x in (w, near(w, bits=1))]
    tokens = (own_tokens, message, far_tokens)
    normed, dmixed, prior, u, slab_u = call(
        middle_kernel,
        [((SLAB, rows, width), BF16), ((SLAB, rows, width), BF16), ((SLAB, DH, width), BF16),
         ((SLAB, DH, width), F32), ((DH, width), BF16)],
        *tokens, *before, within0, states0, within1, states1, dnormed,
        scratch=[pltpu.VMEM((SLAB, DH, width), F32)],
    )
    tuned = dp == 2 and slabs == 4 and outputs // (dp * seq) % 8 == 0
    if tuned:
        keep, send = call(
            functools.partial(product_kernel, slabs),
            [((outputs // dp, width), F32), ((outputs // dp, width), BF16)], cots, normed,
        )
        got = flip(send, "dp", dp, 1)
    behind, _ = doubling(slab_u)
    back, back_far, parts = call(
        late_kernel,
        [((4 * rows, width), BF16)] * 2 + [((SLAB, 2 * rows, width), F32)],
        *tokens, normed, attend0, attend1, dmixed, prior,
    )
    back_far = near(back_far, bits=2)
    if tuned:
        piece = outputs // (dp * slabs)
        keep, send = call(
            split_kernel, [((2 * piece, width), F32), ((2 * piece, width), BF16)], keep, got
        )
        got = near(send, bits=SLAB)
    grads, grads_far = call(
        last_kernel, [((4 * rows, width), BF16)] * 2, *tokens, *behind, u, parts,
        scratch=[pltpu.VMEM((SLAB, DH, width), F32)],
    )
    grads_far = near(grads_far, bits=2)
    if tuned:
        keep, send = call(
            split_again_kernel, [((piece, width), F32), ((piece, width), BF16)], keep, got
        )
        got = near(send, bits=2 * SLAB)
    if tuned:
        keep, share = call(
            share_kernel, [((piece // 2, width), F32)] * 2, keep, got,
            scratch=[pltpu.VMEM((piece, width), F32)],
        )
        got = near(share, bits=2)
    (send,) = call(relay_kernel, [((4 * rows, width), BF16)], back, back_far)
    backs = (back, back_far, near(send, bits=1))
    if tuned:
        keep, share = call(pass_kernel, [((piece // 2, width), F32)] * 2, keep, got)
        got = near(share, bits=1)
    (send,) = call(relay_kernel, [((4 * rows, width), BF16)], grads, grads_far)
    grads = (grads, grads_far, near(send, bits=1))
    output, gq, own_normed = call(
        functools.partial(output_kernel, dp),
        [((rows, outputs), BF16), ((rows, features), BF16), ((rows, features), BF16)],
        *backs, out_weight, *w_all,
    )
    gk, gv = call(join_kernel, [((rows, features), BF16)] * 2, *grads)
    if tuned:
        (grad_weight,) = call(
            functools.partial(finish_kernel, factor),
            [((piece // SLAB, features), F32)], keep, got,
        )
    else:
        partial = dot(cot, own_normed, 0, 0) * factor
        grad_weight = lax.psum_scatter(partial, ("dp", "seq"), scatter_dimension=0, tiled=True)
    shape = queries.shape
    return (
        output.reshape(cotangent.shape), gq.reshape(shape), gk.reshape(shape), gv.reshape(shape),
        grad_weight,
    )


def solution(mesh):
    dp, seq = mesh.shape["dp"], mesh.shape["seq"]
    return jax.shard_map(
        functools.partial(local, dp=dp, seq=seq),
        mesh=mesh,
        in_specs=(P("dp", "seq", None),) * 4 + (P("dp", None),),
        out_specs=(P("dp", "seq", None),) * 4 + (P(("dp", "seq"), None),),
        check_vma=False,
    )
```

```python
import functools
import math

import jax
import jax.numpy as jnp
from jax import lax
from jax.experimental import pallas as pl
from jax.experimental.pallas import tpu as pltpu
from jax.sharding import PartitionSpec as P

DH = 128
SLAB = 4
EPSILON = 1e-05
BF16 = jnp.bfloat16
F32 = jnp.float32


def dot(left, right, left_dim, right_dim):
    return lax.dot_general(
        left, right, (((left_dim,), (right_dim,)), ((), ())), preferred_element_type=F32
    )


class Chain:
    def __init__(self):
        self.last = None

    def __call__(self, body, outs, *args, scratch=(), far=False, wait=(), cost=1, end=False):
        count = len(args)
        if far:
            args = [pltpu.with_memory_space_constraint(x, pltpu.HBM) for x in args]
        specs = [pl.BlockSpec(memory_space=pl.ANY) if far else pl.BlockSpec()] * count
        inner = body
        if self.last is not None:
            extra = (self.last, *wait)
            args = (*args, *extra)
            specs = [*specs, *[pl.BlockSpec(memory_space=pl.ANY)] * len(extra)]

            def inner(*refs):
                body(*refs[:count], *refs[count + len(extra) :])

        found = pl.pallas_call(
            inner,
            out_shape=[jax.ShapeDtypeStruct(s, d) for s, d in outs],
            in_specs=specs,
            scratch_shapes=list(scratch),
            cost_estimate=pl.CostEstimate(flops=cost, bytes_accessed=1, transcendentals=0),
            compiler_params=pltpu.CompilerParams(vmem_limit_bytes=32 * 2**20),
        )(*args)
        if not end:
            self.last = min(reversed(found), key=lambda x: x.size)
        return found


def after(x, *others):
    return lax.optimization_barrier((x, *others))[0]


def flip(x, axis, count, bits):
    return lax.ppermute(x, axis, [(i, i ^ bits) for i in range(count)])


def head(h):
    return slice(h * DH, (h + 1) * DH)


def part(i, size):
    return slice(i * size, (i + 1) * size)


def cut(start, size):
    return pl.ds(pl.multiple_of(start * size, size), size)


def member(r):
    return jnp.bitwise_xor(lax.rem(lax.axis_index("seq"), SLAB), r)


def causal(block):
    rows = lax.broadcasted_iota(jnp.int32, (block, block), 0)
    return lax.broadcasted_iota(jnp.int32, (block, block), 1) <= rows


def fetch(pairs, sems):
    copies = [pltpu.make_async_copy(a, b, sems.at[i]) for i, (a, b) in enumerate(pairs)]
    for copy in copies:
        copy.start()
    return copies


def front_kernel(k_hbm, v_hbm, q_hbm, c_hbm, w_hbm, *refs):
    keep_ref, states_ref, message_ref, own_ref, far_ref, columns_ref = refs[:6]
    k_ref, v_ref, q_ref, c_ref, w_ref, sems = refs[6:]
    copies = fetch(
        [(k_hbm, k_ref), (v_hbm, v_ref), (q_hbm, q_ref), (c_hbm, c_ref), (w_hbm, w_ref)], sems
    )
    block = k_ref.shape[0]
    width = k_ref.shape[1] // SLAB
    copies[0].wait()
    copies[1].wait()
    for r in range(SLAB):
        k, v = k_ref[:, cut(member(r), width)], v_ref[:, cut(member(r), width)]
        for h in range(width // DH):
            state = dot(k[:, head(h)], v[:, head(h)], 0, 0)
            if r < 2:
                keep_ref[r, :, head(h)] = state
            else:
                states_ref[part(r - 2, DH), head(h)] = state.astype(BF16)
    copies[2].wait()
    places = ((own_ref, 0), (message_ref, 0), (far_ref, 0), (message_ref, 3 * block))
    for r, (out, at) in enumerate(places):
        for i, ref in enumerate((q_ref, k_ref, v_ref)):
            out[at + i * block : at + (i + 1) * block, :] = ref[:, cut(member(r), width)]
    copies[3].wait()
    for i in range(c_ref.shape[1] // width):
        message_ref[part(6 + i, block), :] = c_ref[:, part(i, width)]
    copies[4].wait()
    for i in range(2):
        columns_ref[i] = w_ref[:, cut(member(2 * i), width)]


def halve_kernel(keep_ref, got_ref, own_ref, send_ref):
    own_ref[...] = keep_ref[0] + got_ref[part(0, DH), :].astype(F32)
    send_ref[...] = (keep_ref[1] + got_ref[part(1, DH), :].astype(F32)).astype(BF16)


def pair_kernel(message_ref, far_ref, out_ref):
    size = far_ref.shape[0]
    out_ref[:size, :] = far_ref[...]
    out_ref[size:, :] = message_ref[part(1, size), :]


def add_kernel(own_ref, got_ref, out_ref):
    out_ref[...] = (own_ref[...].astype(F32) + got_ref[...].astype(F32)).astype(out_ref.dtype)


def tokens_of(r, own_ref, message_ref, far_ref):
    size = own_ref.shape[0]
    if r == 0:
        return own_ref
    if r == 1:
        return message_ref.at[:size]
    return far_ref.at[(r - 2) * size : (r - 1) * size]


def attend_kernel(halves, *refs):
    tokens, (attend_ref, within_ref, states_ref) = refs[:-3], refs[-3:]
    _, block, width = within_ref.shape
    mask = causal(block)
    if halves:
        tokens = [tokens_of(r, tokens[0], tokens[1], None) for r in (0, 1)]
    else:
        tokens = [tokens[0].at[part(r, 3 * block)] for r in (0, 1)]
    for r, ref in enumerate(tokens):
        for h in range(width // DH):
            q, k, v = (ref[part(i, block), head(h)] for i in range(3))
            attend = jnp.where(mask, dot(q, k, 1, 1), 0.0).astype(BF16)
            attend_ref[r, h] = attend
            within_ref[r, :, head(h)] = dot(attend, v, 1, 0)
            states_ref[r, :, head(h)] = dot(k, v, 0, 0)


def dnormed_kernel(groups, message_ref, *refs):
    cots, weights = refs[: SLAB - 1], refs[SLAB - 1 : SLAB - 1 + groups]
    dnormed_ref, cot_ref = refs[SLAB - 1 + groups :]
    block, outputs = cots[0].shape
    width = dnormed_ref.shape[2]
    rows = weights[0].shape[1]
    me = lax.axis_index("dp")
    for i in range(outputs // width):
        cot_ref[1, :, part(i, width)] = message_ref[part(6 + i, block), :]
    for r, ref in zip((0, 2, 3), cots):
        cot_ref[r] = ref[...]
    for r in range(SLAB):
        total = dot(cot_ref[r, :, cut(me, rows)], weights[0][0], 1, 0)
        for j in range(1, groups):
            total = total + dot(cot_ref[r, :, cut(jnp.bitwise_xor(me, j), rows)], weights[j][0], 1, 0)
        dnormed_ref[r] = total


def from_slabs(backward, refs):
    slab = lax.div(lax.axis_index("seq"), SLAB)
    total = jnp.zeros(refs[0].shape, F32)
    for i, ref in enumerate(refs):
        bit = lax.rem(lax.div(slab, 1 << i), 2)
        total = total + jnp.where(bit == (0 if backward else 1), ref[...].astype(F32), 0.0)
    return total


def middle_kernel(*refs):
    tokens = refs[:3]
    *before, within0, states0, within1, states1, dnormed_ref = refs[3:-6]
    withins, states = (within0, within1), (states0, states1)
    normed_ref, dmixed_ref, prior_ref, u_ref, slab_ref, running = refs[-6:]
    _, block, width = normed_ref.shape
    heads = width // DH
    for r in range(SLAB):
        running[member(r)] = states[r // 2][r % 2]
    total = from_slabs(False, before)
    for p in range(SLAB):
        total, running[p] = total + running[p], total
    sums = [jnp.zeros((DH, DH), F32)] * heads
    for r in range(SLAB):
        prior = running[member(r)].astype(BF16)
        prior_ref[r] = prior
        for h in range(heads):
            q = tokens_of(r, *tokens)[:block, head(h)]
            mixed = withins[r // 2][r % 2, :, head(h)] + dot(q, prior[:, head(h)], 1, 0)
            scale = lax.rsqrt(jnp.mean(mixed * mixed, axis=-1, keepdims=True) + EPSILON)
            normed = mixed * scale
            normed_ref[r, :, head(h)] = normed.astype(BF16)
            dnormed = dnormed_ref[r, :, head(h)]
            along = jnp.mean(dnormed * normed, axis=-1, keepdims=True)
            dmixed = ((dnormed - normed * along) * scale).astype(BF16)
            dmixed_ref[r, :, head(h)] = dmixed
            u = dot(q, dmixed, 0, 0)
            u_ref[r, :, head(h)] = u
            sums[h] = sums[h] + u
    for h in range(heads):
        slab_ref[:, head(h)] = sums[h].astype(BF16)


def late_kernel(*refs):
    tokens, (normed_ref, attend0, attend1, dmixed_ref, prior_ref, *outs, part_ref) = refs[:3], refs[3:]
    _, block, width = normed_ref.shape
    mask = causal(block)
    for r in range(SLAB):
        out = outs[r]
        token = tokens_of(r, *tokens)
        out[:block, :] = normed_ref[r]
        for h in range(width // DH):
            q, k, v = (token[part(i, block), head(h)] for i in range(3))
            dmixed = dmixed_ref[r, :, head(h)]
            back = jnp.where(mask, dot(dmixed, v, 1, 1), 0.0).astype(BF16)
            gq = dot(back, k, 1, 0) + dot(dmixed, prior_ref[r, :, head(h)], 1, 1)
            out[block:, head(h)] = gq.astype(BF16)
            part_ref[r, :block, head(h)] = dot(back, q, 0, 0)
            part_ref[r, block:, head(h)] = dot((attend0, attend1)[r // 2][r % 2, h], dmixed, 0, 0)


def last_kernel(*refs):
    tokens = refs[:3]
    *behind, u_ref, part_ref = refs[3 : -(SLAB + 1)]
    outs, running = refs[-(SLAB + 1) : -1], refs[-1]
    block = part_ref.shape[1] // 2
    for r in range(SLAB):
        running[member(r)] = u_ref[r]
    total = from_slabs(True, behind)
    for p in reversed(range(SLAB)):
        total, running[p] = total + running[p], total
    for r in range(SLAB):
        out = outs[r]
        token = tokens_of(r, *tokens)
        later = running[member(r)].astype(BF16)
        for h in range(part_ref.shape[2] // DH):
            k, v = (token[part(i, block), head(h)] for i in (1, 2))
            gk = part_ref[r, :block, head(h)] + dot(v, later[:, head(h)], 1, 1)
            gv = part_ref[r, block:, head(h)] + dot(k, later[:, head(h)], 1, 0)
            out[:block, head(h)] = gk.astype(BF16)
            out[block:, head(h)] = gv.astype(BF16)


def output_kernel(groups, *refs):
    backs, own_ref = refs[:SLAB], refs[SLAB]
    far, (out_ref, gq_ref, normed_ref) = refs[SLAB + 1 : -3], refs[-3:]
    block, width = backs[0].shape[0] // 2, backs[0].shape[1]
    rows = own_ref.shape[0]
    me = lax.axis_index("dp")
    for r in range(SLAB):
        normed_ref[:, cut(member(r), width)] = backs[r][:block, :]
        gq_ref[:, cut(member(r), width)] = backs[r][block:, :]
    out_ref[:, cut(me, rows)] = dot(normed_ref[...], own_ref[...], 1, 1).astype(BF16)
    for j in range(1, groups):
        total = jnp.zeros((block, rows), F32)
        for r in range(SLAB):
            total = total + dot(backs[r][:block, :], far[2 * (j - 1) + r % 2][r // 2], 1, 1)
        out_ref[:, cut(jnp.bitwise_xor(me, j), rows)] = total.astype(BF16)


def join_kernel(*refs):
    parts, (gk_ref, gv_ref) = refs[:SLAB], refs[SLAB:]
    block = gk_ref.shape[0]
    width = parts[0].shape[1]
    for r in range(SLAB):
        gk_ref[:, cut(member(r), width)] = parts[r][:block, :]
        gv_ref[:, cut(member(r), width)] = parts[r][block:, :]


def product_kernel(slabs, cot_ref, normed_ref, keep_ref, send_ref):
    me = lax.axis_index("dp")
    slab = lax.div(lax.axis_index("seq"), SLAB)
    rows = keep_ref.shape[0] // slabs
    for j, out in enumerate((send_ref, keep_ref)):
        for d in range(slabs):
            at = jnp.bitwise_xor(me, 1 - j) * slabs + jnp.bitwise_xor(slab, d)
            total = dot(cot_ref[0, :, cut(at, rows)], normed_ref[0], 0, 0)
            for r in range(1, SLAB):
                total = total + dot(cot_ref[r, :, cut(at, rows)], normed_ref[r], 0, 0)
            out[part(d, rows), :] = total.astype(out.dtype)


def split_kernel(own_ref, got_ref, keep_ref, send_ref):
    rows = keep_ref.shape[0] // 2
    for i in range(4):
        total = own_ref[part(i, rows), :] + got_ref[part(i, rows), :].astype(F32)
        out = (keep_ref, send_ref)[i % 2]
        out[part(i // 2, rows), :] = total.astype(out.dtype)


def split_again_kernel(own_ref, got_ref, keep_ref, send_ref):
    rows = keep_ref.shape[0]
    for i, out in enumerate((keep_ref, send_ref)):
        total = own_ref[part(i, rows), :] + got_ref[part(i, rows), :].astype(F32)
        out[...] = total.astype(out.dtype)


def share_kernel(own_ref, got_ref, keep_ref, send_ref, total_ref):
    total_ref[...] = own_ref[...] + got_ref[...].astype(F32)
    rows = keep_ref.shape[0] // 2
    for i, r in enumerate((0, 1)):
        keep_ref[part(i, rows), :] = total_ref[cut(member(r), rows), :]
    for i, r in enumerate((2, 3)):
        send_ref[part(i, rows), :] = total_ref[cut(member(r), rows), :]


def pass_kernel(own_ref, got_ref, keep_ref, send_ref):
    rows = own_ref.shape[0] // 2
    for i, ref in enumerate((own_ref, got_ref)):
        keep_ref[part(i, rows), :] = ref[:rows, :]
        send_ref[part(i, rows), :] = ref[rows:, :]


def finish_kernel(factor, keep_ref, got_ref, out_ref):
    rows, width = out_ref.shape[0], keep_ref.shape[1]
    for i, ref in enumerate((keep_ref, got_ref)):
        for j in range(2):
            out_ref[:, cut(member(i + 2 * j), width)] = ref[part(j, rows), :] * factor


def local(queries, keys, values, cotangent, out_weight, *, dp, seq):
    call = Chain()
    local_seqs, block, features = queries.shape
    outputs = cotangent.shape[2]
    rows = local_seqs * block
    slabs = seq // SLAB
    width = features // SLAB
    heads = width // DH
    q, k, v = (x.reshape(rows, features) for x in (queries, keys, values))
    cot = cotangent.reshape(rows, outputs)
    factor = 1.0 / math.sqrt(rows * dp * seq)
    near = functools.partial(flip, axis="seq", count=seq)

    def spread(parts, *first):
        found = {r: near(after(parts[r], *first), bits=r) for r in (2, 3, 1)}
        return [parts[0], found[1], found[2], found[3]]

    def doubling(total, cost=1):
        found = []
        bits = SLAB
        while bits < seq:
            if found:
                (total,) = call(add_kernel, [(total.shape, BF16)], total, found[-1], cost=cost)
            found.append(near(total, bits=bits))
            bits *= 2
        return found, total

    cot_y = near(cot, bits=2)
    keep, send, message, own_tokens, far_tokens, columns = call(
        front_kernel,
        [((2, DH, width), F32), ((2 * DH, width), BF16), (((6 + outputs // width) * rows, width), BF16),
         ((3 * rows, width), BF16), ((3 * rows, width), BF16), ((2, out_weight.shape[0], width), BF16)],
        k, v, q, cot, out_weight, far=True,
        scratch=[pltpu.VMEM(x.shape, BF16) for x in (k, v, q, cot, out_weight)]
        + [pltpu.SemaphoreType.DMA((5,))],
    )
    got = near(send, bits=2)
    message = near(message, bits=1)
    w_far = [flip(columns, "dp", dp, j) for j in range(1, dp)]
    own, send = call(
        halve_kernel, [((DH, width), F32), ((DH, width), BF16)], keep, got, cost=10**10
    )
    got = near(send, bits=1)
    (slab_kv,) = call(add_kernel, [((DH, width), BF16)], own, got)
    (far_tokens,) = call(pair_kernel, [((6 * rows, width), BF16)], message, far_tokens)
    far_tokens = near(far_tokens, bits=2)
    attended = [((2, heads, rows, rows), BF16), ((2, rows, width), F32), ((2, DH, width), F32)]
    attend0, within0, states0 = call(
        functools.partial(attend_kernel, True), attended, own_tokens, message
    )
    cot_yc = near(after(cot_y, within0), bits=1)
    before, _ = doubling(slab_kv, 3 * 10**9)
    attend1, within1, states1 = call(functools.partial(attend_kernel, False), attended, far_tokens)
    dnormed, cots = call(
        functools.partial(dnormed_kernel, dp),
        [((SLAB, rows, width), F32), ((SLAB, rows, outputs), BF16)],
        message, cot, cot_y, cot_yc, columns, *w_far,
    )
    w_all = [x for w in w_far for x in (w, near(after(w, within1), bits=1))]
    tokens = (own_tokens, message, far_tokens)
    normed, dmixed, prior, u, slab_u = call(
        middle_kernel,
        [((SLAB, rows, width), BF16), ((SLAB, rows, width), BF16), ((SLAB, DH, width), BF16),
         ((SLAB, DH, width), F32), ((DH, width), BF16)],
        *tokens, *before, within0, states0, within1, states1, dnormed, cost=10**10,
        scratch=[pltpu.VMEM((SLAB, DH, width), F32)],
    )
    tuned = dp == 2 and slabs == 4 and outputs // (dp * seq) % 8 == 0
    if tuned:
        keep, send = call(
            functools.partial(product_kernel, slabs),
            [((outputs // dp, width), F32), ((outputs // dp, width), BF16)], cots, normed, wait=w_all[1::2],
        )
        got = flip(send, "dp", dp, 1)
    *backs, parts = call(
        late_kernel,
        [((2 * rows, width), BF16)] * SLAB + [((SLAB, 2 * rows, width), F32)],
        *tokens, normed, attend0, attend1, dmixed, prior,
    )
    behind, last_u = doubling(slab_u)
    backs = spread(backs, last_u)
    if tuned:
        piece = outputs // (dp * slabs)
        keep, send = call(
            split_kernel, [((2 * piece, width), F32), ((2 * piece, width), BF16)], keep, got, cost=1
        )
        got = near(send, bits=SLAB)
    grads = call(
        last_kernel, [((2 * rows, width), BF16)] * SLAB, *tokens, *behind, u, parts, cost=3 * 10**9,
        scratch=[pltpu.VMEM((SLAB, DH, width), F32)],
    )
    if tuned:
        keep, send = call(
            split_again_kernel, [((piece, width), F32), ((piece, width), BF16)], keep, got, cost=1
        )
        got = near(send, bits=2 * SLAB)
    grads = spread(grads, keep)
    output, gq, own_normed = call(
        functools.partial(output_kernel, dp),
        [((rows, outputs), BF16), ((rows, features), BF16), ((rows, features), BF16)],
        *backs, out_weight, *w_all,
    )
    if tuned:
        keep, share = call(
            share_kernel, [((piece // 2, width), F32)] * 2, keep, got,
            scratch=[pltpu.VMEM((piece, width), F32)],
        )
        got = near(share, bits=2)
    if tuned:
        keep, share = call(pass_kernel, [((piece // 2, width), F32)] * 2, keep, got)
        got = near(share, bits=1)
    gk, gv = call(join_kernel, [((rows, features), BF16)] * 2, *grads, end=True)
    if tuned:
        (grad_weight,) = call(
            functools.partial(finish_kernel, factor),
            [((piece // SLAB, features), F32)], keep, got,
        )
    else:
        partial = dot(cot, own_normed, 0, 0) * factor
        grad_weight = lax.psum_scatter(partial, ("dp", "seq"), scatter_dimension=0, tiled=True)
    shape = queries.shape
    return (
        output.reshape(cotangent.shape), gq.reshape(shape), gk.reshape(shape), gv.reshape(shape),
        grad_weight,
    )


def solution(mesh):
    dp, seq = mesh.shape["dp"], mesh.shape["seq"]
    return jax.shard_map(
        functools.partial(local, dp=dp, seq=seq),
        mesh=mesh,
        in_specs=(P("dp", "seq", None),) * 4 + (P("dp", None),),
        out_specs=(P("dp", "seq", None),) * 4 + (P(("dp", "seq"), None),),
        check_vma=False,
    )
```

```python
import functools
import math

import jax
import jax.numpy as jnp
from jax import lax
from jax.experimental import pallas as pl
from jax.experimental.pallas import tpu as pltpu
from jax.sharding import PartitionSpec as P

DH = 128
SLAB = 4
EPSILON = 1e-05
BF16 = jnp.bfloat16
F32 = jnp.float32


def dot(left, right, left_dim, right_dim):
    return lax.dot_general(
        left, right, (((left_dim,), (right_dim,)), ((), ())), preferred_element_type=F32
    )


class Chain:
    def __init__(self):
        self.last = None

    def __call__(self, body, outs, *args, scratch=(), far=False, wait=(), cost=1, end=False):
        count = len(args)
        if far:
            args = [pltpu.with_memory_space_constraint(x, pltpu.HBM) for x in args]
        specs = [pl.BlockSpec(memory_space=pl.ANY) if far else pl.BlockSpec()] * count
        inner = body
        if self.last is not None:
            extra = (self.last, *wait)
            args = (*args, *extra)
            specs = [*specs, *[pl.BlockSpec(memory_space=pl.ANY)] * len(extra)]

            def inner(*refs):
                body(*refs[:count], *refs[count + len(extra) :])

        found = pl.pallas_call(
            inner,
            out_shape=[jax.ShapeDtypeStruct(s, d) for s, d in outs],
            in_specs=specs,
            scratch_shapes=list(scratch),
            cost_estimate=pl.CostEstimate(flops=cost, bytes_accessed=1, transcendentals=0),
            compiler_params=pltpu.CompilerParams(vmem_limit_bytes=32 * 2**20),
        )(*args)
        if not end:
            self.last = min(reversed(found), key=lambda x: x.size)
        return found


def after(x, *others):
    return lax.optimization_barrier((x, *others))[0]


def flip(x, axis, count, bits):
    return lax.ppermute(x, axis, [(i, i ^ bits) for i in range(count)])


def head(h):
    return slice(h * DH, (h + 1) * DH)


def part(i, size):
    return slice(i * size, (i + 1) * size)


def cut(start, size):
    return pl.ds(pl.multiple_of(start * size, size), size)


def member(r):
    return jnp.bitwise_xor(lax.rem(lax.axis_index("seq"), SLAB), r)


def causal(block):
    rows = lax.broadcasted_iota(jnp.int32, (block, block), 0)
    return lax.broadcasted_iota(jnp.int32, (block, block), 1) <= rows


def fetch(pairs, sems):
    copies = [pltpu.make_async_copy(a, b, sems.at[i]) for i, (a, b) in enumerate(pairs)]
    for copy in copies:
        copy.start()
    return copies


def front_kernel(k_hbm, v_hbm, w_hbm, own_ref, near_ref, far_ref, columns_ref, k_ref, v_ref, w_ref, sems):
    copies = fetch([(k_hbm, k_ref), (v_hbm, v_ref), (w_hbm, w_ref)], sems)
    width = k_ref.shape[1] // SLAB
    copies[0].wait()
    copies[1].wait()
    places = (own_ref, near_ref, far_ref.at[part(0, DH)], far_ref.at[part(1, DH)])
    for r, out in enumerate(places):
        k, v = k_ref[:, cut(member(r), width)], v_ref[:, cut(member(r), width)]
        for h in range(width // DH):
            out[:, head(h)] = dot(k[:, head(h)], v[:, head(h)], 0, 0).astype(out.dtype)
    copies[2].wait()
    for i in range(2):
        columns_ref[i] = w_ref[:, cut(member(2 * i), width)]


def pack_kernel(q_hbm, k_hbm, v_hbm, c_hbm, *refs):
    attend_ref, own_ref, message_ref, far_ref, q_ref, k_ref, v_ref, c_ref, sems = refs
    copies = fetch([(q_hbm, q_ref), (k_hbm, k_ref), (v_hbm, v_ref), (c_hbm, c_ref)], sems)
    block = q_ref.shape[0]
    width = q_ref.shape[1] // SLAB
    for copy in copies[:3]:
        copy.wait()
    mask = causal(block)
    places = (own_ref, message_ref.at[: 2 * block], far_ref, message_ref.at[2 * block : 4 * block])
    for r, out in enumerate(places):
        q, k, v = (ref[:, cut(member(r), width)] for ref in (q_ref, k_ref, v_ref))
        out[:block, :] = q
        for h in range(width // DH):
            attend = jnp.where(mask, dot(q[:, head(h)], k[:, head(h)], 1, 1), 0.0).astype(BF16)
            attend_ref[r, h] = attend
            out[block:, head(h)] = dot(attend, v[:, head(h)], 1, 0).astype(BF16)
    copies[3].wait()
    for i in range(c_ref.shape[1] // width):
        message_ref[part(4 + i, block), :] = c_ref[:, part(i, width)]


def cross_kernel(near_ref, got_ref, out_ref):
    out_ref[part(0, DH), :] = near_ref[...]
    out_ref[part(1, DH), :] = got_ref[part(1, DH), :]


def total_kernel(own_ref, far_ref, near_ref, out_ref):
    total = own_ref[...] + far_ref[part(0, DH), :].astype(F32)
    total = total + near_ref[part(0, DH), :].astype(F32) + near_ref[part(1, DH), :].astype(F32)
    out_ref[...] = total.astype(BF16)


def pair_kernel(message_ref, far_ref, out_ref):
    size = far_ref.shape[0]
    out_ref[:size, :] = far_ref[...]
    out_ref[size:, :] = message_ref[part(1, size), :]


def add_kernel(own_ref, got_ref, out_ref):
    out_ref[...] = (own_ref[...].astype(F32) + got_ref[...].astype(F32)).astype(out_ref.dtype)


def dnormed_kernel(groups, message_ref, *refs):
    cots, weights = refs[: SLAB - 1], refs[SLAB - 1 : SLAB - 1 + groups]
    dnormed_ref, cot_ref = refs[SLAB - 1 + groups :]
    block, outputs = cots[0].shape
    width = dnormed_ref.shape[2]
    rows = weights[0].shape[1]
    me = lax.axis_index("dp")
    for i in range(outputs // width):
        cot_ref[1, :, part(i, width)] = message_ref[part(4 + i, block), :]
    for r, ref in zip((0, 2, 3), cots):
        cot_ref[r] = ref[...]
    for r in range(SLAB):
        total = dot(cot_ref[r, :, cut(me, rows)], weights[0][0], 1, 0)
        for j in range(1, groups):
            total = total + dot(cot_ref[r, :, cut(jnp.bitwise_xor(me, j), rows)], weights[j][0], 1, 0)
        dnormed_ref[r] = total


def from_slabs(backward, refs):
    slab = lax.div(lax.axis_index("seq"), SLAB)
    total = jnp.zeros(refs[0].shape, F32)
    for i, ref in enumerate(refs):
        bit = lax.rem(lax.div(slab, 1 << i), 2)
        total = total + jnp.where(bit == (0 if backward else 1), ref[...].astype(F32), 0.0)
    return total


def middle_kernel(*refs):
    own_ref, message_ref, token_far, own_state, far_state, near_state, dnormed_ref = refs[:7]
    *before, normed_ref, back0, back1, back2, back3, u_ref, slab_ref, running = refs[7:]
    _, block, width = normed_ref.shape
    heads = width // DH
    size = 2 * block
    tokens = (own_ref, message_ref.at[:size], token_far.at[:size], token_far.at[size:])
    running[member(0)] = own_state[...]
    running[member(1)] = near_state[part(0, DH), :].astype(F32)
    running[member(2)] = far_state[part(0, DH), :].astype(F32)
    running[member(3)] = near_state[part(1, DH), :].astype(F32)
    total = from_slabs(False, before)
    for p in range(SLAB):
        total, running[p] = total + running[p], total
    sums = [jnp.zeros((DH, DH), F32)] * heads
    for r in range(SLAB):
        out = (back0, back1, back2, back3)[r]
        prior = running[member(r)].astype(BF16)
        out[size:, :] = prior
        for h in range(heads):
            q = tokens[r][:block, head(h)]
            mixed = tokens[r][block:, head(h)].astype(F32) + dot(q, prior[:, head(h)], 1, 0)
            scale = lax.rsqrt(jnp.mean(mixed * mixed, axis=-1, keepdims=True) + EPSILON)
            normed = mixed * scale
            normed_ref[r, :, head(h)] = normed.astype(BF16)
            out[:block, head(h)] = normed.astype(BF16)
            dnormed = dnormed_ref[r, :, head(h)]
            along = jnp.mean(dnormed * normed, axis=-1, keepdims=True)
            dmixed = ((dnormed - normed * along) * scale).astype(BF16)
            out[block:size, head(h)] = dmixed
            u = dot(q, dmixed, 0, 0)
            u_ref[r, :, head(h)] = u
            sums[h] = sums[h] + u
    for h in range(heads):
        slab_ref[:, head(h)] = sums[h].astype(BF16)


def later_kernel(*refs):
    *behind, u_ref, near_ref, far_ref, running = refs
    for r in range(SLAB):
        running[member(r)] = u_ref[r]
    total = from_slabs(True, behind)
    for p in reversed(range(SLAB)):
        total, running[p] = total + running[p], total
    for r in range(SLAB):
        (near_ref, far_ref)[r // 2][part(r % 2, DH), :] = running[member(r)].astype(BF16)


def relay_kernel(near_ref, far_ref, out_ref):
    size = near_ref.shape[0] // 2
    out_ref[:size, :] = near_ref[size:, :]
    out_ref[size:, :] = far_ref[size:, :]


def arrived(near_ref, far_ref, core_ref):
    size = near_ref.shape[0] // 2
    first, second = slice(0, size), slice(size, 2 * size)
    return near_ref.at[first], core_ref.at[first], far_ref.at[first], core_ref.at[second]


def late_kernel(groups, *refs):
    backs, (q_ref, k_ref, v_ref, attend_ref, own_ref) = refs[:SLAB], refs[SLAB : SLAB + 5]
    far, (out_ref, gq_ref, gk_ref, gv_ref, normed_ref) = refs[SLAB + 5 : -5], refs[-5:]
    block, width = q_ref.shape[0], backs[0].shape[1]
    size = 2 * block
    rows = own_ref.shape[0]
    me = lax.axis_index("dp")
    mask = causal(block)
    for r in range(SLAB):
        at = cut(member(r), width)
        normed_ref[:, at] = backs[r][:block, :]
        q, k, v = q_ref[:, at], k_ref[:, at], v_ref[:, at]
        gqs, gks, gvs = [], [], []
        for h in range(width // DH):
            dmixed = backs[r][block:size, head(h)]
            back = jnp.where(mask, dot(dmixed, v[:, head(h)], 1, 1), 0.0).astype(BF16)
            gqs.append(dot(back, k[:, head(h)], 1, 0) + dot(dmixed, backs[r][size:, head(h)], 1, 1))
            gks.append(dot(back, q[:, head(h)], 0, 0))
            gvs.append(dot(attend_ref[r, h], dmixed, 0, 0))
        gq_ref[:, at] = jnp.concatenate(gqs, axis=1).astype(BF16)
        gk_ref[r] = jnp.concatenate(gks, axis=1)
        gv_ref[r] = jnp.concatenate(gvs, axis=1)
    out_ref[:, cut(me, rows)] = dot(normed_ref[...], own_ref[...], 1, 1).astype(BF16)
    for j in range(1, groups):
        total = jnp.zeros((block, rows), F32)
        for r in range(SLAB):
            total = total + dot(backs[r][:block, :], far[2 * (j - 1) + r % 2][r // 2], 1, 1)
        out_ref[:, cut(jnp.bitwise_xor(me, j), rows)] = total.astype(BF16)


def last_kernel(near_ref, far_ref, core_ref, k_ref, v_ref, gk_part, gv_part, gk_ref, gv_ref):
    laters = arrived(near_ref, far_ref, core_ref)
    width = near_ref.shape[1]
    for r in range(SLAB):
        at = cut(member(r), width)
        k, v = k_ref[:, at], v_ref[:, at]
        gks, gvs = [], []
        for h in range(width // DH):
            later = laters[r][:, head(h)]
            gks.append(gk_part[r, :, head(h)] + dot(v[:, head(h)], later, 1, 1))
            gvs.append(gv_part[r, :, head(h)] + dot(k[:, head(h)], later, 1, 0))
        gk_ref[:, at] = jnp.concatenate(gks, axis=1).astype(BF16)
        gv_ref[:, at] = jnp.concatenate(gvs, axis=1).astype(BF16)


def product_kernel(slabs, cot_ref, normed_ref, keep_ref, send_ref):
    me = lax.axis_index("dp")
    slab = lax.div(lax.axis_index("seq"), SLAB)
    rows = keep_ref.shape[0] // slabs
    for j, out in enumerate((send_ref, keep_ref)):
        for d in range(slabs):
            at = jnp.bitwise_xor(me, 1 - j) * slabs + jnp.bitwise_xor(slab, d)
            total = dot(cot_ref[0, :, cut(at, rows)], normed_ref[0], 0, 0)
            for r in range(1, SLAB):
                total = total + dot(cot_ref[r, :, cut(at, rows)], normed_ref[r], 0, 0)
            out[part(d, rows), :] = total.astype(out.dtype)


def split_kernel(own_ref, got_ref, keep_ref, send_ref):
    rows = keep_ref.shape[0] // 2
    for i in range(4):
        total = own_ref[part(i, rows), :] + got_ref[part(i, rows), :].astype(F32)
        out = (keep_ref, send_ref)[i % 2]
        out[part(i // 2, rows), :] = total.astype(out.dtype)


def split_again_kernel(own_ref, got_ref, keep_ref, send_ref):
    rows = keep_ref.shape[0]
    for i, out in enumerate((keep_ref, send_ref)):
        total = own_ref[part(i, rows), :] + got_ref[part(i, rows), :].astype(F32)
        out[...] = total.astype(out.dtype)


def share_kernel(own_ref, got_ref, keep_ref, send_ref, total_ref):
    total_ref[...] = own_ref[...] + got_ref[...].astype(F32)
    rows = keep_ref.shape[0] // 2
    for i, r in enumerate((0, 1)):
        keep_ref[part(i, rows), :] = total_ref[cut(member(r), rows), :]
    for i, r in enumerate((2, 3)):
        send_ref[part(i, rows), :] = total_ref[cut(member(r), rows), :]


def pass_kernel(own_ref, got_ref, keep_ref, send_ref):
    rows = own_ref.shape[0] // 2
    for i, ref in enumerate((own_ref, got_ref)):
        keep_ref[part(i, rows), :] = ref[:rows, :]
        send_ref[part(i, rows), :] = ref[rows:, :]


def finish_kernel(factor, keep_ref, got_ref, out_ref):
    rows, width = out_ref.shape[0], keep_ref.shape[1]
    for i, ref in enumerate((keep_ref, got_ref)):
        for j in range(2):
            out_ref[:, cut(member(i + 2 * j), width)] = ref[part(j, rows), :] * factor


def local(queries, keys, values, cotangent, out_weight, *, dp, seq):
    call = Chain()
    local_seqs, block, features = queries.shape
    outputs = cotangent.shape[2]
    rows = local_seqs * block
    slabs = seq // SLAB
    width = features // SLAB
    heads = width // DH
    q, k, v = (x.reshape(rows, features) for x in (queries, keys, values))
    cot = cotangent.reshape(rows, outputs)
    factor = 1.0 / math.sqrt(rows * dp * seq)
    near = functools.partial(flip, axis="seq", count=seq)

    def doubling(total, cost=1):
        found = []
        bits = SLAB
        while bits < seq:
            if found:
                (total,) = call(add_kernel, [(total.shape, BF16)], total, found[-1], cost=cost)
            found.append(near(total, bits=bits))
            bits *= 2
        return found, total

    def scratch(*arrays):
        return [pltpu.VMEM(x.shape, BF16) for x in arrays] + [pltpu.SemaphoreType.DMA((len(arrays),))]

    cot_y = near(cot, bits=2)
    own_state, near_state, far_state, columns = call(
        front_kernel,
        [((DH, width), F32), ((DH, width), BF16), ((2 * DH, width), BF16),
         ((2, out_weight.shape[0], width), BF16)],
        k, v, out_weight, far=True, scratch=scratch(k, v, out_weight),
    )
    far_state = near(far_state, bits=2)
    w_far = [flip(columns, "dp", dp, j) for j in range(1, dp)]
    attend, own_tokens, message, far_tokens = call(
        pack_kernel,
        [((SLAB, heads, rows, rows), BF16), ((2 * rows, width), BF16),
         (((4 + outputs // width) * rows, width), BF16), ((2 * rows, width), BF16)],
        q, k, v, cot, far=True, scratch=scratch(q, k, v, cot),
    )
    message = near(message, bits=1)
    (near_state,) = call(
        cross_kernel, [((2 * DH, width), BF16)], near_state, far_state, cost=5 * 10**9
    )
    near_state = near(near_state, bits=1)
    (slab_kv,) = call(total_kernel, [((DH, width), BF16)], own_state, far_state, near_state)
    (far_tokens,) = call(pair_kernel, [((4 * rows, width), BF16)], message, far_tokens)
    cot_yc = near(after(cot_y, far_tokens), bits=1)
    far_tokens = near(far_tokens, bits=2)
    before, _ = doubling(slab_kv, 2 * 10**9)
    dnormed, cots = call(
        functools.partial(dnormed_kernel, dp),
        [((SLAB, rows, width), F32), ((SLAB, rows, outputs), BF16)],
        message, cot, cot_y, cot_yc, columns, *w_far,
    )
    w_all = [x for w in w_far for x in (w, near(after(w, dnormed), bits=1))]
    normed, *backs, u, slab_u = call(
        middle_kernel,
        [((SLAB, rows, width), BF16)] + [((2 * rows + DH, width), BF16)] * SLAB
        + [((SLAB, DH, width), F32), ((DH, width), BF16)],
        own_tokens, message, far_tokens, own_state, far_state, near_state, dnormed, *before,
        cost=10**10, scratch=[pltpu.VMEM((SLAB, DH, width), F32)],
    )
    tuned = dp == 2 and slabs == 4 and outputs // (dp * seq) % 8 == 0
    piece = outputs // (dp * slabs)
    if tuned:
        keep, send = call(
            functools.partial(product_kernel, slabs),
            [((outputs // dp, width), F32), ((outputs // dp, width), BF16)], cots, normed, wait=w_all[1::2],
        )
        got = flip(send, "dp", dp, 1)
    backs = [backs[0], *(near(backs[r], bits=r) for r in range(1, SLAB))]
    behind, last_u = doubling(slab_u)
    if tuned:
        keep, send = call(
            split_kernel, [((2 * piece, width), F32), ((2 * piece, width), BF16)], keep, got, cost=1
        )
        got = near(send, bits=SLAB)
    later, later_far = call(
        later_kernel, [((2 * DH, width), BF16)] * 2, *behind, u, cost=3 * 10**9,
        scratch=[pltpu.VMEM((SLAB, DH, width), F32)],
    )
    later_far = near(later_far, bits=2)
    if tuned:
        keep, send = call(
            split_again_kernel, [((piece, width), F32), ((piece, width), BF16)], keep, got, cost=1
        )
        got = near(send, bits=2 * SLAB)
    output, gq, gk_part, gv_part, own_normed = call(
        functools.partial(late_kernel, dp),
        [((rows, outputs), BF16), ((rows, features), BF16), ((SLAB, rows, width), F32),
         ((SLAB, rows, width), F32), ((rows, features), BF16)],
        *backs, q, k, v, attend, out_weight, *w_all,
    )
    if tuned:
        keep, share = call(
            share_kernel, [((piece // 2, width), F32)] * 2, keep, got,
            scratch=[pltpu.VMEM((piece, width), F32)],
        )
        got = near(share, bits=2)
    (send,) = call(relay_kernel, [((2 * DH, width), BF16)], later, later_far)
    later_core = near(send, bits=1)
    if tuned:
        keep, share = call(pass_kernel, [((piece // 2, width), F32)] * 2, keep, got)
        got = near(share, bits=1)
    gk, gv = call(
        last_kernel, [((rows, features), BF16)] * 2,
        later, later_far, later_core, k, v, gk_part, gv_part, end=True,
    )
    if tuned:
        (grad_weight,) = call(
            functools.partial(finish_kernel, factor),
            [((piece // SLAB, features), F32)], keep, got, end=True,
        )
    else:
        partial = dot(cot, own_normed, 0, 0) * factor
        grad_weight = lax.psum_scatter(partial, ("dp", "seq"), scatter_dimension=0, tiled=True)
    shape = queries.shape
    return (
        output.reshape(cotangent.shape), gq.reshape(shape), gk.reshape(shape), gv.reshape(shape),
        grad_weight,
    )


def solution(mesh):
    dp, seq = mesh.shape["dp"], mesh.shape["seq"]
    return jax.shard_map(
        functools.partial(local, dp=dp, seq=seq),
        mesh=mesh,
        in_specs=(P("dp", "seq", None),) * 4 + (P("dp", None),),
        out_specs=(P("dp", "seq", None),) * 4 + (P(("dp", "seq"), None),),
        check_vma=False,
    )
```

```python
import functools
import math

import jax
import jax.numpy as jnp
from jax import lax
from jax.experimental import pallas as pl
from jax.experimental.pallas import tpu as pltpu
from jax.sharding import PartitionSpec as P

DH = 128
SLAB = 4
EPSILON = 1e-05
BF16 = jnp.bfloat16
F32 = jnp.float32


def dot(left, right, left_dim, right_dim):
    return lax.dot_general(
        left, right, (((left_dim,), (right_dim,)), ((), ())), preferred_element_type=F32
    )


class Chain:
    def __init__(self):
        self.last = None

    def __call__(self, body, outs, *args, scratch=(), far=False, wait=(), cost=1, end=False):
        count = len(args)
        if far:
            args = [pltpu.with_memory_space_constraint(x, pltpu.HBM) for x in args]
        specs = [pl.BlockSpec(memory_space=pl.ANY) if far else pl.BlockSpec()] * count
        inner = body
        if self.last is not None:
            extra = (self.last, *wait)
            args = (*args, *extra)
            specs = [*specs, *[pl.BlockSpec(memory_space=pl.ANY)] * len(extra)]

            def inner(*refs):
                body(*refs[:count], *refs[count + len(extra) :])

        found = pl.pallas_call(
            inner,
            out_shape=[jax.ShapeDtypeStruct(s, d) for s, d in outs],
            in_specs=specs,
            scratch_shapes=list(scratch),
            cost_estimate=pl.CostEstimate(flops=cost, bytes_accessed=1, transcendentals=0),
            compiler_params=pltpu.CompilerParams(vmem_limit_bytes=32 * 2**20),
        )(*args)
        if not end:
            self.last = min(reversed(found), key=lambda x: x.size)
        return found


def after(x, *others):
    return lax.optimization_barrier((x, *others))[0]


def flip(x, axis, count, bits):
    return lax.ppermute(x, axis, [(i, i ^ bits) for i in range(count)])


def head(h):
    return slice(h * DH, (h + 1) * DH)


def part(i, size):
    return slice(i * size, (i + 1) * size)


def cut(start, size):
    return pl.ds(pl.multiple_of(start * size, size), size)


def member(r):
    return jnp.bitwise_xor(lax.rem(lax.axis_index("seq"), SLAB), r)


def causal(block):
    rows = lax.broadcasted_iota(jnp.int32, (block, block), 0)
    return lax.broadcasted_iota(jnp.int32, (block, block), 1) <= rows


def fetch(pairs, sems):
    copies = [pltpu.make_async_copy(a, b, sems.at[i]) for i, (a, b) in enumerate(pairs)]
    for copy in copies:
        copy.start()
    return copies


def front_kernel(k_hbm, v_hbm, w_hbm, own_ref, near_ref, far_ref, columns_ref, k_ref, v_ref, w_ref, sems):
    copies = fetch([(k_hbm, k_ref), (v_hbm, v_ref), (w_hbm, w_ref)], sems)
    width = k_ref.shape[1] // SLAB
    copies[0].wait()
    copies[1].wait()
    places = (own_ref, near_ref, far_ref.at[part(0, DH)], far_ref.at[part(1, DH)])
    for r, out in enumerate(places):
        k, v = k_ref[:, cut(member(r), width)], v_ref[:, cut(member(r), width)]
        for h in range(width // DH):
            out[:, head(h)] = dot(k[:, head(h)], v[:, head(h)], 0, 0).astype(out.dtype)
    copies[2].wait()
    for i in range(2):
        columns_ref[i] = w_ref[:, cut(member(2 * i), width)]


def pack_kernel(q_hbm, k_hbm, v_hbm, c_hbm, *refs):
    attend_ref, own_ref, message_ref, far_ref, q_ref, k_ref, v_ref, c_ref, sems = refs
    copies = fetch([(q_hbm, q_ref), (k_hbm, k_ref), (v_hbm, v_ref), (c_hbm, c_ref)], sems)
    block = q_ref.shape[0]
    width = q_ref.shape[1] // SLAB
    for copy in copies[:3]:
        copy.wait()
    mask = causal(block)
    places = (own_ref, message_ref.at[: 2 * block], far_ref, message_ref.at[2 * block : 4 * block])
    for r, out in enumerate(places):
        q, k, v = (ref[:, cut(member(r), width)] for ref in (q_ref, k_ref, v_ref))
        out[:block, :] = q
        for h in range(width // DH):
            attend = jnp.where(mask, dot(q[:, head(h)], k[:, head(h)], 1, 1), 0.0).astype(BF16)
            attend_ref[r, h] = attend
            out[block:, head(h)] = dot(attend, v[:, head(h)], 1, 0).astype(BF16)
    copies[3].wait()
    for i in range(c_ref.shape[1] // width):
        message_ref[part(4 + i, block), :] = c_ref[:, part(i, width)]


def cross_kernel(near_ref, got_ref, out_ref):
    out_ref[part(0, DH), :] = near_ref[...]
    out_ref[part(1, DH), :] = got_ref[part(1, DH), :]


def total_kernel(own_ref, far_ref, near_ref, out_ref):
    total = own_ref[...] + far_ref[part(0, DH), :].astype(F32)
    total = total + near_ref[part(0, DH), :].astype(F32) + near_ref[part(1, DH), :].astype(F32)
    out_ref[...] = total.astype(BF16)


def pair_kernel(message_ref, far_ref, out_ref):
    size = far_ref.shape[0]
    out_ref[:size, :] = far_ref[...]
    out_ref[size:, :] = message_ref[part(1, size), :]


def add_kernel(own_ref, got_ref, out_ref):
    out_ref[...] = (own_ref[...].astype(F32) + got_ref[...].astype(F32)).astype(out_ref.dtype)


def dnormed_kernel(groups, message_ref, *refs):
    cots, weights = refs[: SLAB - 1], refs[SLAB - 1 : SLAB - 1 + groups]
    dnormed_ref, cot_ref = refs[SLAB - 1 + groups :]
    block, outputs = cots[0].shape
    width = dnormed_ref.shape[2]
    rows = weights[0].shape[1]
    me = lax.axis_index("dp")
    for i in range(outputs // width):
        cot_ref[1, :, part(i, width)] = message_ref[part(4 + i, block), :]
    for r, ref in zip((0, 2, 3), cots):
        cot_ref[r] = ref[...]
    for r in range(SLAB):
        total = dot(cot_ref[r, :, cut(me, rows)], weights[0][0], 1, 0)
        for j in range(1, groups):
            total = total + dot(cot_ref[r, :, cut(jnp.bitwise_xor(me, j), rows)], weights[j][0], 1, 0)
        dnormed_ref[r] = total


def from_slabs(backward, refs):
    slab = lax.div(lax.axis_index("seq"), SLAB)
    total = jnp.zeros(refs[0].shape, F32)
    for i, ref in enumerate(refs):
        bit = lax.rem(lax.div(slab, 1 << i), 2)
        total = total + jnp.where(bit == (0 if backward else 1), ref[...].astype(F32), 0.0)
    return total


def middle_kernel(*refs):
    own_ref, message_ref, token_far, own_state, far_state, near_state, dnormed_ref = refs[:7]
    *before, normed_ref, back0, back1, back2, back3, u_ref, slab_ref, running = refs[7:]
    _, block, width = normed_ref.shape
    heads = width // DH
    size = 2 * block
    tokens = (own_ref, message_ref.at[:size], token_far.at[:size], token_far.at[size:])
    running[member(0)] = own_state[...]
    running[member(1)] = near_state[part(0, DH), :].astype(F32)
    running[member(2)] = far_state[part(0, DH), :].astype(F32)
    running[member(3)] = near_state[part(1, DH), :].astype(F32)
    total = from_slabs(False, before)
    for p in range(SLAB):
        total, running[p] = total + running[p], total
    sums = [jnp.zeros((DH, DH), F32)] * heads
    for r in range(SLAB):
        out = (back0, back1, back2, back3)[r]
        prior = running[member(r)].astype(BF16)
        out[size:, :] = prior
        for h in range(heads):
            q = tokens[r][:block, head(h)]
            mixed = tokens[r][block:, head(h)].astype(F32) + dot(q, prior[:, head(h)], 1, 0)
            scale = lax.rsqrt(jnp.mean(mixed * mixed, axis=-1, keepdims=True) + EPSILON)
            normed = mixed * scale
            normed_ref[r, :, head(h)] = normed.astype(BF16)
            out[:block, head(h)] = normed.astype(BF16)
            dnormed = dnormed_ref[r, :, head(h)]
            along = jnp.mean(dnormed * normed, axis=-1, keepdims=True)
            dmixed = ((dnormed - normed * along) * scale).astype(BF16)
            out[block:size, head(h)] = dmixed
            u = dot(q, dmixed, 0, 0)
            u_ref[r, :, head(h)] = u
            sums[h] = sums[h] + u
    for h in range(heads):
        slab_ref[:, head(h)] = sums[h].astype(BF16)


def later_kernel(*refs):
    *behind, u_ref, near_ref, far_ref, running = refs
    for r in range(SLAB):
        running[member(r)] = u_ref[r]
    total = from_slabs(True, behind)
    for p in reversed(range(SLAB)):
        total, running[p] = total + running[p], total
    for r in range(SLAB):
        (near_ref, far_ref)[r // 2][part(r % 2, DH), :] = running[member(r)].astype(BF16)


def relay_kernel(near_ref, far_ref, out_ref):
    size = near_ref.shape[0] // 2
    out_ref[:size, :] = near_ref[size:, :]
    out_ref[size:, :] = far_ref[size:, :]


def arrived(near_ref, far_ref, core_ref):
    size = near_ref.shape[0] // 2
    first, second = slice(0, size), slice(size, 2 * size)
    return near_ref.at[first], core_ref.at[first], far_ref.at[first], core_ref.at[second]


def late_kernel(groups, *refs):
    backs, (q_ref, k_ref, v_ref, attend_ref, own_ref) = refs[:SLAB], refs[SLAB : SLAB + 5]
    far, (out_ref, gq_ref, gk_ref, gv_ref, normed_ref) = refs[SLAB + 5 : -5], refs[-5:]
    block, width = q_ref.shape[0], backs[0].shape[1]
    size = 2 * block
    rows = own_ref.shape[0]
    me = lax.axis_index("dp")
    mask = causal(block)
    for r in range(SLAB):
        at = cut(member(r), width)
        normed_ref[:, at] = backs[r][:block, :]
        q, k, v = q_ref[:, at], k_ref[:, at], v_ref[:, at]
        gqs, gks, gvs = [], [], []
        for h in range(width // DH):
            dmixed = backs[r][block:size, head(h)]
            back = jnp.where(mask, dot(dmixed, v[:, head(h)], 1, 1), 0.0).astype(BF16)
            gqs.append(dot(back, k[:, head(h)], 1, 0) + dot(dmixed, backs[r][size:, head(h)], 1, 1))
            gks.append(dot(back, q[:, head(h)], 0, 0))
            gvs.append(dot(attend_ref[r, h], dmixed, 0, 0))
        gq_ref[:, at] = jnp.concatenate(gqs, axis=1).astype(BF16)
        gk_ref[r] = jnp.concatenate(gks, axis=1)
        gv_ref[r] = jnp.concatenate(gvs, axis=1)
    out_ref[:, cut(me, rows)] = dot(normed_ref[...], own_ref[...], 1, 1).astype(BF16)
    for j in range(1, groups):
        total = jnp.zeros((block, rows), F32)
        for r in range(SLAB):
            total = total + dot(backs[r][:block, :], far[2 * (j - 1) + r % 2][r // 2], 1, 1)
        out_ref[:, cut(jnp.bitwise_xor(me, j), rows)] = total.astype(BF16)


def last_kernel(near_ref, far_ref, core_ref, k_ref, v_ref, gk_part, gv_part, gk_ref, gv_ref):
    laters = arrived(near_ref, far_ref, core_ref)
    width = near_ref.shape[1]
    for r in range(SLAB):
        at = cut(member(r), width)
        k, v = k_ref[:, at], v_ref[:, at]
        gks, gvs = [], []
        for h in range(width // DH):
            later = laters[r][:, head(h)]
            gks.append(gk_part[r, :, head(h)] + dot(v[:, head(h)], later, 1, 1))
            gvs.append(gv_part[r, :, head(h)] + dot(k[:, head(h)], later, 1, 0))
        gk_ref[:, at] = jnp.concatenate(gks, axis=1).astype(BF16)
        gv_ref[:, at] = jnp.concatenate(gvs, axis=1).astype(BF16)


def product_kernel(slabs, cot_ref, normed_ref, keep_ref, send_ref):
    me = lax.axis_index("dp")
    slab = lax.div(lax.axis_index("seq"), SLAB)
    rows = keep_ref.shape[0] // slabs
    for j, out in enumerate((send_ref, keep_ref)):
        for d in range(slabs):
            at = jnp.bitwise_xor(me, 1 - j) * slabs + jnp.bitwise_xor(slab, d)
            total = dot(cot_ref[0, :, cut(at, rows)], normed_ref[0], 0, 0)
            for r in range(1, SLAB):
                total = total + dot(cot_ref[r, :, cut(at, rows)], normed_ref[r], 0, 0)
            out[part(d, rows), :] = total.astype(out.dtype)


def split_kernel(own_ref, got_ref, keep_ref, send_ref):
    rows = keep_ref.shape[0] // 2
    for i in range(4):
        total = own_ref[part(i, rows), :] + got_ref[part(i, rows), :].astype(F32)
        out = (keep_ref, send_ref)[i % 2]
        out[part(i // 2, rows), :] = total.astype(out.dtype)


def split_again_kernel(own_ref, got_ref, keep_ref, send_ref):
    rows = keep_ref.shape[0]
    for i, out in enumerate((keep_ref, send_ref)):
        total = own_ref[part(i, rows), :] + got_ref[part(i, rows), :].astype(F32)
        out[...] = total.astype(out.dtype)


def share_kernel(own_ref, got_ref, keep_ref, send_ref, total_ref):
    total_ref[...] = own_ref[...] + got_ref[...].astype(F32)
    rows = keep_ref.shape[0] // 2
    for i, r in enumerate((0, 1)):
        keep_ref[part(i, rows), :] = total_ref[cut(member(r), rows), :]
    for i, r in enumerate((2, 3)):
        send_ref[part(i, rows), :] = total_ref[cut(member(r), rows), :]


def pass_kernel(own_ref, got_ref, keep_ref, send_ref):
    rows = own_ref.shape[0] // 2
    for i, ref in enumerate((own_ref, got_ref)):
        keep_ref[part(i, rows), :] = ref[:rows, :]
        send_ref[part(i, rows), :] = ref[rows:, :]


def finish_kernel(factor, keep_ref, got_ref, out_ref):
    rows, width = out_ref.shape[0], keep_ref.shape[1]
    for i, ref in enumerate((keep_ref, got_ref)):
        for j in range(2):
            out_ref[:, cut(member(i + 2 * j), width)] = ref[part(j, rows), :] * factor


def local(queries, keys, values, cotangent, out_weight, *, dp, seq):
    call = Chain()
    local_seqs, block, features = queries.shape
    outputs = cotangent.shape[2]
    rows = local_seqs * block
    slabs = seq // SLAB
    width = features // SLAB
    heads = width // DH
    q, k, v = (x.reshape(rows, features) for x in (queries, keys, values))
    cot = cotangent.reshape(rows, outputs)
    factor = 1.0 / math.sqrt(rows * dp * seq)
    near = functools.partial(flip, axis="seq", count=seq)

    def doubling(total, cost=1):
        found = []
        bits = SLAB
        while bits < seq:
            if found:
                (total,) = call(add_kernel, [(total.shape, BF16)], total, found[-1], cost=cost)
            found.append(near(total, bits=bits))
            bits *= 2
        return found, total

    def scratch(*arrays):
        return [pltpu.VMEM(x.shape, BF16) for x in arrays] + [pltpu.SemaphoreType.DMA((len(arrays),))]

    cot_y = near(cot, bits=2)
    own_state, near_state, far_state, columns = call(
        front_kernel,
        [((DH, width), F32), ((DH, width), BF16), ((2 * DH, width), BF16),
         ((2, out_weight.shape[0], width), BF16)],
        k, v, out_weight, far=True, scratch=scratch(k, v, out_weight),
    )
    far_state = near(far_state, bits=2)
    w_far = [flip(columns, "dp", dp, j) for j in range(1, dp)]
    attend, own_tokens, message, far_tokens = call(
        pack_kernel,
        [((SLAB, heads, rows, rows), BF16), ((2 * rows, width), BF16),
         (((4 + outputs // width) * rows, width), BF16), ((2 * rows, width), BF16)],
        q, k, v, cot, far=True, scratch=scratch(q, k, v, cot),
    )
    message = near(message, bits=1)
    (near_state,) = call(
        cross_kernel, [((2 * DH, width), BF16)], near_state, far_state, cost=5 * 10**9
    )
    near_state = near(near_state, bits=1)
    (slab_kv,) = call(total_kernel, [((DH, width), BF16)], own_state, far_state, near_state)
    (far_tokens,) = call(pair_kernel, [((4 * rows, width), BF16)], message, far_tokens)
    cot_yc = near(after(cot_y, far_tokens), bits=1)
    far_tokens = near(far_tokens, bits=2)
    before, _ = doubling(slab_kv, 22 * 10**8)
    dnormed, cots = call(
        functools.partial(dnormed_kernel, dp),
        [((SLAB, rows, width), F32), ((SLAB, rows, outputs), BF16)],
        message, cot, cot_y, cot_yc, columns, *w_far,
    )
    w_all = [x for w in w_far for x in (w, near(after(w, dnormed), bits=1))]
    normed, *backs, u, slab_u = call(
        middle_kernel,
        [((SLAB, rows, width), BF16)] + [((2 * rows + DH, width), BF16)] * SLAB
        + [((SLAB, DH, width), F32), ((DH, width), BF16)],
        own_tokens, message, far_tokens, own_state, far_state, near_state, dnormed, *before,
        cost=10**10, scratch=[pltpu.VMEM((SLAB, DH, width), F32)],
    )
    tuned = dp == 2 and slabs == 4 and outputs // (dp * seq) % 8 == 0
    piece = outputs // (dp * slabs)
    if tuned:
        keep, send = call(
            functools.partial(product_kernel, slabs),
            [((outputs // dp, width), F32), ((outputs // dp, width), BF16)], cots, normed, wait=w_all[1::2],
        )
        got = flip(send, "dp", dp, 1)
    backs = [backs[0], *(near(backs[r], bits=r) for r in range(1, SLAB))]
    behind, last_u = doubling(slab_u, 10**9)
    if tuned:
        keep, send = call(
            split_kernel, [((2 * piece, width), F32), ((2 * piece, width), BF16)], keep, got, cost=1
        )
        got = near(send, bits=SLAB)
    later, later_far = call(
        later_kernel, [((2 * DH, width), BF16)] * 2, *behind, u, cost=10**9, wait=backs[1:],
        scratch=[pltpu.VMEM((SLAB, DH, width), F32)],
    )
    later_far = near(later_far, bits=2)
    if tuned:
        keep, send = call(
            split_again_kernel, [((piece, width), F32), ((piece, width), BF16)], keep, got, cost=1
        )
        got = near(send, bits=2 * SLAB)
    (send,) = call(relay_kernel, [((2 * DH, width), BF16)], later, later_far)
    later_core = near(send, bits=1)
    output, gq, gk_part, gv_part, own_normed = call(
        functools.partial(late_kernel, dp),
        [((rows, outputs), BF16), ((rows, features), BF16), ((SLAB, rows, width), F32),
         ((SLAB, rows, width), F32), ((rows, features), BF16)],
        *backs, q, k, v, attend, out_weight, *w_all,
    )
    if tuned:
        keep, share = call(
            share_kernel, [((piece // 2, width), F32)] * 2, keep, got,
            scratch=[pltpu.VMEM((piece, width), F32)],
        )
        got = near(share, bits=2)
    gk, gv = call(
        last_kernel, [((rows, features), BF16)] * 2,
        later, later_far, later_core, k, v, gk_part, gv_part, end=True,
    )
    if tuned:
        keep, share = call(pass_kernel, [((piece // 2, width), F32)] * 2, keep, got)
        got = near(share, bits=1)
    if tuned:
        (grad_weight,) = call(
            functools.partial(finish_kernel, factor),
            [((piece // SLAB, features), F32)], keep, got, end=True,
        )
    else:
        partial = dot(cot, own_normed, 0, 0) * factor
        grad_weight = lax.psum_scatter(partial, ("dp", "seq"), scatter_dimension=0, tiled=True)
    shape = queries.shape
    return (
        output.reshape(cotangent.shape), gq.reshape(shape), gk.reshape(shape), gv.reshape(shape),
        grad_weight,
    )


def solution(mesh):
    dp, seq = mesh.shape["dp"], mesh.shape["seq"]
    return jax.shard_map(
        functools.partial(local, dp=dp, seq=seq),
        mesh=mesh,
        in_specs=(P("dp", "seq", None),) * 4 + (P("dp", None),),
        out_specs=(P("dp", "seq", None),) * 4 + (P(("dp", "seq"), None),),
        check_vma=False,
    )
```

```python
import functools
import math

import jax
import jax.numpy as jnp
from jax import lax
from jax.experimental import pallas as pl
from jax.experimental.pallas import tpu as pltpu
from jax.sharding import PartitionSpec as P

DH = 128
SLAB = 4
EPSILON = 1e-05
BF16 = jnp.bfloat16
F32 = jnp.float32


def dot(left, right, left_dim, right_dim):
    return lax.dot_general(
        left, right, (((left_dim,), (right_dim,)), ((), ())), preferred_element_type=F32
    )


class Chain:
    def __init__(self):
        self.last = None

    def __call__(self, body, outs, *args, scratch=(), far=False, wait=(), cost=1, end=False):
        count = len(args)
        if far:
            args = [pltpu.with_memory_space_constraint(x, pltpu.HBM) for x in args]
        specs = [pl.BlockSpec(memory_space=pl.ANY) if far else pl.BlockSpec()] * count
        inner = body
        if self.last is not None:
            extra = (self.last, *wait)
            args = (*args, *extra)
            specs = [*specs, *[pl.BlockSpec(memory_space=pl.ANY)] * len(extra)]

            def inner(*refs):
                body(*refs[:count], *refs[count + len(extra) :])

        found = pl.pallas_call(
            inner,
            out_shape=[jax.ShapeDtypeStruct(s, d) for s, d in outs],
            in_specs=specs,
            scratch_shapes=list(scratch),
            cost_estimate=pl.CostEstimate(flops=cost, bytes_accessed=1, transcendentals=0),
            compiler_params=pltpu.CompilerParams(vmem_limit_bytes=32 * 2**20),
        )(*args)
        if not end:
            self.last = min(reversed(found), key=lambda x: x.size)
        return found


def after(x, *others):
    return lax.optimization_barrier((x, *others))[0]


def flip(x, axis, count, bits):
    return lax.ppermute(x, axis, [(i, i ^ bits) for i in range(count)])


def head(h):
    return slice(h * DH, (h + 1) * DH)


def part(i, size):
    return slice(i * size, (i + 1) * size)


def cut(start, size):
    return pl.ds(pl.multiple_of(start * size, size), size)


def member(r):
    return jnp.bitwise_xor(lax.rem(lax.axis_index("seq"), SLAB), r)


def causal(block):
    rows = lax.broadcasted_iota(jnp.int32, (block, block), 0)
    return lax.broadcasted_iota(jnp.int32, (block, block), 1) <= rows


def fetch(pairs, sems):
    copies = [pltpu.make_async_copy(a, b, sems.at[i]) for i, (a, b) in enumerate(pairs)]
    for copy in copies:
        copy.start()
    return copies


def front_kernel(k_hbm, v_hbm, w_hbm, own_ref, near_ref, far_ref, columns_ref, k_ref, v_ref, w_ref, sems):
    copies = fetch([(k_hbm, k_ref), (v_hbm, v_ref), (w_hbm, w_ref)], sems)
    width = k_ref.shape[1] // SLAB
    copies[0].wait()
    copies[1].wait()
    places = (own_ref, near_ref, far_ref.at[part(0, DH)], far_ref.at[part(1, DH)])
    for r, out in enumerate(places):
        k, v = k_ref[:, cut(member(r), width)], v_ref[:, cut(member(r), width)]
        for h in range(width // DH):
            out[:, head(h)] = dot(k[:, head(h)], v[:, head(h)], 0, 0).astype(out.dtype)
    copies[2].wait()
    for i in range(2):
        columns_ref[i] = w_ref[:, cut(member(2 * i), width)]


def pack_kernel(q_ref, k_ref, v_ref, c_ref, attend_ref, own_ref, message_ref, far_ref):
    block = q_ref.shape[0]
    width = q_ref.shape[1] // SLAB
    mask = causal(block)
    places = (own_ref, message_ref.at[: 2 * block], far_ref, message_ref.at[2 * block : 4 * block])
    for r, out in enumerate(places):
        q, k, v = (ref[:, cut(member(r), width)] for ref in (q_ref, k_ref, v_ref))
        out[:block, :] = q
        for h in range(width // DH):
            attend = jnp.where(mask, dot(q[:, head(h)], k[:, head(h)], 1, 1), 0.0).astype(BF16)
            attend_ref[r, h] = attend
            out[block:, head(h)] = dot(attend, v[:, head(h)], 1, 0).astype(BF16)
    for i in range(c_ref.shape[1] // width):
        message_ref[part(4 + i, block), :] = c_ref[:, part(i, width)]


def cross_kernel(near_ref, got_ref, out_ref):
    out_ref[part(0, DH), :] = near_ref[...]
    out_ref[part(1, DH), :] = got_ref[part(1, DH), :]


def total_kernel(own_ref, far_ref, near_ref, out_ref):
    total = own_ref[...] + far_ref[part(0, DH), :].astype(F32)
    total = total + near_ref[part(0, DH), :].astype(F32) + near_ref[part(1, DH), :].astype(F32)
    out_ref[...] = total.astype(BF16)


def pair_kernel(message_ref, far_ref, out_ref):
    size = far_ref.shape[0]
    out_ref[:size, :] = far_ref[...]
    out_ref[size:, :] = message_ref[part(1, size), :]


def add_kernel(own_ref, got_ref, out_ref):
    out_ref[...] = (own_ref[...].astype(F32) + got_ref[...].astype(F32)).astype(out_ref.dtype)


def dnormed_kernel(groups, message_ref, *refs):
    cots, weights = refs[: SLAB - 1], refs[SLAB - 1 : SLAB - 1 + groups]
    dnormed_ref, cot_ref = refs[SLAB - 1 + groups :]
    block, outputs = cots[0].shape
    width = dnormed_ref.shape[2]
    rows = weights[0].shape[1]
    me = lax.axis_index("dp")
    for i in range(outputs // width):
        cot_ref[1, :, part(i, width)] = message_ref[part(4 + i, block), :]
    for r, ref in zip((0, 2, 3), cots):
        cot_ref[r] = ref[...]
    for r in range(SLAB):
        total = dot(cot_ref[r, :, cut(me, rows)], weights[0][0], 1, 0)
        for j in range(1, groups):
            total = total + dot(cot_ref[r, :, cut(jnp.bitwise_xor(me, j), rows)], weights[j][0], 1, 0)
        dnormed_ref[r] = total


def from_slabs(backward, refs):
    slab = lax.div(lax.axis_index("seq"), SLAB)
    total = jnp.zeros(refs[0].shape, F32)
    for i, ref in enumerate(refs):
        bit = lax.rem(lax.div(slab, 1 << i), 2)
        total = total + jnp.where(bit == (0 if backward else 1), ref[...].astype(F32), 0.0)
    return total


def middle_kernel(*refs):
    own_ref, message_ref, token_far, own_state, far_state, near_state, dnormed_ref = refs[:7]
    *before, normed_ref, back0, back1, back2, back3, u_ref, slab_ref, running = refs[7:]
    _, block, width = normed_ref.shape
    heads = width // DH
    size = 2 * block
    tokens = (own_ref, message_ref.at[:size], token_far.at[:size], token_far.at[size:])
    running[member(0)] = own_state[...]
    running[member(1)] = near_state[part(0, DH), :].astype(F32)
    running[member(2)] = far_state[part(0, DH), :].astype(F32)
    running[member(3)] = near_state[part(1, DH), :].astype(F32)
    total = from_slabs(False, before)
    for p in range(SLAB):
        total, running[p] = total + running[p], total
    sums = [jnp.zeros((DH, DH), F32)] * heads
    for r in range(SLAB):
        out = (back0, back1, back2, back3)[r]
        prior = running[member(r)].astype(BF16)
        out[size:, :] = prior
        for h in range(heads):
            q = tokens[r][:block, head(h)]
            mixed = tokens[r][block:, head(h)].astype(F32) + dot(q, prior[:, head(h)], 1, 0)
            scale = lax.rsqrt(jnp.mean(mixed * mixed, axis=-1, keepdims=True) + EPSILON)
            normed = mixed * scale
            normed_ref[r, :, head(h)] = normed.astype(BF16)
            out[:block, head(h)] = normed.astype(BF16)
            dnormed = dnormed_ref[r, :, head(h)]
            along = jnp.mean(dnormed * normed, axis=-1, keepdims=True)
            dmixed = ((dnormed - normed * along) * scale).astype(BF16)
            out[block:size, head(h)] = dmixed
            u = dot(q, dmixed, 0, 0)
            u_ref[r, :, head(h)] = u
            sums[h] = sums[h] + u
    for h in range(heads):
        slab_ref[:, head(h)] = sums[h].astype(BF16)


def later_kernel(*refs):
    *behind, u_ref, near_ref, far_ref, running = refs
    for r in range(SLAB):
        running[member(r)] = u_ref[r]
    total = from_slabs(True, behind)
    for p in reversed(range(SLAB)):
        total, running[p] = total + running[p], total
    for r in range(SLAB):
        (near_ref, far_ref)[r // 2][part(r % 2, DH), :] = running[member(r)].astype(BF16)


def relay_kernel(near_ref, far_ref, out_ref):
    size = near_ref.shape[0] // 2
    out_ref[:size, :] = near_ref[size:, :]
    out_ref[size:, :] = far_ref[size:, :]


def arrived(near_ref, far_ref, core_ref):
    size = near_ref.shape[0] // 2
    first, second = slice(0, size), slice(size, 2 * size)
    return near_ref.at[first], core_ref.at[first], far_ref.at[first], core_ref.at[second]


def late_kernel(groups, *refs):
    backs, (q_ref, k_ref, v_ref, attend_ref, own_ref) = refs[:SLAB], refs[SLAB : SLAB + 5]
    far, (out_ref, gq_ref, gk_ref, gv_ref, normed_ref) = refs[SLAB + 5 : -5], refs[-5:]
    block, width = q_ref.shape[0], backs[0].shape[1]
    size = 2 * block
    rows = own_ref.shape[0]
    me = lax.axis_index("dp")
    mask = causal(block)
    for r in range(SLAB):
        at = cut(member(r), width)
        normed_ref[:, at] = backs[r][:block, :]
        q, k, v = q_ref[:, at], k_ref[:, at], v_ref[:, at]
        gqs, gks, gvs = [], [], []
        for h in range(width // DH):
            dmixed = backs[r][block:size, head(h)]
            back = jnp.where(mask, dot(dmixed, v[:, head(h)], 1, 1), 0.0).astype(BF16)
            gqs.append(dot(back, k[:, head(h)], 1, 0) + dot(dmixed, backs[r][size:, head(h)], 1, 1))
            gks.append(dot(back, q[:, head(h)], 0, 0))
            gvs.append(dot(attend_ref[r, h], dmixed, 0, 0))
        gq_ref[:, at] = jnp.concatenate(gqs, axis=1).astype(BF16)
        gk_ref[r] = jnp.concatenate(gks, axis=1)
        gv_ref[r] = jnp.concatenate(gvs, axis=1)
    out_ref[:, cut(me, rows)] = dot(normed_ref[...], own_ref[...], 1, 1).astype(BF16)
    for j in range(1, groups):
        total = jnp.zeros((block, rows), F32)
        for r in range(SLAB):
            total = total + dot(backs[r][:block, :], far[2 * (j - 1) + r % 2][r // 2], 1, 1)
        out_ref[:, cut(jnp.bitwise_xor(me, j), rows)] = total.astype(BF16)


def last_kernel(near_ref, far_ref, core_ref, k_ref, v_ref, gk_part, gv_part, gk_ref, gv_ref):
    laters = arrived(near_ref, far_ref, core_ref)
    width = near_ref.shape[1]
    for r in range(SLAB):
        at = cut(member(r), width)
        k, v = k_ref[:, at], v_ref[:, at]
        gks, gvs = [], []
        for h in range(width // DH):
            later = laters[r][:, head(h)]
            gks.append(gk_part[r, :, head(h)] + dot(v[:, head(h)], later, 1, 1))
            gvs.append(gv_part[r, :, head(h)] + dot(k[:, head(h)], later, 1, 0))
        gk_ref[:, at] = jnp.concatenate(gks, axis=1).astype(BF16)
        gv_ref[:, at] = jnp.concatenate(gvs, axis=1).astype(BF16)


def product_kernel(slabs, cot_ref, normed_ref, keep_ref, send_ref):
    me = lax.axis_index("dp")
    slab = lax.div(lax.axis_index("seq"), SLAB)
    rows = keep_ref.shape[0] // slabs
    for j, out in enumerate((send_ref, keep_ref)):
        for d in range(slabs):
            at = jnp.bitwise_xor(me, 1 - j) * slabs + jnp.bitwise_xor(slab, d)
            total = dot(cot_ref[0, :, cut(at, rows)], normed_ref[0], 0, 0)
            for r in range(1, SLAB):
                total = total + dot(cot_ref[r, :, cut(at, rows)], normed_ref[r], 0, 0)
            out[part(d, rows), :] = total.astype(out.dtype)


def split_kernel(own_ref, got_ref, keep_ref, send_ref):
    rows = keep_ref.shape[0] // 2
    for i in range(4):
        total = own_ref[part(i, rows), :] + got_ref[part(i, rows), :].astype(F32)
        out = (keep_ref, send_ref)[i % 2]
        out[part(i // 2, rows), :] = total.astype(out.dtype)


def split_again_kernel(own_ref, got_ref, keep_ref, send_ref):
    rows = keep_ref.shape[0]
    for i, out in enumerate((keep_ref, send_ref)):
        total = own_ref[part(i, rows), :] + got_ref[part(i, rows), :].astype(F32)
        out[...] = total.astype(out.dtype)


def share_kernel(own_ref, got_ref, keep_ref, send_ref, total_ref):
    total_ref[...] = own_ref[...] + got_ref[...].astype(F32)
    rows = keep_ref.shape[0] // 2
    for i, r in enumerate((0, 1)):
        keep_ref[part(i, rows), :] = total_ref[cut(member(r), rows), :].astype(BF16)
    for i, r in enumerate((2, 3)):
        send_ref[part(i, rows), :] = total_ref[cut(member(r), rows), :].astype(BF16)


def pass_kernel(own_ref, got_ref, keep_ref, send_ref):
    rows = own_ref.shape[0] // 2
    for i, ref in enumerate((own_ref, got_ref)):
        keep_ref[part(i, rows), :] = ref[:rows, :]
        send_ref[part(i, rows), :] = ref[rows:, :]


def finish_kernel(factor, keep_ref, got_ref, out_ref):
    rows, width = out_ref.shape[0], keep_ref.shape[1]
    for i, ref in enumerate((keep_ref, got_ref)):
        for j in range(2):
            out_ref[:, cut(member(i + 2 * j), width)] = ref[part(j, rows), :].astype(F32) * factor


def local(queries, keys, values, cotangent, out_weight, *, dp, seq):
    call = Chain()
    local_seqs, block, features = queries.shape
    outputs = cotangent.shape[2]
    rows = local_seqs * block
    slabs = seq // SLAB
    width = features // SLAB
    heads = width // DH
    q, k, v = (x.reshape(rows, features) for x in (queries, keys, values))
    cot = cotangent.reshape(rows, outputs)
    factor = 1.0 / math.sqrt(rows * dp * seq)
    near = functools.partial(flip, axis="seq", count=seq)

    def doubling(total, cost=1):
        found = []
        bits = SLAB
        while bits < seq:
            if found:
                (total,) = call(add_kernel, [(total.shape, BF16)], total, found[-1], cost=cost)
            found.append(near(total, bits=bits))
            bits *= 2
        return found, total

    def scratch(*arrays):
        return [pltpu.VMEM(x.shape, BF16) for x in arrays] + [pltpu.SemaphoreType.DMA((len(arrays),))]

    cot_y = near(cot, bits=2)
    own_state, near_state, far_state, columns = call(
        front_kernel,
        [((DH, width), F32), ((DH, width), BF16), ((2 * DH, width), BF16),
         ((2, out_weight.shape[0], width), BF16)],
        k, v, out_weight, far=True, scratch=scratch(k, v, out_weight),
    )
    far_state = near(far_state, bits=2)
    w_far = [flip(columns, "dp", dp, j) for j in range(1, dp)]
    attend, own_tokens, message, far_tokens = call(
        pack_kernel,
        [((SLAB, heads, rows, rows), BF16), ((2 * rows, width), BF16),
         (((4 + outputs // width) * rows, width), BF16), ((2 * rows, width), BF16)],
        q, k, v, cot,
    )
    message = near(message, bits=1)
    (near_state,) = call(
        cross_kernel, [((2 * DH, width), BF16)], near_state, far_state, cost=5 * 10**9
    )
    near_state = near(near_state, bits=1)
    (slab_kv,) = call(total_kernel, [((DH, width), BF16)], own_state, far_state, near_state)
    (far_tokens,) = call(pair_kernel, [((4 * rows, width), BF16)], message, far_tokens)
    cot_yc = near(after(cot_y, far_tokens), bits=1)
    far_tokens = near(far_tokens, bits=2)
    before, _ = doubling(slab_kv, 22 * 10**8)
    dnormed, cots = call(
        functools.partial(dnormed_kernel, dp),
        [((SLAB, rows, width), F32), ((SLAB, rows, outputs), BF16)],
        message, cot, cot_y, cot_yc, columns, *w_far,
    )
    w_all = [x for w in w_far for x in (w, near(after(w, dnormed), bits=1))]
    normed, *backs, u, slab_u = call(
        middle_kernel,
        [((SLAB, rows, width), BF16)] + [((2 * rows + DH, width), BF16)] * SLAB
        + [((SLAB, DH, width), F32), ((DH, width), BF16)],
        own_tokens, message, far_tokens, own_state, far_state, near_state, dnormed, *before,
        cost=10**10, scratch=[pltpu.VMEM((SLAB, DH, width), F32)],
    )
    tuned = dp == 2 and slabs == 4 and outputs // (dp * seq) % 8 == 0
    piece = outputs // (dp * slabs)
    if tuned:
        keep, send = call(
            functools.partial(product_kernel, slabs),
            [((outputs // dp, width), F32), ((outputs // dp, width), BF16)], cots, normed,
        )
        got = flip(send, "dp", dp, 1)
    backs = [backs[0], *(near(backs[r], bits=r) for r in range(1, SLAB))]
    behind, last_u = doubling(slab_u, 10**9)
    if tuned:
        keep, send = call(
            split_kernel, [((2 * piece, width), F32), ((2 * piece, width), BF16)], keep, got, wait=w_all[1::2]
        )
        got = near(send, bits=SLAB)
    later, later_far = call(
        later_kernel, [((2 * DH, width), BF16)] * 2, *behind, u, cost=10**9, wait=backs[1:3],
        scratch=[pltpu.VMEM((SLAB, DH, width), F32)],
    )
    later_far = near(later_far, bits=2)
    if tuned:
        keep, send = call(
            split_again_kernel, [((piece, width), F32), ((piece, width), BF16)], keep, got, cost=3 * 10**8
        )
        got = near(send, bits=2 * SLAB)
    output, gq, gk_part, gv_part, own_normed = call(
        functools.partial(late_kernel, dp),
        [((rows, outputs), BF16), ((rows, features), BF16), ((SLAB, rows, width), F32),
         ((SLAB, rows, width), F32), ((rows, features), BF16)],
        *backs, q, k, v, attend, out_weight, *w_all,
    )
    if tuned:
        keep, share = call(
            share_kernel, [((piece // 2, width), BF16)] * 2, keep, got,
            scratch=[pltpu.VMEM((piece, width), F32)],
        )
        got = near(share, bits=2)
    (send,) = call(relay_kernel, [((2 * DH, width), BF16)], later, later_far)
    later_core = near(send, bits=1)
    if tuned:
        keep, share = call(pass_kernel, [((piece // 2, width), BF16)] * 2, keep, got, cost=3 * 10**9)
        got = near(share, bits=1)
    gk, gv = call(
        last_kernel, [((rows, features), BF16)] * 2,
        later, later_far, later_core, k, v, gk_part, gv_part, end=True,
    )
    if tuned:
        (grad_weight,) = call(
            functools.partial(finish_kernel, factor),
            [((piece // SLAB, features), F32)], keep, got, end=True,
            wait=[pltpu.with_memory_space_constraint(gk, pltpu.HBM)],
        )
    else:
        partial = dot(cot, own_normed, 0, 0) * factor
        grad_weight = lax.psum_scatter(partial, ("dp", "seq"), scatter_dimension=0, tiled=True)
    shape = queries.shape
    return (
        output.reshape(cotangent.shape), gq.reshape(shape), gk.reshape(shape), gv.reshape(shape),
        grad_weight,
    )


def solution(mesh):
    dp, seq = mesh.shape["dp"], mesh.shape["seq"]
    return jax.shard_map(
        functools.partial(local, dp=dp, seq=seq),
        mesh=mesh,
        in_specs=(P("dp", "seq", None),) * 4 + (P("dp", None),),
        out_specs=(P("dp", "seq", None),) * 4 + (P(("dp", "seq"), None),),
        check_vma=False,
    )
```

```python
import functools
import math

import jax
import jax.numpy as jnp
from jax import lax
from jax.experimental import pallas as pl
from jax.experimental.pallas import tpu as pltpu
from jax.sharding import PartitionSpec as P

DH = 128
SLAB = 4
EPSILON = 1e-05
BF16 = jnp.bfloat16
F32 = jnp.float32


def dot(left, right, left_dim, right_dim):
    return lax.dot_general(
        left, right, (((left_dim,), (right_dim,)), ((), ())), preferred_element_type=F32
    )


class Chain:
    def __init__(self):
        self.last = None

    def __call__(self, body, outs, *args, scratch=(), far=False, wait=(), cost=1, end=False):
        count = len(args)
        if far:
            args = [pltpu.with_memory_space_constraint(x, pltpu.HBM) for x in args]
        specs = [pl.BlockSpec(memory_space=pl.ANY) if far else pl.BlockSpec()] * count
        inner = body
        if self.last is not None:
            extra = (self.last, *wait)
            args = (*args, *extra)
            specs = [*specs, *[pl.BlockSpec(memory_space=pl.ANY)] * len(extra)]

            def inner(*refs):
                body(*refs[:count], *refs[count + len(extra) :])

        found = pl.pallas_call(
            inner,
            out_shape=[jax.ShapeDtypeStruct(s, d) for s, d in outs],
            in_specs=specs,
            scratch_shapes=list(scratch),
            cost_estimate=pl.CostEstimate(flops=cost, bytes_accessed=1, transcendentals=0),
            compiler_params=pltpu.CompilerParams(vmem_limit_bytes=32 * 2**20),
        )(*args)
        if not end:
            self.last = min(reversed(found), key=lambda x: x.size)
        return found


def after(x, *others):
    return lax.optimization_barrier((x, *others))[0]


def flip(x, axis, count, bits):
    return lax.ppermute(x, axis, [(i, i ^ bits) for i in range(count)])


def head(h):
    return slice(h * DH, (h + 1) * DH)


def part(i, size):
    return slice(i * size, (i + 1) * size)


def cut(start, size):
    return pl.ds(pl.multiple_of(start * size, size), size)


def member(r):
    return jnp.bitwise_xor(lax.rem(lax.axis_index("seq"), SLAB), r)


def causal(block):
    rows = lax.broadcasted_iota(jnp.int32, (block, block), 0)
    return lax.broadcasted_iota(jnp.int32, (block, block), 1) <= rows


def fetch(pairs, sems):
    copies = [pltpu.make_async_copy(a, b, sems.at[i]) for i, (a, b) in enumerate(pairs)]
    for copy in copies:
        copy.start()
    return copies


def front_kernel(k_hbm, v_hbm, w_hbm, own_ref, near_ref, far_ref, columns_ref, k_ref, v_ref, w_ref, sems):
    copies = fetch([(k_hbm, k_ref), (v_hbm, v_ref), (w_hbm, w_ref)], sems)
    width = k_ref.shape[1] // SLAB
    copies[0].wait()
    copies[1].wait()
    places = (own_ref, near_ref, far_ref.at[part(0, DH)], far_ref.at[part(1, DH)])
    for r, out in enumerate(places):
        k, v = k_ref[:, cut(member(r), width)], v_ref[:, cut(member(r), width)]
        for h in range(width // DH):
            out[:, head(h)] = dot(k[:, head(h)], v[:, head(h)], 0, 0).astype(out.dtype)
    copies[2].wait()
    for i in range(2):
        columns_ref[i] = w_ref[:, cut(member(2 * i), width)]


def pack_kernel(q_ref, k_ref, v_ref, c_ref, attend_ref, own_ref, message_ref, far_ref, cot_ref):
    cot_ref[...] = c_ref[...]
    block = q_ref.shape[0]
    width = q_ref.shape[1] // SLAB
    mask = causal(block)
    places = (own_ref, message_ref.at[: 2 * block], far_ref, message_ref.at[2 * block : 4 * block])
    for r, out in enumerate(places):
        q, k, v = (ref[:, cut(member(r), width)] for ref in (q_ref, k_ref, v_ref))
        out[:block, :] = q
        for h in range(width // DH):
            attend = jnp.where(mask, dot(q[:, head(h)], k[:, head(h)], 1, 1), 0.0).astype(BF16)
            attend_ref[r, h] = attend
            out[block:, head(h)] = dot(attend, v[:, head(h)], 1, 0).astype(BF16)
    for i in range(c_ref.shape[1] // width):
        message_ref[part(4 + i, block), :] = c_ref[:, part(i, width)]


def cross_kernel(near_ref, got_ref, out_ref):
    out_ref[part(0, DH), :] = near_ref[...]
    out_ref[part(1, DH), :] = got_ref[part(1, DH), :]


def total_kernel(own_ref, far_ref, near_ref, out_ref):
    total = own_ref[...] + far_ref[part(0, DH), :].astype(F32)
    total = total + near_ref[part(0, DH), :].astype(F32) + near_ref[part(1, DH), :].astype(F32)
    out_ref[...] = total.astype(BF16)


def pair_kernel(message_ref, far_ref, out_ref):
    size = far_ref.shape[0]
    out_ref[:size, :] = far_ref[...]
    out_ref[size:, :] = message_ref[part(1, size), :]


def add_kernel(own_ref, got_ref, out_ref):
    out_ref[...] = (own_ref[...].astype(F32) + got_ref[...].astype(F32)).astype(out_ref.dtype)


def dnormed_kernel(groups, message_ref, *refs):
    cots, weights = refs[: SLAB - 1], refs[SLAB - 1 : SLAB - 1 + groups]
    dnormed_ref, cot_ref = refs[SLAB - 1 + groups :]
    block, outputs = cots[0].shape
    width = dnormed_ref.shape[2]
    rows = weights[0].shape[1]
    me = lax.axis_index("dp")
    for i in range(outputs // width):
        cot_ref[1, :, part(i, width)] = message_ref[part(4 + i, block), :]
    for r, ref in zip((0, 2, 3), cots):
        cot_ref[r] = ref[...]
    for r in range(SLAB):
        total = dot(cot_ref[r, :, cut(me, rows)], weights[0][0], 1, 0)
        for j in range(1, groups):
            total = total + dot(cot_ref[r, :, cut(jnp.bitwise_xor(me, j), rows)], weights[j][0], 1, 0)
        dnormed_ref[r] = total


def from_slabs(backward, refs):
    slab = lax.div(lax.axis_index("seq"), SLAB)
    total = jnp.zeros(refs[0].shape, F32)
    for i, ref in enumerate(refs):
        bit = lax.rem(lax.div(slab, 1 << i), 2)
        total = total + jnp.where(bit == (0 if backward else 1), ref[...].astype(F32), 0.0)
    return total


def middle_kernel(*refs):
    own_ref, message_ref, token_far, own_state, far_state, near_state, dnormed_ref = refs[:7]
    *before, normed_ref, back_near, back_far, u_ref, slab_ref, running = refs[7:]
    _, block, width = normed_ref.shape
    heads = width // DH
    size = 2 * block
    tokens = (own_ref, message_ref.at[:size], token_far.at[:size], token_far.at[size:])
    running[member(0)] = own_state[...]
    running[member(1)] = near_state[part(0, DH), :].astype(F32)
    running[member(2)] = far_state[part(0, DH), :].astype(F32)
    running[member(3)] = near_state[part(1, DH), :].astype(F32)
    total = from_slabs(False, before)
    for p in range(SLAB):
        total, running[p] = total + running[p], total
    sums = [jnp.zeros((DH, DH), F32)] * heads
    for r in range(SLAB):
        out = (back_near, back_far)[r // 2].at[part(r % 2, block + DH)]
        prior = running[member(r)].astype(BF16)
        out[block:, :] = prior
        for h in range(heads):
            q = tokens[r][:block, head(h)]
            mixed = tokens[r][block:, head(h)].astype(F32) + dot(q, prior[:, head(h)], 1, 0)
            scale = lax.rsqrt(jnp.mean(mixed * mixed, axis=-1, keepdims=True) + EPSILON)
            normed = mixed * scale
            normed_ref[r, :, head(h)] = normed.astype(BF16)
            dnormed = dnormed_ref[r, :, head(h)]
            along = jnp.mean(dnormed * normed, axis=-1, keepdims=True)
            dmixed = ((dnormed - normed * along) * scale).astype(BF16)
            out[:block, head(h)] = dmixed
            u = dot(q, dmixed, 0, 0)
            u_ref[r, :, head(h)] = u
            sums[h] = sums[h] + u
    for h in range(heads):
        slab_ref[:, head(h)] = sums[h].astype(BF16)


def later_kernel(*refs):
    *behind, u_ref, near_ref, far_ref, running = refs
    for r in range(SLAB):
        running[member(r)] = u_ref[r]
    total = from_slabs(True, behind)
    for p in reversed(range(SLAB)):
        total, running[p] = total + running[p], total
    for r in range(SLAB):
        (near_ref, far_ref)[r // 2][part(r % 2, DH), :] = running[member(r)].astype(BF16)


def relay_kernel(near_ref, far_ref, out_ref):
    size = near_ref.shape[0] // 2
    out_ref[:size, :] = near_ref[size:, :]
    out_ref[size:, :] = far_ref[size:, :]


def arrived(near_ref, far_ref, core_ref):
    size = near_ref.shape[0] // 2
    first, second = slice(0, size), slice(size, 2 * size)
    return near_ref.at[first], core_ref.at[first], far_ref.at[first], core_ref.at[second]


def late_kernel(groups, *refs):
    backs, (q_ref, k_ref, v_ref, attend_ref, own_ref, message_ref, far_ref) = arrived(*refs[:3]), refs[3:10]
    weight_ref, *far, out_ref, gq_ref, gk_ref, gv_ref, normed_ref = refs[10:]
    block, width = q_ref.shape[0], refs[0].shape[1]
    rows = weight_ref.shape[0]
    me = lax.axis_index("dp")
    mask = causal(block)
    withins = (own_ref.at[part(1, block)], message_ref.at[part(1, block)],
               far_ref.at[part(1, block)], message_ref.at[part(3, block)])
    for r in range(SLAB):
        at = cut(member(r), width)
        q, k, v = q_ref[:, at], k_ref[:, at], v_ref[:, at]
        normeds, gqs, gks, gvs = [], [], [], []
        for h in range(width // DH):
            dmixed, prior = backs[r][:block, head(h)], backs[r][block:, head(h)]
            mixed = withins[r][:, head(h)].astype(F32) + dot(q[:, head(h)], prior, 1, 0)
            scale = lax.rsqrt(jnp.mean(mixed * mixed, axis=-1, keepdims=True) + EPSILON)
            normeds.append(mixed * scale)
            back = jnp.where(mask, dot(dmixed, v[:, head(h)], 1, 1), 0.0).astype(BF16)
            gqs.append(dot(back, k[:, head(h)], 1, 0) + dot(dmixed, prior, 1, 1))
            gks.append(dot(back, q[:, head(h)], 0, 0))
            gvs.append(dot(attend_ref[r, h], dmixed, 0, 0))
        normed_ref[:, at] = jnp.concatenate(normeds, axis=1).astype(BF16)
        gq_ref[:, at] = jnp.concatenate(gqs, axis=1).astype(BF16)
        gk_ref[r] = jnp.concatenate(gks, axis=1)
        gv_ref[r] = jnp.concatenate(gvs, axis=1)
    out_ref[:, cut(me, rows)] = dot(normed_ref[...], weight_ref[...], 1, 1).astype(BF16)
    for j in range(1, groups):
        total = jnp.zeros((block, rows), F32)
        for r in range(SLAB):
            normed = normed_ref[:, cut(member(r), width)]
            total = total + dot(normed, far[2 * (j - 1) + r % 2][r // 2], 1, 1)
        out_ref[:, cut(jnp.bitwise_xor(me, j), rows)] = total.astype(BF16)


def last_kernel(near_ref, far_ref, core_ref, k_ref, v_ref, gk_part, gv_part, gk_ref, gv_ref):
    laters = arrived(near_ref, far_ref, core_ref)
    width = near_ref.shape[1]
    for r in range(SLAB):
        at = cut(member(r), width)
        k, v = k_ref[:, at], v_ref[:, at]
        gks, gvs = [], []
        for h in range(width // DH):
            later = laters[r][:, head(h)]
            gks.append(gk_part[r, :, head(h)] + dot(v[:, head(h)], later, 1, 1))
            gvs.append(gv_part[r, :, head(h)] + dot(k[:, head(h)], later, 1, 0))
        gk_ref[:, at] = jnp.concatenate(gks, axis=1).astype(BF16)
        gv_ref[:, at] = jnp.concatenate(gvs, axis=1).astype(BF16)


def product_kernel(slabs, cot_ref, normed_ref, keep_ref, send_ref):
    me = lax.axis_index("dp")
    slab = lax.div(lax.axis_index("seq"), SLAB)
    rows = keep_ref.shape[0] // slabs
    for j, out in enumerate((send_ref, keep_ref)):
        for d in range(slabs):
            at = jnp.bitwise_xor(me, 1 - j) * slabs + jnp.bitwise_xor(slab, d)
            total = dot(cot_ref[0, :, cut(at, rows)], normed_ref[0], 0, 0)
            for r in range(1, SLAB):
                total = total + dot(cot_ref[r, :, cut(at, rows)], normed_ref[r], 0, 0)
            out[part(d, rows), :] = total.astype(out.dtype)


def split_kernel(own_ref, got_ref, keep_ref, send_ref):
    rows = keep_ref.shape[0] // 2
    for i in range(4):
        total = own_ref[part(i, rows), :] + got_ref[part(i, rows), :].astype(F32)
        out = (keep_ref, send_ref)[i % 2]
        out[part(i // 2, rows), :] = total.astype(out.dtype)


def split_again_kernel(own_ref, got_ref, keep_ref, send_ref):
    rows = keep_ref.shape[0]
    for i, out in enumerate((keep_ref, send_ref)):
        total = own_ref[part(i, rows), :] + got_ref[part(i, rows), :].astype(F32)
        out[...] = total.astype(out.dtype)


def share_kernel(own_ref, got_ref, keep_ref, send_ref, total_ref):
    total_ref[...] = own_ref[...] + got_ref[...].astype(F32)
    rows = keep_ref.shape[0] // 2
    for i, r in enumerate((0, 1)):
        keep_ref[part(i, rows), :] = total_ref[cut(member(r), rows), :].astype(BF16)
    for i, r in enumerate((2, 3)):
        send_ref[part(i, rows), :] = total_ref[cut(member(r), rows), :].astype(BF16)


def pass_kernel(own_ref, got_ref, keep_ref, send_ref):
    rows = own_ref.shape[0] // 2
    for i, ref in enumerate((own_ref, got_ref)):
        keep_ref[part(i, rows), :] = ref[:rows, :]
        send_ref[part(i, rows), :] = ref[rows:, :]


def finish_kernel(factor, keep_ref, got_ref, out_ref):
    rows, width = out_ref.shape[0], keep_ref.shape[1]
    for i, ref in enumerate((keep_ref, got_ref)):
        for j in range(2):
            out_ref[:, cut(member(i + 2 * j), width)] = ref[part(j, rows), :].astype(F32) * factor


def local(queries, keys, values, cotangent, out_weight, *, dp, seq):
    call = Chain()
    local_seqs, block, features = queries.shape
    outputs = cotangent.shape[2]
    rows = local_seqs * block
    slabs = seq // SLAB
    width = features // SLAB
    heads = width // DH
    q, k, v = (x.reshape(rows, features) for x in (queries, keys, values))
    cot = cotangent.reshape(rows, outputs)
    factor = 1.0 / math.sqrt(rows * dp * seq)
    near = functools.partial(flip, axis="seq", count=seq)

    def doubling(total, cost=1):
        found = []
        bits = SLAB
        while bits < seq:
            if found:
                (total,) = call(add_kernel, [(total.shape, BF16)], total, found[-1], cost=cost)
            found.append(near(total, bits=bits))
            bits *= 2
        return found, total

    def scratch(*arrays):
        return [pltpu.VMEM(x.shape, BF16) for x in arrays] + [pltpu.SemaphoreType.DMA((len(arrays),))]

    own_state, near_state, far_state, columns = call(
        front_kernel,
        [((DH, width), F32), ((DH, width), BF16), ((2 * DH, width), BF16),
         ((2, out_weight.shape[0], width), BF16)],
        k, v, out_weight, far=True, scratch=scratch(k, v, out_weight),
    )
    far_state = near(far_state, bits=2)
    w_far = [flip(columns, "dp", dp, j) for j in range(1, dp)]
    attend, own_tokens, message, far_tokens, cot_y = call(
        pack_kernel,
        [((SLAB, heads, rows, rows), BF16), ((2 * rows, width), BF16),
         (((4 + outputs // width) * rows, width), BF16), ((2 * rows, width), BF16),
         ((rows, outputs), BF16)],
        q, k, v, cot,
    )
    cot_y = near(cot_y, bits=2)
    near_tokens, sent = message, (message, far_tokens)
    message = near(message, bits=1)
    (near_state,) = call(
        cross_kernel, [((2 * DH, width), BF16)], near_state, far_state, cost=5 * 10**9
    )
    near_state = near(near_state, bits=1)
    (slab_kv,) = call(total_kernel, [((DH, width), BF16)], own_state, far_state, near_state)
    (far_tokens,) = call(pair_kernel, [((4 * rows, width), BF16)], message, far_tokens)
    cot_yc = near(after(cot_y, far_tokens), bits=1)
    far_tokens = near(far_tokens, bits=2)
    before, _ = doubling(slab_kv, 22 * 10**8)
    dnormed, cots = call(
        functools.partial(dnormed_kernel, dp),
        [((SLAB, rows, width), F32), ((SLAB, rows, outputs), BF16)],
        message, cot, cot_y, cot_yc, columns, *w_far,
    )
    w_all = [x for w in w_far for x in (w, near(after(w, dnormed), bits=1))]
    normed, back, back_far, u, slab_u = call(
        middle_kernel,
        [((SLAB, rows, width), BF16)] + [((2 * rows + 2 * DH, width), BF16)] * 2
        + [((SLAB, DH, width), F32), ((DH, width), BF16)],
        own_tokens, message, far_tokens, own_state, far_state, near_state, dnormed, *before,
        cost=10**10, scratch=[pltpu.VMEM((SLAB, DH, width), F32)],
    )
    tuned = dp == 2 and slabs == 4 and outputs // (dp * seq) % 8 == 0
    piece = outputs // (dp * slabs)
    if tuned:
        keep, send = call(
            functools.partial(product_kernel, slabs),
            [((outputs // dp, width), F32), ((outputs // dp, width), BF16)], cots, normed,
        )
        got = flip(send, "dp", dp, 1)
    back_far = near(back_far, bits=2)
    behind, last_u = doubling(slab_u, 10**9)
    if tuned:
        keep, send = call(
            split_kernel, [((2 * piece, width), F32), ((2 * piece, width), BF16)], keep, got, wait=w_all[1::2]
        )
        got = near(send, bits=SLAB)
    later, later_far = call(
        later_kernel, [((2 * DH, width), BF16)] * 2, *behind, u, cost=2 * 10**9,
        scratch=[pltpu.VMEM((SLAB, DH, width), F32)],
    )
    later_far = near(later_far, bits=2)
    (send,) = call(relay_kernel, [((2 * rows + 2 * DH, width), BF16)], back, back_far)
    back_core = near(send, bits=1)
    if tuned:
        keep, send = call(
            split_again_kernel, [((piece, width), F32), ((piece, width), BF16)], keep, got, cost=2 * 10**9
        )
        got = near(send, bits=2 * SLAB)
    output, gq, gk_part, gv_part, own_normed = call(
        functools.partial(late_kernel, dp),
        [((rows, outputs), BF16), ((rows, features), BF16), ((SLAB, rows, width), F32),
         ((SLAB, rows, width), F32), ((rows, features), BF16)],
        back, back_far, back_core, q, k, v, attend, own_tokens, *sent, out_weight, *w_all,
    )
    (send,) = call(relay_kernel, [((2 * DH, width), BF16)], later, later_far)
    later_core = near(send, bits=1)
    if tuned:
        keep, share = call(
            share_kernel, [((piece // 2, width), BF16)] * 2, keep, got, cost=2 * 10**9,
            scratch=[pltpu.VMEM((piece, width), F32)],
        )
        got = near(share, bits=2)
    gk, gv = call(
        last_kernel, [((rows, features), BF16)] * 2,
        later, later_far, later_core, k, v, gk_part, gv_part, end=True,
    )
    if tuned:
        keep, share = call(pass_kernel, [((piece // 2, width), BF16)] * 2, keep, got, wait=[pltpu.with_memory_space_constraint(gk, pltpu.HBM)])
        got = near(share, bits=1)
    if tuned:
        (grad_weight,) = call(
            functools.partial(finish_kernel, factor),
            [((piece // SLAB, features), F32)], keep, got, end=True,
        )
    else:
        partial = dot(cot, own_normed, 0, 0) * factor
        grad_weight = lax.psum_scatter(partial, ("dp", "seq"), scatter_dimension=0, tiled=True)
    shape = queries.shape
    return (
        output.reshape(cotangent.shape), gq.reshape(shape), gk.reshape(shape), gv.reshape(shape),
        grad_weight,
    )


def solution(mesh):
    dp, seq = mesh.shape["dp"], mesh.shape["seq"]
    return jax.shard_map(
        functools.partial(local, dp=dp, seq=seq),
        mesh=mesh,
        in_specs=(P("dp", "seq", None),) * 4 + (P("dp", None),),
        out_specs=(P("dp", "seq", None),) * 4 + (P(("dp", "seq"), None),),
        check_vma=False,
    )
```

```python
import functools
import math

import jax
import jax.numpy as jnp
from jax import lax
from jax.experimental import pallas as pl
from jax.experimental.pallas import tpu as pltpu
from jax.sharding import PartitionSpec as P

DH = 128
SLAB = 4
EPSILON = 1e-05
BF16 = jnp.bfloat16
F32 = jnp.float32


def dot(left, right, left_dim, right_dim):
    return lax.dot_general(
        left, right, (((left_dim,), (right_dim,)), ((), ())), preferred_element_type=F32
    )


class Chain:
    def __init__(self):
        self.last = None

    def __call__(self, body, outs, *args, scratch=(), far=False, wait=(), cost=1, end=False):
        count = len(args)
        if far:
            args = [pltpu.with_memory_space_constraint(x, pltpu.HBM) for x in args]
        specs = [pl.BlockSpec(memory_space=pl.ANY) if far else pl.BlockSpec()] * count
        inner = body
        if self.last is not None:
            extra = (self.last, *wait)
            args = (*args, *extra)
            specs = [*specs, *[pl.BlockSpec(memory_space=pl.ANY)] * len(extra)]

            def inner(*refs):
                body(*refs[:count], *refs[count + len(extra) :])

        found = pl.pallas_call(
            inner,
            out_shape=[jax.ShapeDtypeStruct(s, d) for s, d in outs],
            in_specs=specs,
            scratch_shapes=list(scratch),
            cost_estimate=pl.CostEstimate(flops=cost, bytes_accessed=1, transcendentals=0),
            compiler_params=pltpu.CompilerParams(vmem_limit_bytes=32 * 2**20),
        )(*args)
        if not end:
            self.last = min(reversed(found), key=lambda x: x.size)
        return found


def after(x, *others):
    return lax.optimization_barrier((x, *others))[0]


def flip(x, axis, count, bits):
    return lax.ppermute(x, axis, [(i, i ^ bits) for i in range(count)])


def head(h):
    return slice(h * DH, (h + 1) * DH)


def part(i, size):
    return slice(i * size, (i + 1) * size)


def cut(start, size):
    return pl.ds(pl.multiple_of(start * size, size), size)


def member(r):
    return jnp.bitwise_xor(lax.rem(lax.axis_index("seq"), SLAB), r)


def causal(block):
    rows = lax.broadcasted_iota(jnp.int32, (block, block), 0)
    return lax.broadcasted_iota(jnp.int32, (block, block), 1) <= rows


def fetch(pairs, sems):
    copies = [pltpu.make_async_copy(a, b, sems.at[i]) for i, (a, b) in enumerate(pairs)]
    for copy in copies:
        copy.start()
    return copies


def front_kernel(k_hbm, v_hbm, w_hbm, own_ref, near_ref, far_ref, columns_ref, k_ref, v_ref, w_ref, sems):
    copies = fetch([(k_hbm, k_ref), (v_hbm, v_ref), (w_hbm, w_ref)], sems)
    width = k_ref.shape[1] // SLAB
    copies[0].wait()
    copies[1].wait()
    places = (own_ref, near_ref, far_ref.at[part(0, DH)], far_ref.at[part(1, DH)])
    for r, out in enumerate(places):
        k, v = k_ref[:, cut(member(r), width)], v_ref[:, cut(member(r), width)]
        for h in range(width // DH):
            out[:, head(h)] = dot(k[:, head(h)], v[:, head(h)], 0, 0).astype(out.dtype)
    copies[2].wait()
    for i in range(2):
        columns_ref[i] = w_ref[:, cut(member(2 * i), width)]


def pack_kernel(q_ref, k_ref, v_ref, c_ref, attend_ref, own_ref, message_ref, far_ref, cot_ref):
    cot_ref[...] = c_ref[...]
    block = q_ref.shape[0]
    width = q_ref.shape[1] // SLAB
    mask = causal(block)
    places = (own_ref, message_ref.at[: 2 * block], far_ref, message_ref.at[2 * block : 4 * block])
    for r, out in enumerate(places):
        q, k, v = (ref[:, cut(member(r), width)] for ref in (q_ref, k_ref, v_ref))
        out[:block, :] = q
        for h in range(width // DH):
            attend = jnp.where(mask, dot(q[:, head(h)], k[:, head(h)], 1, 1), 0.0).astype(BF16)
            attend_ref[r, h] = attend
            out[block:, head(h)] = dot(attend, v[:, head(h)], 1, 0).astype(BF16)
    for i in range(c_ref.shape[1] // width):
        message_ref[part(4 + i, block), :] = c_ref[:, part(i, width)]


def cross_kernel(near_ref, got_ref, out_ref):
    out_ref[part(0, DH), :] = near_ref[...]
    out_ref[part(1, DH), :] = got_ref[part(1, DH), :]


def total_kernel(own_ref, far_ref, near_ref, out_ref):
    total = own_ref[...] + far_ref[part(0, DH), :].astype(F32)
    total = total + near_ref[part(0, DH), :].astype(F32) + near_ref[part(1, DH), :].astype(F32)
    out_ref[...] = total.astype(BF16)


def pair_kernel(message_ref, far_ref, out_ref):
    size = far_ref.shape[0]
    out_ref[:size, :] = far_ref[...]
    out_ref[size:, :] = message_ref[part(1, size), :]


def add_kernel(own_ref, got_ref, out_ref):
    out_ref[...] = (own_ref[...].astype(F32) + got_ref[...].astype(F32)).astype(out_ref.dtype)


def dnormed_kernel(groups, members, *refs):
    cots, weights = refs[: len(members)], refs[len(members) : len(members) + groups]
    dnormed_ref, cot_ref = refs[len(members) + groups :]
    _, block, outputs = cot_ref.shape
    width = dnormed_ref.shape[2]
    rows = weights[0].shape[1]
    me = lax.axis_index("dp")
    for i, (r, ref) in enumerate(zip(members, cots)):
        if r == 1:
            for p in range(outputs // width):
                cot_ref[i, :, part(p, width)] = ref[part(4 + p, block), :]
        else:
            cot_ref[i] = ref[...]
        total = dot(cot_ref[i, :, cut(me, rows)], weights[0][0], 1, 0)
        for j in range(1, groups):
            total = total + dot(cot_ref[i, :, cut(jnp.bitwise_xor(me, j), rows)], weights[j][0], 1, 0)
        dnormed_ref[i] = total


def base_kernel(*refs):
    refs[-1][...] = from_slabs(False, refs[:-1])


def from_slabs(backward, refs):
    slab = lax.div(lax.axis_index("seq"), SLAB)
    total = jnp.zeros(refs[0].shape, F32)
    for i, ref in enumerate(refs):
        bit = lax.rem(lax.div(slab, 1 << i), 2)
        total = total + jnp.where(bit == (0 if backward else 1), ref[...].astype(F32), 0.0)
    return total


def middle_kernel(*refs):
    own_ref, message_ref, token_far, own_state, far_state, near_state, base_ref, dnormed_a, dnormed_b = refs[:9]
    normed_ref, back_near, back_far, u_ref, slab_ref, running = refs[9:]
    _, block, width = normed_ref.shape
    heads = width // DH
    size = 2 * block
    tokens = (own_ref, message_ref.at[:size], token_far.at[:size], token_far.at[size:])
    running[member(0)] = own_state[...]
    running[member(1)] = near_state[part(0, DH), :].astype(F32)
    running[member(2)] = far_state[part(0, DH), :].astype(F32)
    running[member(3)] = near_state[part(1, DH), :].astype(F32)
    total = base_ref[...]
    for p in range(SLAB):
        total, running[p] = total + running[p], total
    sums = [jnp.zeros((DH, DH), F32)] * heads
    for r in range(SLAB):
        out = (back_near, back_far)[r // 2].at[part(r % 2, block + DH)]
        prior = running[member(r)].astype(BF16)
        out[block:, :] = prior
        for h in range(heads):
            q = tokens[r][:block, head(h)]
            mixed = tokens[r][block:, head(h)].astype(F32) + dot(q, prior[:, head(h)], 1, 0)
            scale = lax.rsqrt(jnp.mean(mixed * mixed, axis=-1, keepdims=True) + EPSILON)
            normed = mixed * scale
            normed_ref[r, :, head(h)] = normed.astype(BF16)
            dnormed = dnormed_a[r, :, head(h)] if r < 3 else dnormed_b[0, :, head(h)]
            along = jnp.mean(dnormed * normed, axis=-1, keepdims=True)
            dmixed = ((dnormed - normed * along) * scale).astype(BF16)
            out[:block, head(h)] = dmixed
            u = dot(q, dmixed, 0, 0)
            u_ref[r, :, head(h)] = u
            sums[h] = sums[h] + u
    for h in range(heads):
        slab_ref[:, head(h)] = sums[h].astype(BF16)


def later_kernel(*refs):
    *behind, u_ref, near_ref, far_ref, running = refs
    for r in range(SLAB):
        running[member(r)] = u_ref[r]
    total = from_slabs(True, behind)
    for p in reversed(range(SLAB)):
        total, running[p] = total + running[p], total
    for r in range(SLAB):
        (near_ref, far_ref)[r // 2][part(r % 2, DH), :] = running[member(r)].astype(BF16)


def relay_kernel(near_ref, far_ref, out_ref):
    size = near_ref.shape[0] // 2
    out_ref[:size, :] = near_ref[size:, :]
    out_ref[size:, :] = far_ref[size:, :]


def arrived(near_ref, far_ref, core_ref):
    size = near_ref.shape[0] // 2
    first, second = slice(0, size), slice(size, 2 * size)
    return near_ref.at[first], core_ref.at[first], far_ref.at[first], core_ref.at[second]


def late_kernel(groups, *refs):
    backs, (q_ref, k_ref, v_ref, attend_ref, own_ref, message_ref, far_ref) = arrived(*refs[:3]), refs[3:10]
    weight_ref, *far, out_ref, gq_ref, gk_ref, gv_ref, normed_ref = refs[10:]
    block, width = q_ref.shape[0], refs[0].shape[1]
    rows = weight_ref.shape[0]
    me = lax.axis_index("dp")
    mask = causal(block)
    withins = (own_ref.at[part(1, block)], message_ref.at[part(1, block)],
               far_ref.at[part(1, block)], message_ref.at[part(3, block)])
    for r in range(SLAB):
        at = cut(member(r), width)
        q, k, v = q_ref[:, at], k_ref[:, at], v_ref[:, at]
        normeds, gqs, gks, gvs = [], [], [], []
        for h in range(width // DH):
            dmixed, prior = backs[r][:block, head(h)], backs[r][block:, head(h)]
            mixed = withins[r][:, head(h)].astype(F32) + dot(q[:, head(h)], prior, 1, 0)
            scale = lax.rsqrt(jnp.mean(mixed * mixed, axis=-1, keepdims=True) + EPSILON)
            normeds.append(mixed * scale)
            back = jnp.where(mask, dot(dmixed, v[:, head(h)], 1, 1), 0.0).astype(BF16)
            gqs.append(dot(back, k[:, head(h)], 1, 0) + dot(dmixed, prior, 1, 1))
            gks.append(dot(back, q[:, head(h)], 0, 0))
            gvs.append(dot(attend_ref[r, h], dmixed, 0, 0))
        normed_ref[:, at] = jnp.concatenate(normeds, axis=1).astype(BF16)
        gq_ref[:, at] = jnp.concatenate(gqs, axis=1).astype(BF16)
        gk_ref[r] = jnp.concatenate(gks, axis=1)
        gv_ref[r] = jnp.concatenate(gvs, axis=1)
    out_ref[:, cut(me, rows)] = dot(normed_ref[...], weight_ref[...], 1, 1).astype(BF16)
    for j in range(1, groups):
        total = jnp.zeros((block, rows), F32)
        for r in range(SLAB):
            normed = normed_ref[:, cut(member(r), width)]
            total = total + dot(normed, far[2 * (j - 1) + r % 2][r // 2], 1, 1)
        out_ref[:, cut(jnp.bitwise_xor(me, j), rows)] = total.astype(BF16)


def last_kernel(near_ref, far_ref, core_ref, k_ref, v_ref, gk_part, gv_part, gk_ref, gv_ref):
    laters = arrived(near_ref, far_ref, core_ref)
    width = near_ref.shape[1]
    for r in range(SLAB):
        at = cut(member(r), width)
        k, v = k_ref[:, at], v_ref[:, at]
        gks, gvs = [], []
        for h in range(width // DH):
            later = laters[r][:, head(h)]
            gks.append(gk_part[r, :, head(h)] + dot(v[:, head(h)], later, 1, 1))
            gvs.append(gv_part[r, :, head(h)] + dot(k[:, head(h)], later, 1, 0))
        gk_ref[:, at] = jnp.concatenate(gks, axis=1).astype(BF16)
        gv_ref[:, at] = jnp.concatenate(gvs, axis=1).astype(BF16)


def product_kernel(slabs, cot_a, cot_b, normed_ref, keep_ref, send_ref):
    me = lax.axis_index("dp")
    slab = lax.div(lax.axis_index("seq"), SLAB)
    rows = keep_ref.shape[0] // slabs
    for j, out in enumerate((send_ref, keep_ref)):
        for d in range(slabs):
            at = jnp.bitwise_xor(me, 1 - j) * slabs + jnp.bitwise_xor(slab, d)
            total = dot(cot_b[0, :, cut(at, rows)], normed_ref[3], 0, 0)
            for r in range(3):
                total = total + dot(cot_a[r, :, cut(at, rows)], normed_ref[r], 0, 0)
            out[part(d, rows), :] = total.astype(out.dtype)


def split_kernel(own_ref, got_ref, keep_ref, send_ref):
    rows = keep_ref.shape[0] // 2
    for i in range(4):
        total = own_ref[part(i, rows), :] + got_ref[part(i, rows), :].astype(F32)
        out = (keep_ref, send_ref)[i % 2]
        out[part(i // 2, rows), :] = total.astype(out.dtype)


def split_again_kernel(own_ref, got_ref, keep_ref, send_ref):
    rows = keep_ref.shape[0]
    for i, out in enumerate((keep_ref, send_ref)):
        total = own_ref[part(i, rows), :] + got_ref[part(i, rows), :].astype(F32)
        out[...] = total.astype(out.dtype)


def share_kernel(own_ref, got_ref, keep_ref, send_ref, total_ref):
    total_ref[...] = own_ref[...] + got_ref[...].astype(F32)
    rows = keep_ref.shape[0] // 2
    for i, r in enumerate((0, 1)):
        keep_ref[part(i, rows), :] = total_ref[cut(member(r), rows), :].astype(BF16)
    for i, r in enumerate((2, 3)):
        send_ref[part(i, rows), :] = total_ref[cut(member(r), rows), :].astype(BF16)


def pass_kernel(own_ref, got_ref, keep_ref, send_ref):
    rows = own_ref.shape[0] // 2
    for i, ref in enumerate((own_ref, got_ref)):
        keep_ref[part(i, rows), :] = ref[:rows, :]
        send_ref[part(i, rows), :] = ref[rows:, :]


def finish_kernel(factor, keep_ref, got_ref, out_ref):
    rows, width = out_ref.shape[0], keep_ref.shape[1]
    for i, ref in enumerate((keep_ref, got_ref)):
        for j in range(2):
            out_ref[:, cut(member(i + 2 * j), width)] = ref[part(j, rows), :].astype(F32) * factor


def local(queries, keys, values, cotangent, out_weight, *, dp, seq):
    call = Chain()
    local_seqs, block, features = queries.shape
    outputs = cotangent.shape[2]
    rows = local_seqs * block
    slabs = seq // SLAB
    width = features // SLAB
    heads = width // DH
    q, k, v = (x.reshape(rows, features) for x in (queries, keys, values))
    cot = cotangent.reshape(rows, outputs)
    factor = 1.0 / math.sqrt(rows * dp * seq)
    near = functools.partial(flip, axis="seq", count=seq)

    def doubling(total, cost=1):
        found = []
        bits = SLAB
        while bits < seq:
            if found:
                (total,) = call(add_kernel, [(total.shape, BF16)], total, found[-1], cost=cost)
            found.append(near(total, bits=bits))
            bits *= 2
        return found, total

    def scratch(*arrays):
        return [pltpu.VMEM(x.shape, BF16) for x in arrays] + [pltpu.SemaphoreType.DMA((len(arrays),))]

    own_state, near_state, far_state, columns = call(
        front_kernel,
        [((DH, width), F32), ((DH, width), BF16), ((2 * DH, width), BF16),
         ((2, out_weight.shape[0], width), BF16)],
        k, v, out_weight, far=True, scratch=scratch(k, v, out_weight),
    )
    far_state = near(far_state, bits=2)
    w_far = [flip(columns, "dp", dp, j) for j in range(1, dp)]
    attend, own_tokens, message, far_tokens, cot_y = call(
        pack_kernel,
        [((SLAB, heads, rows, rows), BF16), ((2 * rows, width), BF16),
         (((4 + outputs // width) * rows, width), BF16), ((2 * rows, width), BF16),
         ((rows, outputs), BF16)],
        q, k, v, cot,
    )
    cot_y = near(cot_y, bits=2)
    near_tokens, sent = message, (message, far_tokens)
    message = near(message, bits=1)
    (near_state,) = call(
        cross_kernel, [((2 * DH, width), BF16)], near_state, far_state, cost=5 * 10**9
    )
    near_state = near(near_state, bits=1)
    (slab_kv,) = call(total_kernel, [((DH, width), BF16)], own_state, far_state, near_state)
    (far_tokens,) = call(pair_kernel, [((4 * rows, width), BF16)], message, far_tokens)
    far_tokens = near(far_tokens, bits=2)
    before, last_kv = doubling(slab_kv, 14 * 10**8)
    cot_yc = near(after(cot_y, last_kv), bits=1)
    weights = (columns, *w_far)
    dnormed, cots = call(
        functools.partial(dnormed_kernel, dp, (0, 1, 2)),
        [((3, rows, width), F32), ((3, rows, outputs), BF16)], cot, message, cot_y, *weights,
    )
    (base,) = call(base_kernel, [((DH, width), F32)], *before, cost=23 * 10**8, wait=[far_tokens])
    dnormed_b, cot_b = call(
        functools.partial(dnormed_kernel, dp, (3,)),
        [((1, rows, width), F32), ((1, rows, outputs), BF16)], cot_yc, *weights,
    )
    w_all = [x for w in w_far for x in (w, near(after(w, dnormed), bits=1))]
    normed, back, back_far, u, slab_u = call(
        middle_kernel,
        [((SLAB, rows, width), BF16)] + [((2 * rows + 2 * DH, width), BF16)] * 2
        + [((SLAB, DH, width), F32), ((DH, width), BF16)],
        own_tokens, message, far_tokens, own_state, far_state, near_state, base, dnormed, dnormed_b,
        cost=10**10, scratch=[pltpu.VMEM((SLAB, DH, width), F32)],
    )
    tuned = dp == 2 and slabs == 4 and outputs // (dp * seq) % 8 == 0
    piece = outputs // (dp * slabs)
    if tuned:
        keep, send = call(
            functools.partial(product_kernel, slabs),
            [((outputs // dp, width), F32), ((outputs // dp, width), BF16)], cots, cot_b, normed,
        )
        got = flip(send, "dp", dp, 1)
    back_far = near(back_far, bits=2)
    behind, last_u = doubling(slab_u, 15 * 10**8)
    if tuned:
        keep, send = call(
            split_kernel, [((2 * piece, width), F32), ((2 * piece, width), BF16)], keep, got, wait=w_all[1::2]
        )
        got = near(send, bits=SLAB)
    (send,) = call(relay_kernel, [((2 * rows + 2 * DH, width), BF16)], back, back_far)
    back_core = near(send, bits=1)
    later, later_far = call(
        later_kernel, [((2 * DH, width), BF16)] * 2, *behind, u, cost=2 * 10**9,
        scratch=[pltpu.VMEM((SLAB, DH, width), F32)],
    )
    later_far = near(later_far, bits=2)
    if tuned:
        keep, send = call(
            split_again_kernel, [((piece, width), F32), ((piece, width), BF16)], keep, got, cost=2 * 10**9
        )
        got = near(send, bits=2 * SLAB)
    output, gq, gk_part, gv_part, own_normed = call(
        functools.partial(late_kernel, dp),
        [((rows, outputs), BF16), ((rows, features), BF16), ((SLAB, rows, width), F32),
         ((SLAB, rows, width), F32), ((rows, features), BF16)],
        back, back_far, back_core, q, k, v, attend, own_tokens, *sent, out_weight, *w_all,
    )
    (send,) = call(relay_kernel, [((2 * DH, width), BF16)], later, later_far)
    later_core = near(send, bits=1)
    if tuned:
        keep, share = call(
            share_kernel, [((piece // 2, width), BF16)] * 2, keep, got, cost=3 * 10**9,
            scratch=[pltpu.VMEM((piece, width), F32)],
        )
        got = near(share, bits=2)
    gk, gv = call(
        last_kernel, [((rows, features), BF16)] * 2,
        later, later_far, later_core, k, v, gk_part, gv_part, end=True,
    )
    if tuned:
        keep, share = call(pass_kernel, [((piece // 2, width), BF16)] * 2, keep, got, wait=[pltpu.with_memory_space_constraint(gk, pltpu.HBM)])
        got = near(share, bits=1)
    if tuned:
        (grad_weight,) = call(
            functools.partial(finish_kernel, factor),
            [((piece // SLAB, features), F32)], keep, got, end=True,
        )
    else:
        partial = dot(cot, own_normed, 0, 0) * factor
        grad_weight = lax.psum_scatter(partial, ("dp", "seq"), scatter_dimension=0, tiled=True)
    shape = queries.shape
    return (
        output.reshape(cotangent.shape), gq.reshape(shape), gk.reshape(shape), gv.reshape(shape),
        grad_weight,
    )


def solution(mesh):
    dp, seq = mesh.shape["dp"], mesh.shape["seq"]
    return jax.shard_map(
        functools.partial(local, dp=dp, seq=seq),
        mesh=mesh,
        in_specs=(P("dp", "seq", None),) * 4 + (P("dp", None),),
        out_specs=(P("dp", "seq", None),) * 4 + (P(("dp", "seq"), None),),
        check_vma=False,
    )
```

```python
import functools
import math

import jax
import jax.numpy as jnp
from jax import lax
from jax.experimental import pallas as pl
from jax.experimental.pallas import tpu as pltpu
from jax.sharding import PartitionSpec as P

DH = 128
SLAB = 4
EPSILON = 1e-05
BF16 = jnp.bfloat16
F32 = jnp.float32


def dot(left, right, left_dim, right_dim):
    return lax.dot_general(
        left, right, (((left_dim,), (right_dim,)), ((), ())), preferred_element_type=F32
    )


class Chain:
    def __init__(self):
        self.last = None

    def __call__(self, body, outs, *args, scratch=(), far=False, wait=(), cost=1, end=False):
        count = len(args)
        if far:
            args = [pltpu.with_memory_space_constraint(x, pltpu.HBM) for x in args]
        specs = [pl.BlockSpec(memory_space=pl.ANY) if far else pl.BlockSpec()] * count
        inner = body
        if self.last is not None:
            extra = (self.last, *wait)
            args = (*args, *extra)
            specs = [*specs, *[pl.BlockSpec(memory_space=pl.ANY)] * len(extra)]

            def inner(*refs):
                body(*refs[:count], *refs[count + len(extra) :])

        found = pl.pallas_call(
            inner,
            out_shape=[jax.ShapeDtypeStruct(s, d) for s, d in outs],
            in_specs=specs,
            scratch_shapes=list(scratch),
            cost_estimate=pl.CostEstimate(flops=cost, bytes_accessed=1, transcendentals=0),
            compiler_params=pltpu.CompilerParams(vmem_limit_bytes=32 * 2**20),
        )(*args)
        if not end:
            self.last = min(reversed(found), key=lambda x: x.size)
        return found


def after(x, *others):
    return lax.optimization_barrier((x, *others))[0]


def flip(x, axis, count, bits):
    return lax.ppermute(x, axis, [(i, i ^ bits) for i in range(count)])


def head(h):
    return slice(h * DH, (h + 1) * DH)


def part(i, size):
    return slice(i * size, (i + 1) * size)


def cut(start, size):
    return pl.ds(pl.multiple_of(start * size, size), size)


def member(r):
    return jnp.bitwise_xor(lax.rem(lax.axis_index("seq"), SLAB), r)


def causal(block):
    rows = lax.broadcasted_iota(jnp.int32, (block, block), 0)
    return lax.broadcasted_iota(jnp.int32, (block, block), 1) <= rows


def fetch(pairs, sems):
    copies = [pltpu.make_async_copy(a, b, sems.at[i]) for i, (a, b) in enumerate(pairs)]
    for copy in copies:
        copy.start()
    return copies


def front_kernel(k_hbm, v_hbm, w_hbm, own_ref, near_ref, far_ref, columns_ref, k_ref, v_ref, w_ref, sems):
    copies = fetch([(k_hbm, k_ref), (v_hbm, v_ref), (w_hbm, w_ref)], sems)
    width = k_ref.shape[1] // SLAB
    copies[0].wait()
    copies[1].wait()
    places = (own_ref, near_ref, far_ref.at[part(0, DH)], far_ref.at[part(1, DH)])
    for r, out in enumerate(places):
        k, v = k_ref[:, cut(member(r), width)], v_ref[:, cut(member(r), width)]
        for h in range(width // DH):
            out[:, head(h)] = dot(k[:, head(h)], v[:, head(h)], 0, 0).astype(out.dtype)
    copies[2].wait()
    for i in range(2):
        columns_ref[i] = w_ref[:, cut(member(2 * i), width)]


def pack_kernel(q_ref, k_ref, v_ref, c_ref, attend_ref, own_ref, message_ref, far_ref):
    block = q_ref.shape[0]
    width = q_ref.shape[1] // SLAB
    mask = causal(block)
    places = (own_ref, message_ref.at[: 2 * block], far_ref, message_ref.at[2 * block : 4 * block])
    for r, out in enumerate(places):
        q, k, v = (ref[:, cut(member(r), width)] for ref in (q_ref, k_ref, v_ref))
        out[:block, :] = q
        for h in range(width // DH):
            attend = jnp.where(mask, dot(q[:, head(h)], k[:, head(h)], 1, 1), 0.0).astype(BF16)
            attend_ref[r, h] = attend
            out[block:, head(h)] = dot(attend, v[:, head(h)], 1, 0).astype(BF16)
    for i in range(c_ref.shape[1] // width):
        message_ref[part(4 + i, block), :] = c_ref[:, part(i, width)]


def cross_kernel(near_ref, got_ref, out_ref):
    out_ref[part(0, DH), :] = near_ref[...]
    out_ref[part(1, DH), :] = got_ref[part(1, DH), :]


def total_kernel(own_ref, far_ref, near_ref, out_ref):
    total = own_ref[...] + far_ref[part(0, DH), :].astype(F32)
    total = total + near_ref[part(0, DH), :].astype(F32) + near_ref[part(1, DH), :].astype(F32)
    out_ref[...] = total.astype(BF16)


def pair_kernel(message_ref, far_ref, out_ref):
    size = far_ref.shape[0]
    out_ref[:size, :] = far_ref[...]
    out_ref[size:, :] = message_ref[part(1, size), :]


def add_kernel(own_ref, got_ref, out_ref):
    out_ref[...] = (own_ref[...].astype(F32) + got_ref[...].astype(F32)).astype(out_ref.dtype)


def dnormed_kernel(groups, members, *refs):
    cots, weights = refs[: len(members)], refs[len(members) : len(members) + groups]
    dnormed_ref, cot_ref = refs[len(members) + groups :]
    _, block, outputs = cot_ref.shape
    width = dnormed_ref.shape[2]
    rows = weights[0].shape[1]
    me = lax.axis_index("dp")
    for i, (r, ref) in enumerate(zip(members, cots)):
        if r == 1:
            for p in range(outputs // width):
                cot_ref[i, :, part(p, width)] = ref[part(4 + p, block), :]
        else:
            cot_ref[i] = ref[...]
        total = dot(cot_ref[i, :, cut(me, rows)], weights[0][0], 1, 0)
        for j in range(1, groups):
            total = total + dot(cot_ref[i, :, cut(jnp.bitwise_xor(me, j), rows)], weights[j][0], 1, 0)
        dnormed_ref[i] = total


def base_kernel(*refs):
    refs[-1][...] = from_slabs(False, refs[:-1])


def from_slabs(backward, refs):
    slab = lax.div(lax.axis_index("seq"), SLAB)
    total = jnp.zeros(refs[0].shape, F32)
    for i, ref in enumerate(refs):
        bit = lax.rem(lax.div(slab, 1 << i), 2)
        total = total + jnp.where(bit == (0 if backward else 1), ref[...].astype(F32), 0.0)
    return total


def middle_kernel(*refs):
    own_ref, message_ref, token_far, own_state, far_state, near_state, base_ref, dnormed_a, dnormed_b = refs[:9]
    normed_ref, back_near, back_far, u_ref, slab_ref, running = refs[9:]
    _, block, width = normed_ref.shape
    heads = width // DH
    size = 2 * block
    tokens = (own_ref, message_ref.at[:size], token_far.at[:size], token_far.at[size:])
    running[member(0)] = own_state[...]
    running[member(1)] = near_state[part(0, DH), :].astype(F32)
    running[member(2)] = far_state[part(0, DH), :].astype(F32)
    running[member(3)] = near_state[part(1, DH), :].astype(F32)
    total = base_ref[...]
    for p in range(SLAB):
        total, running[p] = total + running[p], total
    sums = [jnp.zeros((DH, DH), F32)] * heads
    for r in range(SLAB):
        out = (back_near, back_far)[r // 2].at[part(r % 2, block + DH)]
        prior = running[member(r)].astype(BF16)
        out[block:, :] = prior
        for h in range(heads):
            q = tokens[r][:block, head(h)]
            mixed = tokens[r][block:, head(h)].astype(F32) + dot(q, prior[:, head(h)], 1, 0)
            scale = lax.rsqrt(jnp.mean(mixed * mixed, axis=-1, keepdims=True) + EPSILON)
            normed = mixed * scale
            normed_ref[r, :, head(h)] = normed.astype(BF16)
            dnormed = dnormed_a[r, :, head(h)] if r < 3 else dnormed_b[0, :, head(h)]
            along = jnp.mean(dnormed * normed, axis=-1, keepdims=True)
            dmixed = ((dnormed - normed * along) * scale).astype(BF16)
            out[:block, head(h)] = dmixed
            u = dot(q, dmixed, 0, 0)
            u_ref[r, :, head(h)] = u
            sums[h] = sums[h] + u
    for h in range(heads):
        slab_ref[:, head(h)] = sums[h].astype(BF16)


def later_kernel(*refs):
    *behind, u_ref, near_ref, far_ref, running = refs
    for r in range(SLAB):
        running[member(r)] = u_ref[r]
    total = from_slabs(True, behind)
    for p in reversed(range(SLAB)):
        total, running[p] = total + running[p], total
    for r in range(SLAB):
        (near_ref, far_ref)[r // 2][part(r % 2, DH), :] = running[member(r)].astype(BF16)


def relay_kernel(near_ref, far_ref, out_ref):
    size = near_ref.shape[0] // 2
    out_ref[:size, :] = near_ref[size:, :]
    out_ref[size:, :] = far_ref[size:, :]


def arrived(near_ref, far_ref, core_ref):
    size = near_ref.shape[0] // 2
    first, second = slice(0, size), slice(size, 2 * size)
    return near_ref.at[first], core_ref.at[first], far_ref.at[first], core_ref.at[second]


def late_kernel(groups, *refs):
    backs, (q_ref, k_ref, v_ref, attend_ref, own_ref, message_ref, far_ref) = arrived(*refs[:3]), refs[3:10]
    weight_ref, *far, out_ref, gq_ref, gk_ref, gv_ref, normed_ref = refs[10:]
    block, width = q_ref.shape[0], refs[0].shape[1]
    rows = weight_ref.shape[0]
    me = lax.axis_index("dp")
    mask = causal(block)
    withins = (own_ref.at[part(1, block)], message_ref.at[part(1, block)],
               far_ref.at[part(1, block)], message_ref.at[part(3, block)])
    for r in range(SLAB):
        at = cut(member(r), width)
        q, k, v = q_ref[:, at], k_ref[:, at], v_ref[:, at]
        normeds, gqs, gks, gvs = [], [], [], []
        for h in range(width // DH):
            dmixed, prior = backs[r][:block, head(h)], backs[r][block:, head(h)]
            mixed = withins[r][:, head(h)].astype(F32) + dot(q[:, head(h)], prior, 1, 0)
            scale = lax.rsqrt(jnp.mean(mixed * mixed, axis=-1, keepdims=True) + EPSILON)
            normeds.append(mixed * scale)
            back = jnp.where(mask, dot(dmixed, v[:, head(h)], 1, 1), 0.0).astype(BF16)
            gqs.append(dot(back, k[:, head(h)], 1, 0) + dot(dmixed, prior, 1, 1))
            gks.append(dot(back, q[:, head(h)], 0, 0))
            gvs.append(dot(attend_ref[r, h], dmixed, 0, 0))
        normed_ref[:, at] = jnp.concatenate(normeds, axis=1).astype(BF16)
        gq_ref[:, at] = jnp.concatenate(gqs, axis=1).astype(BF16)
        gk_ref[r] = jnp.concatenate(gks, axis=1)
        gv_ref[r] = jnp.concatenate(gvs, axis=1)
    out_ref[:, cut(me, rows)] = dot(normed_ref[...], weight_ref[...], 1, 1).astype(BF16)
    for j in range(1, groups):
        total = jnp.zeros((block, rows), F32)
        for r in range(SLAB):
            normed = normed_ref[:, cut(member(r), width)]
            total = total + dot(normed, far[2 * (j - 1) + r % 2][r // 2], 1, 1)
        out_ref[:, cut(jnp.bitwise_xor(me, j), rows)] = total.astype(BF16)


def last_kernel(near_ref, far_ref, core_ref, k_ref, v_ref, gk_part, gv_part, gk_ref, gv_ref):
    laters = arrived(near_ref, far_ref, core_ref)
    width = near_ref.shape[1]
    for r in range(SLAB):
        at = cut(member(r), width)
        k, v = k_ref[:, at], v_ref[:, at]
        gks, gvs = [], []
        for h in range(width // DH):
            later = laters[r][:, head(h)]
            gks.append(gk_part[r, :, head(h)] + dot(v[:, head(h)], later, 1, 1))
            gvs.append(gv_part[r, :, head(h)] + dot(k[:, head(h)], later, 1, 0))
        gk_ref[:, at] = jnp.concatenate(gks, axis=1).astype(BF16)
        gv_ref[:, at] = jnp.concatenate(gvs, axis=1).astype(BF16)


def product_kernel(slabs, cot_a, cot_b, normed_ref, keep_ref, send_ref):
    me = lax.axis_index("dp")
    slab = lax.div(lax.axis_index("seq"), SLAB)
    rows = keep_ref.shape[0] // slabs
    for j, out in enumerate((send_ref, keep_ref)):
        for d in range(slabs):
            at = jnp.bitwise_xor(me, 1 - j) * slabs + jnp.bitwise_xor(slab, d)
            total = dot(cot_b[0, :, cut(at, rows)], normed_ref[3], 0, 0)
            for r in range(3):
                total = total + dot(cot_a[r, :, cut(at, rows)], normed_ref[r], 0, 0)
            out[part(d, rows), :] = total.astype(out.dtype)


def split_kernel(own_ref, got_ref, keep_ref, send_ref):
    rows = keep_ref.shape[0] // 2
    for i in range(4):
        total = own_ref[part(i, rows), :] + got_ref[part(i, rows), :].astype(F32)
        out = (keep_ref, send_ref)[i % 2]
        out[part(i // 2, rows), :] = total.astype(out.dtype)


def split_again_kernel(own_ref, got_ref, keep_ref, send_ref):
    rows = keep_ref.shape[0]
    for i, out in enumerate((keep_ref, send_ref)):
        total = own_ref[part(i, rows), :] + got_ref[part(i, rows), :].astype(F32)
        out[...] = total.astype(out.dtype)


def share_kernel(own_ref, got_ref, keep_ref, send_ref, total_ref):
    total_ref[...] = own_ref[...] + got_ref[...].astype(F32)
    rows = keep_ref.shape[0] // 2
    for i, r in enumerate((0, 1)):
        keep_ref[part(i, rows), :] = total_ref[cut(member(r), rows), :].astype(BF16)
    for i, r in enumerate((2, 3)):
        send_ref[part(i, rows), :] = total_ref[cut(member(r), rows), :].astype(BF16)


def pass_kernel(own_ref, got_ref, keep_ref, send_ref):
    rows = own_ref.shape[0] // 2
    for i, ref in enumerate((own_ref, got_ref)):
        keep_ref[part(i, rows), :] = ref[:rows, :]
        send_ref[part(i, rows), :] = ref[rows:, :]


def finish_kernel(factor, keep_ref, got_ref, out_ref):
    rows, width = out_ref.shape[0], keep_ref.shape[1]
    for i, ref in enumerate((keep_ref, got_ref)):
        for j in range(2):
            out_ref[:, cut(member(i + 2 * j), width)] = ref[part(j, rows), :].astype(F32) * factor


def local(queries, keys, values, cotangent, out_weight, *, dp, seq):
    call = Chain()
    local_seqs, block, features = queries.shape
    outputs = cotangent.shape[2]
    rows = local_seqs * block
    slabs = seq // SLAB
    width = features // SLAB
    heads = width // DH
    q, k, v = (x.reshape(rows, features) for x in (queries, keys, values))
    cot = cotangent.reshape(rows, outputs)
    factor = 1.0 / math.sqrt(rows * dp * seq)
    near = functools.partial(flip, axis="seq", count=seq)

    def doubling(total, cost=1):
        found = []
        bits = SLAB
        while bits < seq:
            if found:
                (total,) = call(add_kernel, [(total.shape, BF16)], total, found[-1], cost=cost)
            found.append(near(total, bits=bits))
            bits *= 2
        return found, total

    def scratch(*arrays):
        return [pltpu.VMEM(x.shape, BF16) for x in arrays] + [pltpu.SemaphoreType.DMA((len(arrays),))]

    own_state, near_state, far_state, columns = call(
        front_kernel,
        [((DH, width), F32), ((DH, width), BF16), ((2 * DH, width), BF16),
         ((2, out_weight.shape[0], width), BF16)],
        k, v, out_weight, far=True, scratch=scratch(k, v, out_weight),
    )
    far_state = near(far_state, bits=2)
    w_far = [flip(columns, "dp", dp, j) for j in range(1, dp)]
    attend, own_tokens, message, far_tokens = call(
        pack_kernel,
        [((SLAB, heads, rows, rows), BF16), ((2 * rows, width), BF16),
         (((4 + outputs // width) * rows, width), BF16), ((2 * rows, width), BF16)],
        q, k, v, cot,
    )
    cot_y = near(cot, bits=2)
    near_tokens, sent = message, (message, far_tokens)
    message = near(message, bits=1)
    (near_state,) = call(
        cross_kernel, [((2 * DH, width), BF16)], near_state, far_state, cost=5 * 10**9
    )
    near_state = near(near_state, bits=1)
    (slab_kv,) = call(total_kernel, [((DH, width), BF16)], own_state, far_state, near_state)
    (far_tokens,) = call(pair_kernel, [((4 * rows, width), BF16)], message, far_tokens)
    cot_yc = near(after(cot_y, far_tokens), bits=1)
    far_tokens = near(far_tokens, bits=2)
    before, _ = doubling(slab_kv, 22 * 10**8)
    weights = (columns, *w_far)
    dnormed, cots = call(
        functools.partial(dnormed_kernel, dp, (0, 1, 2)),
        [((3, rows, width), F32), ((3, rows, outputs), BF16)], cot, message, cot_y, *weights,
    )
    dnormed_b, cot_b = call(
        functools.partial(dnormed_kernel, dp, (3,)),
        [((1, rows, width), F32), ((1, rows, outputs), BF16)], cot_yc, *weights,
    )
    (base,) = call(base_kernel, [((DH, width), F32)], *before, cost=10**9)
    w_all = [x for w in w_far for x in (w, near(after(w, dnormed), bits=1))]
    normed, back, back_far, u, slab_u = call(
        middle_kernel,
        [((SLAB, rows, width), BF16)] + [((2 * rows + 2 * DH, width), BF16)] * 2
        + [((SLAB, DH, width), F32), ((DH, width), BF16)],
        own_tokens, message, far_tokens, own_state, far_state, near_state, base, dnormed, dnormed_b,
        cost=10**10, scratch=[pltpu.VMEM((SLAB, DH, width), F32)],
    )
    tuned = dp == 2 and slabs == 4 and outputs // (dp * seq) % 8 == 0
    piece = outputs // (dp * slabs)
    if tuned:
        keep, send = call(
            functools.partial(product_kernel, slabs),
            [((outputs // dp, width), F32), ((outputs // dp, width), BF16)], cots, cot_b, normed,
        )
        got = flip(send, "dp", dp, 1)
    back_far = near(back_far, bits=2)
    behind, last_u = doubling(slab_u, 15 * 10**8)
    if tuned:
        keep, send = call(
            split_kernel, [((2 * piece, width), F32), ((2 * piece, width), BF16)], keep, got, wait=w_all[1::2]
        )
        got = near(send, bits=SLAB)
    (send,) = call(relay_kernel, [((2 * rows + 2 * DH, width), BF16)], back, back_far)
    back_core = near(send, bits=1)
    later, later_far = call(
        later_kernel, [((2 * DH, width), BF16)] * 2, *behind, u, cost=2 * 10**9,
        scratch=[pltpu.VMEM((SLAB, DH, width), F32)],
    )
    later_far = near(later_far, bits=2)
    if tuned:
        keep, send = call(
            split_again_kernel, [((piece, width), F32), ((piece, width), BF16)], keep, got, cost=2 * 10**9
        )
        got = near(send, bits=2 * SLAB)
    output, gq, gk_part, gv_part, own_normed = call(
        functools.partial(late_kernel, dp),
        [((rows, outputs), BF16), ((rows, features), BF16), ((SLAB, rows, width), F32),
         ((SLAB, rows, width), F32), ((rows, features), BF16)],
        back, back_far, back_core, q, k, v, attend, own_tokens, *sent, out_weight, *w_all,
    )
    (send,) = call(relay_kernel, [((2 * DH, width), BF16)], later, later_far)
    later_core = near(send, bits=1)
    if tuned:
        keep, share = call(
            share_kernel, [((piece // 2, width), BF16)] * 2, keep, got, cost=3 * 10**9,
            scratch=[pltpu.VMEM((piece, width), F32)],
        )
        got = near(share, bits=2)
    gk, gv = call(
        last_kernel, [((rows, features), BF16)] * 2,
        later, later_far, later_core, k, v, gk_part, gv_part, end=True,
    )
    if tuned:
        keep, share = call(pass_kernel, [((piece // 2, width), BF16)] * 2, keep, got, wait=[pltpu.with_memory_space_constraint(gk, pltpu.HBM)])
        got = near(share, bits=1)
    if tuned:
        (grad_weight,) = call(
            functools.partial(finish_kernel, factor),
            [((piece // SLAB, features), F32)], keep, got, end=True,
        )
    else:
        partial = dot(cot, own_normed, 0, 0) * factor
        grad_weight = lax.psum_scatter(partial, ("dp", "seq"), scatter_dimension=0, tiled=True)
    shape = queries.shape
    return (
        output.reshape(cotangent.shape), gq.reshape(shape), gk.reshape(shape), gv.reshape(shape),
        grad_weight,
    )


def solution(mesh):
    dp, seq = mesh.shape["dp"], mesh.shape["seq"]
    return jax.shard_map(
        functools.partial(local, dp=dp, seq=seq),
        mesh=mesh,
        in_specs=(P("dp", "seq", None),) * 4 + (P("dp", None),),
        out_specs=(P("dp", "seq", None),) * 4 + (P(("dp", "seq"), None),),
        check_vma=False,
    )
```

```python
import functools
import math

import jax
import jax.numpy as jnp
from jax import lax
from jax.experimental import pallas as pl
from jax.experimental.pallas import tpu as pltpu
from jax.sharding import PartitionSpec as P

DH = 128
SLAB = 4
EPSILON = 1e-05
BF16 = jnp.bfloat16
F32 = jnp.float32


def dot(left, right, left_dim, right_dim):
    return lax.dot_general(
        left, right, (((left_dim,), (right_dim,)), ((), ())), preferred_element_type=F32
    )


class Chain:
    def __init__(self):
        self.last = None

    def __call__(self, body, outs, *args, scratch=(), far=False, wait=(), cost=1, end=False):
        count = len(args)
        if far:
            args = [pltpu.with_memory_space_constraint(x, pltpu.HBM) for x in args]
        specs = [pl.BlockSpec(memory_space=pl.ANY) if far else pl.BlockSpec()] * count
        inner = body
        if self.last is not None:
            extra = (self.last, *wait)
            args = (*args, *extra)
            specs = [*specs, *[pl.BlockSpec(memory_space=pl.ANY)] * len(extra)]

            def inner(*refs):
                body(*refs[:count], *refs[count + len(extra) :])

        found = pl.pallas_call(
            inner,
            out_shape=[jax.ShapeDtypeStruct(s, d) for s, d in outs],
            in_specs=specs,
            scratch_shapes=list(scratch),
            cost_estimate=pl.CostEstimate(flops=cost, bytes_accessed=1, transcendentals=0),
            compiler_params=pltpu.CompilerParams(vmem_limit_bytes=32 * 2**20),
        )(*args)
        if not end:
            self.last = min(reversed(found), key=lambda x: x.size)
        return found


def after(x, *others):
    return lax.optimization_barrier((x, *others))[0]


def flip(x, axis, count, bits):
    return lax.ppermute(x, axis, [(i, i ^ bits) for i in range(count)])


def head(h):
    return slice(h * DH, (h + 1) * DH)


def part(i, size):
    return slice(i * size, (i + 1) * size)


def cut(start, size):
    return pl.ds(pl.multiple_of(start * size, size), size)


def member(r):
    return jnp.bitwise_xor(lax.rem(lax.axis_index("seq"), SLAB), r)


def causal(block):
    rows = lax.broadcasted_iota(jnp.int32, (block, block), 0)
    return lax.broadcasted_iota(jnp.int32, (block, block), 1) <= rows


def fetch(pairs, sems):
    copies = [pltpu.make_async_copy(a, b, sems.at[i]) for i, (a, b) in enumerate(pairs)]
    for copy in copies:
        copy.start()
    return copies


def front_kernel(k_hbm, v_hbm, w_hbm, own_ref, near_ref, far_ref, columns_ref, k_ref, v_ref, w_ref, sems):
    copies = fetch([(k_hbm, k_ref), (v_hbm, v_ref), (w_hbm, w_ref)], sems)
    width = k_ref.shape[1] // SLAB
    copies[0].wait()
    copies[1].wait()
    places = (own_ref, near_ref, far_ref.at[part(0, DH)], far_ref.at[part(1, DH)])
    for r, out in enumerate(places):
        k, v = k_ref[:, cut(member(r), width)], v_ref[:, cut(member(r), width)]
        for h in range(width // DH):
            out[:, head(h)] = dot(k[:, head(h)], v[:, head(h)], 0, 0).astype(out.dtype)
    copies[2].wait()
    for i in range(2):
        columns_ref[i] = w_ref[:, cut(member(2 * i), width)]


def pack_kernel(q_ref, k_ref, v_ref, c_ref, attend_ref, own_ref, message_ref, far_ref):
    block = q_ref.shape[0]
    width = q_ref.shape[1] // SLAB
    mask = causal(block)
    places = (own_ref, message_ref.at[: 2 * block], far_ref, message_ref.at[2 * block : 4 * block])
    for r, out in enumerate(places):
        q, k, v = (ref[:, cut(member(r), width)] for ref in (q_ref, k_ref, v_ref))
        out[:block, :] = q
        for h in range(width // DH):
            attend = jnp.where(mask, dot(q[:, head(h)], k[:, head(h)], 1, 1), 0.0).astype(BF16)
            attend_ref[r, h] = attend
            out[block:, head(h)] = dot(attend, v[:, head(h)], 1, 0).astype(BF16)
    for i in range(c_ref.shape[1] // width):
        message_ref[part(4 + i, block), :] = c_ref[:, part(i, width)]


def cross_kernel(near_ref, got_ref, out_ref):
    out_ref[part(0, DH), :] = near_ref[...]
    out_ref[part(1, DH), :] = got_ref[part(1, DH), :]


def total_kernel(own_ref, far_ref, near_ref, out_ref):
    total = own_ref[...] + far_ref[part(0, DH), :].astype(F32)
    total = total + near_ref[part(0, DH), :].astype(F32) + near_ref[part(1, DH), :].astype(F32)
    out_ref[...] = total.astype(BF16)


def pair_kernel(message_ref, far_ref, out_ref):
    size = far_ref.shape[0]
    out_ref[:size, :] = far_ref[...]
    out_ref[size:, :] = message_ref[part(1, size), :]


def add_kernel(own_ref, got_ref, out_ref):
    out_ref[...] = (own_ref[...].astype(F32) + got_ref[...].astype(F32)).astype(out_ref.dtype)


def dnormed_kernel(groups, members, *refs):
    cots, weights = refs[: len(members)], refs[len(members) : len(members) + groups]
    dnormed_ref, cot_ref = refs[len(members) + groups :]
    _, block, outputs = cot_ref.shape
    width = dnormed_ref.shape[2]
    rows = weights[0].shape[1]
    me = lax.axis_index("dp")
    for i, (r, ref) in enumerate(zip(members, cots)):
        if r == 1:
            for p in range(outputs // width):
                cot_ref[i, :, part(p, width)] = ref[part(4 + p, block), :]
        else:
            cot_ref[i] = ref[...]
        total = dot(cot_ref[i, :, cut(me, rows)], weights[0][0], 1, 0)
        for j in range(1, groups):
            total = total + dot(cot_ref[i, :, cut(jnp.bitwise_xor(me, j), rows)], weights[j][0], 1, 0)
        dnormed_ref[i] = total


def base_kernel(*refs):
    refs[-1][...] = from_slabs(False, refs[:-1])


def from_slabs(backward, refs):
    slab = lax.div(lax.axis_index("seq"), SLAB)
    total = jnp.zeros(refs[0].shape, F32)
    for i, ref in enumerate(refs):
        bit = lax.rem(lax.div(slab, 1 << i), 2)
        total = total + jnp.where(bit == (0 if backward else 1), ref[...].astype(F32), 0.0)
    return total


def middle_kernel(*refs):
    own_ref, message_ref, token_far, own_state, far_state, near_state, base_ref, dnormed_a, dnormed_b = refs[:9]
    normed_ref, back_near, back_far, u_ref, slab_ref, running = refs[9:]
    _, block, width = normed_ref.shape
    heads = width // DH
    size = 2 * block
    tokens = (own_ref, message_ref.at[:size], token_far.at[:size], token_far.at[size:])
    running[member(0)] = own_state[...]
    running[member(1)] = near_state[part(0, DH), :].astype(F32)
    running[member(2)] = far_state[part(0, DH), :].astype(F32)
    running[member(3)] = near_state[part(1, DH), :].astype(F32)
    total = base_ref[...]
    for p in range(SLAB):
        total, running[p] = total + running[p], total
    sums = [jnp.zeros((DH, DH), F32)] * heads
    for r in range(SLAB):
        out = (back_near, back_far)[r // 2].at[part(r % 2, block + DH)]
        prior = running[member(r)].astype(BF16)
        out[block:, :] = prior
        for h in range(heads):
            q = tokens[r][:block, head(h)]
            mixed = tokens[r][block:, head(h)].astype(F32) + dot(q, prior[:, head(h)], 1, 0)
            scale = lax.rsqrt(jnp.mean(mixed * mixed, axis=-1, keepdims=True) + EPSILON)
            normed = mixed * scale
            normed_ref[r, :, head(h)] = normed.astype(BF16)
            dnormed = dnormed_a[r, :, head(h)] if r < 3 else dnormed_b[0, :, head(h)]
            along = jnp.mean(dnormed * normed, axis=-1, keepdims=True)
            dmixed = ((dnormed - normed * along) * scale).astype(BF16)
            out[:block, head(h)] = dmixed
            u = dot(q, dmixed, 0, 0)
            u_ref[r, :, head(h)] = u
            sums[h] = sums[h] + u
    for h in range(heads):
        slab_ref[:, head(h)] = sums[h].astype(BF16)


def later_kernel(*refs):
    *behind, u_ref, near_ref, far_ref, running = refs
    for r in range(SLAB):
        running[member(r)] = u_ref[r]
    total = from_slabs(True, behind)
    for p in reversed(range(SLAB)):
        total, running[p] = total + running[p], total
    for r in range(SLAB):
        (near_ref, far_ref)[r // 2][part(r % 2, DH), :] = running[member(r)].astype(BF16)


def relay_kernel(near_ref, far_ref, out_ref):
    size = near_ref.shape[0] // 2
    out_ref[:size, :] = near_ref[size:, :]
    out_ref[size:, :] = far_ref[size:, :]


def arrived(near_ref, far_ref, core_ref):
    size = near_ref.shape[0] // 2
    first, second = slice(0, size), slice(size, 2 * size)
    return near_ref.at[first], core_ref.at[first], far_ref.at[first], core_ref.at[second]


def late_kernel(*refs):
    backs, (q_ref, k_ref, v_ref, attend_ref, own_ref, message_ref, far_ref) = arrived(*refs[:3]), refs[3:10]
    gq_ref, gk_ref, gv_ref, normed_ref = refs[10:]
    block, width = q_ref.shape[0], refs[0].shape[1]
    mask = causal(block)
    withins = (own_ref.at[part(1, block)], message_ref.at[part(1, block)],
               far_ref.at[part(1, block)], message_ref.at[part(3, block)])
    for r in range(SLAB):
        at = cut(member(r), width)
        q, k, v = q_ref[:, at], k_ref[:, at], v_ref[:, at]
        normeds, gqs, gks, gvs = [], [], [], []
        for h in range(width // DH):
            dmixed, prior = backs[r][:block, head(h)], backs[r][block:, head(h)]
            mixed = withins[r][:, head(h)].astype(F32) + dot(q[:, head(h)], prior, 1, 0)
            scale = lax.rsqrt(jnp.mean(mixed * mixed, axis=-1, keepdims=True) + EPSILON)
            normeds.append(mixed * scale)
            back = jnp.where(mask, dot(dmixed, v[:, head(h)], 1, 1), 0.0).astype(BF16)
            gqs.append(dot(back, k[:, head(h)], 1, 0) + dot(dmixed, prior, 1, 1))
            gks.append(dot(back, q[:, head(h)], 0, 0))
            gvs.append(dot(attend_ref[r, h], dmixed, 0, 0))
        normed_ref[:, at] = jnp.concatenate(normeds, axis=1).astype(BF16)
        gq_ref[:, at] = jnp.concatenate(gqs, axis=1).astype(BF16)
        gk_ref[r] = jnp.concatenate(gks, axis=1)
        gv_ref[r] = jnp.concatenate(gvs, axis=1)


def output_kernel(normed_ref, weight_ref, *refs):
    *far, out_ref = refs
    width = normed_ref.shape[1] // SLAB
    rows = weight_ref.shape[0]
    me = lax.axis_index("dp")
    out_ref[:, cut(me, rows)] = dot(normed_ref[...], weight_ref[...], 1, 1).astype(BF16)
    for j in range(1, len(far) // 2 + 1):
        total = jnp.zeros((normed_ref.shape[0], rows), F32)
        for r in range(SLAB):
            normed = normed_ref[:, cut(member(r), width)]
            total = total + dot(normed, far[2 * (j - 1) + r % 2][r // 2], 1, 1)
        out_ref[:, cut(jnp.bitwise_xor(me, j), rows)] = total.astype(BF16)


def last_kernel(near_ref, far_ref, core_ref, k_ref, v_ref, gk_part, gv_part, gk_ref, gv_ref):
    laters = arrived(near_ref, far_ref, core_ref)
    width = near_ref.shape[1]
    for r in range(SLAB):
        at = cut(member(r), width)
        k, v = k_ref[:, at], v_ref[:, at]
        gks, gvs = [], []
        for h in range(width // DH):
            later = laters[r][:, head(h)]
            gks.append(gk_part[r, :, head(h)] + dot(v[:, head(h)], later, 1, 1))
            gvs.append(gv_part[r, :, head(h)] + dot(k[:, head(h)], later, 1, 0))
        gk_ref[:, at] = jnp.concatenate(gks, axis=1).astype(BF16)
        gv_ref[:, at] = jnp.concatenate(gvs, axis=1).astype(BF16)


def product_kernel(slabs, cot_a, cot_b, normed_ref, keep_ref, send_ref):
    me = lax.axis_index("dp")
    slab = lax.div(lax.axis_index("seq"), SLAB)
    rows = keep_ref.shape[0] // slabs
    for j, out in enumerate((send_ref, keep_ref)):
        for d in range(slabs):
            at = jnp.bitwise_xor(me, 1 - j) * slabs + jnp.bitwise_xor(slab, d)
            total = dot(cot_b[0, :, cut(at, rows)], normed_ref[3], 0, 0)
            for r in range(3):
                total = total + dot(cot_a[r, :, cut(at, rows)], normed_ref[r], 0, 0)
            out[part(d, rows), :] = total.astype(out.dtype)


def split_kernel(own_ref, got_ref, keep_ref, send_ref):
    rows = keep_ref.shape[0] // 2
    for i in range(4):
        total = own_ref[part(i, rows), :] + got_ref[part(i, rows), :].astype(F32)
        out = (keep_ref, send_ref)[i % 2]
        out[part(i // 2, rows), :] = total.astype(out.dtype)


def split_again_kernel(own_ref, got_ref, keep_ref, send_ref):
    rows = keep_ref.shape[0]
    for i, out in enumerate((keep_ref, send_ref)):
        total = own_ref[part(i, rows), :] + got_ref[part(i, rows), :].astype(F32)
        out[...] = total.astype(out.dtype)


def share_kernel(own_ref, got_ref, keep_ref, send_ref, total_ref):
    total_ref[...] = own_ref[...] + got_ref[...].astype(F32)
    rows = keep_ref.shape[0] // 2
    for i, r in enumerate((0, 1)):
        keep_ref[part(i, rows), :] = total_ref[cut(member(r), rows), :].astype(BF16)
    for i, r in enumerate((2, 3)):
        send_ref[part(i, rows), :] = total_ref[cut(member(r), rows), :].astype(BF16)


def pass_kernel(own_ref, got_ref, keep_ref, send_ref):
    rows = own_ref.shape[0] // 2
    for i, ref in enumerate((own_ref, got_ref)):
        keep_ref[part(i, rows), :] = ref[:rows, :]
        send_ref[part(i, rows), :] = ref[rows:, :]


def finish_kernel(factor, keep_ref, got_ref, out_ref):
    rows, width = out_ref.shape[0], keep_ref.shape[1]
    for i, ref in enumerate((keep_ref, got_ref)):
        for j in range(2):
            out_ref[:, cut(member(i + 2 * j), width)] = ref[part(j, rows), :].astype(F32) * factor


def local(queries, keys, values, cotangent, out_weight, *, dp, seq):
    call = Chain()
    local_seqs, block, features = queries.shape
    outputs = cotangent.shape[2]
    rows = local_seqs * block
    slabs = seq // SLAB
    width = features // SLAB
    heads = width // DH
    q, k, v = (x.reshape(rows, features) for x in (queries, keys, values))
    cot = cotangent.reshape(rows, outputs)
    factor = 1.0 / math.sqrt(rows * dp * seq)
    near = functools.partial(flip, axis="seq", count=seq)

    def doubling(total, cost=1):
        found = []
        bits = SLAB
        while bits < seq:
            if found:
                (total,) = call(add_kernel, [(total.shape, BF16)], total, found[-1], cost=cost)
            found.append(near(total, bits=bits))
            bits *= 2
        return found, total

    def scratch(*arrays):
        return [pltpu.VMEM(x.shape, BF16) for x in arrays] + [pltpu.SemaphoreType.DMA((len(arrays),))]

    own_state, near_state, far_state, columns = call(
        front_kernel,
        [((DH, width), F32), ((DH, width), BF16), ((2 * DH, width), BF16),
         ((2, out_weight.shape[0], width), BF16)],
        k, v, out_weight, far=True, scratch=scratch(k, v, out_weight),
    )
    far_state = near(far_state, bits=2)
    w_far = [flip(columns, "dp", dp, j) for j in range(1, dp)]
    attend, own_tokens, message, far_tokens = call(
        pack_kernel,
        [((SLAB, heads, rows, rows), BF16), ((2 * rows, width), BF16),
         (((4 + outputs // width) * rows, width), BF16), ((2 * rows, width), BF16)],
        q, k, v, cot,
    )
    cot_y = near(cot, bits=2)
    near_tokens, sent = message, (message, far_tokens)
    message = near(message, bits=1)
    (near_state,) = call(
        cross_kernel, [((2 * DH, width), BF16)], near_state, far_state, cost=5 * 10**9
    )
    near_state = near(near_state, bits=1)
    (slab_kv,) = call(total_kernel, [((DH, width), BF16)], own_state, far_state, near_state)
    (far_tokens,) = call(pair_kernel, [((4 * rows, width), BF16)], message, far_tokens)
    cot_yc = near(after(cot_y, far_tokens), bits=1)
    far_tokens = near(far_tokens, bits=2)
    before, _ = doubling(slab_kv, 22 * 10**8)
    weights = (columns, *w_far)
    dnormed, cots = call(
        functools.partial(dnormed_kernel, dp, (0, 1, 2)),
        [((3, rows, width), F32), ((3, rows, outputs), BF16)], cot, message, cot_y, *weights,
    )
    dnormed_b, cot_b = call(
        functools.partial(dnormed_kernel, dp, (3,)),
        [((1, rows, width), F32), ((1, rows, outputs), BF16)], cot_yc, *weights,
    )
    (base,) = call(base_kernel, [((DH, width), F32)], *before, cost=10**9)
    w_all = [x for w in w_far for x in (w, near(after(w, dnormed), bits=1))]
    normed, back, back_far, u, slab_u = call(
        middle_kernel,
        [((SLAB, rows, width), BF16)] + [((2 * rows + 2 * DH, width), BF16)] * 2
        + [((SLAB, DH, width), F32), ((DH, width), BF16)],
        own_tokens, message, far_tokens, own_state, far_state, near_state, base, dnormed, dnormed_b,
        cost=10**10, scratch=[pltpu.VMEM((SLAB, DH, width), F32)],
    )
    tuned = dp == 2 and slabs == 4 and outputs // (dp * seq) % 8 == 0
    piece = outputs // (dp * slabs)
    if tuned:
        keep, send = call(
            functools.partial(product_kernel, slabs),
            [((outputs // dp, width), F32), ((outputs // dp, width), BF16)], cots, cot_b, normed,
        )
        got = flip(send, "dp", dp, 1)
    back_far = near(back_far, bits=2)
    behind, last_u = doubling(slab_u, 15 * 10**8)
    if tuned:
        keep, send = call(
            split_kernel, [((2 * piece, width), F32), ((2 * piece, width), BF16)], keep, got, wait=w_all[1::2]
        )
        got = near(send, bits=SLAB)
    (send,) = call(relay_kernel, [((2 * rows + 2 * DH, width), BF16)], back, back_far)
    back_core = near(send, bits=1)
    later, later_far = call(
        later_kernel, [((2 * DH, width), BF16)] * 2, *behind, u, cost=2 * 10**9,
        scratch=[pltpu.VMEM((SLAB, DH, width), F32)],
    )
    later_far = near(later_far, bits=2)
    if tuned:
        keep, send = call(
            split_again_kernel, [((piece, width), F32), ((piece, width), BF16)], keep, got, cost=2 * 10**9
        )
        got = near(send, bits=2 * SLAB)
    gq, gk_part, gv_part, own_normed = call(
        late_kernel,
        [((rows, features), BF16), ((SLAB, rows, width), F32), ((SLAB, rows, width), F32), ((rows, features), BF16)],
        back, back_far, back_core, q, k, v, attend, own_tokens, *sent,
    )
    (send,) = call(relay_kernel, [((2 * DH, width), BF16)], later, later_far)
    later_core = near(send, bits=1)
    if tuned:
        keep, share = call(
            share_kernel, [((piece // 2, width), BF16)] * 2, keep, got, cost=3 * 10**9,
            scratch=[pltpu.VMEM((piece, width), F32)],
        )
        got = near(share, bits=2)
    gk, gv = call(
        last_kernel, [((rows, features), BF16)] * 2,
        later, later_far, later_core, k, v, gk_part, gv_part, end=True,
    )
    (output,) = call(
        output_kernel, [((rows, outputs), BF16)], own_normed, out_weight, *w_all, end=True,
    )
    if tuned:
        keep, share = call(
            pass_kernel, [((piece // 2, width), BF16)] * 2, keep, got,
            wait=[pltpu.with_memory_space_constraint(x, pltpu.HBM) for x in (gk, output)],
        )
        got = near(share, bits=1)
    if tuned:
        (grad_weight,) = call(
            functools.partial(finish_kernel, factor),
            [((piece // SLAB, features), F32)], keep, got, end=True,
        )
    else:
        partial = dot(cot, own_normed, 0, 0) * factor
        grad_weight = lax.psum_scatter(partial, ("dp", "seq"), scatter_dimension=0, tiled=True)
    shape = queries.shape
    return (
        output.reshape(cotangent.shape), gq.reshape(shape), gk.reshape(shape), gv.reshape(shape),
        grad_weight,
    )


def solution(mesh):
    dp, seq = mesh.shape["dp"], mesh.shape["seq"]
    return jax.shard_map(
        functools.partial(local, dp=dp, seq=seq),
        mesh=mesh,
        in_specs=(P("dp", "seq", None),) * 4 + (P("dp", None),),
        out_specs=(P("dp", "seq", None),) * 4 + (P(("dp", "seq"), None),),
        check_vma=False,
    )
```

```python
import functools
import math

import jax
import jax.numpy as jnp
from jax import lax
from jax.experimental import pallas as pl
from jax.experimental.pallas import tpu as pltpu
from jax.sharding import PartitionSpec as P

DH = 128
SLAB = 4
EPSILON = 1e-05
BF16 = jnp.bfloat16
F32 = jnp.float32


def dot(left, right, left_dim, right_dim):
    return lax.dot_general(
        left, right, (((left_dim,), (right_dim,)), ((), ())), preferred_element_type=F32
    )


class Chain:
    def __init__(self):
        self.last = None

    def __call__(self, body, outs, *args, scratch=(), far=False, wait=(), cost=1, end=False):
        count = len(args)
        if far:
            args = [pltpu.with_memory_space_constraint(x, pltpu.HBM) for x in args]
        specs = [pl.BlockSpec(memory_space=pl.ANY) if far else pl.BlockSpec()] * count
        inner = body
        if self.last is not None:
            extra = (self.last, *wait)
            args = (*args, *extra)
            specs = [*specs, *[pl.BlockSpec(memory_space=pl.ANY)] * len(extra)]

            def inner(*refs):
                body(*refs[:count], *refs[count + len(extra) :])

        found = pl.pallas_call(
            inner,
            out_shape=[jax.ShapeDtypeStruct(s, d) for s, d in outs],
            in_specs=specs,
            scratch_shapes=list(scratch),
            cost_estimate=pl.CostEstimate(flops=cost, bytes_accessed=1, transcendentals=0),
            compiler_params=pltpu.CompilerParams(vmem_limit_bytes=32 * 2**20),
        )(*args)
        if not end:
            self.last = min(reversed(found), key=lambda x: x.size)
        return found


def after(x, *others):
    return lax.optimization_barrier((x, *others))[0]


def flip(x, axis, count, bits):
    return lax.ppermute(x, axis, [(i, i ^ bits) for i in range(count)])


def head(h):
    return slice(h * DH, (h + 1) * DH)


def part(i, size):
    return slice(i * size, (i + 1) * size)


def cut(start, size):
    return pl.ds(pl.multiple_of(start * size, size), size)


def member(r):
    return jnp.bitwise_xor(lax.rem(lax.axis_index("seq"), SLAB), r)


def causal(block):
    rows = lax.broadcasted_iota(jnp.int32, (block, block), 0)
    return lax.broadcasted_iota(jnp.int32, (block, block), 1) <= rows


def fetch(pairs, sems):
    copies = [pltpu.make_async_copy(a, b, sems.at[i]) for i, (a, b) in enumerate(pairs)]
    for copy in copies:
        copy.start()
    return copies


def front_kernel(k_hbm, v_hbm, w_hbm, own_ref, near_ref, far_ref, columns_ref, k_ref, v_ref, w_ref, sems):
    copies = fetch([(k_hbm, k_ref), (v_hbm, v_ref), (w_hbm, w_ref)], sems)
    width = k_ref.shape[1] // SLAB
    copies[0].wait()
    copies[1].wait()
    places = (own_ref, near_ref, far_ref.at[part(0, DH)], far_ref.at[part(1, DH)])
    for r, out in enumerate(places):
        k, v = k_ref[:, cut(member(r), width)], v_ref[:, cut(member(r), width)]
        for h in range(width // DH):
            out[:, head(h)] = dot(k[:, head(h)], v[:, head(h)], 0, 0).astype(out.dtype)
    copies[2].wait()
    for i in range(2):
        columns_ref[i] = w_ref[:, cut(member(2 * i), width)]


def pack_kernel(q_ref, k_ref, v_ref, c_ref, attend_ref, own_ref, message_ref, far_ref):
    block = q_ref.shape[0]
    width = q_ref.shape[1] // SLAB
    mask = causal(block)
    places = (own_ref, message_ref.at[: 2 * block], far_ref, message_ref.at[2 * block : 4 * block])
    for r, out in enumerate(places):
        q, k, v = (ref[:, cut(member(r), width)] for ref in (q_ref, k_ref, v_ref))
        out[:block, :] = q
        for h in range(width // DH):
            attend = jnp.where(mask, dot(q[:, head(h)], k[:, head(h)], 1, 1), 0.0).astype(BF16)
            attend_ref[r, h] = attend
            out[block:, head(h)] = dot(attend, v[:, head(h)], 1, 0).astype(BF16)
    for i in range(c_ref.shape[1] // width):
        message_ref[part(4 + i, block), :] = c_ref[:, part(i, width)]


def cross_kernel(near_ref, got_ref, out_ref):
    out_ref[part(0, DH), :] = near_ref[...]
    out_ref[part(1, DH), :] = got_ref[part(1, DH), :]


def total_kernel(own_ref, far_ref, near_ref, out_ref):
    total = own_ref[...] + far_ref[part(0, DH), :].astype(F32)
    total = total + near_ref[part(0, DH), :].astype(F32) + near_ref[part(1, DH), :].astype(F32)
    out_ref[...] = total.astype(BF16)


def pair_kernel(message_ref, far_ref, out_ref):
    size = far_ref.shape[0]
    out_ref[:size, :] = far_ref[...]
    out_ref[size:, :] = message_ref[part(1, size), :]


def add_kernel(own_ref, got_ref, out_ref):
    out_ref[...] = (own_ref[...].astype(F32) + got_ref[...].astype(F32)).astype(out_ref.dtype)


def dnormed_kernel(groups, members, *refs):
    cots, weights = refs[: len(members)], refs[len(members) : len(members) + groups]
    dnormed_ref, cot_ref = refs[len(members) + groups :]
    _, block, outputs = cot_ref.shape
    width = dnormed_ref.shape[2]
    rows = weights[0].shape[1]
    me = lax.axis_index("dp")
    for i, (r, ref) in enumerate(zip(members, cots)):
        if r == 1:
            for p in range(outputs // width):
                cot_ref[i, :, part(p, width)] = ref[part(4 + p, block), :]
        else:
            cot_ref[i] = ref[...]
        total = dot(cot_ref[i, :, cut(me, rows)], weights[0][0], 1, 0)
        for j in range(1, groups):
            total = total + dot(cot_ref[i, :, cut(jnp.bitwise_xor(me, j), rows)], weights[j][0], 1, 0)
        dnormed_ref[i] = total


def base_kernel(*refs):
    refs[-1][...] = from_slabs(False, refs[:-1])


def from_slabs(backward, refs):
    slab = lax.div(lax.axis_index("seq"), SLAB)
    total = jnp.zeros(refs[0].shape, F32)
    for i, ref in enumerate(refs):
        bit = lax.rem(lax.div(slab, 1 << i), 2)
        total = total + jnp.where(bit == (0 if backward else 1), ref[...].astype(F32), 0.0)
    return total


def middle_kernel(*refs):
    own_ref, message_ref, token_far, own_state, far_state, near_state, base_ref, dnormed_a, dnormed_b = refs[:9]
    normed_ref, back_near, back_far, u_ref, slab_ref, running = refs[9:]
    _, block, width = normed_ref.shape
    heads = width // DH
    size = 2 * block
    tokens = (own_ref, message_ref.at[:size], token_far.at[:size], token_far.at[size:])
    running[member(0)] = own_state[...]
    running[member(1)] = near_state[part(0, DH), :].astype(F32)
    running[member(2)] = far_state[part(0, DH), :].astype(F32)
    running[member(3)] = near_state[part(1, DH), :].astype(F32)
    total = base_ref[...]
    for p in range(SLAB):
        total, running[p] = total + running[p], total
    sums = [jnp.zeros((DH, DH), F32)] * heads
    for r in range(SLAB):
        out = (back_near, back_far)[r // 2].at[part(r % 2, block + DH)]
        prior = running[member(r)].astype(BF16)
        out[block:, :] = prior
        for h in range(heads):
            q = tokens[r][:block, head(h)]
            mixed = tokens[r][block:, head(h)].astype(F32) + dot(q, prior[:, head(h)], 1, 0)
            scale = lax.rsqrt(jnp.mean(mixed * mixed, axis=-1, keepdims=True) + EPSILON)
            normed = mixed * scale
            normed_ref[r, :, head(h)] = normed.astype(BF16)
            dnormed = dnormed_a[r, :, head(h)] if r < 3 else dnormed_b[0, :, head(h)]
            along = jnp.mean(dnormed * normed, axis=-1, keepdims=True)
            dmixed = ((dnormed - normed * along) * scale).astype(BF16)
            out[:block, head(h)] = dmixed
            u = dot(q, dmixed, 0, 0)
            u_ref[r, :, head(h)] = u
            sums[h] = sums[h] + u
    for h in range(heads):
        slab_ref[:, head(h)] = sums[h].astype(BF16)


def later_kernel(*refs):
    *behind, u_ref, near_ref, far_ref, running = refs
    for r in range(SLAB):
        running[member(r)] = u_ref[r]
    total = from_slabs(True, behind)
    for p in reversed(range(SLAB)):
        total, running[p] = total + running[p], total
    for r in range(SLAB):
        (near_ref, far_ref)[r // 2][part(r % 2, DH), :] = running[member(r)].astype(BF16)


def relay_kernel(near_ref, far_ref, out_ref):
    size = near_ref.shape[0] // 2
    out_ref[:size, :] = near_ref[size:, :]
    out_ref[size:, :] = far_ref[size:, :]


def arrived(near_ref, far_ref, core_ref):
    size = near_ref.shape[0] // 2
    first, second = slice(0, size), slice(size, 2 * size)
    return near_ref.at[first], core_ref.at[first], far_ref.at[first], core_ref.at[second]


def late_kernel(*refs):
    backs, (q_ref, k_ref, v_ref, attend_ref, own_ref, message_ref, far_ref) = arrived(*refs[:3]), refs[3:10]
    gq_ref, gk_ref, gv_ref, normed_ref = refs[10:]
    block, width = q_ref.shape[0], refs[0].shape[1]
    mask = causal(block)
    withins = (own_ref.at[part(1, block)], message_ref.at[part(1, block)],
               far_ref.at[part(1, block)], message_ref.at[part(3, block)])
    for r in range(SLAB):
        at = cut(member(r), width)
        q, k, v = q_ref[:, at], k_ref[:, at], v_ref[:, at]
        normeds, gqs, gks, gvs = [], [], [], []
        for h in range(width // DH):
            dmixed, prior = backs[r][:block, head(h)], backs[r][block:, head(h)]
            mixed = withins[r][:, head(h)].astype(F32) + dot(q[:, head(h)], prior, 1, 0)
            scale = lax.rsqrt(jnp.mean(mixed * mixed, axis=-1, keepdims=True) + EPSILON)
            normeds.append(mixed * scale)
            back = jnp.where(mask, dot(dmixed, v[:, head(h)], 1, 1), 0.0).astype(BF16)
            gqs.append(dot(back, k[:, head(h)], 1, 0) + dot(dmixed, prior, 1, 1))
            gks.append(dot(back, q[:, head(h)], 0, 0))
            gvs.append(dot(attend_ref[r, h], dmixed, 0, 0))
        normed_ref[:, at] = jnp.concatenate(normeds, axis=1).astype(BF16)
        gq_ref[:, at] = jnp.concatenate(gqs, axis=1).astype(BF16)
        gk_ref[r] = jnp.concatenate(gks, axis=1)
        gv_ref[r] = jnp.concatenate(gvs, axis=1)


def output_kernel(normed_ref, weight_ref, *refs):
    *far, out_ref = refs
    width = normed_ref.shape[1] // SLAB
    rows = weight_ref.shape[0]
    me = lax.axis_index("dp")
    out_ref[:, cut(me, rows)] = dot(normed_ref[...], weight_ref[...], 1, 1).astype(BF16)
    for j in range(1, len(far) // 2 + 1):
        total = jnp.zeros((normed_ref.shape[0], rows), F32)
        for r in range(SLAB):
            normed = normed_ref[:, cut(member(r), width)]
            total = total + dot(normed, far[2 * (j - 1) + r % 2][r // 2], 1, 1)
        out_ref[:, cut(jnp.bitwise_xor(me, j), rows)] = total.astype(BF16)


def last_kernel(near_ref, far_ref, core_ref, k_ref, v_ref, gk_part, gv_part, gk_ref, gv_ref):
    laters = arrived(near_ref, far_ref, core_ref)
    width = near_ref.shape[1]
    for r in range(SLAB):
        at = cut(member(r), width)
        k, v = k_ref[:, at], v_ref[:, at]
        gks, gvs = [], []
        for h in range(width // DH):
            later = laters[r][:, head(h)]
            gks.append(gk_part[r, :, head(h)] + dot(v[:, head(h)], later, 1, 1))
            gvs.append(gv_part[r, :, head(h)] + dot(k[:, head(h)], later, 1, 0))
        gk_ref[:, at] = jnp.concatenate(gks, axis=1).astype(BF16)
        gv_ref[:, at] = jnp.concatenate(gvs, axis=1).astype(BF16)


def product_kernel(slabs, cot_a, cot_b, normed_ref, keep_ref, send_ref):
    me = lax.axis_index("dp")
    slab = lax.div(lax.axis_index("seq"), SLAB)
    rows = keep_ref.shape[0] // slabs
    for j, out in enumerate((send_ref, keep_ref)):
        for d in range(slabs):
            at = jnp.bitwise_xor(me, 1 - j) * slabs + jnp.bitwise_xor(slab, d)
            total = dot(cot_b[0, :, cut(at, rows)], normed_ref[3], 0, 0)
            for r in range(3):
                total = total + dot(cot_a[r, :, cut(at, rows)], normed_ref[r], 0, 0)
            out[part(d, rows), :] = total.astype(out.dtype)


def split_kernel(own_ref, got_ref, keep_ref, send_ref):
    rows = keep_ref.shape[0] // 2
    for i in range(4):
        total = own_ref[part(i, rows), :] + got_ref[part(i, rows), :].astype(F32)
        out = (keep_ref, send_ref)[i % 2]
        out[part(i // 2, rows), :] = total.astype(out.dtype)


def split_again_kernel(own_ref, got_ref, keep_ref, send_ref):
    rows = keep_ref.shape[0]
    for i, out in enumerate((keep_ref, send_ref)):
        total = own_ref[part(i, rows), :] + got_ref[part(i, rows), :].astype(F32)
        out[...] = total.astype(out.dtype)


def share_kernel(own_ref, got_ref, keep_ref, send_ref, total_ref):
    total_ref[...] = own_ref[...] + got_ref[...].astype(F32)
    rows = keep_ref.shape[0] // 2
    for i, r in enumerate((0, 1)):
        keep_ref[part(i, rows), :] = total_ref[cut(member(r), rows), :].astype(BF16)
    for i, r in enumerate((2, 3)):
        send_ref[part(i, rows), :] = total_ref[cut(member(r), rows), :].astype(BF16)


def pass_kernel(own_ref, got_ref, keep_ref, send_ref):
    rows = own_ref.shape[0] // 2
    for i, ref in enumerate((own_ref, got_ref)):
        keep_ref[part(i, rows), :] = ref[:rows, :]
        send_ref[part(i, rows), :] = ref[rows:, :]


def finish_kernel(factor, keep_ref, got_ref, out_ref):
    rows, width = out_ref.shape[0], keep_ref.shape[1]
    for i, ref in enumerate((keep_ref, got_ref)):
        for j in range(2):
            out_ref[:, cut(member(i + 2 * j), width)] = ref[part(j, rows), :].astype(F32) * factor


def local(queries, keys, values, cotangent, out_weight, *, dp, seq):
    call = Chain()
    local_seqs, block, features = queries.shape
    outputs = cotangent.shape[2]
    rows = local_seqs * block
    slabs = seq // SLAB
    width = features // SLAB
    heads = width // DH
    q, k, v = (x.reshape(rows, features) for x in (queries, keys, values))
    cot = cotangent.reshape(rows, outputs)
    factor = 1.0 / math.sqrt(rows * dp * seq)
    near = functools.partial(flip, axis="seq", count=seq)

    def doubling(total, cost=1):
        found = []
        bits = SLAB
        while bits < seq:
            if found:
                (total,) = call(add_kernel, [(total.shape, BF16)], total, found[-1], cost=cost)
            found.append(near(total, bits=bits))
            bits *= 2
        return found, total

    def scratch(*arrays):
        return [pltpu.VMEM(x.shape, BF16) for x in arrays] + [pltpu.SemaphoreType.DMA((len(arrays),))]

    own_state, near_state, far_state, columns = call(
        front_kernel,
        [((DH, width), F32), ((DH, width), BF16), ((2 * DH, width), BF16),
         ((2, out_weight.shape[0], width), BF16)],
        k, v, out_weight, far=True, scratch=scratch(k, v, out_weight),
    )
    far_state = near(far_state, bits=2)
    w_far = [flip(columns, "dp", dp, j) for j in range(1, dp)]
    attend, own_tokens, message, far_tokens = call(
        pack_kernel,
        [((SLAB, heads, rows, rows), BF16), ((2 * rows, width), BF16),
         (((4 + outputs // width) * rows, width), BF16), ((2 * rows, width), BF16)],
        q, k, v, cot,
    )
    cot_y = near(cot, bits=2)
    near_tokens, sent = message, (message, far_tokens)
    message = near(message, bits=1)
    (near_state,) = call(
        cross_kernel, [((2 * DH, width), BF16)], near_state, far_state, cost=5 * 10**9
    )
    near_state = near(near_state, bits=1)
    (slab_kv,) = call(total_kernel, [((DH, width), BF16)], own_state, far_state, near_state)
    (far_tokens,) = call(pair_kernel, [((4 * rows, width), BF16)], message, far_tokens)
    cot_yc = near(after(cot_y, far_tokens), bits=1)
    far_tokens = near(far_tokens, bits=2)
    before, _ = doubling(slab_kv, 22 * 10**8)
    weights = (columns, *w_far)
    dnormed, cots = call(
        functools.partial(dnormed_kernel, dp, (0, 1, 2)),
        [((3, rows, width), F32), ((3, rows, outputs), BF16)], cot, message, cot_y, *weights,
    )
    dnormed_b, cot_b = call(
        functools.partial(dnormed_kernel, dp, (3,)),
        [((1, rows, width), F32), ((1, rows, outputs), BF16)], cot_yc, *weights,
    )
    (base,) = call(base_kernel, [((DH, width), F32)], *before, cost=10**9)
    w_all = [x for w in w_far for x in (w, near(after(w, dnormed), bits=1))]
    normed, back, back_far, u, slab_u = call(
        middle_kernel,
        [((SLAB, rows, width), BF16)] + [((2 * rows + 2 * DH, width), BF16)] * 2
        + [((SLAB, DH, width), F32), ((DH, width), BF16)],
        own_tokens, message, far_tokens, own_state, far_state, near_state, base, dnormed, dnormed_b,
        cost=10**10, scratch=[pltpu.VMEM((SLAB, DH, width), F32)],
    )
    tuned = dp == 2 and slabs == 4 and outputs // (dp * seq) % 8 == 0
    piece = outputs // (dp * slabs)
    if tuned:
        keep, send = call(
            functools.partial(product_kernel, slabs),
            [((outputs // dp, width), F32), ((outputs // dp, width), BF16)], cots, cot_b, normed,
        )
        got = flip(send, "dp", dp, 1)
    back_far = near(back_far, bits=2)
    behind, last_u = doubling(slab_u, 15 * 10**8)
    if tuned:
        keep, send = call(
            split_kernel, [((2 * piece, width), F32), ((2 * piece, width), BF16)], keep, got, wait=w_all[1::2]
        )
        got = near(send, bits=SLAB)
    (send,) = call(relay_kernel, [((2 * rows + 2 * DH, width), BF16)], back, back_far)
    back_core = near(send, bits=1)
    later, later_far = call(
        later_kernel, [((2 * DH, width), BF16)] * 2, *behind, u, cost=2 * 10**9,
        scratch=[pltpu.VMEM((SLAB, DH, width), F32)],
    )
    later_far = near(later_far, bits=2)
    if tuned:
        keep, send = call(
            split_again_kernel, [((piece, width), F32), ((piece, width), BF16)], keep, got, cost=2 * 10**9
        )
        got = near(send, bits=2 * SLAB)
    gq, gk_part, gv_part, own_normed = call(
        late_kernel,
        [((rows, features), BF16), ((SLAB, rows, width), F32), ((SLAB, rows, width), F32), ((rows, features), BF16)],
        back, back_far, back_core, q, k, v, attend, own_tokens, *sent,
    )
    (send,) = call(relay_kernel, [((2 * DH, width), BF16)], later, later_far)
    later_core = near(send, bits=1)
    if tuned:
        keep, share = call(
            share_kernel, [((piece // 2, width), BF16)] * 2, keep, got, cost=3 * 10**9,
            scratch=[pltpu.VMEM((piece, width), F32)],
        )
        got = near(share, bits=2)
    (output,) = call(
        output_kernel, [((rows, outputs), BF16)], own_normed, out_weight, *w_all, end=True,
    )
    if tuned:
        keep, share = call(
            pass_kernel, [((piece // 2, width), BF16)] * 2, keep, got,
            wait=[pltpu.with_memory_space_constraint(x, pltpu.HBM) for x in (output,)],
        )
        got = near(share, bits=1)
    gk, gv = call(
        last_kernel, [((rows, features), BF16)] * 2,
        later, later_far, later_core, k, v, gk_part, gv_part, end=True,
    )
    if tuned:
        (grad_weight,) = call(
            functools.partial(finish_kernel, factor),
            [((piece // SLAB, features), F32)], keep, got, end=True,
            wait=[pltpu.with_memory_space_constraint(gk, pltpu.HBM)],
        )
    else:
        partial = dot(cot, own_normed, 0, 0) * factor
        grad_weight = lax.psum_scatter(partial, ("dp", "seq"), scatter_dimension=0, tiled=True)
    shape = queries.shape
    return (
        output.reshape(cotangent.shape), gq.reshape(shape), gk.reshape(shape), gv.reshape(shape),
        grad_weight,
    )


def solution(mesh):
    dp, seq = mesh.shape["dp"], mesh.shape["seq"]
    return jax.shard_map(
        functools.partial(local, dp=dp, seq=seq),
        mesh=mesh,
        in_specs=(P("dp", "seq", None),) * 4 + (P("dp", None),),
        out_specs=(P("dp", "seq", None),) * 4 + (P(("dp", "seq"), None),),
        check_vma=False,
    )
```

```python
import functools
import math

import jax
import jax.numpy as jnp
from jax import lax
from jax.experimental import pallas as pl
from jax.experimental.pallas import tpu as pltpu
from jax.sharding import PartitionSpec as P

DH = 128
SLAB = 4
EPSILON = 1e-05
BF16 = jnp.bfloat16
F32 = jnp.float32


def dot(left, right, left_dim, right_dim):
    return lax.dot_general(
        left, right, (((left_dim,), (right_dim,)), ((), ())), preferred_element_type=F32
    )


class Chain:
    def __init__(self):
        self.last = None

    def __call__(self, body, outs, *args, scratch=(), far=False, wait=(), cost=1, end=False):
        count = len(args)
        if far:
            args = [pltpu.with_memory_space_constraint(x, pltpu.HBM) for x in args]
        specs = [pl.BlockSpec(memory_space=pl.ANY) if far else pl.BlockSpec()] * count
        inner = body
        if self.last is not None:
            extra = (self.last, *wait)
            args = (*args, *extra)
            specs = [*specs, *[pl.BlockSpec(memory_space=pl.ANY)] * len(extra)]

            def inner(*refs):
                body(*refs[:count], *refs[count + len(extra) :])

        found = pl.pallas_call(
            inner,
            out_shape=[jax.ShapeDtypeStruct(s, d) for s, d in outs],
            in_specs=specs,
            scratch_shapes=list(scratch),
            cost_estimate=pl.CostEstimate(flops=cost, bytes_accessed=1, transcendentals=0),
            compiler_params=pltpu.CompilerParams(vmem_limit_bytes=32 * 2**20),
        )(*args)
        if not end:
            self.last = min(reversed(found), key=lambda x: x.size)
        return found


def after(x, *others):
    return lax.optimization_barrier((x, *others))[0]


def flip(x, axis, count, bits):
    return lax.ppermute(x, axis, [(i, i ^ bits) for i in range(count)])


def head(h):
    return slice(h * DH, (h + 1) * DH)


def part(i, size):
    return slice(i * size, (i + 1) * size)


def cut(start, size):
    return pl.ds(pl.multiple_of(start * size, size), size)


def member(r):
    return jnp.bitwise_xor(lax.rem(lax.axis_index("seq"), SLAB), r)


def causal(block):
    rows = lax.broadcasted_iota(jnp.int32, (block, block), 0)
    return lax.broadcasted_iota(jnp.int32, (block, block), 1) <= rows


def fetch(pairs, sems):
    copies = [pltpu.make_async_copy(a, b, sems.at[i]) for i, (a, b) in enumerate(pairs)]
    for copy in copies:
        copy.start()
    return copies


def front_kernel(k_hbm, v_hbm, w_hbm, own_ref, near_ref, far_ref, columns_ref, k_ref, v_ref, w_ref, sems):
    copies = fetch([(k_hbm, k_ref), (v_hbm, v_ref), (w_hbm, w_ref)], sems)
    width = k_ref.shape[1] // SLAB
    copies[0].wait()
    copies[1].wait()
    places = (own_ref, near_ref, far_ref.at[part(0, DH)], far_ref.at[part(1, DH)])
    for r, out in enumerate(places):
        k, v = k_ref[:, cut(member(r), width)], v_ref[:, cut(member(r), width)]
        for h in range(width // DH):
            out[:, head(h)] = dot(k[:, head(h)], v[:, head(h)], 0, 0).astype(out.dtype)
    copies[2].wait()
    for i in range(2):
        columns_ref[i] = w_ref[:, cut(member(2 * i), width)]


def pack_kernel(q_ref, k_ref, v_ref, c_ref, attend_ref, own_ref, message_ref, far_ref):
    block = q_ref.shape[0]
    width = q_ref.shape[1] // SLAB
    mask = causal(block)
    places = (own_ref, message_ref.at[: 2 * block], far_ref, message_ref.at[2 * block : 4 * block])
    for r, out in enumerate(places):
        q, k, v = (ref[:, cut(member(r), width)] for ref in (q_ref, k_ref, v_ref))
        out[:block, :] = q
        for h in range(width // DH):
            attend = jnp.where(mask, dot(q[:, head(h)], k[:, head(h)], 1, 1), 0.0).astype(BF16)
            attend_ref[r, h] = attend
            out[block:, head(h)] = dot(attend, v[:, head(h)], 1, 0).astype(BF16)
    for i in range(c_ref.shape[1] // width):
        message_ref[part(4 + i, block), :] = c_ref[:, part(i, width)]


def cross_kernel(near_ref, got_ref, out_ref):
    out_ref[part(0, DH), :] = near_ref[...]
    out_ref[part(1, DH), :] = got_ref[part(1, DH), :]


def total_kernel(own_ref, far_ref, near_ref, out_ref):
    total = own_ref[...] + far_ref[part(0, DH), :].astype(F32)
    total = total + near_ref[part(0, DH), :].astype(F32) + near_ref[part(1, DH), :].astype(F32)
    out_ref[...] = total.astype(BF16)


def pair_kernel(message_ref, far_ref, out_ref):
    size = far_ref.shape[0]
    out_ref[:size, :] = far_ref[...]
    out_ref[size:, :] = message_ref[part(1, size), :]


def add_kernel(own_ref, got_ref, out_ref):
    out_ref[...] = (own_ref[...].astype(F32) + got_ref[...].astype(F32)).astype(out_ref.dtype)


def dnormed_kernel(groups, members, *refs):
    cots, weights = refs[: len(members)], refs[len(members) : len(members) + groups]
    dnormed_ref, cot_ref = refs[len(members) + groups :]
    _, block, outputs = cot_ref.shape
    width = dnormed_ref.shape[2]
    rows = weights[0].shape[1]
    me = lax.axis_index("dp")
    for i, (r, ref) in enumerate(zip(members, cots)):
        if r == 1:
            for p in range(outputs // width):
                cot_ref[i, :, part(p, width)] = ref[part(4 + p, block), :]
        else:
            cot_ref[i] = ref[...]
        total = dot(cot_ref[i, :, cut(me, rows)], weights[0][0], 1, 0)
        for j in range(1, groups):
            total = total + dot(cot_ref[i, :, cut(jnp.bitwise_xor(me, j), rows)], weights[j][0], 1, 0)
        dnormed_ref[i] = total


def base_kernel(*refs):
    refs[-1][...] = from_slabs(False, refs[:-1])


def from_slabs(backward, refs):
    slab = lax.div(lax.axis_index("seq"), SLAB)
    total = jnp.zeros(refs[0].shape, F32)
    for i, ref in enumerate(refs):
        bit = lax.rem(lax.div(slab, 1 << i), 2)
        total = total + jnp.where(bit == (0 if backward else 1), ref[...].astype(F32), 0.0)
    return total


def middle_kernel(*refs):
    own_ref, message_ref, token_far, own_state, far_state, near_state, base_ref, dnormed_a, dnormed_b = refs[:9]
    normed_ref, back_near, back_far, u_ref, slab_ref, running = refs[9:]
    _, block, width = normed_ref.shape
    heads = width // DH
    size = 2 * block
    tokens = (own_ref, message_ref.at[:size], token_far.at[:size], token_far.at[size:])
    running[member(0)] = own_state[...]
    running[member(1)] = near_state[part(0, DH), :].astype(F32)
    running[member(2)] = far_state[part(0, DH), :].astype(F32)
    running[member(3)] = near_state[part(1, DH), :].astype(F32)
    total = base_ref[...]
    for p in range(SLAB):
        total, running[p] = total + running[p], total
    sums = [jnp.zeros((DH, DH), F32)] * heads
    for r in range(SLAB):
        out = (back_near, back_far)[r // 2].at[part(r % 2, block + DH)]
        prior = running[member(r)].astype(BF16)
        out[block:, :] = prior
        for h in range(heads):
            q = tokens[r][:block, head(h)]
            mixed = tokens[r][block:, head(h)].astype(F32) + dot(q, prior[:, head(h)], 1, 0)
            scale = lax.rsqrt(jnp.mean(mixed * mixed, axis=-1, keepdims=True) + EPSILON)
            normed = mixed * scale
            normed_ref[r, :, head(h)] = normed.astype(BF16)
            dnormed = dnormed_a[r, :, head(h)] if r < 3 else dnormed_b[0, :, head(h)]
            along = jnp.mean(dnormed * normed, axis=-1, keepdims=True)
            dmixed = ((dnormed - normed * along) * scale).astype(BF16)
            out[:block, head(h)] = dmixed
            u = dot(q, dmixed, 0, 0)
            u_ref[r, :, head(h)] = u
            sums[h] = sums[h] + u
    for h in range(heads):
        slab_ref[:, head(h)] = sums[h].astype(BF16)


def later_kernel(*refs):
    *behind, u_ref, near_ref, far_ref, running = refs
    for r in range(SLAB):
        running[member(r)] = u_ref[r]
    total = from_slabs(True, behind)
    for p in reversed(range(SLAB)):
        total, running[p] = total + running[p], total
    for r in range(SLAB):
        (near_ref, far_ref)[r // 2][part(r % 2, DH), :] = running[member(r)].astype(BF16)


def relay_kernel(near_ref, far_ref, out_ref):
    size = near_ref.shape[0] // 2
    out_ref[:size, :] = near_ref[size:, :]
    out_ref[size:, :] = far_ref[size:, :]


def arrived(near_ref, far_ref, core_ref):
    size = near_ref.shape[0] // 2
    first, second = slice(0, size), slice(size, 2 * size)
    return near_ref.at[first], core_ref.at[first], far_ref.at[first], core_ref.at[second]


def late_kernel(*refs):
    backs, (q_ref, k_ref, v_ref, attend_ref, own_ref, message_ref, far_ref) = arrived(*refs[:3]), refs[3:10]
    gq_ref, gk_ref, gv_ref, normed_ref = refs[10:]
    block, width = q_ref.shape[0], refs[0].shape[1]
    mask = causal(block)
    withins = (own_ref.at[part(1, block)], message_ref.at[part(1, block)],
               far_ref.at[part(1, block)], message_ref.at[part(3, block)])
    for r in range(SLAB):
        at = cut(member(r), width)
        q, k, v = q_ref[:, at], k_ref[:, at], v_ref[:, at]
        normeds, gqs, gks, gvs = [], [], [], []
        for h in range(width // DH):
            dmixed, prior = backs[r][:block, head(h)], backs[r][block:, head(h)]
            mixed = withins[r][:, head(h)].astype(F32) + dot(q[:, head(h)], prior, 1, 0)
            scale = lax.rsqrt(jnp.mean(mixed * mixed, axis=-1, keepdims=True) + EPSILON)
            normeds.append(mixed * scale)
            back = jnp.where(mask, dot(dmixed, v[:, head(h)], 1, 1), 0.0).astype(BF16)
            gqs.append(dot(back, k[:, head(h)], 1, 0) + dot(dmixed, prior, 1, 1))
            gks.append(dot(back, q[:, head(h)], 0, 0))
            gvs.append(dot(attend_ref[r, h], dmixed, 0, 0))
        normed_ref[:, at] = jnp.concatenate(normeds, axis=1).astype(BF16)
        gq_ref[:, at] = jnp.concatenate(gqs, axis=1).astype(BF16)
        gk_ref[r] = jnp.concatenate(gks, axis=1)
        gv_ref[r] = jnp.concatenate(gvs, axis=1)


def output_kernel(normed_ref, weight_ref, *refs):
    *far, out_ref = refs
    width = normed_ref.shape[1] // SLAB
    rows = weight_ref.shape[0]
    me = lax.axis_index("dp")
    out_ref[:, cut(me, rows)] = dot(normed_ref[...], weight_ref[...], 1, 1).astype(BF16)
    for j in range(1, len(far) // 2 + 1):
        total = jnp.zeros((normed_ref.shape[0], rows), F32)
        for r in range(SLAB):
            normed = normed_ref[:, cut(member(r), width)]
            total = total + dot(normed, far[2 * (j - 1) + r % 2][r // 2], 1, 1)
        out_ref[:, cut(jnp.bitwise_xor(me, j), rows)] = total.astype(BF16)


def last_kernel(near_ref, far_ref, core_ref, k_ref, v_ref, gk_part, gv_part, gk_ref, gv_ref):
    laters = arrived(near_ref, far_ref, core_ref)
    width = near_ref.shape[1]
    for r in range(SLAB):
        at = cut(member(r), width)
        k, v = k_ref[:, at], v_ref[:, at]
        gks, gvs = [], []
        for h in range(width // DH):
            later = laters[r][:, head(h)]
            gks.append(gk_part[r, :, head(h)] + dot(v[:, head(h)], later, 1, 1))
            gvs.append(gv_part[r, :, head(h)] + dot(k[:, head(h)], later, 1, 0))
        gk_ref[:, at] = jnp.concatenate(gks, axis=1).astype(BF16)
        gv_ref[:, at] = jnp.concatenate(gvs, axis=1).astype(BF16)


def product_kernel(slabs, cot_a, cot_b, normed_ref, keep_a, send_a, keep_b, send_b):
    me = lax.axis_index("dp")
    slab = lax.div(lax.axis_index("seq"), SLAB)
    rows, width = keep_a.shape[0] // 4, keep_a.shape[1]
    for j in range(2):
        for l in range(2):
            for h in range(2):
                at = jnp.bitwise_xor(me, j) * slabs + jnp.bitwise_xor(slab, l + 2 * h)
                total = dot(cot_b[0, :, cut(at, rows)], normed_ref[3], 0, 0)
                for r in range(3):
                    total = total + dot(cot_a[r, :, cut(at, rows)], normed_ref[r], 0, 0)
                out = (keep_a, send_a)[j]
                out[part(2 * l + h, rows), :] = total[:, :width].astype(out.dtype)
                out = (keep_b, send_b)[l]
                out[part(2 * j + h, rows), :] = total[:, width:].astype(out.dtype)


def split_kernel(own_a, got_a, own_b, got_b, keep_a, send_a, keep_b, send_b):
    size = keep_a.shape[0]
    for own, got, keep, send in ((own_a, got_a, keep_a, send_a), (own_b, got_b, keep_b, send_b)):
        keep[...] = own[:size, :] + got[:size, :].astype(F32)
        send[...] = (own[size:, :] + got[size:, :].astype(F32)).astype(BF16)


def split_again_kernel(own_a, got_a, own_b, got_b, keep_ref, send_ref):
    rows, width = keep_ref.shape[0], own_a.shape[1]
    for i, (own, got) in enumerate(((own_a, got_a), (own_b, got_b))):
        total = own[...] + got[...].astype(F32)
        keep_ref[:, part(i, width)] = total[:rows, :]
        send_ref[:, part(i, width)] = total[rows:, :].astype(BF16)


def share_kernel(own_ref, got_ref, keep_ref, send_ref, total_ref):
    total_ref[...] = own_ref[...] + got_ref[...].astype(F32)
    rows = keep_ref.shape[0] // 2
    for i, r in enumerate((0, 1)):
        keep_ref[part(i, rows), :] = total_ref[cut(member(r), rows), :].astype(BF16)
    for i, r in enumerate((2, 3)):
        send_ref[part(i, rows), :] = total_ref[cut(member(r), rows), :].astype(BF16)


def pass_kernel(own_ref, got_ref, keep_ref, send_ref):
    rows = own_ref.shape[0] // 2
    for i, ref in enumerate((own_ref, got_ref)):
        keep_ref[part(i, rows), :] = ref[:rows, :]
        send_ref[part(i, rows), :] = ref[rows:, :]


def finish_kernel(factor, keep_ref, got_ref, out_ref):
    rows, width = out_ref.shape[0], keep_ref.shape[1]
    for i, ref in enumerate((keep_ref, got_ref)):
        for j in range(2):
            out_ref[:, cut(member(i + 2 * j), width)] = ref[part(j, rows), :].astype(F32) * factor


def local(queries, keys, values, cotangent, out_weight, *, dp, seq):
    call = Chain()
    local_seqs, block, features = queries.shape
    outputs = cotangent.shape[2]
    rows = local_seqs * block
    slabs = seq // SLAB
    width = features // SLAB
    heads = width // DH
    q, k, v = (x.reshape(rows, features) for x in (queries, keys, values))
    cot = cotangent.reshape(rows, outputs)
    factor = 1.0 / math.sqrt(rows * dp * seq)
    near = functools.partial(flip, axis="seq", count=seq)

    def doubling(total, cost=1):
        found = []
        bits = SLAB
        while bits < seq:
            if found:
                (total,) = call(add_kernel, [(total.shape, BF16)], total, found[-1], cost=cost)
            found.append(near(total, bits=bits))
            bits *= 2
        return found, total

    def scratch(*arrays):
        return [pltpu.VMEM(x.shape, BF16) for x in arrays] + [pltpu.SemaphoreType.DMA((len(arrays),))]

    own_state, near_state, far_state, columns = call(
        front_kernel,
        [((DH, width), F32), ((DH, width), BF16), ((2 * DH, width), BF16),
         ((2, out_weight.shape[0], width), BF16)],
        k, v, out_weight, far=True, scratch=scratch(k, v, out_weight),
    )
    far_state = near(far_state, bits=2)
    w_far = [flip(columns, "dp", dp, j) for j in range(1, dp)]
    attend, own_tokens, message, far_tokens = call(
        pack_kernel,
        [((SLAB, heads, rows, rows), BF16), ((2 * rows, width), BF16),
         (((4 + outputs // width) * rows, width), BF16), ((2 * rows, width), BF16)],
        q, k, v, cot,
    )
    cot_y = near(cot, bits=2)
    near_tokens, sent = message, (message, far_tokens)
    message = near(message, bits=1)
    (near_state,) = call(
        cross_kernel, [((2 * DH, width), BF16)], near_state, far_state, cost=5 * 10**9
    )
    near_state = near(near_state, bits=1)
    (slab_kv,) = call(total_kernel, [((DH, width), BF16)], own_state, far_state, near_state)
    (far_tokens,) = call(pair_kernel, [((4 * rows, width), BF16)], message, far_tokens)
    cot_yc = near(after(cot_y, far_tokens), bits=1)
    far_tokens = near(far_tokens, bits=2)
    before, _ = doubling(slab_kv, 22 * 10**8)
    weights = (columns, *w_far)
    dnormed, cots = call(
        functools.partial(dnormed_kernel, dp, (0, 1, 2)),
        [((3, rows, width), F32), ((3, rows, outputs), BF16)], cot, message, cot_y, *weights,
    )
    dnormed_b, cot_b = call(
        functools.partial(dnormed_kernel, dp, (3,)),
        [((1, rows, width), F32), ((1, rows, outputs), BF16)], cot_yc, *weights,
    )
    (base,) = call(base_kernel, [((DH, width), F32)], *before, cost=10**9)
    w_all = [x for w in w_far for x in (w, near(after(w, dnormed), bits=1))]
    normed, back, back_far, u, slab_u = call(
        middle_kernel,
        [((SLAB, rows, width), BF16)] + [((2 * rows + 2 * DH, width), BF16)] * 2
        + [((SLAB, DH, width), F32), ((DH, width), BF16)],
        own_tokens, message, far_tokens, own_state, far_state, near_state, base, dnormed, dnormed_b,
        cost=10**10, scratch=[pltpu.VMEM((SLAB, DH, width), F32)],
    )
    tuned = dp == 2 and slabs == 4 and outputs // (dp * seq) % 8 == 0
    piece = outputs // (dp * slabs)
    if tuned:
        keep_a, send_a, keep_b, send_b = call(
            functools.partial(product_kernel, slabs),
            [((4 * piece, width // 2), F32), ((4 * piece, width // 2), BF16)] * 2, cots, cot_b, normed,
        )
        got_a, got_b = flip(send_a, "dp", dp, 1), near(send_b, bits=SLAB)
    back_far = near(back_far, bits=2)
    if tuned:
        keep_a, send_a, keep_b, send_b = call(
            split_kernel, [((2 * piece, width // 2), F32), ((2 * piece, width // 2), BF16)] * 2,
            keep_a, got_a, keep_b, got_b, wait=w_all[1::2],
        )
        got_a, got_b = near(send_a, bits=SLAB), flip(send_b, "dp", dp, 1)
    behind, last_u = doubling(slab_u)
    (send,) = call(relay_kernel, [((2 * rows + 2 * DH, width), BF16)], back, back_far)
    back_core = near(send, bits=1)
    if tuned:
        keep, send = call(
            split_again_kernel, [((piece, width), F32), ((piece, width), BF16)],
            keep_a, got_a, keep_b, got_b, cost=3 * 10**9,
        )
        got = near(send, bits=2 * SLAB)
    later, later_far = call(
        later_kernel, [((2 * DH, width), BF16)] * 2, *behind, u,
        scratch=[pltpu.VMEM((SLAB, DH, width), F32)],
    )
    later_far = near(later_far, bits=2)
    gq, gk_part, gv_part, own_normed = call(
        late_kernel,
        [((rows, features), BF16), ((SLAB, rows, width), F32), ((SLAB, rows, width), F32), ((rows, features), BF16)],
        back, back_far, back_core, q, k, v, attend, own_tokens, *sent,
    )
    if tuned:
        keep, share = call(
            share_kernel, [((piece // 2, width), BF16)] * 2, keep, got, cost=3 * 10**9,
            scratch=[pltpu.VMEM((piece, width), F32)],
        )
        got = near(share, bits=2)
    (send,) = call(relay_kernel, [((2 * DH, width), BF16)], later, later_far)
    later_core = near(send, bits=1)
    (output,) = call(
        output_kernel, [((rows, outputs), BF16)], own_normed, out_weight, *w_all, end=True,
    )
    if tuned:
        keep, share = call(
            pass_kernel, [((piece // 2, width), BF16)] * 2, keep, got, cost=3 * 10**9,
            wait=[pltpu.with_memory_space_constraint(x, pltpu.HBM) for x in (output,)],
        )
        got = near(share, bits=1)
    gk, gv = call(
        last_kernel, [((rows, features), BF16)] * 2,
        later, later_far, later_core, k, v, gk_part, gv_part, end=True,
    )
    if tuned:
        (grad_weight,) = call(
            functools.partial(finish_kernel, factor),
            [((piece // SLAB, features), F32)], keep, got, end=True,
            wait=[pltpu.with_memory_space_constraint(gk, pltpu.HBM)],
        )
    else:
        partial = dot(cot, own_normed, 0, 0) * factor
        grad_weight = lax.psum_scatter(partial, ("dp", "seq"), scatter_dimension=0, tiled=True)
    shape = queries.shape
    return (
        output.reshape(cotangent.shape), gq.reshape(shape), gk.reshape(shape), gv.reshape(shape),
        grad_weight,
    )


def solution(mesh):
    dp, seq = mesh.shape["dp"], mesh.shape["seq"]
    return jax.shard_map(
        functools.partial(local, dp=dp, seq=seq),
        mesh=mesh,
        in_specs=(P("dp", "seq", None),) * 4 + (P("dp", None),),
        out_specs=(P("dp", "seq", None),) * 4 + (P(("dp", "seq"), None),),
        check_vma=False,
    )
```

```python
import functools
import math

import jax
import jax.numpy as jnp
from jax import lax
from jax.experimental import pallas as pl
from jax.experimental.pallas import tpu as pltpu
from jax.sharding import PartitionSpec as P

DH = 128
SLAB = 4
EPSILON = 1e-05
BF16 = jnp.bfloat16
F32 = jnp.float32


def dot(left, right, left_dim, right_dim):
    return lax.dot_general(
        left, right, (((left_dim,), (right_dim,)), ((), ())), preferred_element_type=F32
    )


class Chain:
    def __init__(self):
        self.last = None

    def __call__(self, body, outs, *args, scratch=(), far=False, wait=(), cost=1, end=False):
        count = len(args)
        if far:
            args = [pltpu.with_memory_space_constraint(x, pltpu.HBM) for x in args]
        specs = [pl.BlockSpec(memory_space=pl.ANY) if far else pl.BlockSpec()] * count
        inner = body
        if self.last is not None:
            extra = (self.last, *wait)
            args = (*args, *extra)
            specs = [*specs, *[pl.BlockSpec(memory_space=pl.ANY)] * len(extra)]

            def inner(*refs):
                body(*refs[:count], *refs[count + len(extra) :])

        found = pl.pallas_call(
            inner,
            out_shape=[jax.ShapeDtypeStruct(s, d) for s, d in outs],
            in_specs=specs,
            scratch_shapes=list(scratch),
            cost_estimate=pl.CostEstimate(flops=cost, bytes_accessed=1, transcendentals=0),
            compiler_params=pltpu.CompilerParams(vmem_limit_bytes=32 * 2**20),
        )(*args)
        if not end:
            self.last = min(reversed(found), key=lambda x: x.size)
        return found


def after(x, *others):
    return lax.optimization_barrier((x, *others))[0]


def flip(x, axis, count, bits):
    return lax.ppermute(x, axis, [(i, i ^ bits) for i in range(count)])


def head(h):
    return slice(h * DH, (h + 1) * DH)


def part(i, size):
    return slice(i * size, (i + 1) * size)


def cut(start, size):
    return pl.ds(pl.multiple_of(start * size, size), size)


def member(r):
    return jnp.bitwise_xor(lax.rem(lax.axis_index("seq"), SLAB), r)


def causal(block):
    rows = lax.broadcasted_iota(jnp.int32, (block, block), 0)
    return lax.broadcasted_iota(jnp.int32, (block, block), 1) <= rows


def fetch(pairs, sems):
    copies = [pltpu.make_async_copy(a, b, sems.at[i]) for i, (a, b) in enumerate(pairs)]
    for copy in copies:
        copy.start()
    return copies


def front_kernel(k_hbm, v_hbm, w_hbm, own_ref, near_ref, far_ref, columns_ref, k_ref, v_ref, w_ref, sems):
    copies = fetch([(k_hbm, k_ref), (v_hbm, v_ref), (w_hbm, w_ref)], sems)
    width = k_ref.shape[1] // SLAB
    copies[0].wait()
    copies[1].wait()
    places = (own_ref, near_ref, far_ref.at[part(0, DH)], far_ref.at[part(1, DH)])
    for r, out in enumerate(places):
        k, v = k_ref[:, cut(member(r), width)], v_ref[:, cut(member(r), width)]
        for h in range(width // DH):
            out[:, head(h)] = dot(k[:, head(h)], v[:, head(h)], 0, 0).astype(out.dtype)
    copies[2].wait()
    for i in range(2):
        columns_ref[i] = w_ref[:, cut(member(2 * i), width)]


def pack_kernel(q_ref, k_ref, v_ref, c_ref, attend_ref, own_ref, message_ref, far_ref):
    block = q_ref.shape[0]
    width = q_ref.shape[1] // SLAB
    mask = causal(block)
    places = (own_ref, message_ref.at[: 2 * block], far_ref, message_ref.at[2 * block : 4 * block])
    for r, out in enumerate(places):
        q, k, v = (ref[:, cut(member(r), width)] for ref in (q_ref, k_ref, v_ref))
        out[:block, :] = q
        for h in range(width // DH):
            attend = jnp.where(mask, dot(q[:, head(h)], k[:, head(h)], 1, 1), 0.0).astype(BF16)
            attend_ref[r, h] = attend
            out[block:, head(h)] = dot(attend, v[:, head(h)], 1, 0).astype(BF16)
    for i in range(c_ref.shape[1] // width):
        message_ref[part(4 + i, block), :] = c_ref[:, part(i, width)]


def cross_kernel(near_ref, got_ref, out_ref):
    out_ref[part(0, DH), :] = near_ref[...]
    out_ref[part(1, DH), :] = got_ref[part(1, DH), :]


def total_kernel(own_ref, far_ref, near_ref, out_ref):
    total = own_ref[...] + far_ref[part(0, DH), :].astype(F32)
    total = total + near_ref[part(0, DH), :].astype(F32) + near_ref[part(1, DH), :].astype(F32)
    out_ref[...] = total.astype(BF16)


def pair_kernel(message_ref, far_ref, out_ref):
    size = far_ref.shape[0]
    out_ref[:size, :] = far_ref[...]
    out_ref[size:, :] = message_ref[part(1, size), :]


def add_kernel(own_ref, got_ref, out_ref):
    out_ref[...] = (own_ref[...].astype(F32) + got_ref[...].astype(F32)).astype(out_ref.dtype)


def dnormed_kernel(groups, members, *refs):
    cots, weights = refs[: len(members)], refs[len(members) : len(members) + groups]
    dnormed_ref, cot_ref = refs[len(members) + groups :]
    _, block, outputs = cot_ref.shape
    width = dnormed_ref.shape[2]
    rows = weights[0].shape[1]
    me = lax.axis_index("dp")
    for i, (r, ref) in enumerate(zip(members, cots)):
        if r == 1:
            for p in range(outputs // width):
                cot_ref[i, :, part(p, width)] = ref[part(4 + p, block), :]
        else:
            cot_ref[i] = ref[...]
        total = dot(cot_ref[i, :, cut(me, rows)], weights[0][0], 1, 0)
        for j in range(1, groups):
            total = total + dot(cot_ref[i, :, cut(jnp.bitwise_xor(me, j), rows)], weights[j][0], 1, 0)
        dnormed_ref[i] = total


def base_kernel(*refs):
    refs[-1][...] = from_slabs(False, refs[:-1])


def from_slabs(backward, refs):
    slab = lax.div(lax.axis_index("seq"), SLAB)
    total = jnp.zeros(refs[0].shape, F32)
    for i, ref in enumerate(refs):
        bit = lax.rem(lax.div(slab, 1 << i), 2)
        total = total + jnp.where(bit == (0 if backward else 1), ref[...].astype(F32), 0.0)
    return total


def middle_kernel(*refs):
    own_ref, message_ref, token_far, own_state, far_state, near_state, base_ref, dnormed_a, dnormed_b = refs[:9]
    normed_ref, back_near, back_far, u_ref, slab_ref, running = refs[9:]
    _, block, width = normed_ref.shape
    heads = width // DH
    size = 2 * block
    tokens = (own_ref, message_ref.at[:size], token_far.at[:size], token_far.at[size:])
    running[member(0)] = own_state[...]
    running[member(1)] = near_state[part(0, DH), :].astype(F32)
    running[member(2)] = far_state[part(0, DH), :].astype(F32)
    running[member(3)] = near_state[part(1, DH), :].astype(F32)
    total = base_ref[...]
    for p in range(SLAB):
        total, running[p] = total + running[p], total
    sums = [jnp.zeros((DH, DH), F32)] * heads
    for r in range(SLAB):
        out = (back_near, back_far)[r // 2].at[part(r % 2, block + DH)]
        prior = running[member(r)].astype(BF16)
        out[block:, :] = prior
        for h in range(heads):
            q = tokens[r][:block, head(h)]
            mixed = tokens[r][block:, head(h)].astype(F32) + dot(q, prior[:, head(h)], 1, 0)
            scale = lax.rsqrt(jnp.mean(mixed * mixed, axis=-1, keepdims=True) + EPSILON)
            normed = mixed * scale
            normed_ref[r, :, head(h)] = normed.astype(BF16)
            dnormed = dnormed_a[r, :, head(h)] if r < 3 else dnormed_b[0, :, head(h)]
            along = jnp.mean(dnormed * normed, axis=-1, keepdims=True)
            dmixed = ((dnormed - normed * along) * scale).astype(BF16)
            out[:block, head(h)] = dmixed
            u = dot(q, dmixed, 0, 0)
            u_ref[r, :, head(h)] = u
            sums[h] = sums[h] + u
    for h in range(heads):
        slab_ref[:, head(h)] = sums[h].astype(BF16)


def later_kernel(*refs):
    *behind, u_ref, near_ref, far_ref, running = refs
    for r in range(SLAB):
        running[member(r)] = u_ref[r]
    total = from_slabs(True, behind)
    for p in reversed(range(SLAB)):
        total, running[p] = total + running[p], total
    for r in range(SLAB):
        (near_ref, far_ref)[r // 2][part(r % 2, DH), :] = running[member(r)].astype(BF16)


def relay_kernel(near_ref, far_ref, out_ref):
    size = near_ref.shape[0] // 2
    out_ref[:size, :] = near_ref[size:, :]
    out_ref[size:, :] = far_ref[size:, :]


def arrived(near_ref, far_ref, core_ref):
    size = near_ref.shape[0] // 2
    first, second = slice(0, size), slice(size, 2 * size)
    return near_ref.at[first], core_ref.at[first], far_ref.at[first], core_ref.at[second]


def late_kernel(near_ref, far_ref, core_ref, q_ref, k_ref, v_ref, attend_ref, gq_ref, gk_ref, gv_ref):
    backs = arrived(near_ref, far_ref, core_ref)
    block, width = q_ref.shape[0], near_ref.shape[1]
    mask = causal(block)
    for r in range(SLAB):
        at = cut(member(r), width)
        q, k, v = q_ref[:, at], k_ref[:, at], v_ref[:, at]
        gqs, gks, gvs = [], [], []
        for h in range(width // DH):
            dmixed, prior = backs[r][:block, head(h)], backs[r][block:, head(h)]
            back = jnp.where(mask, dot(dmixed, v[:, head(h)], 1, 1), 0.0).astype(BF16)
            gqs.append(dot(back, k[:, head(h)], 1, 0) + dot(dmixed, prior, 1, 1))
            gks.append(dot(back, q[:, head(h)], 0, 0))
            gvs.append(dot(attend_ref[r, h], dmixed, 0, 0))
        gq_ref[:, at] = jnp.concatenate(gqs, axis=1).astype(BF16)
        gk_ref[r] = jnp.concatenate(gks, axis=1)
        gv_ref[r] = jnp.concatenate(gvs, axis=1)


def output_kernel(near_ref, back_far, core_ref, q_ref, own_ref, message_ref, far_ref, weight_ref, *refs):
    *far, out_ref, normed_ref = refs
    backs = arrived(near_ref, back_far, core_ref)
    block, width = q_ref.shape[0], near_ref.shape[1]
    rows = weight_ref.shape[0]
    me = lax.axis_index("dp")
    withins = (own_ref.at[part(1, block)], message_ref.at[part(1, block)],
               far_ref.at[part(1, block)], message_ref.at[part(3, block)])
    totals = [jnp.zeros((block, rows), F32)] * (len(far) // 2)
    for r in range(SLAB):
        at = cut(member(r), width)
        q = q_ref[:, at]
        normeds = []
        for h in range(width // DH):
            mixed = withins[r][:, head(h)].astype(F32) + dot(q[:, head(h)], backs[r][block:, head(h)], 1, 0)
            scale = lax.rsqrt(jnp.mean(mixed * mixed, axis=-1, keepdims=True) + EPSILON)
            normeds.append(mixed * scale)
        normed = jnp.concatenate(normeds, axis=1).astype(BF16)
        normed_ref[:, at] = normed
        for j in range(len(totals)):
            totals[j] = totals[j] + dot(normed, far[2 * j + r % 2][r // 2], 1, 1)
    out_ref[:, cut(me, rows)] = dot(normed_ref[...], weight_ref[...], 1, 1).astype(BF16)
    for j, total in enumerate(totals, 1):
        out_ref[:, cut(jnp.bitwise_xor(me, j), rows)] = total.astype(BF16)


def last_kernel(near_ref, far_ref, core_ref, k_ref, v_ref, gk_part, gv_part, gk_ref, gv_ref):
    laters = arrived(near_ref, far_ref, core_ref)
    width = near_ref.shape[1]
    for r in range(SLAB):
        at = cut(member(r), width)
        k, v = k_ref[:, at], v_ref[:, at]
        gks, gvs = [], []
        for h in range(width // DH):
            later = laters[r][:, head(h)]
            gks.append(gk_part[r, :, head(h)] + dot(v[:, head(h)], later, 1, 1))
            gvs.append(gv_part[r, :, head(h)] + dot(k[:, head(h)], later, 1, 0))
        gk_ref[:, at] = jnp.concatenate(gks, axis=1).astype(BF16)
        gv_ref[:, at] = jnp.concatenate(gvs, axis=1).astype(BF16)


def product_kernel(slabs, cot_a, cot_b, normed_ref, keep_ref, send_ref):
    me = lax.axis_index("dp")
    slab = lax.div(lax.axis_index("seq"), SLAB)
    rows = keep_ref.shape[0] // slabs
    for j, out in enumerate((send_ref, keep_ref)):
        for d in range(slabs):
            at = jnp.bitwise_xor(me, 1 - j) * slabs + jnp.bitwise_xor(slab, d)
            total = dot(cot_b[0, :, cut(at, rows)], normed_ref[3], 0, 0)
            for r in range(3):
                total = total + dot(cot_a[r, :, cut(at, rows)], normed_ref[r], 0, 0)
            out[part(d, rows), :] = total.astype(out.dtype)


def split_kernel(own_ref, got_ref, keep_ref, send_ref):
    rows = keep_ref.shape[0] // 2
    for i in range(4):
        total = own_ref[part(i, rows), :] + got_ref[part(i, rows), :].astype(F32)
        out = (keep_ref, send_ref)[i % 2]
        out[part(i // 2, rows), :] = total.astype(out.dtype)


def split_again_kernel(own_ref, got_ref, keep_ref, send_ref):
    rows = keep_ref.shape[0]
    for i, out in enumerate((keep_ref, send_ref)):
        total = own_ref[part(i, rows), :] + got_ref[part(i, rows), :].astype(F32)
        out[...] = total.astype(out.dtype)


def share_kernel(own_ref, got_ref, keep_ref, send_ref, total_ref):
    total_ref[...] = own_ref[...] + got_ref[...].astype(F32)
    rows = keep_ref.shape[0] // 2
    for i, r in enumerate((0, 1)):
        keep_ref[part(i, rows), :] = total_ref[cut(member(r), rows), :].astype(BF16)
    for i, r in enumerate((2, 3)):
        send_ref[part(i, rows), :] = total_ref[cut(member(r), rows), :].astype(BF16)


def pass_kernel(own_ref, got_ref, keep_ref, send_ref):
    rows = own_ref.shape[0] // 2
    for i, ref in enumerate((own_ref, got_ref)):
        keep_ref[part(i, rows), :] = ref[:rows, :]
        send_ref[part(i, rows), :] = ref[rows:, :]


def finish_kernel(factor, keep_ref, got_ref, out_ref):
    rows, width = out_ref.shape[0], keep_ref.shape[1]
    for i, ref in enumerate((keep_ref, got_ref)):
        for j in range(2):
            out_ref[:, cut(member(i + 2 * j), width)] = ref[part(j, rows), :].astype(F32) * factor


def local(queries, keys, values, cotangent, out_weight, *, dp, seq):
    call = Chain()
    local_seqs, block, features = queries.shape
    outputs = cotangent.shape[2]
    rows = local_seqs * block
    slabs = seq // SLAB
    width = features // SLAB
    heads = width // DH
    q, k, v = (x.reshape(rows, features) for x in (queries, keys, values))
    cot = cotangent.reshape(rows, outputs)
    factor = 1.0 / math.sqrt(rows * dp * seq)
    near = functools.partial(flip, axis="seq", count=seq)

    def doubling(total, cost=1):
        found = []
        bits = SLAB
        while bits < seq:
            if found:
                (total,) = call(add_kernel, [(total.shape, BF16)], total, found[-1], cost=cost)
            found.append(near(total, bits=bits))
            bits *= 2
        return found, total

    def scratch(*arrays):
        return [pltpu.VMEM(x.shape, BF16) for x in arrays] + [pltpu.SemaphoreType.DMA((len(arrays),))]

    own_state, near_state, far_state, columns = call(
        front_kernel,
        [((DH, width), F32), ((DH, width), BF16), ((2 * DH, width), BF16),
         ((2, out_weight.shape[0], width), BF16)],
        k, v, out_weight, far=True, scratch=scratch(k, v, out_weight),
    )
    far_state = near(far_state, bits=2)
    w_far = [flip(columns, "dp", dp, j) for j in range(1, dp)]
    attend, own_tokens, message, far_tokens = call(
        pack_kernel,
        [((SLAB, heads, rows, rows), BF16), ((2 * rows, width), BF16),
         (((4 + outputs // width) * rows, width), BF16), ((2 * rows, width), BF16)],
        q, k, v, cot,
    )
    cot_y = near(cot, bits=2)
    near_tokens, sent = message, (message, far_tokens)
    message = near(message, bits=1)
    (near_state,) = call(
        cross_kernel, [((2 * DH, width), BF16)], near_state, far_state, cost=5 * 10**9
    )
    near_state = near(near_state, bits=1)
    (slab_kv,) = call(total_kernel, [((DH, width), BF16)], own_state, far_state, near_state)
    (far_tokens,) = call(pair_kernel, [((4 * rows, width), BF16)], message, far_tokens)
    cot_yc = near(after(cot_y, far_tokens), bits=1)
    far_tokens = near(far_tokens, bits=2)
    before, _ = doubling(slab_kv, 22 * 10**8)
    weights = (columns, *w_far)
    dnormed, cots = call(
        functools.partial(dnormed_kernel, dp, (0, 1, 2)),
        [((3, rows, width), F32), ((3, rows, outputs), BF16)], cot, message, cot_y, *weights,
    )
    dnormed_b, cot_b = call(
        functools.partial(dnormed_kernel, dp, (3,)),
        [((1, rows, width), F32), ((1, rows, outputs), BF16)], cot_yc, *weights,
    )
    (base,) = call(base_kernel, [((DH, width), F32)], *before, cost=10**9)
    w_all = [x for w in w_far for x in (w, near(after(w, dnormed), bits=1))]
    normed, back, back_far, u, slab_u = call(
        middle_kernel,
        [((SLAB, rows, width), BF16)] + [((2 * rows + 2 * DH, width), BF16)] * 2
        + [((SLAB, DH, width), F32), ((DH, width), BF16)],
        own_tokens, message, far_tokens, own_state, far_state, near_state, base, dnormed, dnormed_b,
        cost=10**10, scratch=[pltpu.VMEM((SLAB, DH, width), F32)],
    )
    tuned = dp == 2 and slabs == 4 and outputs // (dp * seq) % 8 == 0
    piece = outputs // (dp * slabs)
    if tuned:
        keep, send = call(
            functools.partial(product_kernel, slabs),
            [((outputs // dp, width), F32), ((outputs // dp, width), BF16)], cots, cot_b, normed,
        )
        got = flip(send, "dp", dp, 1)
    back_far = near(back_far, bits=2)
    if tuned:
        keep, send = call(
            split_kernel, [((2 * piece, width), F32), ((2 * piece, width), BF16)], keep, got, wait=w_all[1::2]
        )
        got = near(send, bits=SLAB)
    behind, last_u = doubling(slab_u, 10**9)
    (send,) = call(relay_kernel, [((2 * rows + 2 * DH, width), BF16)], back, back_far)
    back_core = near(send, bits=1)
    if tuned:
        keep, send = call(
            split_again_kernel, [((piece, width), F32), ((piece, width), BF16)], keep, got, cost=3 * 10**9
        )
        got = near(send, bits=2 * SLAB)
    later, later_far = call(
        later_kernel, [((2 * DH, width), BF16)] * 2, *behind, u,
        scratch=[pltpu.VMEM((SLAB, DH, width), F32)],
    )
    later_far = near(later_far, bits=2)
    gq, gk_part, gv_part = call(
        late_kernel,
        [((rows, features), BF16), ((SLAB, rows, width), F32), ((SLAB, rows, width), F32)],
        back, back_far, back_core, q, k, v, attend,
    )
    if tuned:
        keep, share = call(
            share_kernel, [((piece // 2, width), BF16)] * 2, keep, got, cost=3 * 10**9,
            scratch=[pltpu.VMEM((piece, width), F32)],
        )
        got = near(share, bits=2)
    (send,) = call(relay_kernel, [((2 * DH, width), BF16)], later, later_far)
    later_core = near(send, bits=1)
    output, own_normed = call(
        output_kernel, [((rows, outputs), BF16), ((rows, features), BF16)],
        back, back_far, back_core, q, own_tokens, *sent, out_weight, *w_all, end=True,
    )
    if tuned:
        keep, share = call(
            pass_kernel, [((piece // 2, width), BF16)] * 2, keep, got, cost=3 * 10**9,
            wait=[pltpu.with_memory_space_constraint(x, pltpu.HBM) for x in (output,)],
        )
        got = near(share, bits=1)
    gk, gv = call(
        last_kernel, [((rows, features), BF16)] * 2,
        later, later_far, later_core, k, v, gk_part, gv_part, end=True,
    )
    if tuned:
        (grad_weight,) = call(
            functools.partial(finish_kernel, factor),
            [((piece // SLAB, features), F32)], keep, got, end=True,
            wait=[pltpu.with_memory_space_constraint(gk, pltpu.HBM)],
        )
    else:
        partial = dot(cot, own_normed, 0, 0) * factor
        grad_weight = lax.psum_scatter(partial, ("dp", "seq"), scatter_dimension=0, tiled=True)
    shape = queries.shape
    return (
        output.reshape(cotangent.shape), gq.reshape(shape), gk.reshape(shape), gv.reshape(shape),
        grad_weight,
    )


def solution(mesh):
    dp, seq = mesh.shape["dp"], mesh.shape["seq"]
    return jax.shard_map(
        functools.partial(local, dp=dp, seq=seq),
        mesh=mesh,
        in_specs=(P("dp", "seq", None),) * 4 + (P("dp", None),),
        out_specs=(P("dp", "seq", None),) * 4 + (P(("dp", "seq"), None),),
        check_vma=False,
    )
```

```python
import functools
import math

import jax
import jax.numpy as jnp
from jax import lax
from jax.experimental import pallas as pl
from jax.experimental.pallas import tpu as pltpu
from jax.sharding import PartitionSpec as P

DH = 128
SLAB = 4
EPSILON = 1e-05
BF16 = jnp.bfloat16
F32 = jnp.float32


def dot(left, right, left_dim, right_dim):
    return lax.dot_general(
        left, right, (((left_dim,), (right_dim,)), ((), ())), preferred_element_type=F32
    )


class Chain:
    def __init__(self):
        self.last = None

    def __call__(self, body, outs, *args, scratch=(), far=False, wait=(), cost=1, end=False):
        count = len(args)
        if far:
            args = [pltpu.with_memory_space_constraint(x, pltpu.HBM) for x in args]
        specs = [pl.BlockSpec(memory_space=pl.ANY) if far else pl.BlockSpec()] * count
        inner = body
        if self.last is not None:
            extra = (self.last, *wait)
            args = (*args, *extra)
            specs = [*specs, *[pl.BlockSpec(memory_space=pl.ANY)] * len(extra)]

            def inner(*refs):
                body(*refs[:count], *refs[count + len(extra) :])

        found = pl.pallas_call(
            inner,
            out_shape=[jax.ShapeDtypeStruct(s, d) for s, d in outs],
            in_specs=specs,
            scratch_shapes=list(scratch),
            cost_estimate=pl.CostEstimate(flops=cost, bytes_accessed=1, transcendentals=0),
            compiler_params=pltpu.CompilerParams(vmem_limit_bytes=32 * 2**20),
        )(*args)
        if not end:
            self.last = min(reversed(found), key=lambda x: x.size)
        return found


def after(x, *others):
    return lax.optimization_barrier((x, *others))[0]


def flip(x, axis, count, bits):
    return lax.ppermute(x, axis, [(i, i ^ bits) for i in range(count)])


def head(h):
    return slice(h * DH, (h + 1) * DH)


def part(i, size):
    return slice(i * size, (i + 1) * size)


def cut(start, size):
    return pl.ds(pl.multiple_of(start * size, size), size)


def member(r):
    return jnp.bitwise_xor(lax.rem(lax.axis_index("seq"), SLAB), r)


def causal(block):
    rows = lax.broadcasted_iota(jnp.int32, (block, block), 0)
    return lax.broadcasted_iota(jnp.int32, (block, block), 1) <= rows


def fetch(pairs, sems):
    copies = [pltpu.make_async_copy(a, b, sems.at[i]) for i, (a, b) in enumerate(pairs)]
    for copy in copies:
        copy.start()
    return copies


def front_kernel(k_hbm, v_hbm, w_hbm, own_ref, near_ref, far_ref, columns_ref, k_ref, v_ref, w_ref, sems):
    copies = fetch([(k_hbm, k_ref), (v_hbm, v_ref), (w_hbm, w_ref)], sems)
    width = k_ref.shape[1] // SLAB
    copies[0].wait()
    copies[1].wait()
    places = (own_ref, near_ref, far_ref.at[part(0, DH)], far_ref.at[part(1, DH)])
    for r, out in enumerate(places):
        k, v = k_ref[:, cut(member(r), width)], v_ref[:, cut(member(r), width)]
        for h in range(width // DH):
            out[:, head(h)] = dot(k[:, head(h)], v[:, head(h)], 0, 0).astype(out.dtype)
    copies[2].wait()
    for i in range(2):
        columns_ref[i] = w_ref[:, cut(member(2 * i), width)]


def pack_kernel(q_ref, k_ref, v_ref, c_ref, attend_ref, own_ref, message_ref, far_ref):
    block = q_ref.shape[0]
    width = q_ref.shape[1] // SLAB
    mask = causal(block)
    places = (own_ref, message_ref.at[: 2 * block], far_ref, message_ref.at[2 * block : 4 * block])
    for r, out in enumerate(places):
        q, k, v = (ref[:, cut(member(r), width)] for ref in (q_ref, k_ref, v_ref))
        out[:block, :] = q
        for h in range(width // DH):
            attend = jnp.where(mask, dot(q[:, head(h)], k[:, head(h)], 1, 1), 0.0).astype(BF16)
            attend_ref[r, h] = attend
            out[block:, head(h)] = dot(attend, v[:, head(h)], 1, 0).astype(BF16)
    for i in range(c_ref.shape[1] // width):
        message_ref[part(4 + i, block), :] = c_ref[:, part(i, width)]


def cross_kernel(near_ref, got_ref, out_ref):
    out_ref[part(0, DH), :] = near_ref[...]
    out_ref[part(1, DH), :] = got_ref[part(1, DH), :]


def total_kernel(own_ref, far_ref, near_ref, out_ref):
    total = own_ref[...] + far_ref[part(0, DH), :].astype(F32)
    total = total + near_ref[part(0, DH), :].astype(F32) + near_ref[part(1, DH), :].astype(F32)
    out_ref[...] = total.astype(BF16)


def pair_kernel(message_ref, far_ref, out_ref):
    size = far_ref.shape[0]
    out_ref[:size, :] = far_ref[...]
    out_ref[size:, :] = message_ref[part(1, size), :]


def add_kernel(own_ref, got_ref, out_ref):
    out_ref[...] = (own_ref[...].astype(F32) + got_ref[...].astype(F32)).astype(out_ref.dtype)


def dnormed_kernel(groups, members, *refs):
    cots, weights = refs[: len(members)], refs[len(members) : len(members) + groups]
    dnormed_ref, cot_ref = refs[len(members) + groups :]
    _, block, outputs = cot_ref.shape
    width = dnormed_ref.shape[2]
    rows = weights[0].shape[1]
    me = lax.axis_index("dp")
    for i, (r, ref) in enumerate(zip(members, cots)):
        if r == 1:
            for p in range(outputs // width):
                cot_ref[i, :, part(p, width)] = ref[part(4 + p, block), :]
        else:
            cot_ref[i] = ref[...]
        total = dot(cot_ref[i, :, cut(me, rows)], weights[0][0], 1, 0)
        for j in range(1, groups):
            total = total + dot(cot_ref[i, :, cut(jnp.bitwise_xor(me, j), rows)], weights[j][0], 1, 0)
        dnormed_ref[i] = total


def base_kernel(*refs):
    refs[-1][...] = from_slabs(False, refs[:-1])


def from_slabs(backward, refs):
    slab = lax.div(lax.axis_index("seq"), SLAB)
    total = jnp.zeros(refs[0].shape, F32)
    for i, ref in enumerate(refs):
        bit = lax.rem(lax.div(slab, 1 << i), 2)
        total = total + jnp.where(bit == (0 if backward else 1), ref[...].astype(F32), 0.0)
    return total


def middle_kernel(*refs):
    own_ref, message_ref, token_far, own_state, far_state, near_state, base_ref, dnormed_a, dnormed_b = refs[:9]
    normed_ref, back_near, back_far, u_ref, slab_ref, running = refs[9:]
    _, block, width = normed_ref.shape
    heads = width // DH
    size = 2 * block
    tokens = (own_ref, message_ref.at[:size], token_far.at[:size], token_far.at[size:])
    running[member(0)] = own_state[...]
    running[member(1)] = near_state[part(0, DH), :].astype(F32)
    running[member(2)] = far_state[part(0, DH), :].astype(F32)
    running[member(3)] = near_state[part(1, DH), :].astype(F32)
    total = base_ref[...]
    for p in range(SLAB):
        total, running[p] = total + running[p], total
    sums = [jnp.zeros((DH, DH), F32)] * heads
    for r in range(SLAB):
        out = (back_near, back_far)[r // 2].at[part(r % 2, block + DH)]
        prior = running[member(r)].astype(BF16)
        out[block:, :] = prior
        for h in range(heads):
            q = tokens[r][:block, head(h)]
            mixed = tokens[r][block:, head(h)].astype(F32) + dot(q, prior[:, head(h)], 1, 0)
            scale = lax.rsqrt(jnp.mean(mixed * mixed, axis=-1, keepdims=True) + EPSILON)
            normed = mixed * scale
            normed_ref[r, :, head(h)] = normed.astype(BF16)
            dnormed = dnormed_a[r, :, head(h)] if r < 3 else dnormed_b[0, :, head(h)]
            along = jnp.mean(dnormed * normed, axis=-1, keepdims=True)
            dmixed = ((dnormed - normed * along) * scale).astype(BF16)
            out[:block, head(h)] = dmixed
            u = dot(q, dmixed, 0, 0)
            u_ref[r, :, head(h)] = u
            sums[h] = sums[h] + u
    for h in range(heads):
        slab_ref[:, head(h)] = sums[h].astype(BF16)


def later_kernel(*refs):
    *behind, u_ref, near_ref, far_ref, running = refs
    for r in range(SLAB):
        running[member(r)] = u_ref[r]
    total = from_slabs(True, behind)
    for p in reversed(range(SLAB)):
        total, running[p] = total + running[p], total
    for r in range(SLAB):
        (near_ref, far_ref)[r // 2][part(r % 2, DH), :] = running[member(r)].astype(BF16)


def relay_kernel(near_ref, far_ref, out_ref):
    size = near_ref.shape[0] // 2
    out_ref[:size, :] = near_ref[size:, :]
    out_ref[size:, :] = far_ref[size:, :]


def arrived(near_ref, far_ref, core_ref):
    size = near_ref.shape[0] // 2
    first, second = slice(0, size), slice(size, 2 * size)
    return near_ref.at[first], core_ref.at[first], far_ref.at[first], core_ref.at[second]


def late_kernel(near_ref, far_ref, core_ref, q_ref, k_ref, v_ref, gq_ref, gk_ref):
    backs = arrived(near_ref, far_ref, core_ref)
    block, width = q_ref.shape[0], near_ref.shape[1]
    mask = causal(block)
    for r in range(SLAB):
        at = cut(member(r), width)
        q, k, v = q_ref[:, at], k_ref[:, at], v_ref[:, at]
        gqs, gks = [], []
        for h in range(width // DH):
            dmixed, prior = backs[r][:block, head(h)], backs[r][block:, head(h)]
            back = jnp.where(mask, dot(dmixed, v[:, head(h)], 1, 1), 0.0).astype(BF16)
            gqs.append(dot(back, k[:, head(h)], 1, 0) + dot(dmixed, prior, 1, 1))
            gks.append(dot(back, q[:, head(h)], 0, 0))
        gq_ref[:, at] = jnp.concatenate(gqs, axis=1).astype(BF16)
        gk_ref[r] = jnp.concatenate(gks, axis=1)


def turn_kernel(weight_ref, *refs):
    *far, out_ref = refs
    rows = weight_ref.shape[0]
    width = weight_ref.shape[1] // SLAB
    me = lax.axis_index("dp")
    for p in range(SLAB):
        out_ref[part(p, width), cut(me, rows)] = weight_ref[:, part(p, width)].T
    for j in range(1, len(far) // 2 + 1):
        for r in range(SLAB):
            place = (cut(member(r), width), cut(jnp.bitwise_xor(me, j), rows))
            out_ref[place] = far[2 * (j - 1) + r % 2][r // 2].T


def output_kernel(
    near_ref, back_far, core_ref, q_ref, own_ref, message_ref, far_ref, attend_ref, turned_ref,
    out_ref, gv_ref, normed_ref,
):
    backs = arrived(near_ref, back_far, core_ref)
    block, width = q_ref.shape[0], near_ref.shape[1]
    withins = (own_ref.at[part(1, block)], message_ref.at[part(1, block)],
               far_ref.at[part(1, block)], message_ref.at[part(3, block)])
    for r in range(SLAB):
        at = cut(member(r), width)
        q = q_ref[:, at]
        normeds, gvs = [], []
        for h in range(width // DH):
            mixed = withins[r][:, head(h)].astype(F32) + dot(q[:, head(h)], backs[r][block:, head(h)], 1, 0)
            scale = lax.rsqrt(jnp.mean(mixed * mixed, axis=-1, keepdims=True) + EPSILON)
            normeds.append(mixed * scale)
            gvs.append(dot(attend_ref[r, h], backs[r][:block, head(h)], 0, 0))
        normed_ref[:, at] = jnp.concatenate(normeds, axis=1).astype(BF16)
        gv_ref[r] = jnp.concatenate(gvs, axis=1)
    out_ref[...] = dot(normed_ref[...], turned_ref[...], 1, 0).astype(BF16)


def last_kernel(near_ref, far_ref, core_ref, k_ref, v_ref, gk_part, gv_part, gk_ref, gv_ref):
    laters = arrived(near_ref, far_ref, core_ref)
    width = near_ref.shape[1]
    for r in range(SLAB):
        at = cut(member(r), width)
        k, v = k_ref[:, at], v_ref[:, at]
        gks, gvs = [], []
        for h in range(width // DH):
            later = laters[r][:, head(h)]
            gks.append(gk_part[r, :, head(h)] + dot(v[:, head(h)], later, 1, 1))
            gvs.append(gv_part[r, :, head(h)] + dot(k[:, head(h)], later, 1, 0))
        gk_ref[:, at] = jnp.concatenate(gks, axis=1).astype(BF16)
        gv_ref[:, at] = jnp.concatenate(gvs, axis=1).astype(BF16)


def product_kernel(slabs, cot_a, cot_b, normed_ref, keep_ref, send_ref):
    me = lax.axis_index("dp")
    slab = lax.div(lax.axis_index("seq"), SLAB)
    rows = keep_ref.shape[0] // slabs
    for j, out in enumerate((send_ref, keep_ref)):
        for d in range(slabs):
            at = jnp.bitwise_xor(me, 1 - j) * slabs + jnp.bitwise_xor(slab, d)
            total = dot(cot_b[0, :, cut(at, rows)], normed_ref[3], 0, 0)
            for r in range(3):
                total = total + dot(cot_a[r, :, cut(at, rows)], normed_ref[r], 0, 0)
            out[part(d, rows), :] = total.astype(out.dtype)


def split_kernel(own_ref, got_ref, keep_ref, send_ref):
    rows = keep_ref.shape[0] // 2
    for i in range(4):
        total = own_ref[part(i, rows), :] + got_ref[part(i, rows), :].astype(F32)
        out = (keep_ref, send_ref)[i % 2]
        out[part(i // 2, rows), :] = total.astype(out.dtype)


def split_again_kernel(own_ref, got_ref, keep_ref, send_ref):
    rows = keep_ref.shape[0]
    for i, out in enumerate((keep_ref, send_ref)):
        total = own_ref[part(i, rows), :] + got_ref[part(i, rows), :].astype(F32)
        out[...] = total.astype(out.dtype)


def share_kernel(own_ref, got_ref, keep_ref, send_ref, total_ref):
    total_ref[...] = own_ref[...] + got_ref[...].astype(F32)
    rows = keep_ref.shape[0] // 2
    for i, r in enumerate((0, 1)):
        keep_ref[part(i, rows), :] = total_ref[cut(member(r), rows), :].astype(BF16)
    for i, r in enumerate((2, 3)):
        send_ref[part(i, rows), :] = total_ref[cut(member(r), rows), :].astype(BF16)


def pass_kernel(own_ref, got_ref, keep_ref, send_ref):
    rows = own_ref.shape[0] // 2
    for i, ref in enumerate((own_ref, got_ref)):
        keep_ref[part(i, rows), :] = ref[:rows, :]
        send_ref[part(i, rows), :] = ref[rows:, :]


def finish_kernel(factor, keep_ref, got_ref, out_ref):
    rows, width = out_ref.shape[0], keep_ref.shape[1]
    for i, ref in enumerate((keep_ref, got_ref)):
        for j in range(2):
            out_ref[:, cut(member(i + 2 * j), width)] = ref[part(j, rows), :].astype(F32) * factor


def local(queries, keys, values, cotangent, out_weight, *, dp, seq):
    call = Chain()
    local_seqs, block, features = queries.shape
    outputs = cotangent.shape[2]
    rows = local_seqs * block
    slabs = seq // SLAB
    width = features // SLAB
    heads = width // DH
    q, k, v = (x.reshape(rows, features) for x in (queries, keys, values))
    cot = cotangent.reshape(rows, outputs)
    factor = 1.0 / math.sqrt(rows * dp * seq)
    near = functools.partial(flip, axis="seq", count=seq)

    def doubling(total, cost=1):
        found = []
        bits = SLAB
        while bits < seq:
            if found:
                (total,) = call(add_kernel, [(total.shape, BF16)], total, found[-1], cost=cost)
            found.append(near(total, bits=bits))
            bits *= 2
        return found, total

    def scratch(*arrays):
        return [pltpu.VMEM(x.shape, BF16) for x in arrays] + [pltpu.SemaphoreType.DMA((len(arrays),))]

    own_state, near_state, far_state, columns = call(
        front_kernel,
        [((DH, width), F32), ((DH, width), BF16), ((2 * DH, width), BF16),
         ((2, out_weight.shape[0], width), BF16)],
        k, v, out_weight, far=True, scratch=scratch(k, v, out_weight),
    )
    far_state = near(far_state, bits=2)
    w_far = [flip(columns, "dp", dp, j) for j in range(1, dp)]
    attend, own_tokens, message, far_tokens = call(
        pack_kernel,
        [((SLAB, heads, rows, rows), BF16), ((2 * rows, width), BF16),
         (((4 + outputs // width) * rows, width), BF16), ((2 * rows, width), BF16)],
        q, k, v, cot,
    )
    cot_y = near(cot, bits=2)
    near_tokens, sent = message, (message, far_tokens)
    message = near(message, bits=1)
    (near_state,) = call(
        cross_kernel, [((2 * DH, width), BF16)], near_state, far_state, cost=5 * 10**9
    )
    near_state = near(near_state, bits=1)
    (slab_kv,) = call(total_kernel, [((DH, width), BF16)], own_state, far_state, near_state)
    (far_tokens,) = call(pair_kernel, [((4 * rows, width), BF16)], message, far_tokens)
    cot_yc = near(after(cot_y, far_tokens), bits=1)
    far_tokens = near(far_tokens, bits=2)
    before, _ = doubling(slab_kv, 22 * 10**8)
    weights = (columns, *w_far)
    dnormed, cots = call(
        functools.partial(dnormed_kernel, dp, (0, 1, 2)),
        [((3, rows, width), F32), ((3, rows, outputs), BF16)], cot, message, cot_y, *weights,
    )
    dnormed_b, cot_b = call(
        functools.partial(dnormed_kernel, dp, (3,)),
        [((1, rows, width), F32), ((1, rows, outputs), BF16)], cot_yc, *weights,
    )
    (base,) = call(base_kernel, [((DH, width), F32)], *before, cost=10**9)
    w_all = [x for w in w_far for x in (w, near(after(w, dnormed), bits=1))]
    normed, back, back_far, u, slab_u = call(
        middle_kernel,
        [((SLAB, rows, width), BF16)] + [((2 * rows + 2 * DH, width), BF16)] * 2
        + [((SLAB, DH, width), F32), ((DH, width), BF16)],
        own_tokens, message, far_tokens, own_state, far_state, near_state, base, dnormed, dnormed_b,
        cost=10**10, scratch=[pltpu.VMEM((SLAB, DH, width), F32)],
    )
    tuned = dp == 2 and slabs == 4 and outputs // (dp * seq) % 8 == 0
    piece = outputs // (dp * slabs)
    if tuned:
        keep, send = call(
            functools.partial(product_kernel, slabs),
            [((outputs // dp, width), F32), ((outputs // dp, width), BF16)], cots, cot_b, normed,
        )
        got = flip(send, "dp", dp, 1)
    back_far = near(back_far, bits=2)
    (turned,) = call(turn_kernel, [((features, outputs), BF16)], out_weight, *w_all)
    if tuned:
        keep, send = call(
            split_kernel, [((2 * piece, width), F32), ((2 * piece, width), BF16)], keep, got, cost=1
        )
        got = near(send, bits=SLAB)
    behind, last_u = doubling(slab_u, 10**9)
    (send,) = call(relay_kernel, [((2 * rows + 2 * DH, width), BF16)], back, back_far)
    back_core = near(send, bits=1)
    if tuned:
        keep, send = call(
            split_again_kernel, [((piece, width), F32), ((piece, width), BF16)], keep, got, cost=3 * 10**9
        )
        got = near(send, bits=2 * SLAB)
    later, later_far = call(
        later_kernel, [((2 * DH, width), BF16)] * 2, *behind, u,
        scratch=[pltpu.VMEM((SLAB, DH, width), F32)],
    )
    later_far = near(later_far, bits=2)
    gq, gk_part = call(
        late_kernel, [((rows, features), BF16), ((SLAB, rows, width), F32)],
        back, back_far, back_core, q, k, v,
    )
    if tuned:
        keep, share = call(
            share_kernel, [((piece // 2, width), BF16)] * 2, keep, got, cost=3 * 10**9,
            scratch=[pltpu.VMEM((piece, width), F32)],
        )
        got = near(share, bits=2)
    (send,) = call(relay_kernel, [((2 * DH, width), BF16)], later, later_far)
    later_core = near(send, bits=1)
    output, gv_part, own_normed = call(
        output_kernel, [((rows, outputs), BF16), ((SLAB, rows, width), F32), ((rows, features), BF16)],
        back, back_far, back_core, q, own_tokens, *sent, attend, turned, end=True,
    )
    if tuned:
        keep, share = call(
            pass_kernel, [((piece // 2, width), BF16)] * 2, keep, got, cost=3 * 10**9,
            wait=[pltpu.with_memory_space_constraint(x, pltpu.HBM) for x in (output,)],
        )
        got = near(share, bits=1)
    gk, gv = call(
        last_kernel, [((rows, features), BF16)] * 2,
        later, later_far, later_core, k, v, gk_part, gv_part, end=True,
    )
    if tuned:
        (grad_weight,) = call(
            functools.partial(finish_kernel, factor),
            [((piece // SLAB, features), F32)], keep, got, end=True,
            wait=[pltpu.with_memory_space_constraint(gk, pltpu.HBM)],
        )
    else:
        partial = dot(cot, own_normed, 0, 0) * factor
        grad_weight = lax.psum_scatter(partial, ("dp", "seq"), scatter_dimension=0, tiled=True)
    shape = queries.shape
    return (
        output.reshape(cotangent.shape), gq.reshape(shape), gk.reshape(shape), gv.reshape(shape),
        grad_weight,
    )


def solution(mesh):
    dp, seq = mesh.shape["dp"], mesh.shape["seq"]
    return jax.shard_map(
        functools.partial(local, dp=dp, seq=seq),
        mesh=mesh,
        in_specs=(P("dp", "seq", None),) * 4 + (P("dp", None),),
        out_specs=(P("dp", "seq", None),) * 4 + (P(("dp", "seq"), None),),
        check_vma=False,
    )
```

```python
import functools
import math

import jax
import jax.numpy as jnp
from jax import lax
from jax.experimental import pallas as pl
from jax.experimental.pallas import tpu as pltpu
from jax.sharding import PartitionSpec as P

DH = 128
SLAB = 4
EPSILON = 1e-05
BF16 = jnp.bfloat16
F32 = jnp.float32


def dot(left, right, left_dim, right_dim):
    return lax.dot_general(
        left, right, (((left_dim,), (right_dim,)), ((), ())), preferred_element_type=F32
    )


class Chain:
    def __init__(self):
        self.last = None

    def __call__(self, body, outs, *args, scratch=(), far=False, wait=(), cost=1, end=False):
        count = len(args)
        if far:
            args = [pltpu.with_memory_space_constraint(x, pltpu.HBM) for x in args]
        specs = [pl.BlockSpec(memory_space=pl.ANY) if far else pl.BlockSpec()] * count
        inner = body
        if self.last is not None:
            extra = (self.last, *wait)
            args = (*args, *extra)
            specs = [*specs, *[pl.BlockSpec(memory_space=pl.ANY)] * len(extra)]

            def inner(*refs):
                body(*refs[:count], *refs[count + len(extra) :])

        found = pl.pallas_call(
            inner,
            out_shape=[jax.ShapeDtypeStruct(s, d) for s, d in outs],
            in_specs=specs,
            scratch_shapes=list(scratch),
            cost_estimate=pl.CostEstimate(flops=cost, bytes_accessed=1, transcendentals=0),
            compiler_params=pltpu.CompilerParams(vmem_limit_bytes=32 * 2**20),
        )(*args)
        if not end:
            self.last = min(reversed(found), key=lambda x: x.size)
        return found


def after(x, *others):
    return lax.optimization_barrier((x, *others))[0]


def flip(x, axis, count, bits):
    return lax.ppermute(x, axis, [(i, i ^ bits) for i in range(count)])


def head(h):
    return slice(h * DH, (h + 1) * DH)


def part(i, size):
    return slice(i * size, (i + 1) * size)


def cut(start, size):
    return pl.ds(pl.multiple_of(start * size, size), size)


def member(r):
    return jnp.bitwise_xor(lax.rem(lax.axis_index("seq"), SLAB), r)


def causal(block):
    rows = lax.broadcasted_iota(jnp.int32, (block, block), 0)
    return lax.broadcasted_iota(jnp.int32, (block, block), 1) <= rows


def fetch(pairs, sems):
    copies = [pltpu.make_async_copy(a, b, sems.at[i]) for i, (a, b) in enumerate(pairs)]
    for copy in copies:
        copy.start()
    return copies


def front_kernel(k_hbm, v_hbm, w_hbm, own_ref, near_ref, far_ref, columns_ref, k_ref, v_ref, w_ref, sems):
    copies = fetch([(k_hbm, k_ref), (v_hbm, v_ref), (w_hbm, w_ref)], sems)
    width = k_ref.shape[1] // SLAB
    copies[0].wait()
    copies[1].wait()
    places = (own_ref, near_ref, far_ref.at[part(0, DH)], far_ref.at[part(1, DH)])
    for r, out in enumerate(places):
        k, v = k_ref[:, cut(member(r), width)], v_ref[:, cut(member(r), width)]
        for h in range(width // DH):
            out[:, head(h)] = dot(k[:, head(h)], v[:, head(h)], 0, 0).astype(out.dtype)
    copies[2].wait()
    for i in range(2):
        columns_ref[i] = w_ref[:, cut(member(2 * i), width)]


def pack_kernel(q_ref, k_ref, v_ref, c_ref, attend_ref, own_ref, message_ref, far_ref):
    block = q_ref.shape[0]
    width = q_ref.shape[1] // SLAB
    mask = causal(block)
    places = (own_ref, message_ref.at[: 2 * block], far_ref, message_ref.at[2 * block : 4 * block])
    for r, out in enumerate(places):
        q, k, v = (ref[:, cut(member(r), width)] for ref in (q_ref, k_ref, v_ref))
        out[:block, :] = q
        for h in range(width // DH):
            attend = jnp.where(mask, dot(q[:, head(h)], k[:, head(h)], 1, 1), 0.0).astype(BF16)
            attend_ref[r, h] = attend
            out[block:, head(h)] = dot(attend, v[:, head(h)], 1, 0).astype(BF16)
    for i in range(c_ref.shape[1] // width):
        message_ref[part(4 + i, block), :] = c_ref[:, part(i, width)]


def cross_kernel(near_ref, got_ref, out_ref):
    out_ref[part(0, DH), :] = near_ref[...]
    out_ref[part(1, DH), :] = got_ref[part(1, DH), :]


def total_kernel(own_ref, far_ref, near_ref, out_ref):
    total = own_ref[...] + far_ref[part(0, DH), :].astype(F32)
    total = total + near_ref[part(0, DH), :].astype(F32) + near_ref[part(1, DH), :].astype(F32)
    out_ref[...] = total.astype(BF16)


def pair_kernel(message_ref, far_ref, out_ref):
    size = far_ref.shape[0]
    out_ref[:size, :] = far_ref[...]
    out_ref[size:, :] = message_ref[part(1, size), :]


def add_kernel(own_ref, got_ref, out_ref):
    out_ref[...] = (own_ref[...].astype(F32) + got_ref[...].astype(F32)).astype(out_ref.dtype)


def dnormed_kernel(groups, members, *refs):
    cots, weights = refs[: len(members)], refs[len(members) : len(members) + groups]
    dnormed_ref, cot_ref = refs[len(members) + groups :]
    _, block, outputs = cot_ref.shape
    width = dnormed_ref.shape[2]
    rows = weights[0].shape[1]
    me = lax.axis_index("dp")
    for i, (r, ref) in enumerate(zip(members, cots)):
        if r == 1:
            for p in range(outputs // width):
                cot_ref[i, :, part(p, width)] = ref[part(4 + p, block), :]
        else:
            cot_ref[i] = ref[...]
        total = dot(cot_ref[i, :, cut(me, rows)], weights[0][0], 1, 0)
        for j in range(1, groups):
            total = total + dot(cot_ref[i, :, cut(jnp.bitwise_xor(me, j), rows)], weights[j][0], 1, 0)
        dnormed_ref[i] = total


def base_kernel(*refs):
    refs[-1][...] = from_slabs(False, refs[:-1])


def from_slabs(backward, refs):
    slab = lax.div(lax.axis_index("seq"), SLAB)
    total = jnp.zeros(refs[0].shape, F32)
    for i, ref in enumerate(refs):
        bit = lax.rem(lax.div(slab, 1 << i), 2)
        total = total + jnp.where(bit == (0 if backward else 1), ref[...].astype(F32), 0.0)
    return total


def middle_kernel(*refs):
    own_ref, message_ref, token_far, own_state, far_state, near_state, base_ref, dnormed_a, dnormed_b = refs[:9]
    normed_ref, back_near, back_far, u_ref, slab_ref, running = refs[9:]
    _, block, width = normed_ref.shape
    heads = width // DH
    size = 2 * block
    tokens = (own_ref, message_ref.at[:size], token_far.at[:size], token_far.at[size:])
    running[member(0)] = own_state[...]
    running[member(1)] = near_state[part(0, DH), :].astype(F32)
    running[member(2)] = far_state[part(0, DH), :].astype(F32)
    running[member(3)] = near_state[part(1, DH), :].astype(F32)
    total = base_ref[...]
    for p in range(SLAB):
        total, running[p] = total + running[p], total
    sums = [jnp.zeros((DH, DH), F32)] * heads
    for r in range(SLAB):
        out = (back_near, back_far)[r // 2].at[part(r % 2, block + DH)]
        prior = running[member(r)].astype(BF16)
        out[block:, :] = prior
        for h in range(heads):
            q = tokens[r][:block, head(h)]
            mixed = tokens[r][block:, head(h)].astype(F32) + dot(q, prior[:, head(h)], 1, 0)
            scale = lax.rsqrt(jnp.mean(mixed * mixed, axis=-1, keepdims=True) + EPSILON)
            normed = mixed * scale
            normed_ref[r, :, head(h)] = normed.astype(BF16)
            dnormed = dnormed_a[r, :, head(h)] if r < 3 else dnormed_b[0, :, head(h)]
            along = jnp.mean(dnormed * normed, axis=-1, keepdims=True)
            dmixed = ((dnormed - normed * along) * scale).astype(BF16)
            out[:block, head(h)] = dmixed
            u = dot(q, dmixed, 0, 0)
            u_ref[r, :, head(h)] = u
            sums[h] = sums[h] + u
    for h in range(heads):
        slab_ref[:, head(h)] = sums[h].astype(BF16)


def later_kernel(*refs):
    *behind, u_ref, near_ref, far_ref, running = refs
    for r in range(SLAB):
        running[member(r)] = u_ref[r]
    total = from_slabs(True, behind)
    for p in reversed(range(SLAB)):
        total, running[p] = total + running[p], total
    for r in range(SLAB):
        (near_ref, far_ref)[r // 2][part(r % 2, DH), :] = running[member(r)].astype(BF16)


def relay_kernel(near_ref, far_ref, out_ref):
    size = near_ref.shape[0] // 2
    out_ref[:size, :] = near_ref[size:, :]
    out_ref[size:, :] = far_ref[size:, :]


def arrived(near_ref, far_ref, core_ref):
    size = near_ref.shape[0] // 2
    first, second = slice(0, size), slice(size, 2 * size)
    return near_ref.at[first], core_ref.at[first], far_ref.at[first], core_ref.at[second]


def late_kernel(near_ref, far_ref, core_ref, q_ref, k_ref, v_ref, attend_ref, gq_ref, gk_ref, gv_ref):
    backs = arrived(near_ref, far_ref, core_ref)
    block, width = q_ref.shape[0], near_ref.shape[1]
    mask = causal(block)
    for r in range(SLAB):
        at = cut(member(r), width)
        q, k, v = q_ref[:, at], k_ref[:, at], v_ref[:, at]
        gqs, gks, gvs = [], [], []
        for h in range(width // DH):
            dmixed, prior = backs[r][:block, head(h)], backs[r][block:, head(h)]
            back = jnp.where(mask, dot(dmixed, v[:, head(h)], 1, 1), 0.0).astype(BF16)
            gqs.append(dot(back, k[:, head(h)], 1, 0) + dot(dmixed, prior, 1, 1))
            gks.append(dot(back, q[:, head(h)], 0, 0))
            gvs.append(dot(attend_ref[r, h], dmixed, 0, 0))
        gq_ref[:, at] = jnp.concatenate(gqs, axis=1).astype(BF16)
        gk_ref[r] = jnp.concatenate(gks, axis=1)
        gv_ref[r] = jnp.concatenate(gvs, axis=1)


def output_kernel(near_ref, back_far, core_ref, q_ref, own_ref, message_ref, far_ref, weight_ref, *refs):
    *far, out_ref, normed_ref = refs
    backs = arrived(near_ref, back_far, core_ref)
    block, width = q_ref.shape[0], near_ref.shape[1]
    rows = weight_ref.shape[0]
    me = lax.axis_index("dp")
    withins = (own_ref.at[part(1, block)], message_ref.at[part(1, block)],
               far_ref.at[part(1, block)], message_ref.at[part(3, block)])
    totals = [jnp.zeros((block, rows), F32)] * (len(far) // 2)
    for r in range(SLAB):
        at = cut(member(r), width)
        q = q_ref[:, at]
        normeds = []
        for h in range(width // DH):
            mixed = withins[r][:, head(h)].astype(F32) + dot(q[:, head(h)], backs[r][block:, head(h)], 1, 0)
            scale = lax.rsqrt(jnp.mean(mixed * mixed, axis=-1, keepdims=True) + EPSILON)
            normeds.append(mixed * scale)
        normed = jnp.concatenate(normeds, axis=1).astype(BF16)
        normed_ref[:, at] = normed
        for j in range(len(totals)):
            totals[j] = totals[j] + dot(normed, far[2 * j + r % 2][r // 2], 1, 1)
    out_ref[:, cut(me, rows)] = dot(normed_ref[...], weight_ref[...], 1, 1).astype(BF16)
    for j, total in enumerate(totals, 1):
        out_ref[:, cut(jnp.bitwise_xor(me, j), rows)] = total.astype(BF16)


def last_kernel(near_ref, far_ref, core_ref, k_ref, v_ref, gk_part, gv_part, gk_ref, gv_ref):
    laters = arrived(near_ref, far_ref, core_ref)
    width = near_ref.shape[1]
    for r in range(SLAB):
        at = cut(member(r), width)
        k, v = k_ref[:, at], v_ref[:, at]
        gks, gvs = [], []
        for h in range(width // DH):
            later = laters[r][:, head(h)]
            gks.append(gk_part[r, :, head(h)] + dot(v[:, head(h)], later, 1, 1))
            gvs.append(gv_part[r, :, head(h)] + dot(k[:, head(h)], later, 1, 0))
        gk_ref[:, at] = jnp.concatenate(gks, axis=1).astype(BF16)
        gv_ref[:, at] = jnp.concatenate(gvs, axis=1).astype(BF16)


def product_kernel(slabs, j, cot_a, cot_b, normed_ref, out_ref):
    me = lax.axis_index("dp")
    slab = lax.div(lax.axis_index("seq"), SLAB)
    rows = out_ref.shape[0] // slabs
    for d in range(slabs):
        at = jnp.bitwise_xor(me, j) * slabs + jnp.bitwise_xor(slab, d)
        total = dot(cot_b[0, :, cut(at, rows)], normed_ref[3], 0, 0)
        for r in range(3):
            total = total + dot(cot_a[r, :, cut(at, rows)], normed_ref[r], 0, 0)
        out_ref[part(d, rows), :] = total.astype(out_ref.dtype)


def split_kernel(own_ref, got_ref, keep_ref, send_ref):
    rows = keep_ref.shape[0] // 2
    for i in range(4):
        total = own_ref[part(i, rows), :] + got_ref[part(i, rows), :].astype(F32)
        out = (keep_ref, send_ref)[i % 2]
        out[part(i // 2, rows), :] = total.astype(out.dtype)


def split_again_kernel(own_ref, got_ref, keep_ref, send_ref):
    rows = keep_ref.shape[0]
    for i, out in enumerate((keep_ref, send_ref)):
        total = own_ref[part(i, rows), :] + got_ref[part(i, rows), :].astype(F32)
        out[...] = total.astype(out.dtype)


def share_kernel(own_ref, got_ref, keep_ref, send_ref, total_ref):
    total_ref[...] = own_ref[...] + got_ref[...].astype(F32)
    rows = keep_ref.shape[0] // 2
    for i, r in enumerate((0, 1)):
        keep_ref[part(i, rows), :] = total_ref[cut(member(r), rows), :].astype(BF16)
    for i, r in enumerate((2, 3)):
        send_ref[part(i, rows), :] = total_ref[cut(member(r), rows), :].astype(BF16)


def pass_kernel(own_ref, got_ref, keep_ref, send_ref):
    rows = own_ref.shape[0] // 2
    for i, ref in enumerate((own_ref, got_ref)):
        keep_ref[part(i, rows), :] = ref[:rows, :]
        send_ref[part(i, rows), :] = ref[rows:, :]


def finish_kernel(factor, keep_ref, got_ref, out_ref):
    rows, width = out_ref.shape[0], keep_ref.shape[1]
    for i, ref in enumerate((keep_ref, got_ref)):
        for j in range(2):
            out_ref[:, cut(member(i + 2 * j), width)] = ref[part(j, rows), :].astype(F32) * factor


def local(queries, keys, values, cotangent, out_weight, *, dp, seq):
    call = Chain()
    local_seqs, block, features = queries.shape
    outputs = cotangent.shape[2]
    rows = local_seqs * block
    slabs = seq // SLAB
    width = features // SLAB
    heads = width // DH
    q, k, v = (x.reshape(rows, features) for x in (queries, keys, values))
    cot = cotangent.reshape(rows, outputs)
    factor = 1.0 / math.sqrt(rows * dp * seq)
    near = functools.partial(flip, axis="seq", count=seq)

    def doubling(total, cost=1):
        found = []
        bits = SLAB
        while bits < seq:
            if found:
                (total,) = call(add_kernel, [(total.shape, BF16)], total, found[-1], cost=cost)
            found.append(near(total, bits=bits))
            bits *= 2
        return found, total

    def scratch(*arrays):
        return [pltpu.VMEM(x.shape, BF16) for x in arrays] + [pltpu.SemaphoreType.DMA((len(arrays),))]

    own_state, near_state, far_state, columns = call(
        front_kernel,
        [((DH, width), F32), ((DH, width), BF16), ((2 * DH, width), BF16),
         ((2, out_weight.shape[0], width), BF16)],
        k, v, out_weight, far=True, scratch=scratch(k, v, out_weight),
    )
    far_state = near(far_state, bits=2)
    w_far = [flip(columns, "dp", dp, j) for j in range(1, dp)]
    attend, own_tokens, message, far_tokens = call(
        pack_kernel,
        [((SLAB, heads, rows, rows), BF16), ((2 * rows, width), BF16),
         (((4 + outputs // width) * rows, width), BF16), ((2 * rows, width), BF16)],
        q, k, v, cot,
    )
    cot_y = near(cot, bits=2)
    near_tokens, sent = message, (message, far_tokens)
    message = near(message, bits=1)
    (near_state,) = call(
        cross_kernel, [((2 * DH, width), BF16)], near_state, far_state, cost=5 * 10**9
    )
    near_state = near(near_state, bits=1)
    (slab_kv,) = call(total_kernel, [((DH, width), BF16)], own_state, far_state, near_state)
    (far_tokens,) = call(pair_kernel, [((4 * rows, width), BF16)], message, far_tokens)
    cot_yc = near(after(cot_y, far_tokens), bits=1)
    far_tokens = near(far_tokens, bits=2)
    before, _ = doubling(slab_kv, 22 * 10**8)
    weights = (columns, *w_far)
    dnormed, cots = call(
        functools.partial(dnormed_kernel, dp, (0, 1, 2)),
        [((3, rows, width), F32), ((3, rows, outputs), BF16)], cot, message, cot_y, *weights,
    )
    dnormed_b, cot_b = call(
        functools.partial(dnormed_kernel, dp, (3,)),
        [((1, rows, width), F32), ((1, rows, outputs), BF16)], cot_yc, *weights,
    )
    (base,) = call(base_kernel, [((DH, width), F32)], *before, cost=10**9)
    w_all = [x for w in w_far for x in (w, near(after(w, dnormed), bits=1))]
    normed, back, back_far, u, slab_u = call(
        middle_kernel,
        [((SLAB, rows, width), BF16)] + [((2 * rows + 2 * DH, width), BF16)] * 2
        + [((SLAB, DH, width), F32), ((DH, width), BF16)],
        own_tokens, message, far_tokens, own_state, far_state, near_state, base, dnormed, dnormed_b,
        cost=10**10, scratch=[pltpu.VMEM((SLAB, DH, width), F32)],
    )
    tuned = dp == 2 and slabs == 4 and outputs // (dp * seq) % 8 == 0
    piece = outputs // (dp * slabs)
    if tuned:
        (send,) = call(
            functools.partial(product_kernel, slabs, 1), [((outputs // dp, width), BF16)], cots, cot_b, normed
        )
        got = flip(send, "dp", dp, 1)
        (keep,) = call(
            functools.partial(product_kernel, slabs, 0), [((outputs // dp, width), F32)], cots, cot_b, normed
        )
    back_far = near(back_far, bits=2)
    if tuned:
        keep, send = call(
            split_kernel, [((2 * piece, width), F32), ((2 * piece, width), BF16)], keep, got, wait=w_all[1::2]
        )
        got = near(send, bits=SLAB)
    behind, last_u = doubling(slab_u, 10**9)
    (send,) = call(relay_kernel, [((2 * rows + 2 * DH, width), BF16)], back, back_far)
    back_core = near(send, bits=1)
    if tuned:
        keep, send = call(
            split_again_kernel, [((piece, width), F32), ((piece, width), BF16)], keep, got, cost=3 * 10**9
        )
        got = near(send, bits=2 * SLAB)
    later, later_far = call(
        later_kernel, [((2 * DH, width), BF16)] * 2, *behind, u,
        scratch=[pltpu.VMEM((SLAB, DH, width), F32)],
    )
    later_far = near(later_far, bits=2)
    gq, gk_part, gv_part = call(
        late_kernel,
        [((rows, features), BF16), ((SLAB, rows, width), F32), ((SLAB, rows, width), F32)],
        back, back_far, back_core, q, k, v, attend,
    )
    if tuned:
        keep, share = call(
            share_kernel, [((piece // 2, width), BF16)] * 2, keep, got, cost=3 * 10**9,
            scratch=[pltpu.VMEM((piece, width), F32)],
        )
        got = near(share, bits=2)
    (send,) = call(relay_kernel, [((2 * DH, width), BF16)], later, later_far)
    later_core = near(send, bits=1)
    output, own_normed = call(
        output_kernel, [((rows, outputs), BF16), ((rows, features), BF16)],
        back, back_far, back_core, q, own_tokens, *sent, out_weight, *w_all, end=True,
    )
    if tuned:
        keep, share = call(
            pass_kernel, [((piece // 2, width), BF16)] * 2, keep, got, cost=3 * 10**9,
            wait=[pltpu.with_memory_space_constraint(x, pltpu.HBM) for x in (output,)],
        )
        got = near(share, bits=1)
    gk, gv = call(
        last_kernel, [((rows, features), BF16)] * 2,
        later, later_far, later_core, k, v, gk_part, gv_part, end=True,
    )
    if tuned:
        (grad_weight,) = call(
            functools.partial(finish_kernel, factor),
            [((piece // SLAB, features), F32)], keep, got, end=True,
            wait=[pltpu.with_memory_space_constraint(gk, pltpu.HBM)],
        )
    else:
        partial = dot(cot, own_normed, 0, 0) * factor
        grad_weight = lax.psum_scatter(partial, ("dp", "seq"), scatter_dimension=0, tiled=True)
    shape = queries.shape
    return (
        output.reshape(cotangent.shape), gq.reshape(shape), gk.reshape(shape), gv.reshape(shape),
        grad_weight,
    )


def solution(mesh):
    dp, seq = mesh.shape["dp"], mesh.shape["seq"]
    return jax.shard_map(
        functools.partial(local, dp=dp, seq=seq),
        mesh=mesh,
        in_specs=(P("dp", "seq", None),) * 4 + (P("dp", None),),
        out_specs=(P("dp", "seq", None),) * 4 + (P(("dp", "seq"), None),),
        check_vma=False,
    )
```

```python
import functools
import math

import jax
import jax.numpy as jnp
from jax import lax
from jax.experimental import pallas as pl
from jax.experimental.pallas import tpu as pltpu
from jax.sharding import PartitionSpec as P

DH = 128
SLAB = 4
EPSILON = 1e-05
BF16 = jnp.bfloat16
F32 = jnp.float32


def dot(left, right, left_dim, right_dim):
    return lax.dot_general(
        left, right, (((left_dim,), (right_dim,)), ((), ())), preferred_element_type=F32
    )


class Chain:
    def __init__(self):
        self.last = None

    def __call__(self, body, outs, *args, scratch=(), far=False, wait=(), cost=1, end=False):
        count = len(args)
        if far:
            args = [pltpu.with_memory_space_constraint(x, pltpu.HBM) for x in args]
        specs = [pl.BlockSpec(memory_space=pl.ANY) if far else pl.BlockSpec()] * count
        inner = body
        if self.last is not None:
            extra = (self.last, *wait)
            args = (*args, *extra)
            specs = [*specs, *[pl.BlockSpec(memory_space=pl.ANY)] * len(extra)]

            def inner(*refs):
                body(*refs[:count], *refs[count + len(extra) :])

        found = pl.pallas_call(
            inner,
            out_shape=[jax.ShapeDtypeStruct(s, d) for s, d in outs],
            in_specs=specs,
            scratch_shapes=list(scratch),
            cost_estimate=pl.CostEstimate(flops=cost, bytes_accessed=1, transcendentals=0),
            compiler_params=pltpu.CompilerParams(vmem_limit_bytes=32 * 2**20),
        )(*args)
        if not end:
            self.last = min(reversed(found), key=lambda x: x.size)
        return found


def after(x, *others):
    return lax.optimization_barrier((x, *others))[0]


def flip(x, axis, count, bits):
    return lax.ppermute(x, axis, [(i, i ^ bits) for i in range(count)])


def head(h):
    return slice(h * DH, (h + 1) * DH)


def part(i, size):
    return slice(i * size, (i + 1) * size)


def cut(start, size):
    return pl.ds(pl.multiple_of(start * size, size), size)


def member(r):
    return jnp.bitwise_xor(lax.rem(lax.axis_index("seq"), SLAB), r)


def causal(block):
    rows = lax.broadcasted_iota(jnp.int32, (block, block), 0)
    return lax.broadcasted_iota(jnp.int32, (block, block), 1) <= rows


def fetch(pairs, sems):
    copies = [pltpu.make_async_copy(a, b, sems.at[i]) for i, (a, b) in enumerate(pairs)]
    for copy in copies:
        copy.start()
    return copies


def front_kernel(k_hbm, v_hbm, w_hbm, own_ref, near_ref, far_ref, columns_ref, k_ref, v_ref, w_ref, sems):
    copies = fetch([(k_hbm, k_ref), (v_hbm, v_ref), (w_hbm, w_ref)], sems)
    width = k_ref.shape[1] // SLAB
    copies[0].wait()
    copies[1].wait()
    places = (own_ref, near_ref, far_ref.at[part(0, DH)], far_ref.at[part(1, DH)])
    for r, out in enumerate(places):
        k, v = k_ref[:, cut(member(r), width)], v_ref[:, cut(member(r), width)]
        for h in range(width // DH):
            out[:, head(h)] = dot(k[:, head(h)], v[:, head(h)], 0, 0).astype(out.dtype)
    copies[2].wait()
    for i in range(2):
        columns_ref[i] = w_ref[:, cut(member(2 * i), width)]


def pack_kernel(q_ref, k_ref, v_ref, c_ref, attend_ref, own_ref, message_ref, far_ref):
    block = q_ref.shape[0]
    width = q_ref.shape[1] // SLAB
    mask = causal(block)
    places = (own_ref, message_ref.at[: 2 * block], far_ref, message_ref.at[2 * block : 4 * block])
    for r, out in enumerate(places):
        q, k, v = (ref[:, cut(member(r), width)] for ref in (q_ref, k_ref, v_ref))
        out[:block, :] = q
        for h in range(width // DH):
            attend = jnp.where(mask, dot(q[:, head(h)], k[:, head(h)], 1, 1), 0.0).astype(BF16)
            attend_ref[r, h] = attend
            out[block:, head(h)] = dot(attend, v[:, head(h)], 1, 0).astype(BF16)
    for i in range(c_ref.shape[1] // width):
        message_ref[part(4 + i, block), :] = c_ref[:, part(i, width)]


def cross_kernel(near_ref, got_ref, out_ref):
    out_ref[part(0, DH), :] = near_ref[...]
    out_ref[part(1, DH), :] = got_ref[part(1, DH), :]


def total_kernel(own_ref, far_ref, near_ref, out_ref):
    total = own_ref[...] + far_ref[part(0, DH), :].astype(F32)
    total = total + near_ref[part(0, DH), :].astype(F32) + near_ref[part(1, DH), :].astype(F32)
    out_ref[...] = total.astype(BF16)


def pair_kernel(message_ref, far_ref, out_ref):
    size = far_ref.shape[0]
    out_ref[:size, :] = far_ref[...]
    out_ref[size:, :] = message_ref[part(1, size), :]


def add_kernel(own_ref, got_ref, out_ref):
    out_ref[...] = (own_ref[...].astype(F32) + got_ref[...].astype(F32)).astype(out_ref.dtype)


def dnormed_kernel(groups, members, *refs):
    cots, weights = refs[: len(members)], refs[len(members) : len(members) + groups]
    dnormed_ref, cot_ref = refs[len(members) + groups :]
    _, block, outputs = cot_ref.shape
    width = dnormed_ref.shape[2]
    rows = weights[0].shape[1]
    me = lax.axis_index("dp")
    for i, (r, ref) in enumerate(zip(members, cots)):
        if r == 1:
            for p in range(outputs // width):
                cot_ref[i, :, part(p, width)] = ref[part(4 + p, block), :]
        else:
            cot_ref[i] = ref[...]
        total = dot(cot_ref[i, :, cut(me, rows)], weights[0][0], 1, 0)
        for j in range(1, groups):
            total = total + dot(cot_ref[i, :, cut(jnp.bitwise_xor(me, j), rows)], weights[j][0], 1, 0)
        dnormed_ref[i] = total


def base_kernel(*refs):
    refs[-1][...] = from_slabs(False, refs[:-1])


def from_slabs(backward, refs):
    slab = lax.div(lax.axis_index("seq"), SLAB)
    total = jnp.zeros(refs[0].shape, F32)
    for i, ref in enumerate(refs):
        bit = lax.rem(lax.div(slab, 1 << i), 2)
        total = total + jnp.where(bit == (0 if backward else 1), ref[...].astype(F32), 0.0)
    return total


def mixed_kernel(
    own_ref, message_ref, token_far, own_state, far_state, near_state, base_ref,
    normed_ref, mixed_ref, prior_ref, running,
):
    _, block, width = normed_ref.shape
    size = 2 * block
    tokens = (own_ref, message_ref.at[:size], token_far.at[:size], token_far.at[size:])
    running[member(0)] = own_state[...]
    running[member(1)] = near_state[part(0, DH), :].astype(F32)
    running[member(2)] = far_state[part(0, DH), :].astype(F32)
    running[member(3)] = near_state[part(1, DH), :].astype(F32)
    total = base_ref[...]
    for p in range(SLAB):
        total, running[p] = total + running[p], total
    for r in range(SLAB):
        prior = running[member(r)].astype(BF16)
        prior_ref[r] = prior
        for h in range(width // DH):
            q = tokens[r][:block, head(h)]
            mixed = tokens[r][block:, head(h)].astype(F32) + dot(q, prior[:, head(h)], 1, 0)
            scale = lax.rsqrt(jnp.mean(mixed * mixed, axis=-1, keepdims=True) + EPSILON)
            mixed_ref[r, :, head(h)] = mixed
            normed_ref[r, :, head(h)] = (mixed * scale).astype(BF16)


def middle_kernel(
    own_ref, message_ref, token_far, mixed_ref, prior_ref, dnormed_a, dnormed_b,
    near_ref, far_ref, u_ref, slab_ref,
):
    _, block, width = mixed_ref.shape
    size = 2 * block
    tokens = (own_ref, message_ref.at[:size], token_far.at[:size], token_far.at[size:])
    sums = [jnp.zeros((DH, DH), F32)] * (width // DH)
    for r in range(SLAB):
        out = (near_ref, far_ref)[r // 2].at[part(r % 2, block + DH)]
        out[block:, :] = prior_ref[r]
        for h in range(width // DH):
            mixed = mixed_ref[r, :, head(h)]
            scale = lax.rsqrt(jnp.mean(mixed * mixed, axis=-1, keepdims=True) + EPSILON)
            normed = mixed * scale
            dnormed = dnormed_a[r, :, head(h)] if r < 3 else dnormed_b[0, :, head(h)]
            along = jnp.mean(dnormed * normed, axis=-1, keepdims=True)
            dmixed = ((dnormed - normed * along) * scale).astype(BF16)
            out[:block, head(h)] = dmixed
            u = dot(tokens[r][:block, head(h)], dmixed, 0, 0)
            u_ref[r, :, head(h)] = u
            sums[h] = sums[h] + u
    for h in range(width // DH):
        slab_ref[:, head(h)] = sums[h].astype(BF16)


def later_kernel(*refs):
    *behind, u_ref, near_ref, far_ref, running = refs
    for r in range(SLAB):
        running[member(r)] = u_ref[r]
    total = from_slabs(True, behind)
    for p in reversed(range(SLAB)):
        total, running[p] = total + running[p], total
    for r in range(SLAB):
        (near_ref, far_ref)[r // 2][part(r % 2, DH), :] = running[member(r)].astype(BF16)


def relay_kernel(near_ref, far_ref, out_ref):
    size = near_ref.shape[0] // 2
    out_ref[:size, :] = near_ref[size:, :]
    out_ref[size:, :] = far_ref[size:, :]


def arrived(near_ref, far_ref, core_ref):
    size = near_ref.shape[0] // 2
    first, second = slice(0, size), slice(size, 2 * size)
    return near_ref.at[first], core_ref.at[first], far_ref.at[first], core_ref.at[second]


def late_kernel(near_ref, far_ref, core_ref, q_ref, k_ref, v_ref, attend_ref, gq_ref, gk_ref, gv_ref):
    backs = arrived(near_ref, far_ref, core_ref)
    block, width = q_ref.shape[0], near_ref.shape[1]
    mask = causal(block)
    for r in range(SLAB):
        at = cut(member(r), width)
        q, k, v = q_ref[:, at], k_ref[:, at], v_ref[:, at]
        gqs, gks, gvs = [], [], []
        for h in range(width // DH):
            dmixed, prior = backs[r][:block, head(h)], backs[r][block:, head(h)]
            back = jnp.where(mask, dot(dmixed, v[:, head(h)], 1, 1), 0.0).astype(BF16)
            gqs.append(dot(back, k[:, head(h)], 1, 0) + dot(dmixed, prior, 1, 1))
            gks.append(dot(back, q[:, head(h)], 0, 0))
            gvs.append(dot(attend_ref[r, h], dmixed, 0, 0))
        gq_ref[:, at] = jnp.concatenate(gqs, axis=1).astype(BF16)
        gk_ref[r] = jnp.concatenate(gks, axis=1)
        gv_ref[r] = jnp.concatenate(gvs, axis=1)


def output_kernel(near_ref, back_far, core_ref, q_ref, own_ref, message_ref, far_ref, weight_ref, *refs):
    *far, out_ref, normed_ref = refs
    backs = arrived(near_ref, back_far, core_ref)
    block, width = q_ref.shape[0], near_ref.shape[1]
    rows = weight_ref.shape[0]
    me = lax.axis_index("dp")
    withins = (own_ref.at[part(1, block)], message_ref.at[part(1, block)],
               far_ref.at[part(1, block)], message_ref.at[part(3, block)])
    totals = [jnp.zeros((block, rows), F32)] * (len(far) // 2)
    for r in range(SLAB):
        at = cut(member(r), width)
        q = q_ref[:, at]
        normeds = []
        for h in range(width // DH):
            mixed = withins[r][:, head(h)].astype(F32) + dot(q[:, head(h)], backs[r][block:, head(h)], 1, 0)
            scale = lax.rsqrt(jnp.mean(mixed * mixed, axis=-1, keepdims=True) + EPSILON)
            normeds.append(mixed * scale)
        normed = jnp.concatenate(normeds, axis=1).astype(BF16)
        normed_ref[:, at] = normed
        for j in range(len(totals)):
            totals[j] = totals[j] + dot(normed, far[2 * j + r % 2][r // 2], 1, 1)
    out_ref[:, cut(me, rows)] = dot(normed_ref[...], weight_ref[...], 1, 1).astype(BF16)
    for j, total in enumerate(totals, 1):
        out_ref[:, cut(jnp.bitwise_xor(me, j), rows)] = total.astype(BF16)


def last_kernel(near_ref, far_ref, core_ref, k_ref, v_ref, gk_part, gv_part, gk_ref, gv_ref):
    laters = arrived(near_ref, far_ref, core_ref)
    width = near_ref.shape[1]
    for r in range(SLAB):
        at = cut(member(r), width)
        k, v = k_ref[:, at], v_ref[:, at]
        gks, gvs = [], []
        for h in range(width // DH):
            later = laters[r][:, head(h)]
            gks.append(gk_part[r, :, head(h)] + dot(v[:, head(h)], later, 1, 1))
            gvs.append(gv_part[r, :, head(h)] + dot(k[:, head(h)], later, 1, 0))
        gk_ref[:, at] = jnp.concatenate(gks, axis=1).astype(BF16)
        gv_ref[:, at] = jnp.concatenate(gvs, axis=1).astype(BF16)


def product_kernel(slabs, j, cot_a, cot_b, normed_ref, out_ref):
    me = lax.axis_index("dp")
    slab = lax.div(lax.axis_index("seq"), SLAB)
    rows = out_ref.shape[0] // slabs
    for d in range(slabs):
        at = jnp.bitwise_xor(me, j) * slabs + jnp.bitwise_xor(slab, d)
        total = dot(cot_b[0, :, cut(at, rows)], normed_ref[3], 0, 0)
        for r in range(3):
            total = total + dot(cot_a[r, :, cut(at, rows)], normed_ref[r], 0, 0)
        out_ref[part(d, rows), :] = total.astype(out_ref.dtype)


def split_kernel(own_ref, got_ref, keep_ref, send_ref):
    rows = keep_ref.shape[0] // 2
    for i in range(4):
        total = own_ref[part(i, rows), :] + got_ref[part(i, rows), :].astype(F32)
        out = (keep_ref, send_ref)[i % 2]
        out[part(i // 2, rows), :] = total.astype(out.dtype)


def split_again_kernel(own_ref, got_ref, keep_ref, send_ref):
    rows = keep_ref.shape[0]
    for i, out in enumerate((keep_ref, send_ref)):
        total = own_ref[part(i, rows), :] + got_ref[part(i, rows), :].astype(F32)
        out[...] = total.astype(out.dtype)


def share_kernel(own_ref, got_ref, keep_ref, send_ref, total_ref):
    total_ref[...] = own_ref[...] + got_ref[...].astype(F32)
    rows = keep_ref.shape[0] // 2
    for i, r in enumerate((0, 1)):
        keep_ref[part(i, rows), :] = total_ref[cut(member(r), rows), :].astype(BF16)
    for i, r in enumerate((2, 3)):
        send_ref[part(i, rows), :] = total_ref[cut(member(r), rows), :].astype(BF16)


def pass_kernel(own_ref, got_ref, keep_ref, send_ref):
    rows = own_ref.shape[0] // 2
    for i, ref in enumerate((own_ref, got_ref)):
        keep_ref[part(i, rows), :] = ref[:rows, :]
        send_ref[part(i, rows), :] = ref[rows:, :]


def finish_kernel(factor, keep_ref, got_ref, out_ref):
    rows, width = out_ref.shape[0], keep_ref.shape[1]
    for i, ref in enumerate((keep_ref, got_ref)):
        for j in range(2):
            out_ref[:, cut(member(i + 2 * j), width)] = ref[part(j, rows), :].astype(F32) * factor


def local(queries, keys, values, cotangent, out_weight, *, dp, seq):
    call = Chain()
    local_seqs, block, features = queries.shape
    outputs = cotangent.shape[2]
    rows = local_seqs * block
    slabs = seq // SLAB
    width = features // SLAB
    heads = width // DH
    q, k, v = (x.reshape(rows, features) for x in (queries, keys, values))
    cot = cotangent.reshape(rows, outputs)
    factor = 1.0 / math.sqrt(rows * dp * seq)
    near = functools.partial(flip, axis="seq", count=seq)

    def doubling(total, cost=1):
        found = []
        bits = SLAB
        while bits < seq:
            if found:
                (total,) = call(add_kernel, [(total.shape, BF16)], total, found[-1], cost=cost)
            found.append(near(total, bits=bits))
            bits *= 2
        return found, total

    def scratch(*arrays):
        return [pltpu.VMEM(x.shape, BF16) for x in arrays] + [pltpu.SemaphoreType.DMA((len(arrays),))]

    own_state, near_state, far_state, columns = call(
        front_kernel,
        [((DH, width), F32), ((DH, width), BF16), ((2 * DH, width), BF16),
         ((2, out_weight.shape[0], width), BF16)],
        k, v, out_weight, far=True, scratch=scratch(k, v, out_weight),
    )
    far_state = near(far_state, bits=2)
    w_far = [flip(columns, "dp", dp, j) for j in range(1, dp)]
    attend, own_tokens, message, far_tokens = call(
        pack_kernel,
        [((SLAB, heads, rows, rows), BF16), ((2 * rows, width), BF16),
         (((4 + outputs // width) * rows, width), BF16), ((2 * rows, width), BF16)],
        q, k, v, cot,
    )
    cot_y = near(cot, bits=2)
    near_tokens, sent = message, (message, far_tokens)
    message = near(message, bits=1)
    (near_state,) = call(
        cross_kernel, [((2 * DH, width), BF16)], near_state, far_state, cost=5 * 10**9
    )
    near_state = near(near_state, bits=1)
    (slab_kv,) = call(total_kernel, [((DH, width), BF16)], own_state, far_state, near_state)
    (far_tokens,) = call(pair_kernel, [((4 * rows, width), BF16)], message, far_tokens)
    cot_yc = near(after(cot_y, far_tokens), bits=1)
    far_tokens = near(far_tokens, bits=2)
    before, _ = doubling(slab_kv, 22 * 10**8)
    weights = (columns, *w_far)
    dnormed, cots = call(
        functools.partial(dnormed_kernel, dp, (0, 1, 2)),
        [((3, rows, width), F32), ((3, rows, outputs), BF16)], cot, message, cot_y, *weights,
    )
    dnormed_b, cot_b = call(
        functools.partial(dnormed_kernel, dp, (3,)),
        [((1, rows, width), F32), ((1, rows, outputs), BF16)], cot_yc, *weights,
    )
    (base,) = call(base_kernel, [((DH, width), F32)], *before, cost=10**9)
    w_all = [x for w in w_far for x in (w, near(after(w, dnormed), bits=1))]
    tokens = (own_tokens, message, far_tokens)
    normed, mixed, prior = call(
        mixed_kernel,
        [((SLAB, rows, width), BF16), ((SLAB, rows, width), F32), ((SLAB, DH, width), BF16)],
        *tokens, own_state, far_state, near_state, base, cost=10**10,
        scratch=[pltpu.VMEM((SLAB, DH, width), F32)],
    )
    tuned = dp == 2 and slabs == 4 and outputs // (dp * seq) % 8 == 0
    piece = outputs // (dp * slabs)
    if tuned:
        (send,) = call(
            functools.partial(product_kernel, slabs, 1), [((outputs // dp, width), BF16)], cots, cot_b, normed
        )
        got = flip(send, "dp", dp, 1)
    back, back_far, u, slab_u = call(
        middle_kernel,
        [((2 * rows + 2 * DH, width), BF16)] * 2 + [((SLAB, DH, width), F32), ((DH, width), BF16)],
        *tokens, mixed, prior, dnormed, dnormed_b,
    )
    if tuned:
        (keep,) = call(
            functools.partial(product_kernel, slabs, 0), [((outputs // dp, width), F32)], cots, cot_b, normed
        )
    back_far = near(back_far, bits=2)
    if tuned:
        keep, send = call(
            split_kernel, [((2 * piece, width), F32), ((2 * piece, width), BF16)], keep, got, wait=w_all[1::2]
        )
        got = near(send, bits=SLAB)
    behind, last_u = doubling(slab_u, 10**9)
    (send,) = call(relay_kernel, [((2 * rows + 2 * DH, width), BF16)], back, back_far)
    back_core = near(send, bits=1)
    if tuned:
        keep, send = call(
            split_again_kernel, [((piece, width), F32), ((piece, width), BF16)], keep, got, cost=3 * 10**9
        )
        got = near(send, bits=2 * SLAB)
    later, later_far = call(
        later_kernel, [((2 * DH, width), BF16)] * 2, *behind, u,
        scratch=[pltpu.VMEM((SLAB, DH, width), F32)],
    )
    later_far = near(later_far, bits=2)
    gq, gk_part, gv_part = call(
        late_kernel,
        [((rows, features), BF16), ((SLAB, rows, width), F32), ((SLAB, rows, width), F32)],
        back, back_far, back_core, q, k, v, attend,
    )
    if tuned:
        keep, share = call(
            share_kernel, [((piece // 2, width), BF16)] * 2, keep, got, cost=3 * 10**9,
            scratch=[pltpu.VMEM((piece, width), F32)],
        )
        got = near(share, bits=2)
    (send,) = call(relay_kernel, [((2 * DH, width), BF16)], later, later_far)
    later_core = near(send, bits=1)
    output, own_normed = call(
        output_kernel, [((rows, outputs), BF16), ((rows, features), BF16)],
        back, back_far, back_core, q, own_tokens, *sent, out_weight, *w_all, end=True,
    )
    if tuned:
        keep, share = call(
            pass_kernel, [((piece // 2, width), BF16)] * 2, keep, got, cost=3 * 10**9,
            wait=[pltpu.with_memory_space_constraint(x, pltpu.HBM) for x in (output,)],
        )
        got = near(share, bits=1)
    gk, gv = call(
        last_kernel, [((rows, features), BF16)] * 2,
        later, later_far, later_core, k, v, gk_part, gv_part, end=True,
    )
    if tuned:
        (grad_weight,) = call(
            functools.partial(finish_kernel, factor),
            [((piece // SLAB, features), F32)], keep, got, end=True,
            wait=[pltpu.with_memory_space_constraint(gk, pltpu.HBM)],
        )
    else:
        partial = dot(cot, own_normed, 0, 0) * factor
        grad_weight = lax.psum_scatter(partial, ("dp", "seq"), scatter_dimension=0, tiled=True)
    shape = queries.shape
    return (
        output.reshape(cotangent.shape), gq.reshape(shape), gk.reshape(shape), gv.reshape(shape),
        grad_weight,
    )


def solution(mesh):
    dp, seq = mesh.shape["dp"], mesh.shape["seq"]
    return jax.shard_map(
        functools.partial(local, dp=dp, seq=seq),
        mesh=mesh,
        in_specs=(P("dp", "seq", None),) * 4 + (P("dp", None),),
        out_specs=(P("dp", "seq", None),) * 4 + (P(("dp", "seq"), None),),
        check_vma=False,
    )
```

```python
import functools
import math

import jax
import jax.numpy as jnp
from jax import lax
from jax.experimental import pallas as pl
from jax.experimental.pallas import tpu as pltpu
from jax.sharding import PartitionSpec as P

DH = 128
SLAB = 4
EPSILON = 1e-05
BF16 = jnp.bfloat16
F32 = jnp.float32


def dot(left, right, left_dim, right_dim):
    return lax.dot_general(
        left, right, (((left_dim,), (right_dim,)), ((), ())), preferred_element_type=F32
    )


class Chain:
    def __init__(self):
        self.last = None

    def __call__(self, body, outs, *args, scratch=(), far=False, wait=(), cost=1, end=False):
        count = len(args)
        if far:
            args = [pltpu.with_memory_space_constraint(x, pltpu.HBM) for x in args]
        specs = [pl.BlockSpec(memory_space=pl.ANY) if far else pl.BlockSpec()] * count
        inner = body
        if self.last is not None:
            extra = (self.last, *wait)
            args = (*args, *extra)
            specs = [*specs, *[pl.BlockSpec(memory_space=pl.ANY)] * len(extra)]

            def inner(*refs):
                body(*refs[:count], *refs[count + len(extra) :])

        found = pl.pallas_call(
            inner,
            out_shape=[jax.ShapeDtypeStruct(s, d) for s, d in outs],
            in_specs=specs,
            scratch_shapes=list(scratch),
            cost_estimate=pl.CostEstimate(flops=cost, bytes_accessed=1, transcendentals=0),
            compiler_params=pltpu.CompilerParams(vmem_limit_bytes=32 * 2**20),
        )(*args)
        if not end:
            self.last = min(reversed(found), key=lambda x: x.size)
        return found


def after(x, *others):
    return lax.optimization_barrier((x, *others))[0]


def flip(x, axis, count, bits):
    return lax.ppermute(x, axis, [(i, i ^ bits) for i in range(count)])


def head(h):
    return slice(h * DH, (h + 1) * DH)


def part(i, size):
    return slice(i * size, (i + 1) * size)


def cut(start, size):
    return pl.ds(pl.multiple_of(start * size, size), size)


def member(r):
    return jnp.bitwise_xor(lax.rem(lax.axis_index("seq"), SLAB), r)


def causal(block):
    rows = lax.broadcasted_iota(jnp.int32, (block, block), 0)
    return lax.broadcasted_iota(jnp.int32, (block, block), 1) <= rows


def fetch(pairs, sems):
    copies = [pltpu.make_async_copy(a, b, sems.at[i]) for i, (a, b) in enumerate(pairs)]
    for copy in copies:
        copy.start()
    return copies


def front_kernel(k_hbm, v_hbm, w_hbm, own_ref, near_ref, far_ref, columns_ref, k_ref, v_ref, w_ref, sems):
    copies = fetch([(k_hbm, k_ref), (v_hbm, v_ref), (w_hbm, w_ref)], sems)
    width = k_ref.shape[1] // SLAB
    copies[0].wait()
    copies[1].wait()
    places = (own_ref, near_ref, far_ref.at[part(0, DH)], far_ref.at[part(1, DH)])
    for r, out in enumerate(places):
        k, v = k_ref[:, cut(member(r), width)], v_ref[:, cut(member(r), width)]
        for h in range(width // DH):
            out[:, head(h)] = dot(k[:, head(h)], v[:, head(h)], 0, 0).astype(out.dtype)
    copies[2].wait()
    for i in range(2):
        columns_ref[i] = w_ref[:, cut(member(2 * i), width)]


def pack_kernel(q_ref, k_ref, v_ref, c_ref, attend_ref, own_ref, message_ref, far_ref):
    block = q_ref.shape[0]
    width = q_ref.shape[1] // SLAB
    mask = causal(block)
    places = (own_ref, message_ref.at[: 2 * block], far_ref, message_ref.at[2 * block : 4 * block])
    for r, out in enumerate(places):
        q, k, v = (ref[:, cut(member(r), width)] for ref in (q_ref, k_ref, v_ref))
        out[:block, :] = q
        for h in range(width // DH):
            attend = jnp.where(mask, dot(q[:, head(h)], k[:, head(h)], 1, 1), 0.0).astype(BF16)
            attend_ref[r, h] = attend
            out[block:, head(h)] = dot(attend, v[:, head(h)], 1, 0).astype(BF16)
    for i in range(c_ref.shape[1] // width):
        message_ref[part(4 + i, block), :] = c_ref[:, part(i, width)]


def cross_kernel(near_ref, got_ref, out_ref):
    out_ref[part(0, DH), :] = near_ref[...]
    out_ref[part(1, DH), :] = got_ref[part(1, DH), :]


def total_kernel(own_ref, far_ref, near_ref, out_ref):
    total = own_ref[...] + far_ref[part(0, DH), :].astype(F32)
    total = total + near_ref[part(0, DH), :].astype(F32) + near_ref[part(1, DH), :].astype(F32)
    out_ref[...] = total.astype(BF16)


def pair_kernel(message_ref, far_ref, out_ref):
    size = far_ref.shape[0]
    out_ref[:size, :] = far_ref[...]
    out_ref[size:, :] = message_ref[part(1, size), :]


def add_kernel(own_ref, got_ref, out_ref):
    out_ref[...] = (own_ref[...].astype(F32) + got_ref[...].astype(F32)).astype(out_ref.dtype)


def dnormed_kernel(groups, members, *refs):
    cots, weights = refs[: len(members)], refs[len(members) : len(members) + groups]
    dnormed_ref, cot_ref = refs[len(members) + groups :]
    _, block, outputs = cot_ref.shape
    width = dnormed_ref.shape[2]
    rows = weights[0].shape[1]
    me = lax.axis_index("dp")
    for i, (r, ref) in enumerate(zip(members, cots)):
        if r == 1:
            for p in range(outputs // width):
                cot_ref[i, :, part(p, width)] = ref[part(4 + p, block), :]
        else:
            cot_ref[i] = ref[...]
        total = dot(cot_ref[i, :, cut(me, rows)], weights[0][0], 1, 0)
        for j in range(1, groups):
            total = total + dot(cot_ref[i, :, cut(jnp.bitwise_xor(me, j), rows)], weights[j][0], 1, 0)
        dnormed_ref[i] = total


def base_kernel(*refs):
    refs[-1][...] = from_slabs(False, refs[:-1])


def from_slabs(backward, refs):
    slab = lax.div(lax.axis_index("seq"), SLAB)
    total = jnp.zeros(refs[0].shape, F32)
    for i, ref in enumerate(refs):
        bit = lax.rem(lax.div(slab, 1 << i), 2)
        total = total + jnp.where(bit == (0 if backward else 1), ref[...].astype(F32), 0.0)
    return total


def mixed_kernel(
    own_ref, message_ref, token_far, own_state, far_state, near_state, base_ref,
    normed_ref, mixed_ref, prior_ref, running,
):
    _, block, width = normed_ref.shape
    size = 2 * block
    tokens = (own_ref, message_ref.at[:size], token_far.at[:size], token_far.at[size:])
    running[member(0)] = own_state[...]
    running[member(1)] = near_state[part(0, DH), :].astype(F32)
    running[member(2)] = far_state[part(0, DH), :].astype(F32)
    running[member(3)] = near_state[part(1, DH), :].astype(F32)
    total = base_ref[...]
    for p in range(SLAB):
        total, running[p] = total + running[p], total
    for r in range(SLAB):
        prior = running[member(r)].astype(BF16)
        prior_ref[r] = prior
        for h in range(width // DH):
            q = tokens[r][:block, head(h)]
            mixed = tokens[r][block:, head(h)].astype(F32) + dot(q, prior[:, head(h)], 1, 0)
            scale = lax.rsqrt(jnp.mean(mixed * mixed, axis=-1, keepdims=True) + EPSILON)
            mixed_ref[r, :, head(h)] = mixed
            normed_ref[r, :, head(h)] = (mixed * scale).astype(BF16)


def middle_kernel(
    own_ref, message_ref, token_far, mixed_ref, prior_ref, dnormed_a, dnormed_b,
    near_ref, far_ref, u_ref, slab_ref,
):
    _, block, width = mixed_ref.shape
    size = 2 * block
    tokens = (own_ref, message_ref.at[:size], token_far.at[:size], token_far.at[size:])
    sums = [jnp.zeros((DH, DH), F32)] * (width // DH)
    for r in range(SLAB):
        out = (near_ref, far_ref)[r // 2].at[part(r % 2, block + DH)]
        out[block:, :] = prior_ref[r]
        for h in range(width // DH):
            mixed = mixed_ref[r, :, head(h)]
            scale = lax.rsqrt(jnp.mean(mixed * mixed, axis=-1, keepdims=True) + EPSILON)
            normed = mixed * scale
            dnormed = dnormed_a[r, :, head(h)] if r < 3 else dnormed_b[0, :, head(h)]
            along = jnp.mean(dnormed * normed, axis=-1, keepdims=True)
            dmixed = ((dnormed - normed * along) * scale).astype(BF16)
            out[:block, head(h)] = dmixed
            u = dot(tokens[r][:block, head(h)], dmixed, 0, 0)
            u_ref[r, :, head(h)] = u
            sums[h] = sums[h] + u
    for h in range(width // DH):
        slab_ref[:, head(h)] = sums[h].astype(BF16)


def later_kernel(*refs):
    *behind, u_ref, near_ref, far_ref, running = refs
    for r in range(SLAB):
        running[member(r)] = u_ref[r]
    total = from_slabs(True, behind)
    for p in reversed(range(SLAB)):
        total, running[p] = total + running[p], total
    for r in range(SLAB):
        (near_ref, far_ref)[r // 2][part(r % 2, DH), :] = running[member(r)].astype(BF16)


def relay_kernel(near_ref, far_ref, out_ref):
    size = near_ref.shape[0] // 2
    out_ref[:size, :] = near_ref[size:, :]
    out_ref[size:, :] = far_ref[size:, :]


def arrived(near_ref, far_ref, core_ref):
    size = near_ref.shape[0] // 2
    first, second = slice(0, size), slice(size, 2 * size)
    return near_ref.at[first], core_ref.at[first], far_ref.at[first], core_ref.at[second]


def late_kernel(near_ref, far_ref, core_ref, q_ref, k_ref, v_ref, attend_ref, gq_ref, gk_ref, gv_ref):
    backs = arrived(near_ref, far_ref, core_ref)
    block, width = q_ref.shape[0], near_ref.shape[1]
    mask = causal(block)
    for r in range(SLAB):
        at = cut(member(r), width)
        q, k, v = q_ref[:, at], k_ref[:, at], v_ref[:, at]
        gqs, gks, gvs = [], [], []
        for h in range(width // DH):
            dmixed, prior = backs[r][:block, head(h)], backs[r][block:, head(h)]
            back = jnp.where(mask, dot(dmixed, v[:, head(h)], 1, 1), 0.0).astype(BF16)
            gqs.append(dot(back, k[:, head(h)], 1, 0) + dot(dmixed, prior, 1, 1))
            gks.append(dot(back, q[:, head(h)], 0, 0))
            gvs.append(dot(attend_ref[r, h], dmixed, 0, 0))
        gq_ref[:, at] = jnp.concatenate(gqs, axis=1).astype(BF16)
        gk_ref[r] = jnp.concatenate(gks, axis=1)
        gv_ref[r] = jnp.concatenate(gvs, axis=1)


def output_kernel(near_ref, back_far, core_ref, q_ref, own_ref, message_ref, far_ref, weight_ref, *refs):
    *far, out_ref, normed_ref = refs
    backs = arrived(near_ref, back_far, core_ref)
    block, width = q_ref.shape[0], near_ref.shape[1]
    rows = weight_ref.shape[0]
    me = lax.axis_index("dp")
    withins = (own_ref.at[part(1, block)], message_ref.at[part(1, block)],
               far_ref.at[part(1, block)], message_ref.at[part(3, block)])
    totals = [jnp.zeros((block, rows), F32)] * (len(far) // 2)
    for r in range(SLAB):
        at = cut(member(r), width)
        q = q_ref[:, at]
        normeds = []
        for h in range(width // DH):
            mixed = withins[r][:, head(h)].astype(F32) + dot(q[:, head(h)], backs[r][block:, head(h)], 1, 0)
            scale = lax.rsqrt(jnp.mean(mixed * mixed, axis=-1, keepdims=True) + EPSILON)
            normeds.append(mixed * scale)
        normed = jnp.concatenate(normeds, axis=1).astype(BF16)
        normed_ref[:, at] = normed
        for j in range(len(totals)):
            totals[j] = totals[j] + dot(normed, far[2 * j + r % 2][r // 2], 1, 1)
    out_ref[:, cut(me, rows)] = dot(normed_ref[...], weight_ref[...], 1, 1).astype(BF16)
    for j, total in enumerate(totals, 1):
        out_ref[:, cut(jnp.bitwise_xor(me, j), rows)] = total.astype(BF16)


def last_kernel(near_ref, far_ref, core_ref, k_ref, v_ref, gk_part, gv_part, gk_ref, gv_ref):
    laters = arrived(near_ref, far_ref, core_ref)
    width = near_ref.shape[1]
    for r in range(SLAB):
        at = cut(member(r), width)
        k, v = k_ref[:, at], v_ref[:, at]
        gks, gvs = [], []
        for h in range(width // DH):
            later = laters[r][:, head(h)]
            gks.append(gk_part[r, :, head(h)] + dot(v[:, head(h)], later, 1, 1))
            gvs.append(gv_part[r, :, head(h)] + dot(k[:, head(h)], later, 1, 0))
        gk_ref[:, at] = jnp.concatenate(gks, axis=1).astype(BF16)
        gv_ref[:, at] = jnp.concatenate(gvs, axis=1).astype(BF16)


def product_kernel(slabs, j, cot_a, cot_b, normed_ref, out_ref):
    me = lax.axis_index("dp")
    slab = lax.div(lax.axis_index("seq"), SLAB)
    rows = out_ref.shape[0] // slabs
    for d in range(slabs):
        at = jnp.bitwise_xor(me, j) * slabs + jnp.bitwise_xor(slab, d)
        total = dot(cot_b[0, :, cut(at, rows)], normed_ref[3], 0, 0)
        for r in range(3):
            total = total + dot(cot_a[r, :, cut(at, rows)], normed_ref[r], 0, 0)
        out_ref[part(d, rows), :] = total.astype(out_ref.dtype)


def split_kernel(own_ref, got_ref, keep_ref, send_ref):
    rows = keep_ref.shape[0] // 2
    for i in range(4):
        total = own_ref[part(i, rows), :] + got_ref[part(i, rows), :].astype(F32)
        out = (keep_ref, send_ref)[i % 2]
        out[part(i // 2, rows), :] = total.astype(out.dtype)


def split_again_kernel(own_ref, got_ref, keep_ref, send_ref):
    rows = keep_ref.shape[0]
    for i, out in enumerate((keep_ref, send_ref)):
        total = own_ref[part(i, rows), :] + got_ref[part(i, rows), :].astype(F32)
        out[...] = total.astype(out.dtype)


def share_kernel(own_ref, got_ref, keep_ref, send_ref, total_ref):
    total_ref[...] = own_ref[...] + got_ref[...].astype(F32)
    rows = keep_ref.shape[0] // 2
    for i, r in enumerate((0, 1)):
        keep_ref[part(i, rows), :] = total_ref[cut(member(r), rows), :].astype(BF16)
    for i, r in enumerate((2, 3)):
        send_ref[part(i, rows), :] = total_ref[cut(member(r), rows), :].astype(BF16)


def pass_kernel(own_ref, got_ref, keep_ref, send_ref):
    rows = own_ref.shape[0] // 2
    for i, ref in enumerate((own_ref, got_ref)):
        keep_ref[part(i, rows), :] = ref[:rows, :]
        send_ref[part(i, rows), :] = ref[rows:, :]


def finish_kernel(factor, keep_ref, got_ref, out_ref):
    rows, width = out_ref.shape[0], keep_ref.shape[1]
    for i, ref in enumerate((keep_ref, got_ref)):
        for j in range(2):
            out_ref[:, cut(member(i + 2 * j), width)] = ref[part(j, rows), :].astype(F32) * factor


def local(queries, keys, values, cotangent, out_weight, *, dp, seq):
    call = Chain()
    local_seqs, block, features = queries.shape
    outputs = cotangent.shape[2]
    rows = local_seqs * block
    slabs = seq // SLAB
    width = features // SLAB
    heads = width // DH
    q, k, v = (x.reshape(rows, features) for x in (queries, keys, values))
    cot = cotangent.reshape(rows, outputs)
    factor = 1.0 / math.sqrt(rows * dp * seq)
    near = functools.partial(flip, axis="seq", count=seq)

    def doubling(total, backward, price=1):
        found = []
        bits = SLAB
        while bits < seq:
            if found:
                (total,) = call(add_kernel, [(total.shape, BF16)], total, found[-1], cost=price)
            last = 2 * bits >= seq
            pairs = [(i, i ^ bits) for i in range(seq) if not last or bool(i & bits) == backward]
            found.append(lax.ppermute(total, "seq", pairs))
            bits *= 2
        return found, total

    def scratch(*arrays):
        return [pltpu.VMEM(x.shape, BF16) for x in arrays] + [pltpu.SemaphoreType.DMA((len(arrays),))]

    own_state, near_state, far_state, columns = call(
        front_kernel,
        [((DH, width), F32), ((DH, width), BF16), ((2 * DH, width), BF16),
         ((2, out_weight.shape[0], width), BF16)],
        k, v, out_weight, far=True, scratch=scratch(k, v, out_weight),
    )
    far_state = near(far_state, bits=2)
    w_far = [flip(columns, "dp", dp, j) for j in range(1, dp)]
    attend, own_tokens, message, far_tokens = call(
        pack_kernel,
        [((SLAB, heads, rows, rows), BF16), ((2 * rows, width), BF16),
         (((4 + outputs // width) * rows, width), BF16), ((2 * rows, width), BF16)],
        q, k, v, cot,
    )
    cot_y = near(cot, bits=2)
    near_tokens, sent = message, (message, far_tokens)
    message = near(message, bits=1)
    (near_state,) = call(
        cross_kernel, [((2 * DH, width), BF16)], near_state, far_state, cost=5 * 10**9
    )
    near_state = near(near_state, bits=1)
    (slab_kv,) = call(total_kernel, [((DH, width), BF16)], own_state, far_state, near_state)
    (far_tokens,) = call(pair_kernel, [((4 * rows, width), BF16)], message, far_tokens)
    cot_yc = near(after(cot_y, far_tokens), bits=1)
    far_tokens = near(far_tokens, bits=2)
    before, _ = doubling(slab_kv, False, 22 * 10**8)
    weights = (columns, *w_far)
    dnormed, cots = call(
        functools.partial(dnormed_kernel, dp, (0, 1, 2)),
        [((3, rows, width), F32), ((3, rows, outputs), BF16)], cot, message, cot_y, *weights,
    )
    dnormed_b, cot_b = call(
        functools.partial(dnormed_kernel, dp, (3,)),
        [((1, rows, width), F32), ((1, rows, outputs), BF16)], cot_yc, *weights,
    )
    (base,) = call(base_kernel, [((DH, width), F32)], *before, cost=10**9)
    w_all = [x for w in w_far for x in (w, near(after(w, dnormed), bits=1))]
    tokens = (own_tokens, message, far_tokens)
    normed, mixed, prior = call(
        mixed_kernel,
        [((SLAB, rows, width), BF16), ((SLAB, rows, width), F32), ((SLAB, DH, width), BF16)],
        *tokens, own_state, far_state, near_state, base, cost=10**10,
        scratch=[pltpu.VMEM((SLAB, DH, width), F32)],
    )
    tuned = dp == 2 and slabs == 4 and outputs // (dp * seq) % 8 == 0
    piece = outputs // (dp * slabs)
    if tuned:
        (send,) = call(
            functools.partial(product_kernel, slabs, 1), [((outputs // dp, width), BF16)], cots, cot_b, normed
        )
        got = flip(send, "dp", dp, 1)
    back, back_far, u, slab_u = call(
        middle_kernel,
        [((2 * rows + 2 * DH, width), BF16)] * 2 + [((SLAB, DH, width), F32), ((DH, width), BF16)],
        *tokens, mixed, prior, dnormed, dnormed_b,
    )
    if tuned:
        (keep,) = call(
            functools.partial(product_kernel, slabs, 0), [((outputs // dp, width), F32)], cots, cot_b, normed
        )
    back_far = near(back_far, bits=2)
    if tuned:
        keep, send = call(
            split_kernel, [((2 * piece, width), F32), ((2 * piece, width), BF16)], keep, got, wait=w_all[1::2]
        )
        got = near(send, bits=SLAB)
    behind, last_u = doubling(slab_u, True, 10**9)
    (send,) = call(relay_kernel, [((2 * rows + 2 * DH, width), BF16)], back, back_far)
    back_core = near(send, bits=1)
    if tuned:
        keep, send = call(
            split_again_kernel, [((piece, width), F32), ((piece, width), BF16)], keep, got, cost=3 * 10**9
        )
        got = near(send, bits=2 * SLAB)
    later, later_far = call(
        later_kernel, [((2 * DH, width), BF16)] * 2, *behind, u,
        scratch=[pltpu.VMEM((SLAB, DH, width), F32)],
    )
    later_far = near(later_far, bits=2)
    gq, gk_part, gv_part = call(
        late_kernel,
        [((rows, features), BF16), ((SLAB, rows, width), F32), ((SLAB, rows, width), F32)],
        back, back_far, back_core, q, k, v, attend,
    )
    if tuned:
        keep, share = call(
            share_kernel, [((piece // 2, width), BF16)] * 2, keep, got, cost=3 * 10**9,
            scratch=[pltpu.VMEM((piece, width), F32)],
        )
        got = near(share, bits=2)
    (send,) = call(relay_kernel, [((2 * DH, width), BF16)], later, later_far)
    later_core = near(send, bits=1)
    output, own_normed = call(
        output_kernel, [((rows, outputs), BF16), ((rows, features), BF16)],
        back, back_far, back_core, q, own_tokens, *sent, out_weight, *w_all, end=True,
    )
    if tuned:
        keep, share = call(
            pass_kernel, [((piece // 2, width), BF16)] * 2, keep, got, cost=3 * 10**9,
            wait=[pltpu.with_memory_space_constraint(x, pltpu.HBM) for x in (output,)],
        )
        got = near(share, bits=1)
    gk, gv = call(
        last_kernel, [((rows, features), BF16)] * 2,
        later, later_far, later_core, k, v, gk_part, gv_part, end=True,
    )
    if tuned:
        (grad_weight,) = call(
            functools.partial(finish_kernel, factor),
            [((piece // SLAB, features), F32)], keep, got, end=True,
            wait=[pltpu.with_memory_space_constraint(gk, pltpu.HBM)],
        )
    else:
        partial = dot(cot, own_normed, 0, 0) * factor
        grad_weight = lax.psum_scatter(partial, ("dp", "seq"), scatter_dimension=0, tiled=True)
    shape = queries.shape
    return (
        output.reshape(cotangent.shape), gq.reshape(shape), gk.reshape(shape), gv.reshape(shape),
        grad_weight,
    )


def solution(mesh):
    dp, seq = mesh.shape["dp"], mesh.shape["seq"]
    return jax.shard_map(
        functools.partial(local, dp=dp, seq=seq),
        mesh=mesh,
        in_specs=(P("dp", "seq", None),) * 4 + (P("dp", None),),
        out_specs=(P("dp", "seq", None),) * 4 + (P(("dp", "seq"), None),),
        check_vma=False,
    )
```

```python
import functools
import math

import jax
import jax.numpy as jnp
from jax import lax
from jax.experimental import pallas as pl
from jax.experimental.pallas import tpu as pltpu
from jax.sharding import PartitionSpec as P

DH = 128
SLAB = 4
EPSILON = 1e-05
BF16 = jnp.bfloat16
F32 = jnp.float32


def dot(left, right, left_dim, right_dim):
    return lax.dot_general(
        left, right, (((left_dim,), (right_dim,)), ((), ())), preferred_element_type=F32
    )


class Chain:
    def __init__(self):
        self.last = None

    def __call__(self, body, outs, *args, scratch=(), far=False, wait=(), cost=1, end=False):
        count = len(args)
        if far:
            args = [pltpu.with_memory_space_constraint(x, pltpu.HBM) for x in args]
        specs = [pl.BlockSpec(memory_space=pl.ANY) if far else pl.BlockSpec()] * count
        inner = body
        if self.last is not None:
            extra = (self.last, *wait)
            args = (*args, *extra)
            specs = [*specs, *[pl.BlockSpec(memory_space=pl.ANY)] * len(extra)]

            def inner(*refs):
                body(*refs[:count], *refs[count + len(extra) :])

        found = pl.pallas_call(
            inner,
            out_shape=[jax.ShapeDtypeStruct(s, d) for s, d in outs],
            in_specs=specs,
            scratch_shapes=list(scratch),
            cost_estimate=pl.CostEstimate(flops=cost, bytes_accessed=1, transcendentals=0),
            compiler_params=pltpu.CompilerParams(vmem_limit_bytes=32 * 2**20),
        )(*args)
        if not end:
            self.last = min(reversed(found), key=lambda x: x.size)
        return found


def after(x, *others):
    return lax.optimization_barrier((x, *others))[0]


def flip(x, axis, count, bits):
    return lax.ppermute(x, axis, [(i, i ^ bits) for i in range(count)])


def head(h):
    return slice(h * DH, (h + 1) * DH)


def part(i, size):
    return slice(i * size, (i + 1) * size)


def cut(start, size):
    return pl.ds(pl.multiple_of(start * size, size), size)


def member(r):
    return jnp.bitwise_xor(lax.rem(lax.axis_index("seq"), SLAB), r)


def causal(block):
    rows = lax.broadcasted_iota(jnp.int32, (block, block), 0)
    return lax.broadcasted_iota(jnp.int32, (block, block), 1) <= rows


def fetch(pairs, sems):
    copies = [pltpu.make_async_copy(a, b, sems.at[i]) for i, (a, b) in enumerate(pairs)]
    for copy in copies:
        copy.start()
    return copies


def front_kernel(k_hbm, v_hbm, w_hbm, own_ref, near_ref, far_ref, columns_ref, k_ref, v_ref, sems):
    width = k_ref.shape[1] // SLAB
    blocks = [(w_hbm.at[:, cut(member(2 * i), width)], columns_ref.at[i]) for i in range(2)]
    copies = fetch([(k_hbm, k_ref), (v_hbm, v_ref), *blocks], sems)
    copies[0].wait()
    copies[1].wait()
    places = (own_ref, near_ref, far_ref.at[part(0, DH)], far_ref.at[part(1, DH)])
    for r, out in enumerate(places):
        k, v = k_ref[:, cut(member(r), width)], v_ref[:, cut(member(r), width)]
        for h in range(width // DH):
            out[:, head(h)] = dot(k[:, head(h)], v[:, head(h)], 0, 0).astype(out.dtype)
    copies[2].wait()
    copies[3].wait()


def pack_kernel(q_ref, k_ref, v_ref, c_ref, attend_ref, own_ref, message_ref, far_ref):
    block = q_ref.shape[0]
    width = q_ref.shape[1] // SLAB
    mask = causal(block)
    places = (own_ref, message_ref.at[: 2 * block], far_ref, message_ref.at[2 * block : 4 * block])
    for r, out in enumerate(places):
        q, k, v = (ref[:, cut(member(r), width)] for ref in (q_ref, k_ref, v_ref))
        out[:block, :] = q
        for h in range(width // DH):
            attend = jnp.where(mask, dot(q[:, head(h)], k[:, head(h)], 1, 1), 0.0).astype(BF16)
            attend_ref[r, h] = attend
            out[block:, head(h)] = dot(attend, v[:, head(h)], 1, 0).astype(BF16)
    for i in range(c_ref.shape[1] // width):
        message_ref[part(4 + i, block), :] = c_ref[:, part(i, width)]


def cross_kernel(near_ref, got_ref, out_ref):
    out_ref[part(0, DH), :] = near_ref[...]
    out_ref[part(1, DH), :] = got_ref[part(1, DH), :]


def total_kernel(own_ref, far_ref, near_ref, out_ref):
    total = own_ref[...] + far_ref[part(0, DH), :].astype(F32)
    total = total + near_ref[part(0, DH), :].astype(F32) + near_ref[part(1, DH), :].astype(F32)
    out_ref[...] = total.astype(BF16)


def pair_kernel(message_ref, far_ref, out_ref):
    size = far_ref.shape[0]
    out_ref[:size, :] = far_ref[...]
    out_ref[size:, :] = message_ref[part(1, size), :]


def add_kernel(own_ref, got_ref, out_ref):
    out_ref[...] = (own_ref[...].astype(F32) + got_ref[...].astype(F32)).astype(out_ref.dtype)


def dnormed_kernel(groups, members, *refs):
    cots, weights = refs[: len(members)], refs[len(members) : len(members) + groups]
    dnormed_ref, cot_ref = refs[len(members) + groups :]
    _, block, outputs = cot_ref.shape
    width = dnormed_ref.shape[2]
    rows = weights[0].shape[1]
    me = lax.axis_index("dp")
    for i, (r, ref) in enumerate(zip(members, cots)):
        if r == 1:
            for p in range(outputs // width):
                cot_ref[i, :, part(p, width)] = ref[part(4 + p, block), :]
        else:
            cot_ref[i] = ref[...]
        total = dot(cot_ref[i, :, cut(me, rows)], weights[0][0], 1, 0)
        for j in range(1, groups):
            total = total + dot(cot_ref[i, :, cut(jnp.bitwise_xor(me, j), rows)], weights[j][0], 1, 0)
        dnormed_ref[i] = total


def base_kernel(*refs):
    refs[-1][...] = from_slabs(False, refs[:-1])


def from_slabs(backward, refs):
    slab = lax.div(lax.axis_index("seq"), SLAB)
    total = jnp.zeros(refs[0].shape, F32)
    for i, ref in enumerate(refs):
        bit = lax.rem(lax.div(slab, 1 << i), 2)
        total = total + jnp.where(bit == (0 if backward else 1), ref[...].astype(F32), 0.0)
    return total


def mixed_kernel(
    own_ref, message_ref, token_far, own_state, far_state, near_state, base_ref,
    normed_ref, mixed_ref, prior_ref, running,
):
    _, block, width = normed_ref.shape
    size = 2 * block
    tokens = (own_ref, message_ref.at[:size], token_far.at[:size], token_far.at[size:])
    running[member(0)] = own_state[...]
    running[member(1)] = near_state[part(0, DH), :].astype(F32)
    running[member(2)] = far_state[part(0, DH), :].astype(F32)
    running[member(3)] = near_state[part(1, DH), :].astype(F32)
    total = base_ref[...]
    for p in range(SLAB):
        total, running[p] = total + running[p], total
    for r in range(SLAB):
        prior = running[member(r)].astype(BF16)
        prior_ref[r] = prior
        for h in range(width // DH):
            q = tokens[r][:block, head(h)]
            mixed = tokens[r][block:, head(h)].astype(F32) + dot(q, prior[:, head(h)], 1, 0)
            scale = lax.rsqrt(jnp.mean(mixed * mixed, axis=-1, keepdims=True) + EPSILON)
            mixed_ref[r, :, head(h)] = mixed
            normed_ref[r, :, head(h)] = (mixed * scale).astype(BF16)


def middle_kernel(
    own_ref, message_ref, token_far, mixed_ref, prior_ref, dnormed_a, dnormed_b,
    near_ref, far_ref, u_ref, slab_ref,
):
    _, block, width = mixed_ref.shape
    size = 2 * block
    tokens = (own_ref, message_ref.at[:size], token_far.at[:size], token_far.at[size:])
    sums = [jnp.zeros((DH, DH), F32)] * (width // DH)
    for r in range(SLAB):
        out = (near_ref, far_ref)[r // 2].at[part(r % 2, block + DH)]
        out[block:, :] = prior_ref[r]
        for h in range(width // DH):
            mixed = mixed_ref[r, :, head(h)]
            scale = lax.rsqrt(jnp.mean(mixed * mixed, axis=-1, keepdims=True) + EPSILON)
            normed = mixed * scale
            dnormed = dnormed_a[r, :, head(h)] if r < 3 else dnormed_b[0, :, head(h)]
            along = jnp.mean(dnormed * normed, axis=-1, keepdims=True)
            dmixed = ((dnormed - normed * along) * scale).astype(BF16)
            out[:block, head(h)] = dmixed
            u = dot(tokens[r][:block, head(h)], dmixed, 0, 0)
            u_ref[r, :, head(h)] = u
            sums[h] = sums[h] + u
    for h in range(width // DH):
        slab_ref[:, head(h)] = sums[h].astype(BF16)


def later_kernel(*refs):
    *behind, u_ref, near_ref, far_ref, running = refs
    for r in range(SLAB):
        running[member(r)] = u_ref[r]
    total = from_slabs(True, behind)
    for p in reversed(range(SLAB)):
        total, running[p] = total + running[p], total
    for r in range(SLAB):
        (near_ref, far_ref)[r // 2][part(r % 2, DH), :] = running[member(r)].astype(BF16)


def relay_kernel(near_ref, far_ref, out_ref):
    size = near_ref.shape[0] // 2
    out_ref[:size, :] = near_ref[size:, :]
    out_ref[size:, :] = far_ref[size:, :]


def arrived(near_ref, far_ref, core_ref):
    size = near_ref.shape[0] // 2
    first, second = slice(0, size), slice(size, 2 * size)
    return near_ref.at[first], core_ref.at[first], far_ref.at[first], core_ref.at[second]


def late_kernel(near_ref, far_ref, core_ref, q_ref, k_ref, v_ref, attend_ref, gq_ref, gk_ref, gv_ref):
    backs = arrived(near_ref, far_ref, core_ref)
    block, width = q_ref.shape[0], near_ref.shape[1]
    mask = causal(block)
    for r in range(SLAB):
        at = cut(member(r), width)
        q, k, v = q_ref[:, at], k_ref[:, at], v_ref[:, at]
        gqs, gks, gvs = [], [], []
        for h in range(width // DH):
            dmixed, prior = backs[r][:block, head(h)], backs[r][block:, head(h)]
            back = jnp.where(mask, dot(dmixed, v[:, head(h)], 1, 1), 0.0).astype(BF16)
            gqs.append(dot(back, k[:, head(h)], 1, 0) + dot(dmixed, prior, 1, 1))
            gks.append(dot(back, q[:, head(h)], 0, 0))
            gvs.append(dot(attend_ref[r, h], dmixed, 0, 0))
        gq_ref[:, at] = jnp.concatenate(gqs, axis=1).astype(BF16)
        gk_ref[r] = jnp.concatenate(gks, axis=1)
        gv_ref[r] = jnp.concatenate(gvs, axis=1)


def output_kernel(near_ref, back_far, core_ref, q_ref, own_ref, message_ref, far_ref, weight_ref, *refs):
    *far, out_ref, normed_ref = refs
    backs = arrived(near_ref, back_far, core_ref)
    block, width = q_ref.shape[0], near_ref.shape[1]
    rows = weight_ref.shape[0]
    me = lax.axis_index("dp")
    withins = (own_ref.at[part(1, block)], message_ref.at[part(1, block)],
               far_ref.at[part(1, block)], message_ref.at[part(3, block)])
    totals = [jnp.zeros((block, rows), F32)] * (len(far) // 2)
    for r in range(SLAB):
        at = cut(member(r), width)
        q = q_ref[:, at]
        normeds = []
        for h in range(width // DH):
            mixed = withins[r][:, head(h)].astype(F32) + dot(q[:, head(h)], backs[r][block:, head(h)], 1, 0)
            scale = lax.rsqrt(jnp.mean(mixed * mixed, axis=-1, keepdims=True) + EPSILON)
            normeds.append(mixed * scale)
        normed = jnp.concatenate(normeds, axis=1).astype(BF16)
        normed_ref[:, at] = normed
        for j in range(len(totals)):
            totals[j] = totals[j] + dot(normed, far[2 * j + r % 2][r // 2], 1, 1)
    out_ref[:, cut(me, rows)] = dot(normed_ref[...], weight_ref[...], 1, 1).astype(BF16)
    for j, total in enumerate(totals, 1):
        out_ref[:, cut(jnp.bitwise_xor(me, j), rows)] = total.astype(BF16)


def last_kernel(near_ref, far_ref, core_ref, k_ref, v_ref, gk_part, gv_part, gk_ref, gv_ref):
    laters = arrived(near_ref, far_ref, core_ref)
    width = near_ref.shape[1]
    for r in range(SLAB):
        at = cut(member(r), width)
        k, v = k_ref[:, at], v_ref[:, at]
        gks, gvs = [], []
        for h in range(width // DH):
            later = laters[r][:, head(h)]
            gks.append(gk_part[r, :, head(h)] + dot(v[:, head(h)], later, 1, 1))
            gvs.append(gv_part[r, :, head(h)] + dot(k[:, head(h)], later, 1, 0))
        gk_ref[:, at] = jnp.concatenate(gks, axis=1).astype(BF16)
        gv_ref[:, at] = jnp.concatenate(gvs, axis=1).astype(BF16)


def product_kernel(slabs, j, cot_a, cot_b, normed_ref, out_ref):
    me = lax.axis_index("dp")
    slab = lax.div(lax.axis_index("seq"), SLAB)
    rows = out_ref.shape[0] // slabs
    for d in range(slabs):
        at = jnp.bitwise_xor(me, j) * slabs + jnp.bitwise_xor(slab, d)
        total = dot(cot_b[0, :, cut(at, rows)], normed_ref[3], 0, 0)
        for r in range(3):
            total = total + dot(cot_a[r, :, cut(at, rows)], normed_ref[r], 0, 0)
        out_ref[part(d, rows), :] = total.astype(out_ref.dtype)


def split_kernel(own_ref, got_ref, keep_ref, send_ref):
    rows = keep_ref.shape[0] // 2
    for i in range(4):
        total = own_ref[part(i, rows), :] + got_ref[part(i, rows), :].astype(F32)
        out = (keep_ref, send_ref)[i % 2]
        out[part(i // 2, rows), :] = total.astype(out.dtype)


def split_again_kernel(own_ref, got_ref, keep_ref, send_ref):
    rows = keep_ref.shape[0]
    for i, out in enumerate((keep_ref, send_ref)):
        total = own_ref[part(i, rows), :] + got_ref[part(i, rows), :].astype(F32)
        out[...] = total.astype(out.dtype)


def share_kernel(own_ref, got_ref, keep_ref, send_ref, total_ref):
    total_ref[...] = own_ref[...] + got_ref[...].astype(F32)
    rows = keep_ref.shape[0] // 2
    for i, r in enumerate((0, 1)):
        keep_ref[part(i, rows), :] = total_ref[cut(member(r), rows), :].astype(BF16)
    for i, r in enumerate((2, 3)):
        send_ref[part(i, rows), :] = total_ref[cut(member(r), rows), :].astype(BF16)


def pass_kernel(own_ref, got_ref, keep_ref, send_ref):
    rows = own_ref.shape[0] // 2
    for i, ref in enumerate((own_ref, got_ref)):
        keep_ref[part(i, rows), :] = ref[:rows, :]
        send_ref[part(i, rows), :] = ref[rows:, :]


def finish_kernel(factor, keep_ref, got_ref, out_ref):
    rows, width = out_ref.shape[0], keep_ref.shape[1]
    for i, ref in enumerate((keep_ref, got_ref)):
        for j in range(2):
            out_ref[:, cut(member(i + 2 * j), width)] = ref[part(j, rows), :].astype(F32) * factor


def local(queries, keys, values, cotangent, out_weight, *, dp, seq):
    call = Chain()
    local_seqs, block, features = queries.shape
    outputs = cotangent.shape[2]
    rows = local_seqs * block
    slabs = seq // SLAB
    width = features // SLAB
    heads = width // DH
    q, k, v = (x.reshape(rows, features) for x in (queries, keys, values))
    cot = cotangent.reshape(rows, outputs)
    factor = 1.0 / math.sqrt(rows * dp * seq)
    near = functools.partial(flip, axis="seq", count=seq)

    def doubling(total, cost=1):
        found = []
        bits = SLAB
        while bits < seq:
            if found:
                (total,) = call(add_kernel, [(total.shape, BF16)], total, found[-1], cost=cost)
            found.append(near(total, bits=bits))
            bits *= 2
        return found, total

    def scratch(*arrays):
        return [pltpu.VMEM(x.shape, BF16) for x in arrays] + [pltpu.SemaphoreType.DMA((len(arrays),))]

    own_state, near_state, far_state, columns = call(
        front_kernel,
        [((DH, width), F32), ((DH, width), BF16), ((2 * DH, width), BF16),
         ((2, out_weight.shape[0], width), BF16)],
        k, v, out_weight, far=True, scratch=scratch(k, v)[:2] + [pltpu.SemaphoreType.DMA((4,))],
    )
    far_state = near(far_state, bits=2)
    w_far = [flip(columns, "dp", dp, j) for j in range(1, dp)]
    attend, own_tokens, message, far_tokens = call(
        pack_kernel,
        [((SLAB, heads, rows, rows), BF16), ((2 * rows, width), BF16),
         (((4 + outputs // width) * rows, width), BF16), ((2 * rows, width), BF16)],
        q, k, v, cot,
    )
    cot_y = near(cot, bits=2)
    near_tokens, sent = message, (message, far_tokens)
    message = near(message, bits=1)
    (near_state,) = call(
        cross_kernel, [((2 * DH, width), BF16)], near_state, far_state, cost=5 * 10**9
    )
    near_state = near(near_state, bits=1)
    (slab_kv,) = call(total_kernel, [((DH, width), BF16)], own_state, far_state, near_state)
    (far_tokens,) = call(pair_kernel, [((4 * rows, width), BF16)], message, far_tokens)
    cot_yc = near(after(cot_y, far_tokens), bits=1)
    far_tokens = near(far_tokens, bits=2)
    before, _ = doubling(slab_kv, 22 * 10**8)
    weights = (columns, *w_far)
    dnormed, cots = call(
        functools.partial(dnormed_kernel, dp, (0, 1, 2)),
        [((3, rows, width), F32), ((3, rows, outputs), BF16)], cot, message, cot_y, *weights,
    )
    dnormed_b, cot_b = call(
        functools.partial(dnormed_kernel, dp, (3,)),
        [((1, rows, width), F32), ((1, rows, outputs), BF16)], cot_yc, *weights,
    )
    (base,) = call(base_kernel, [((DH, width), F32)], *before, cost=10**9)
    w_all = [x for w in w_far for x in (w, near(after(w, dnormed), bits=1))]
    tokens = (own_tokens, message, far_tokens)
    normed, mixed, prior = call(
        mixed_kernel,
        [((SLAB, rows, width), BF16), ((SLAB, rows, width), F32), ((SLAB, DH, width), BF16)],
        *tokens, own_state, far_state, near_state, base, cost=10**10,
        scratch=[pltpu.VMEM((SLAB, DH, width), F32)],
    )
    tuned = dp == 2 and slabs == 4 and outputs // (dp * seq) % 8 == 0
    piece = outputs // (dp * slabs)
    if tuned:
        (send,) = call(
            functools.partial(product_kernel, slabs, 1), [((outputs // dp, width), BF16)], cots, cot_b, normed
        )
        got = flip(send, "dp", dp, 1)
    back, back_far, u, slab_u = call(
        middle_kernel,
        [((2 * rows + 2 * DH, width), BF16)] * 2 + [((SLAB, DH, width), F32), ((DH, width), BF16)],
        *tokens, mixed, prior, dnormed, dnormed_b,
    )
    if tuned:
        (keep,) = call(
            functools.partial(product_kernel, slabs, 0), [((outputs // dp, width), F32)], cots, cot_b, normed
        )
    back_far = near(back_far, bits=2)
    if tuned:
        keep, send = call(
            split_kernel, [((2 * piece, width), F32), ((2 * piece, width), BF16)], keep, got, wait=w_all[1::2]
        )
        got = near(send, bits=SLAB)
    behind, last_u = doubling(slab_u, 10**9)
    (send,) = call(relay_kernel, [((2 * rows + 2 * DH, width), BF16)], back, back_far)
    back_core = near(send, bits=1)
    if tuned:
        keep, send = call(
            split_again_kernel, [((piece, width), F32), ((piece, width), BF16)], keep, got, cost=3 * 10**9
        )
        got = near(send, bits=2 * SLAB)
    later, later_far = call(
        later_kernel, [((2 * DH, width), BF16)] * 2, *behind, u,
        scratch=[pltpu.VMEM((SLAB, DH, width), F32)],
    )
    later_far = near(later_far, bits=2)
    gq, gk_part, gv_part = call(
        late_kernel,
        [((rows, features), BF16), ((SLAB, rows, width), F32), ((SLAB, rows, width), F32)],
        back, back_far, back_core, q, k, v, attend,
    )
    if tuned:
        keep, share = call(
            share_kernel, [((piece // 2, width), BF16)] * 2, keep, got, cost=3 * 10**9,
            scratch=[pltpu.VMEM((piece, width), F32)],
        )
        got = near(share, bits=2)
    (send,) = call(relay_kernel, [((2 * DH, width), BF16)], later, later_far)
    later_core = near(send, bits=1)
    output, own_normed = call(
        output_kernel, [((rows, outputs), BF16), ((rows, features), BF16)],
        back, back_far, back_core, q, own_tokens, *sent, out_weight, *w_all, end=True,
    )
    if tuned:
        keep, share = call(
            pass_kernel, [((piece // 2, width), BF16)] * 2, keep, got, cost=3 * 10**9,
            wait=[pltpu.with_memory_space_constraint(x, pltpu.HBM) for x in (output,)],
        )
        got = near(share, bits=1)
    gk, gv = call(
        last_kernel, [((rows, features), BF16)] * 2,
        later, later_far, later_core, k, v, gk_part, gv_part, end=True,
    )
    if tuned:
        (grad_weight,) = call(
            functools.partial(finish_kernel, factor),
            [((piece // SLAB, features), F32)], keep, got, end=True,
            wait=[pltpu.with_memory_space_constraint(gk, pltpu.HBM)],
        )
    else:
        partial = dot(cot, own_normed, 0, 0) * factor
        grad_weight = lax.psum_scatter(partial, ("dp", "seq"), scatter_dimension=0, tiled=True)
    shape = queries.shape
    return (
        output.reshape(cotangent.shape), gq.reshape(shape), gk.reshape(shape), gv.reshape(shape),
        grad_weight,
    )


def solution(mesh):
    dp, seq = mesh.shape["dp"], mesh.shape["seq"]
    return jax.shard_map(
        functools.partial(local, dp=dp, seq=seq),
        mesh=mesh,
        in_specs=(P("dp", "seq", None),) * 4 + (P("dp", None),),
        out_specs=(P("dp", "seq", None),) * 4 + (P(("dp", "seq"), None),),
        check_vma=False,
    )
```

```python
import functools
import math

import jax
import jax.numpy as jnp
from jax import lax
from jax.experimental import pallas as pl
from jax.experimental.pallas import tpu as pltpu
from jax.sharding import PartitionSpec as P

DH = 128
SLAB = 4
EPSILON = 1e-05
BF16 = jnp.bfloat16
F32 = jnp.float32


def dot(left, right, left_dim, right_dim):
    return lax.dot_general(
        left, right, (((left_dim,), (right_dim,)), ((), ())), preferred_element_type=F32
    )


class Chain:
    def __init__(self):
        self.last = None

    def __call__(self, body, outs, *args, scratch=(), far=False, wait=(), cost=1, end=False):
        count = len(args)
        if far:
            args = [pltpu.with_memory_space_constraint(x, pltpu.HBM) for x in args]
        specs = [pl.BlockSpec(memory_space=pl.ANY) if far else pl.BlockSpec()] * count
        inner = body
        if self.last is not None:
            extra = (self.last, *wait)
            args = (*args, *extra)
            specs = [*specs, *[pl.BlockSpec(memory_space=pl.ANY)] * len(extra)]

            def inner(*refs):
                body(*refs[:count], *refs[count + len(extra) :])

        found = pl.pallas_call(
            inner,
            out_shape=[jax.ShapeDtypeStruct(s, d) for s, d in outs],
            in_specs=specs,
            scratch_shapes=list(scratch),
            cost_estimate=pl.CostEstimate(flops=cost, bytes_accessed=1, transcendentals=0),
            compiler_params=pltpu.CompilerParams(vmem_limit_bytes=32 * 2**20),
        )(*args)
        if not end:
            self.last = min(reversed(found), key=lambda x: x.size)
        return found


def after(x, *others):
    return lax.optimization_barrier((x, *others))[0]


def flip(x, axis, count, bits):
    return lax.ppermute(x, axis, [(i, i ^ bits) for i in range(count)])


def head(h):
    return slice(h * DH, (h + 1) * DH)


def part(i, size):
    return slice(i * size, (i + 1) * size)


def cut(start, size):
    return pl.ds(pl.multiple_of(start * size, size), size)


def member(r):
    return jnp.bitwise_xor(lax.rem(lax.axis_index("seq"), SLAB), r)


def causal(block):
    rows = lax.broadcasted_iota(jnp.int32, (block, block), 0)
    return lax.broadcasted_iota(jnp.int32, (block, block), 1) <= rows


def fetch(pairs, sems):
    copies = [pltpu.make_async_copy(a, b, sems.at[i]) for i, (a, b) in enumerate(pairs)]
    for copy in copies:
        copy.start()
    return copies


def front_kernel(k_hbm, v_hbm, w_hbm, own_ref, near_ref, far_ref, columns_ref, k_ref, v_ref, sems):
    width = k_ref.shape[1] // SLAB
    blocks = [(w_hbm.at[:, cut(member(2 * i), width)], columns_ref.at[i]) for i in range(2)]
    copies = fetch([(k_hbm, k_ref), (v_hbm, v_ref), *blocks], sems)
    copies[0].wait()
    copies[1].wait()
    places = (own_ref, near_ref, far_ref.at[part(0, DH)], far_ref.at[part(1, DH)])
    for r, out in enumerate(places):
        k, v = k_ref[:, cut(member(r), width)], v_ref[:, cut(member(r), width)]
        for h in range(width // DH):
            out[:, head(h)] = dot(k[:, head(h)], v[:, head(h)], 0, 0).astype(out.dtype)
    copies[2].wait()
    copies[3].wait()


def pack_kernel(q_ref, k_ref, v_ref, c_ref, attend_ref, own_ref, message_ref, far_ref):
    block = q_ref.shape[0]
    width = q_ref.shape[1] // SLAB
    mask = causal(block)
    places = (own_ref, message_ref.at[: 2 * block], far_ref, message_ref.at[2 * block : 4 * block])
    for r, out in enumerate(places):
        q, k, v = (ref[:, cut(member(r), width)] for ref in (q_ref, k_ref, v_ref))
        out[:block, :] = q
        for h in range(width // DH):
            attend = jnp.where(mask, dot(q[:, head(h)], k[:, head(h)], 1, 1), 0.0).astype(BF16)
            attend_ref[r, h] = attend
            out[block:, head(h)] = dot(attend, v[:, head(h)], 1, 0).astype(BF16)
    for i in range(c_ref.shape[1] // width):
        message_ref[part(4 + i, block), :] = c_ref[:, part(i, width)]


def cross_kernel(near_ref, got_ref, out_ref):
    out_ref[part(0, DH), :] = near_ref[...]
    out_ref[part(1, DH), :] = got_ref[part(1, DH), :]


def total_kernel(own_ref, far_ref, near_ref, out_ref):
    total = own_ref[...] + far_ref[part(0, DH), :].astype(F32)
    total = total + near_ref[part(0, DH), :].astype(F32) + near_ref[part(1, DH), :].astype(F32)
    out_ref[...] = total.astype(BF16)


def pair_kernel(message_ref, far_ref, out_ref):
    size = far_ref.shape[0]
    out_ref[:size, :] = far_ref[...]
    out_ref[size:, :] = message_ref[part(1, size), :]


def add_kernel(own_ref, got_ref, out_ref):
    out_ref[...] = (own_ref[...].astype(F32) + got_ref[...].astype(F32)).astype(out_ref.dtype)


def dnormed_kernel(groups, members, *refs):
    cots, weights = refs[: len(members)], refs[len(members) : len(members) + groups]
    dnormed_ref, cot_ref = refs[len(members) + groups :]
    _, block, outputs = cot_ref.shape
    width = dnormed_ref.shape[2]
    rows = weights[0].shape[1]
    me = lax.axis_index("dp")
    for i, (r, ref) in enumerate(zip(members, cots)):
        if r == 1:
            for p in range(outputs // width):
                cot_ref[i, :, part(p, width)] = ref[part(4 + p, block), :]
        else:
            cot_ref[i] = ref[...]
        total = dot(cot_ref[i, :, cut(me, rows)], weights[0][0], 1, 0)
        for j in range(1, groups):
            total = total + dot(cot_ref[i, :, cut(jnp.bitwise_xor(me, j), rows)], weights[j][0], 1, 0)
        dnormed_ref[i] = total


def base_kernel(*refs):
    refs[-1][...] = from_slabs(False, refs[:-1])


def from_slabs(backward, refs):
    slab = lax.div(lax.axis_index("seq"), SLAB)
    total = jnp.zeros(refs[0].shape, F32)
    for i, ref in enumerate(refs):
        bit = lax.rem(lax.div(slab, 1 << i), 2)
        total = total + jnp.where(bit == (0 if backward else 1), ref[...].astype(F32), 0.0)
    return total


def mixed_kernel(
    own_ref, message_ref, token_far, own_state, far_state, near_state, base_ref,
    normed_ref, mixed_ref, prior_ref, running,
):
    _, block, width = normed_ref.shape
    size = 2 * block
    tokens = (own_ref, message_ref.at[:size], token_far.at[:size], token_far.at[size:])
    running[member(0)] = own_state[...]
    running[member(1)] = near_state[part(0, DH), :].astype(F32)
    running[member(2)] = far_state[part(0, DH), :].astype(F32)
    running[member(3)] = near_state[part(1, DH), :].astype(F32)
    total = base_ref[...]
    for p in range(SLAB):
        total, running[p] = total + running[p], total
    for r in range(SLAB):
        prior = running[member(r)].astype(BF16)
        prior_ref[r] = prior
        for h in range(width // DH):
            q = tokens[r][:block, head(h)]
            mixed = tokens[r][block:, head(h)].astype(F32) + dot(q, prior[:, head(h)], 1, 0)
            scale = lax.rsqrt(jnp.mean(mixed * mixed, axis=-1, keepdims=True) + EPSILON)
            mixed_ref[r, :, head(h)] = mixed
            normed_ref[r, :, head(h)] = (mixed * scale).astype(BF16)


def middle_kernel(
    own_ref, message_ref, token_far, mixed_ref, prior_ref, dnormed_a, dnormed_b,
    near_ref, far_ref, u_ref, slab_ref,
):
    _, block, width = mixed_ref.shape
    size = 2 * block
    tokens = (own_ref, message_ref.at[:size], token_far.at[:size], token_far.at[size:])
    sums = [jnp.zeros((DH, DH), F32)] * (width // DH)
    for r in range(SLAB):
        out = (near_ref, far_ref)[r // 2].at[part(r % 2, block + DH)]
        out[block:, :] = prior_ref[r]
        for h in range(width // DH):
            mixed = mixed_ref[r, :, head(h)]
            scale = lax.rsqrt(jnp.mean(mixed * mixed, axis=-1, keepdims=True) + EPSILON)
            normed = mixed * scale
            dnormed = dnormed_a[r, :, head(h)] if r < 3 else dnormed_b[0, :, head(h)]
            along = jnp.mean(dnormed * normed, axis=-1, keepdims=True)
            dmixed = ((dnormed - normed * along) * scale).astype(BF16)
            out[:block, head(h)] = dmixed
            u = dot(tokens[r][:block, head(h)], dmixed, 0, 0)
            u_ref[r, :, head(h)] = u
            sums[h] = sums[h] + u
    for h in range(width // DH):
        slab_ref[:, head(h)] = sums[h].astype(BF16)


def later_kernel(*refs):
    *behind, u_ref, near_ref, far_ref, running = refs
    for r in range(SLAB):
        running[member(r)] = u_ref[r]
    total = from_slabs(True, behind)
    for p in reversed(range(SLAB)):
        total, running[p] = total + running[p], total
    for r in range(SLAB):
        (near_ref, far_ref)[r // 2][part(r % 2, DH), :] = running[member(r)].astype(BF16)


def relay_kernel(near_ref, far_ref, out_ref):
    size = near_ref.shape[0] // 2
    out_ref[:size, :] = near_ref[size:, :]
    out_ref[size:, :] = far_ref[size:, :]


def arrived(near_ref, far_ref, core_ref):
    size = near_ref.shape[0] // 2
    first, second = slice(0, size), slice(size, 2 * size)
    return near_ref.at[first], core_ref.at[first], far_ref.at[first], core_ref.at[second]


def late_kernel(near_ref, far_ref, core_ref, q_ref, k_ref, v_ref, attend_ref, gq_ref, gk_ref, gv_ref):
    backs = arrived(near_ref, far_ref, core_ref)
    block, width = q_ref.shape[0], near_ref.shape[1]
    mask = causal(block)
    for r in range(SLAB):
        at = cut(member(r), width)
        q, k, v = q_ref[:, at], k_ref[:, at], v_ref[:, at]
        gqs, gks, gvs = [], [], []
        for h in range(width // DH):
            dmixed, prior = backs[r][:block, head(h)], backs[r][block:, head(h)]
            back = jnp.where(mask, dot(dmixed, v[:, head(h)], 1, 1), 0.0).astype(BF16)
            gqs.append(dot(back, k[:, head(h)], 1, 0) + dot(dmixed, prior, 1, 1))
            gks.append(dot(back, q[:, head(h)], 0, 0))
            gvs.append(dot(attend_ref[r, h], dmixed, 0, 0))
        gq_ref[:, at] = jnp.concatenate(gqs, axis=1).astype(BF16)
        gk_ref[r] = jnp.concatenate(gks, axis=1)
        gv_ref[r] = jnp.concatenate(gvs, axis=1)


def output_kernel(near_ref, back_far, core_ref, q_ref, own_ref, message_ref, far_ref, weight_ref, *refs):
    *far, out_ref, normed_ref = refs
    backs = arrived(near_ref, back_far, core_ref)
    block, width = q_ref.shape[0], near_ref.shape[1]
    rows = weight_ref.shape[0]
    me = lax.axis_index("dp")
    withins = (own_ref.at[part(1, block)], message_ref.at[part(1, block)],
               far_ref.at[part(1, block)], message_ref.at[part(3, block)])
    totals = [jnp.zeros((block, rows), F32)] * (len(far) // 2)
    for r in range(SLAB):
        at = cut(member(r), width)
        q = q_ref[:, at]
        normeds = []
        for h in range(width // DH):
            mixed = withins[r][:, head(h)].astype(F32) + dot(q[:, head(h)], backs[r][block:, head(h)], 1, 0)
            scale = lax.rsqrt(jnp.mean(mixed * mixed, axis=-1, keepdims=True) + EPSILON)
            normeds.append(mixed * scale)
        normed = jnp.concatenate(normeds, axis=1).astype(BF16)
        normed_ref[:, at] = normed
        for j in range(len(totals)):
            totals[j] = totals[j] + dot(normed, far[2 * j + r % 2][r // 2], 1, 1)
    out_ref[:, cut(me, rows)] = dot(normed_ref[...], weight_ref[...], 1, 1).astype(BF16)
    for j, total in enumerate(totals, 1):
        out_ref[:, cut(jnp.bitwise_xor(me, j), rows)] = total.astype(BF16)


def last_kernel(near_ref, far_ref, core_ref, k_ref, v_ref, gk_part, gv_part, gk_ref, gv_ref):
    laters = arrived(near_ref, far_ref, core_ref)
    width = near_ref.shape[1]
    for r in range(SLAB):
        at = cut(member(r), width)
        k, v = k_ref[:, at], v_ref[:, at]
        gks, gvs = [], []
        for h in range(width // DH):
            later = laters[r][:, head(h)]
            gks.append(gk_part[r, :, head(h)] + dot(v[:, head(h)], later, 1, 1))
            gvs.append(gv_part[r, :, head(h)] + dot(k[:, head(h)], later, 1, 0))
        gk_ref[:, at] = jnp.concatenate(gks, axis=1).astype(BF16)
        gv_ref[:, at] = jnp.concatenate(gvs, axis=1).astype(BF16)


def product_kernel(slabs, j, cot_a, cot_b, normed_ref, out_ref):
    me = lax.axis_index("dp")
    slab = lax.div(lax.axis_index("seq"), SLAB)
    rows = out_ref.shape[0] // slabs
    for d in range(slabs):
        at = jnp.bitwise_xor(me, j) * slabs + jnp.bitwise_xor(slab, d)
        total = dot(cot_b[0, :, cut(at, rows)], normed_ref[3], 0, 0)
        for r in range(3):
            total = total + dot(cot_a[r, :, cut(at, rows)], normed_ref[r], 0, 0)
        out_ref[part(d, rows), :] = total.astype(out_ref.dtype)


def split_kernel(own_ref, got_ref, keep_ref, send_ref):
    rows = keep_ref.shape[0] // 2
    for i in range(4):
        total = own_ref[part(i, rows), :] + got_ref[part(i, rows), :].astype(F32)
        out = (keep_ref, send_ref)[i % 2]
        out[part(i // 2, rows), :] = total.astype(out.dtype)


def split_again_kernel(own_ref, got_ref, keep_ref, send_ref):
    rows = keep_ref.shape[0]
    for i, out in enumerate((keep_ref, send_ref)):
        total = own_ref[part(i, rows), :] + got_ref[part(i, rows), :].astype(F32)
        out[...] = total.astype(out.dtype)


def share_kernel(own_ref, got_ref, keep_ref, send_ref, total_ref):
    total_ref[...] = own_ref[...] + got_ref[...].astype(F32)
    rows = keep_ref.shape[0] // 2
    for i, r in enumerate((0, 1)):
        keep_ref[part(i, rows), :] = total_ref[cut(member(r), rows), :].astype(BF16)
    for i, r in enumerate((2, 3)):
        send_ref[part(i, rows), :] = total_ref[cut(member(r), rows), :].astype(BF16)


def pass_kernel(own_ref, got_ref, keep_ref, send_ref):
    rows = own_ref.shape[0] // 2
    for i, ref in enumerate((own_ref, got_ref)):
        keep_ref[part(i, rows), :] = ref[:rows, :]
        send_ref[part(i, rows), :] = ref[rows:, :]


def finish_kernel(factor, keep_ref, got_ref, out_ref):
    rows, width = out_ref.shape[0], keep_ref.shape[1]
    for i, ref in enumerate((keep_ref, got_ref)):
        for j in range(2):
            out_ref[:, cut(member(i + 2 * j), width)] = ref[part(j, rows), :].astype(F32) * factor


def local(queries, keys, values, cotangent, out_weight, *, dp, seq):
    call = Chain()
    local_seqs, block, features = queries.shape
    outputs = cotangent.shape[2]
    rows = local_seqs * block
    slabs = seq // SLAB
    width = features // SLAB
    heads = width // DH
    q, k, v = (x.reshape(rows, features) for x in (queries, keys, values))
    cot = cotangent.reshape(rows, outputs)
    factor = 1.0 / math.sqrt(rows * dp * seq)
    near = functools.partial(flip, axis="seq", count=seq)

    def doubling(total, cost=1):
        found = []
        bits = SLAB
        while bits < seq:
            if found:
                (total,) = call(add_kernel, [(total.shape, BF16)], total, found[-1], cost=cost)
            found.append(near(total, bits=bits))
            bits *= 2
        return found, total

    def scratch(*arrays):
        return [pltpu.VMEM(x.shape, BF16) for x in arrays] + [pltpu.SemaphoreType.DMA((len(arrays),))]

    own_state, near_state, far_state, columns = call(
        front_kernel,
        [((DH, width), F32), ((DH, width), BF16), ((2 * DH, width), BF16),
         ((2, out_weight.shape[0], width), BF16)],
        k, v, out_weight, far=True, scratch=scratch(k, v)[:2] + [pltpu.SemaphoreType.DMA((4,))],
    )
    far_state = near(far_state, bits=2)
    w_far = [flip(columns, "dp", dp, j) for j in range(1, dp)]
    attend, own_tokens, message, far_tokens = call(
        pack_kernel,
        [((SLAB, heads, rows, rows), BF16), ((2 * rows, width), BF16),
         (((4 + outputs // width) * rows, width), BF16), ((2 * rows, width), BF16)],
        q, k, v, cot,
    )
    cot_y = near(cot, bits=2)
    near_tokens, sent = message, (message, far_tokens)
    message = near(message, bits=1)
    (near_state,) = call(
        cross_kernel, [((2 * DH, width), BF16)], near_state, far_state, cost=5 * 10**9
    )
    near_state = near(near_state, bits=1)
    (slab_kv,) = call(total_kernel, [((DH, width), BF16)], own_state, far_state, near_state)
    (far_tokens,) = call(pair_kernel, [((4 * rows, width), BF16)], message, far_tokens)
    cot_yc = near(after(cot_y, far_tokens), bits=1)
    far_tokens = near(far_tokens, bits=2)
    before, _ = doubling(slab_kv, 22 * 10**8)
    weights = (columns, *w_far)
    dnormed, cots = call(
        functools.partial(dnormed_kernel, dp, (0, 1, 2)),
        [((3, rows, width), F32), ((3, rows, outputs), BF16)], cot, message, cot_y, *weights,
    )
    dnormed_b, cot_b = call(
        functools.partial(dnormed_kernel, dp, (3,)),
        [((1, rows, width), F32), ((1, rows, outputs), BF16)], cot_yc, *weights,
    )
    (base,) = call(base_kernel, [((DH, width), F32)], *before, cost=10**9)
    w_all = [x for w in w_far for x in (w, near(after(w, dnormed), bits=1))]
    tokens = (own_tokens, message, far_tokens)
    normed, mixed, prior = call(
        mixed_kernel,
        [((SLAB, rows, width), BF16), ((SLAB, rows, width), F32), ((SLAB, DH, width), BF16)],
        *tokens, own_state, far_state, near_state, base, cost=10**10,
        scratch=[pltpu.VMEM((SLAB, DH, width), F32)],
    )
    tuned = dp == 2 and slabs == 4 and outputs // (dp * seq) % 8 == 0
    piece = outputs // (dp * slabs)
    if tuned:
        (send,) = call(
            functools.partial(product_kernel, slabs, 1), [((outputs // dp, width), BF16)], cots, cot_b, normed
        )
        got = flip(send, "dp", dp, 1)
    back, back_far, u, slab_u = call(
        middle_kernel,
        [((2 * rows + 2 * DH, width), BF16)] * 2 + [((SLAB, DH, width), F32), ((DH, width), BF16)],
        *tokens, mixed, prior, dnormed, dnormed_b,
    )
    if tuned:
        (keep,) = call(
            functools.partial(product_kernel, slabs, 0), [((outputs // dp, width), F32)], cots, cot_b, normed
        )
    back_far = near(back_far, bits=2)
    if tuned:
        keep, send = call(
            split_kernel, [((2 * piece, width), F32), ((2 * piece, width), BF16)], keep, got, wait=w_all[1::2]
        )
        got = near(send, bits=SLAB)
    behind, last_u = doubling(slab_u, 10**9)
    (send,) = call(relay_kernel, [((2 * rows + 2 * DH, width), BF16)], back, back_far)
    back_core = near(send, bits=1)
    if tuned:
        keep, send = call(
            split_again_kernel, [((piece, width), F32), ((piece, width), BF16)], keep, got, cost=3 * 10**9
        )
        got = near(send, bits=2 * SLAB)
    later, later_far = call(
        later_kernel, [((2 * DH, width), BF16)] * 2, *behind, u,
        scratch=[pltpu.VMEM((SLAB, DH, width), F32)],
    )
    later_far = near(later_far, bits=2)
    gq, gk_part, gv_part = call(
        late_kernel,
        [((rows, features), BF16), ((SLAB, rows, width), F32), ((SLAB, rows, width), F32)],
        back, back_far, back_core, q, k, v, attend,
    )
    if tuned:
        keep, share = call(
            share_kernel, [((piece // 2, width), BF16)] * 2, keep, got, cost=3 * 10**9,
            scratch=[pltpu.VMEM((piece, width), F32)],
        )
        got = near(share, bits=2)
    output, own_normed = call(
        output_kernel, [((rows, outputs), BF16), ((rows, features), BF16)],
        back, back_far, back_core, q, own_tokens, *sent, out_weight, *w_all, end=True,
    )
    (send,) = call(
        relay_kernel, [((2 * DH, width), BF16)], later, later_far,
        wait=[pltpu.with_memory_space_constraint(output, pltpu.HBM)],
    )
    later_core = near(send, bits=1)
    if tuned:
        keep, share = call(
            pass_kernel, [((piece // 2, width), BF16)] * 2, keep, got, cost=3 * 10**9,
            wait=[pltpu.with_memory_space_constraint(x, pltpu.HBM) for x in (output,)],
        )
        got = near(share, bits=1)
    gk, gv = call(
        last_kernel, [((rows, features), BF16)] * 2,
        later, later_far, later_core, k, v, gk_part, gv_part, end=True,
    )
    if tuned:
        (grad_weight,) = call(
            functools.partial(finish_kernel, factor),
            [((piece // SLAB, features), F32)], keep, got, end=True,
            wait=[pltpu.with_memory_space_constraint(gk, pltpu.HBM)],
        )
    else:
        partial = dot(cot, own_normed, 0, 0) * factor
        grad_weight = lax.psum_scatter(partial, ("dp", "seq"), scatter_dimension=0, tiled=True)
    shape = queries.shape
    return (
        output.reshape(cotangent.shape), gq.reshape(shape), gk.reshape(shape), gv.reshape(shape),
        grad_weight,
    )


def solution(mesh):
    dp, seq = mesh.shape["dp"], mesh.shape["seq"]
    return jax.shard_map(
        functools.partial(local, dp=dp, seq=seq),
        mesh=mesh,
        in_specs=(P("dp", "seq", None),) * 4 + (P("dp", None),),
        out_specs=(P("dp", "seq", None),) * 4 + (P(("dp", "seq"), None),),
        check_vma=False,
    )
```
